32 devices in a mesh: groups: 2 (over y), dp: 2 (over x), seq: 4 (over z), mp: 2 (over core).
Axes of the slice: x: 2, y: 2, z: 4, core: 2. Of those that a mesh axis runs over, the one named last changes fastest.
Arguments:
- queries: bfloat16 [4, 512, 1024], P(('groups', 'dp'), 'seq', 'mp'), parts along dimension 0, may hold values from -6 to 6
- keys: bfloat16 [4, 512, 1024], P(('groups', 'dp'), 'seq', 'mp'), parts along dimension 0, may hold values from -6 to 6
- values: bfloat16 [4, 512, 1024], P(('groups', 'dp'), 'seq', 'mp'), parts along dimension 0, may hold values from -6 to 6
- cotangent: bfloat16 [4, 512, 1024], P(('groups', 'dp'), 'seq', 'mp'), parts along dimension 0, may hold values from -6 to 6
- conv_weight: float32 [31, 1024], P(None, 'mp'), may hold values from -2 to 2
- rec_lengths: int32 [4, 16], P(('groups', 'dp')), parts along dimension 0, may hold values from 1 to 320, 512 in all within a row
Outputs:
- mixed: bfloat16 [4, 512, 1024], P(('groups', 'dp'), 'seq', 'mp'), parts along dimension 0
- grad_queries: bfloat16 [4, 512, 1024], P(('groups', 'dp'), 'seq', 'mp'), parts along dimension 0
- grad_keys: bfloat16 [4, 512, 1024], P(('groups', 'dp'), 'seq', 'mp'), parts along dimension 0
- grad_values: bfloat16 [4, 512, 1024], P(('groups', 'dp'), 'seq', 'mp'), parts along dimension 0
- grad_kernel: float32 [62, 1024], P('groups', 'mp'), parts along dimension 0
The draws below stay inside these ranges and needn't reach their ends.
There are 2 independent parts, one for each index of `groups`. The reference program is written for one: setup_inputs(seed, part) draws one part's arguments, and reference() takes and returns one part's arrays. A program takes and returns all parts, laid end to end along the dimension named above; an argument that names none is the same for every part. Nothing has to cross between parts.
Inputs may be any that keep to these rules, and one draw needn't show every extreme that they name: `rec_lengths`: each row holds the lengths of 16 recordings in the order they are packed; they sum to 512 and the longest is 320.
All inputs are finite; a program needn't handle non-finite values.
Results may differ from the reference program's by a relative error of at most 0.012.
The reference program's roundings to bfloat16 on the way (of `soft_rounded`, `attended`, `conv_grad`, `grad_attended` and `mixed_grad`) count: a program that leaves them out, or rounds other values in their place, can miss the bound.
Values may be sent and summed in bfloat16 or wider, within the bound.
No kernel may reach another device: no remote copies, remote signals or barrier semaphores. Data moves between devices by JAX's collectives and lax.ppermute only.
A program may use at most 64 MiB of HBM per device.

```python
import math
import jax
import jax.numpy as jnp
import numpy as np
from jax import lax

D = 1024
HEADS = 16
HDIM = 64
KERNEL = 31
HALF = 15
RECS = 16
BATCH = 2
LENGTH = 512
MOST = 320


def draw_queries(key, part):
    key = jax.random.fold_in(key, 11)
    first_key, second_key = jax.random.split(key)
    base_values = 1.2 * jax.random.normal(first_key, (BATCH, LENGTH, D), jnp.float32)
    column_scale = jnp.exp(jax.random.uniform(second_key, (D,), jnp.float32, math.log(0.3), math.log(3.0)))
    values_out = jnp.clip(base_values * column_scale, -6.0, 6.0)
    return values_out.astype(jnp.bfloat16)


def draw_keys(key, part):
    key = jax.random.fold_in(key, 23)
    first_key, second_key = jax.random.split(key)
    base_values = jax.random.normal(first_key, (BATCH, LENGTH, D), jnp.float32)
    row_scale = jnp.exp(jax.random.uniform(second_key, (BATCH, LENGTH, 1), jnp.float32, math.log(0.4), math.log(4.0)))
    values_out = jnp.clip(base_values * row_scale, -6.0, 6.0)
    return values_out.astype(jnp.bfloat16)


def block_levels(rng, shape, pieces, smallest, high):
    factor_of = 1.0
    for position, blocks in pieces:
        steps = jax.random.uniform(jax.random.fold_in(jax.random.fold_in(rng, 6), position), (blocks,), jnp.float32, smallest / len(pieces), high / len(pieces))
        factor_of = factor_of * jnp.repeat(jnp.exp(steps), shape[position] // blocks).reshape((-1,) + (1,) * (len(shape) - 1 - position))
    return factor_of


def split_up(count, total, most, lean):
    weights = [(1 << 20) // math.isqrt(rank ** lean) + 1 for rank in range(2, count + 1)]
    surplus, given = total - most - (count - 1), [1] * (count - 1)
    while surplus > 0:
        free = [i for i in range(count - 1) if given[i] < most]
        mass, budget = sum([weights[i] for i in free]), surplus
        for i in free:
            more = min(most - given[i], max(1, budget * weights[i] // mass), surplus)
            given[i] = given[i] + more
            surplus = surplus - more
    return np.array([most] + given)


def ragged_sizes(stream_key, amount, total, reach, slope):
    if amount == 2:
        one = jax.random.randint(stream_key, (), max(1, total - reach), min(reach, total - 1) + 1)
        return jnp.stack([one, total - one])
    sizes = jnp.asarray(split_up(amount, total, reach, slope), jnp.int32)
    pairs = (amount - 1) // 2
    giver, sink = sizes[1:1 + 2 * pairs:2], sizes[2:2 + 2 * pairs:2]
    room = jnp.minimum(giver - 1, reach - sink)
    passed = jax.random.randint(jax.random.fold_in(stream_key, 1), (pairs,), 0, 1 << 20) % (room + 1)
    sizes = sizes.at[1:1 + 2 * pairs:2].set(giver - passed).at[2:2 + 2 * pairs:2].set(sink + passed)
    return sizes[jax.random.permutation(jax.random.fold_in(stream_key, 2), amount)]


def scatter_about(stream_key, dims, width, bound, cuts=(), kind=jnp.bfloat16):
    result = jax.random.normal(stream_key, dims, jnp.float32) * width
    if len(cuts) > 0:
        result = block_levels(stream_key, dims, cuts, -0.22, 0.18) * result
    return jnp.clip(result, min=-bound, max=bound).astype(kind)


def setup_inputs(seed: int = 0, part: int = 0) -> dict:
    streams_of = jax.random.split(jax.random.key(seed), 7)
    part_splits = jax.random.split(jax.random.fold_in(streams_of[6], part), 7)
    queries = draw_queries(jax.random.fold_in(jax.random.fold_in(streams_of[6], part), 71), part)
    keys = draw_keys(jax.random.fold_in(jax.random.fold_in(streams_of[6], part), 71), part)
    values = scatter_about(part_splits[2], (BATCH, LENGTH, D), 1.0, 6.0, ((0, 2), (1, 4), (2, 2)))
    cotangent = scatter_about(part_splits[3], (BATCH, LENGTH, D), 1.0, 6.0, ((0, 2), (1, 4), (2, 2)))
    conv_weight = scatter_about(streams_of[4], (KERNEL, D), 8 ** -0.5, 2.0, ((1, 2),), jnp.float32)
    rec_lengths = jax.vmap(lambda own: ragged_sizes(own, RECS, LENGTH, MOST, 2))(jax.random.split(part_splits[5], BATCH)).reshape((BATCH, RECS)).astype(jnp.int32)
    return dict(queries=queries, keys=keys, values=values, cotangent=cotangent, conv_weight=conv_weight, rec_lengths=rec_lengths)


NEGATIVE_FILL = -1e+30

def segment_ids(lengths_row, positions):
    record_ends = jnp.cumsum(lengths_row, dtype=jnp.int32)
    return lax.optimization_barrier(jnp.sum((record_ends[None, :] <= positions[:, None]).astype(jnp.int32), axis=1))

def split_heads(array):
    return array.reshape(BATCH, LENGTH, HEADS, HDIM).transpose(0, 2, 1, 3).reshape(BATCH * HEADS, LENGTH, HDIM)

def join_heads(array):
    return array.reshape(BATCH, HEADS, LENGTH, HDIM).transpose(0, 2, 1, 3).reshape(BATCH, LENGTH, D)

def masked_scores(query_head, key_head, segment_row):
    score_scale = 1.0 / math.sqrt(HDIM)
    same_record = segment_row[:, None] == segment_row[None, :]
    raw_scores = jnp.dot(query_head, key_head.T, preferred_element_type=jnp.float32) * score_scale
    return jnp.where(same_record, raw_scores, NEGATIVE_FILL)

def head_forward(head_item):
    query_head, key_head, value_head, segment_row = head_item
    scores = masked_scores(query_head, key_head, segment_row)
    top_score = lax.optimization_barrier(jnp.max(scores, axis=1))
    log_total = top_score + jnp.log(lax.optimization_barrier(jnp.sum(jnp.exp(scores - top_score[:, None]), axis=1)))
    soft_rounded = jnp.exp(scores - log_total[:, None]).astype(jnp.bfloat16)
    return (jnp.dot(soft_rounded, value_head, preferred_element_type=jnp.float32), log_total)

def head_backward(head_item):
    query_head, key_head, value_head, segment_row, log_total, grad_head, attended_head = head_item
    score_scale = 1.0 / math.sqrt(HDIM)
    scores = masked_scores(query_head, key_head, segment_row)
    soft_weights = jnp.exp(scores - log_total[:, None])
    soft_rounded = soft_weights.astype(jnp.bfloat16)
    row_delta = lax.optimization_barrier(jnp.sum(grad_head.astype(jnp.float32) * attended_head.astype(jnp.float32), axis=1))
    slopes = jnp.dot(grad_head, value_head.T, preferred_element_type=jnp.float32)
    mixed_grad = (soft_weights * (slopes - row_delta[:, None])).astype(jnp.bfloat16)
    grad_query = (jnp.dot(mixed_grad, key_head, preferred_element_type=jnp.float32) * score_scale).astype(jnp.bfloat16)
    grad_key = (jnp.dot(mixed_grad.T, query_head, preferred_element_type=jnp.float32) * score_scale).astype(jnp.bfloat16)
    grad_value = jnp.dot(soft_rounded.T, grad_head, preferred_element_type=jnp.float32).astype(jnp.bfloat16)
    return (grad_query, grad_key, grad_value)

def reference(queries, keys, values, cotangent, conv_weight, rec_lengths):
    positions = jnp.arange(LENGTH, dtype=jnp.int32)
    segments = jax.vmap(lambda lengths_row: segment_ids(lengths_row, positions))(rec_lengths)
    segment_items = jnp.repeat(segments, HEADS, axis=0)
    query_items = split_heads(queries)
    key_items = split_heads(keys)
    value_items = split_heads(values)
    head_outputs, log_totals = lax.map(head_forward, (query_items, key_items, value_items, segment_items))
    attended = join_heads(head_outputs).astype(jnp.bfloat16)
    padded_segments = jnp.pad(segments, ((0, 0), (HALF, HALF)), constant_values=-1)
    padded_attended = jnp.pad(attended, ((0, 0), (HALF, HALF), (0, 0)))
    conv_pre = jnp.zeros((BATCH, LENGTH, D), jnp.float32)
    for tap_index in range(KERNEL):
        tap_mask = (padded_segments[:, tap_index:tap_index + LENGTH] == segments)[:, :, None]
        shifted = padded_attended[:, tap_index:tap_index + LENGTH].astype(jnp.float32)
        conv_pre = conv_pre + jnp.where(tap_mask, conv_weight[tap_index] * shifted, 0.0)
    gate_value = jax.nn.sigmoid(conv_pre)
    mixed = (conv_pre * gate_value).astype(jnp.bfloat16)
    conv_grad = (cotangent.astype(jnp.float32) * gate_value * (1.0 + conv_pre * (1.0 - gate_value))).astype(jnp.bfloat16)
    padded_grad = jnp.pad(conv_grad, ((0, 0), (HALF, HALF), (0, 0)))
    grad_attended = jnp.zeros((BATCH, LENGTH, D), jnp.float32)
    kernel_rows = []
    for tap_index in range(KERNEL):
        back_start = 2 * HALF - tap_index
        back_mask = (padded_segments[:, back_start:back_start + LENGTH] == segments)[:, :, None]
        grad_attended = grad_attended + jnp.where(back_mask, conv_weight[tap_index] * padded_grad[:, back_start:back_start + LENGTH].astype(jnp.float32), 0.0)
        tap_mask = (padded_segments[:, tap_index:tap_index + LENGTH] == segments)[:, :, None]
        product = conv_grad.astype(jnp.float32) * padded_attended[:, tap_index:tap_index + LENGTH].astype(jnp.float32)
        kernel_rows.append(lax.optimization_barrier(jnp.sum(jnp.where(tap_mask, product, 0.0), axis=(0, 1))))
    grad_kernel = jnp.stack(kernel_rows)
    grad_attended = grad_attended.astype(jnp.bfloat16)
    grad_query, grad_key, grad_value = lax.map(head_backward, (query_items, key_items, value_items, segment_items, log_totals, split_heads(grad_attended), split_heads(attended)))
    return (mixed, join_heads(grad_query), join_heads(grad_key), join_heads(grad_value), grad_kernel)
```

```python
import functools
import math

import jax
import jax.numpy as jnp
from jax import lax
from jax.experimental import pallas as pl
from jax.experimental.pallas import tpu as pltpu
from jax.sharding import PartitionSpec as P

HDIM = 64
KERNEL = 31
HALF = 15


NEGATIVE_FILL = -1e30


def extended(block, sides, width):
    for axis, dim in sides:
        count = lax.axis_size(axis)
        forward = [(i, i + 1) for i in range(count - 1)]
        backward = [(target, source) for source, target in forward]
        low = lax.ppermute(
            lax.slice_in_dim(block, block.shape[dim] - width, None, axis=dim), axis, forward
        )
        high = lax.ppermute(lax.slice_in_dim(block, 0, width, axis=dim), axis, backward)
        block = jnp.concatenate([low, block, high], axis=dim)
    return block


def pick_block(total_rows):
    for candidate in (512, 256, 128):
        return candidate
    return total_rows


def over_blocks(total_rows, advance, initial):
    block_rows = pick_block(total_rows)
    block_count = total_rows // block_rows
    if block_count == 1:
        return advance(initial, 0, block_rows)
    return lax.fori_loop(
        0,
        block_count,
        lambda number, running: advance(running, number * block_rows, block_rows),
        initial,
    )


def when_shared(compute, running):
    result = compute(running)
    return result


def on_device(queries, keys, values, cotangent, conv_weight, rec_lengths):
    frames = queries.shape[1]
    channels = queries.shape[2]
    local_heads = channels // HDIM
    score_scale = 1.0 / math.sqrt(HDIM)
    length_all = frames * lax.axis_size("seq")
    offset = lax.axis_index("seq") * frames
    record_ends = jnp.cumsum(rec_lengths[0], dtype=jnp.int32)

    def segment_of(positions):
        return jnp.sum((record_ends[None, :] <= positions[:, None]).astype(jnp.int32), axis=1)

    own_seg = segment_of(offset + jnp.arange(frames, dtype=jnp.int32))

    def to_heads(array):
        return array.reshape(array.shape[0], local_heads, HDIM).transpose(1, 0, 2)

    def from_heads(array):
        return array.transpose(1, 0, 2).reshape(array.shape[1], channels)

    q_heads = to_heads(queries[0])
    k_heads = to_heads(keys[0])
    v_heads = to_heads(values[0])

    def over_rows(advance, initial, members, first_row):
        total_rows = members[0].shape[1]

        def one_block(running, block_start, block_rows):
            sliced = tuple(
                (lax.dynamic_slice_in_dim(member, block_start, block_rows, 1) for member in members)
            )
            other_seg = segment_of(
                first_row + block_start + jnp.arange(block_rows, dtype=jnp.int32)
            )
            return when_shared(lambda current: advance(current, sliced, other_seg), running)

        return over_blocks(total_rows, one_block, initial)

    def query_scores(key_block, key_seg):
        raw_scores = (
            jnp.einsum("hqd,hkd->hqk", q_heads, key_block, preferred_element_type=jnp.float32)
            * score_scale
        )
        return jnp.where((own_seg[:, None] == key_seg[None, :])[None], raw_scores, NEGATIVE_FILL)

    def stats_step(running, sliced, key_seg):
        top_now, total_now = running
        scores = query_scores(sliced[0], key_seg)
        top_new = jnp.maximum(top_now, jnp.max(scores, axis=2))
        total_new = total_now * jnp.exp(top_now - top_new) + jnp.sum(
            jnp.exp(scores - top_new[:, :, None]), axis=2
        )
        return (top_new, total_new)

    stats_init = (
        jnp.full((local_heads, frames), NEGATIVE_FILL, jnp.float32),
        jnp.zeros((local_heads, frames), jnp.float32),
    )
    gathered = (
        lax.all_gather(keys, "seq", axis=1, tiled=True),
        lax.all_gather(values, "seq", axis=1, tiled=True),
    )
    key_whole = to_heads(gathered[0][0])
    value_whole = to_heads(gathered[1][0])
    row_stats = over_rows(stats_step, stats_init, (key_whole,), 0)
    log_total = row_stats[0] + jnp.log(row_stats[1])

    def output_step(running, sliced, key_seg):
        scores = query_scores(sliced[0], key_seg)
        soft_rounded = jnp.exp(scores - log_total[:, :, None]).astype(jnp.bfloat16)
        return running + jnp.einsum(
            "hqk,hkd->hqd", soft_rounded, sliced[1], preferred_element_type=jnp.float32
        )

    frame_zeros = jnp.zeros((local_heads, frames, HDIM), jnp.float32)
    attended_sum = over_rows(output_step, frame_zeros, (key_whole, value_whole), 0)
    attended_heads = attended_sum.astype(jnp.bfloat16)
    attended = from_heads(attended_heads)
    padded = extended(attended[None], (("seq", 1),), HALF)
    padded_wide = padded[0].astype(jnp.float32)
    pad_positions = offset - HALF + jnp.arange(frames + 2 * HALF, dtype=jnp.int32)
    inside = jnp.logical_and(pad_positions >= 0, pad_positions < length_all)
    pad_seg = jnp.where(inside, segment_of(pad_positions), -1)
    conv_pre = jnp.zeros((frames, channels), jnp.float32)
    for tap_index in range(KERNEL):
        tap_mask = (pad_seg[tap_index : tap_index + frames] == own_seg)[:, None]
        conv_pre = conv_pre + jnp.where(
            tap_mask, conv_weight[tap_index] * padded_wide[tap_index : tap_index + frames], 0.0
        )
    gate_value = jax.nn.sigmoid(conv_pre)
    mixed = (conv_pre * gate_value).astype(jnp.bfloat16)
    conv_grad = (
        cotangent[0].astype(jnp.float32) * gate_value * (1.0 + conv_pre * (1.0 - gate_value))
    ).astype(jnp.bfloat16)
    padded_grad = extended(conv_grad[None], (("seq", 1),), HALF)
    grad_wide = padded_grad[0].astype(jnp.float32)
    conv_grad_wide = conv_grad.astype(jnp.float32)
    grad_attended = jnp.zeros((frames, channels), jnp.float32)
    kernel_rows = []
    for tap_index in range(KERNEL):
        back_start = 2 * HALF - tap_index
        back_mask = (pad_seg[back_start : back_start + frames] == own_seg)[:, None]
        grad_attended = grad_attended + jnp.where(
            back_mask, conv_weight[tap_index] * grad_wide[back_start : back_start + frames], 0.0
        )
        tap_mask = (pad_seg[tap_index : tap_index + frames] == own_seg)[:, None]
        product = conv_grad_wide * padded_wide[tap_index : tap_index + frames]
        kernel_rows.append(jnp.sum(jnp.where(tap_mask, product, 0.0), axis=0))
    grad_kernel = lax.psum(jnp.stack(kernel_rows), ("dp", "seq"))
    grad_attended = grad_attended.astype(jnp.bfloat16)
    g_heads = to_heads(grad_attended)
    row_delta = jnp.sum(g_heads.astype(jnp.float32) * attended_heads.astype(jnp.float32), axis=2)

    def query_grad_step(running, sliced, key_seg):
        key_block = sliced[0]
        value_block = sliced[1]
        soft_weights = jnp.exp(query_scores(key_block, key_seg) - log_total[:, :, None])
        slopes = jnp.einsum(
            "hqd,hkd->hqk", g_heads, value_block, preferred_element_type=jnp.float32
        )
        mixed_grad = (soft_weights * (slopes - row_delta[:, :, None])).astype(jnp.bfloat16)
        return running + jnp.einsum(
            "hqk,hkd->hqd", mixed_grad, key_block, preferred_element_type=jnp.float32
        )

    grad_query = over_rows(query_grad_step, frame_zeros, (key_whole, value_whole), 0)

    def key_grad_step(running, sliced, query_seg):
        grad_key_now, grad_value_now = running
        query_block = sliced[0]
        grad_block = sliced[1]
        total_block = sliced[2]
        delta_block = sliced[3]
        raw_scores = (
            jnp.einsum("hqd,hkd->hqk", query_block, k_heads, preferred_element_type=jnp.float32)
            * score_scale
        )
        scores = jnp.where(
            (query_seg[:, None] == own_seg[None, :])[None], raw_scores, NEGATIVE_FILL
        )
        soft_weights = jnp.exp(scores - total_block[:, :, None])
        grad_value_new = grad_value_now + jnp.einsum(
            "hqk,hqd->hkd",
            soft_weights.astype(jnp.bfloat16),
            grad_block,
            preferred_element_type=jnp.float32,
        )
        slopes = jnp.einsum("hqd,hkd->hqk", grad_block, v_heads, preferred_element_type=jnp.float32)
        mixed_grad = (soft_weights * (slopes - delta_block[:, :, None])).astype(jnp.bfloat16)
        grad_key_new = grad_key_now + jnp.einsum(
            "hqk,hqd->hkd", mixed_grad, query_block, preferred_element_type=jnp.float32
        )
        return (grad_key_new, grad_value_new)

    all_totals, all_deltas = (
        lax.all_gather(log_total[None], "seq", axis=2, tiled=True),
        lax.all_gather(row_delta[None], "seq", axis=2, tiled=True),
    )
    member = (
        lax.all_gather(queries, "seq", axis=1, tiled=True),
        lax.all_gather(grad_attended[None], "seq", axis=1, tiled=True),
    )
    totals_piece = all_totals[0]
    deltas_piece = all_deltas[0]
    grad_key, grad_value = over_rows(
        key_grad_step,
        (frame_zeros, frame_zeros),
        (to_heads(member[0][0]), to_heads(member[1][0]), totals_piece, deltas_piece),
        jnp.int32(0),
    )
    grad_queries = from_heads(grad_query * score_scale).astype(jnp.bfloat16)[None]
    grad_keys = from_heads(grad_key * score_scale).astype(jnp.bfloat16)[None]
    grad_values = from_heads(grad_value).astype(jnp.bfloat16)[None]
    return (mixed[None], grad_queries, grad_keys, grad_values, grad_kernel)


LANES = 128
PAD = 16
VMEM = pltpu.VMEM
MIB = 1024 * 1024


def mm(left, right):
    return lax.dot_general(
        left, right, (((1,), (0,)), ((), ())), preferred_element_type=jnp.float32
    )


def mm_nt(left, right):
    return lax.dot_general(
        left, right, (((1,), (1,)), ((), ())), preferred_element_type=jnp.float32
    )


def rows_at(block, frames):
    return pl.ds(pl.multiple_of(block * frames, frames), frames)


def lanes_at(block):
    return pl.ds(pl.multiple_of(block * LANES, LANES), LANES)


def pack_kernel(ranks, q_ref, k_ref, v_ref, c_ref, *rest):
    outs, sems = rest[:-1], rest[-1]
    me = lax.axis_index("seq")
    copies = []
    for step in range(1, ranks):
        lanes = lanes_at(me ^ step)
        three, one = outs[step - 1], outs[ranks - 1 + step - 1]
        for place, source in enumerate((q_ref, k_ref, v_ref)):
            copies.append((source.at[0, :, lanes], three.at[place]))
        copies.append((c_ref.at[0, :, lanes], one))
    copies = [
        pltpu.make_async_copy(source, target, sems.at[number])
        for number, (source, target) in enumerate(copies)
    ]
    for copy in copies:
        copy.start()
    for copy in copies:
        copy.wait()


def mask_kernel(length, lens_ref, q_ref, k_ref, v_ref, c_ref, own_ref, col_ref, row_ref, after_ref, before_ref, sems):
    me = lax.axis_index("seq")
    lanes = lanes_at(me)
    copies = [
        pltpu.make_async_copy(source.at[0, :, lanes], own_ref.at[place], sems.at[place])
        for place, source in enumerate((q_ref, k_ref, v_ref, c_ref))
    ]
    for copy in copies:
        copy.start()
    count = lens_ref.shape[1]
    ends = []
    running = jnp.int32(0)
    for number in range(count):
        running = running + lens_ref[0, number]
        ends.append(running)

    row_time = lax.broadcasted_iota(jnp.int32, row_ref.shape, 1)
    row_first = jnp.zeros(row_ref.shape, jnp.int32)
    for end in ends:
        row_first = jnp.where(row_time >= end, end, row_first)
    row_ref[...] = row_first

    chunk = 64

    def some_rows(number, carry):
        base = pl.multiple_of(number * chunk, chunk)
        time = base + lax.broadcasted_iota(jnp.int32, (chunk, LANES), 0)
        first = jnp.zeros((chunk, LANES), jnp.int32)
        last = jnp.full((chunk, LANES), length, jnp.int32)
        for end in ends:
            first = jnp.where(time >= end, end, first)
        for end in reversed(ends):
            last = jnp.where(time < end, end, last)
        rows = pl.ds(base, chunk)
        col_ref[rows, :] = first
        after_ref[rows, :] = last - 1 - time
        before_ref[rows, :] = time - first
        return carry

    lax.fori_loop(0, length // chunk, some_rows, 0)
    for copy in copies:
        copy.wait()


def forward_kernel(ranks, frames, *refs):
    recvs = refs[: ranks - 1]
    own_ref, col_ref, row_ref, after_ref, before_ref, w_ref = refs[ranks - 1 : ranks + 5]
    soft_ref, att_ref, att_t_ref, pre_ref, q_ref, k_t_ref, v_ref = refs[ranks + 5 : ranks + 12]
    k_full, q_full, w_own, w_sem = refs[ranks + 12 :]
    me = lax.axis_index("seq")
    length = ranks * frames
    copy = pltpu.make_async_copy(w_ref.at[:, lanes_at(me)], w_own, w_sem)
    copy.start()
    for place, target in enumerate((q_full, k_full, v_ref)):
        target[rows_at(me, frames), :] = own_ref[place]
        for step in range(1, ranks):
            target[rows_at(me ^ step, frames), :] = recvs[step - 1][place]
    heads = LANES // HDIM
    lane_head = lax.broadcasted_iota(jnp.int32, (1, LANES), 1) // HDIM
    scaled = q_full[...].astype(jnp.float32) * (1.0 / math.sqrt(HDIM))
    for head in range(heads):
        q_ref[head] = jnp.where(lane_head == head, scaled, 0.0).astype(jnp.bfloat16)
    k_t_ref[...] = k_full[...].astype(jnp.float32).T.astype(jnp.bfloat16)
    v_t = v_ref[...].astype(jnp.float32).T.astype(jnp.bfloat16)
    wide = 256
    for head in range(heads):
        for start in range(0, length, wide):
            cols = slice(start, start + wide)
            raw = mm_nt(k_full[...], q_ref[head, cols, :])
            same = jnp.concatenate([col_ref[...]] * (wide // LANES), axis=1) == row_ref[0:1, cols]
            scores = jnp.where(same, raw, NEGATIVE_FILL)
            top = jnp.max(scores, axis=0, keepdims=True)
            powers = jnp.exp(scores - top)
            share = 1.0 / jnp.sum(powers, axis=0, keepdims=True)
            soft = (powers * share).astype(jnp.bfloat16)
            soft_ref[head, :, cols] = soft
            rows = slice(head * HDIM, (head + 1) * HDIM)
            att_t_ref[rows, cols] = mm(v_t[rows], soft).astype(jnp.bfloat16).astype(jnp.float32)
    zeros = jnp.zeros((PAD, LANES), jnp.float32)
    att_ref[0:PAD, :] = zeros
    att_ref[PAD : PAD + length, :] = att_t_ref[...].T
    att_ref[PAD + length :, :] = zeros
    copy.wait()

    chunk = 64

    def some_rows(number, carry):
        base = pl.multiple_of(number * chunk, chunk)
        rows = pl.ds(base, chunk)
        after, before = after_ref[rows, :], before_ref[rows, :]
        total = jnp.zeros((chunk, LANES), jnp.float32)
        for tap in range(KERNEL):
            off = tap - HALF
            piece = att_ref[pl.ds(base + (PAD + off), chunk), :]
            if off > 0:
                piece = jnp.where(after >= off, piece, 0.0)
            if off < 0:
                piece = jnp.where(before >= -off, piece, 0.0)
            total = total + w_own[tap : tap + 1, :] * piece
        pre_ref[rows, :] = total
        return carry

    lax.fori_loop(0, length // chunk, some_rows, 0)


def backward_kernel(ranks, frames, *refs):
    cots = refs[: ranks - 1]
    own_ref, soft_ref, att_ref, att_t_ref, pre_ref, q_ref, k_t_ref, v_ref, after_ref, before_ref, w_ref = refs[
        ranks - 1 : ranks + 10
    ]
    outs = refs[ranks + 10 : 2 * ranks + 10]
    taps_ref = refs[2 * ranks + 10]
    cot, grad_pad, mixed, g_att, res_q, res_k, res_v, tap_sum, w_own, w_sem = refs[2 * ranks + 11 :]
    me = lax.axis_index("seq")
    length = ranks * frames
    copy = pltpu.make_async_copy(w_ref.at[:, lanes_at(me)], w_own, w_sem)
    copy.start()
    cot[rows_at(me, frames), :] = own_ref[3]
    for step in range(1, ranks):
        cot[rows_at(me ^ step, frames), :] = cots[step - 1][...]
    zeros = jnp.zeros((PAD, LANES), jnp.float32)
    grad_pad[0:PAD, :] = zeros
    grad_pad[PAD + length :, :] = zeros
    pre = pre_ref[...]
    gate = jax.nn.sigmoid(pre)
    mixed[...] = (pre * gate).astype(jnp.bfloat16)
    conv_grad = cot[...].astype(jnp.float32) * gate * (1.0 + pre * (1.0 - gate))
    grad_pad[PAD : PAD + length, :] = conv_grad.astype(jnp.bfloat16).astype(jnp.float32)
    tap_sum[...] = jnp.zeros(tap_sum.shape, jnp.float32)
    copy.wait()

    chunk = 64

    def some_rows(number, carry):
        base = pl.multiple_of(number * chunk, chunk)
        rows = pl.ds(base, chunk)
        after, before = after_ref[rows, :], before_ref[rows, :]
        own_att = att_ref[pl.ds(base + PAD, chunk), :]
        total = jnp.zeros((chunk, LANES), jnp.float32)
        for tap in range(KERNEL):
            off = tap - HALF
            piece = grad_pad[pl.ds(base + (PAD - off), chunk), :]
            if off > 0:
                piece = jnp.where(before >= off, piece, 0.0)
            if off < 0:
                piece = jnp.where(after >= -off, piece, 0.0)
            total = total + w_own[tap : tap + 1, :] * piece
            part = (own_att * piece).reshape(chunk // 8, 8, LANES)
            tap_sum[tap] = tap_sum[tap] + jnp.sum(part, axis=0)
        g_att[rows, :] = total.astype(jnp.bfloat16)
        return carry

    lax.fori_loop(0, length // chunk, some_rows, 0)
    taps = jnp.sum(tap_sum[...], axis=1).astype(jnp.bfloat16)
    taps_ref[...] = taps

    heads = LANES // HDIM
    lane_head = lax.broadcasted_iota(jnp.int32, (1, LANES), 1) // HDIM
    g_wide = g_att[...].astype(jnp.float32)
    products_t = (g_wide * att_ref[PAD : PAD + length, :]).T
    g_heads = [jnp.where(lane_head == head, g_wide, 0.0).astype(jnp.bfloat16) for head in range(heads)]
    wide = 256
    grad_v = jnp.zeros((length, LANES), jnp.float32)
    grad_k = jnp.zeros((length, LANES), jnp.float32)
    for head in range(heads):
        rows = slice(head * HDIM, (head + 1) * HDIM)
        delta = jnp.sum(products_t[rows], axis=0, keepdims=True)
        for start in range(0, length, wide):
            cols = slice(start, start + wide)
            soft = soft_ref[head, :, cols]
            slopes = mm_nt(v_ref[...], g_heads[head][cols])
            mixed_grad = (soft.astype(jnp.float32) * (slopes - delta[:, cols])).astype(jnp.bfloat16)
            grad_v = grad_v + mm(soft, g_heads[head][cols])
            grad_k = grad_k + mm(mixed_grad, q_ref[head, cols, :])
            res_q[rows, cols] = mm(k_t_ref[rows, :], mixed_grad) * (1.0 / math.sqrt(HDIM))
    res_k[...] = grad_k.astype(jnp.bfloat16)
    res_v[...] = grad_v.astype(jnp.bfloat16)
    grad_q = res_q[...].T.astype(jnp.bfloat16)
    g_att[...] = grad_q
    for step in range(ranks):
        rows = rows_at(me ^ step, frames)
        out = outs[step]
        out[0:frames, :] = mixed[rows, :]
        out[frames : 2 * frames, :] = g_att[rows, :]
        out[2 * frames : 3 * frames, :] = res_k[rows, :]
        out[3 * frames : 4 * frames, :] = res_v[rows, :]
        out[4 * frames :, :] = taps


def spread_kernel(ranks, frames, *refs):
    blocks = refs[:ranks]
    others = refs[ranks : 2 * ranks]
    mixed_ref, q_ref, k_ref, v_ref, taps_ref = refs[2 * ranks : 2 * ranks + 5]
    me = lax.axis_index("seq")
    for step in range(ranks):
        lanes = lanes_at(me ^ step)
        for place, target in enumerate((mixed_ref, q_ref, k_ref, v_ref)):
            target[0, :, lanes] = blocks[step][place * frames : (place + 1) * frames, :]
        both = blocks[step][4 * frames :, :].astype(jnp.float32) + others[step][...].astype(jnp.float32)
        taps_ref[:, lanes] = both[:KERNEL]


def cost(flops, moved):
    return pl.CostEstimate(flops=flops, bytes_accessed=moved, transcendentals=0)


def on_device_heads(queries, keys, values, cotangent, conv_weight, rec_lengths):
    ranks = lax.axis_size("seq")
    frames = queries.shape[1]
    length = ranks * frames
    heads = LANES // HDIM
    bf16, f32, i32 = jnp.bfloat16, jnp.float32, jnp.int32
    struct = jax.ShapeDtypeStruct
    hbm = pl.BlockSpec(memory_space=pl.ANY)
    vmem = pl.BlockSpec(memory_space=VMEM)
    smem = pl.BlockSpec(memory_space=pltpu.SMEM)
    params = pltpu.CompilerParams(vmem_limit_bytes=24 * MIB)
    taps = KERNEL + 1

    sends = pl.pallas_call(
        functools.partial(pack_kernel, ranks),
        out_shape=[struct((3, frames, LANES), bf16)] * (ranks - 1)
        + [struct((frames, LANES), bf16)] * (ranks - 1),
        in_specs=[hbm] * 4,
        out_specs=[hbm] * (2 * ranks - 2),
        scratch_shapes=[pltpu.SemaphoreType.DMA((4 * (ranks - 1),))],
        compiler_params=params,
        name="pack",
    )(queries, keys, values, cotangent)

    def swap(array, step):
        return lax.ppermute(array, "seq", [(rank, rank ^ step) for rank in range(ranks)])

    order = list(range(ranks - 1, 0, -1))
    received = {step: swap(sends[step - 1], step) for step in order}
    cots = {step: swap(sends[ranks - 1 + step - 1], step) for step in order}

    own, col, row, after, before = pl.pallas_call(
        functools.partial(mask_kernel, length),
        out_shape=[
            struct((4, frames, LANES), bf16),
            struct((length, LANES), i32),
            struct((8, length), i32),
            struct((length, LANES), i32),
            struct((length, LANES), i32),
        ],
        in_specs=[smem] + [hbm] * 4,
        out_specs=[vmem] * 5,
        scratch_shapes=[pltpu.SemaphoreType.DMA((4,))],
        compiler_params=params,
        cost_estimate=cost(4 * MIB, MIB),
        name="masks",
    )(rec_lengths, queries, keys, values, cotangent)

    soft, att, att_t, pre, q_heads, k_t, v_full = pl.pallas_call(
        functools.partial(forward_kernel, ranks, frames),
        out_shape=[
            struct((heads, length, length), bf16),
            struct((length + 2 * PAD, LANES), f32),
            struct((LANES, length), f32),
            struct((length, LANES), f32),
            struct((heads, length, LANES), bf16),
            struct((LANES, length), bf16),
            struct((length, LANES), bf16),
        ],
        in_specs=[vmem] * (ranks + 4) + [hbm],
        out_specs=[vmem] * 7,
        scratch_shapes=[
            VMEM((length, LANES), bf16),
            VMEM((length, LANES), bf16),
            VMEM((KERNEL, LANES), f32),
            pltpu.SemaphoreType.DMA,
        ],
        compiler_params=params,
        cost_estimate=cost(400 * MIB, 3 * MIB),
        name="forward",
    )(*[received[step] for step in range(1, ranks)], own, col, row, after, before, conv_weight)

    *blocks, own_taps = pl.pallas_call(
        functools.partial(backward_kernel, ranks, frames),
        out_shape=[struct((4 * frames + taps, LANES), bf16)] * ranks + [struct((taps, LANES), bf16)],
        in_specs=[vmem] * (ranks + 9) + [hbm],
        out_specs=[vmem] * (ranks + 1),
        scratch_shapes=[
            VMEM((length, LANES), bf16),
            VMEM((length + 2 * PAD, LANES), f32),
            VMEM((length, LANES), bf16),
            VMEM((length, LANES), bf16),
            VMEM((LANES, length), f32),
            VMEM((length, LANES), bf16),
            VMEM((length, LANES), bf16),
            VMEM((taps, 8, LANES), f32),
            VMEM((KERNEL, LANES), f32),
            pltpu.SemaphoreType.DMA,
        ],
        compiler_params=params,
        cost_estimate=cost(800 * MIB, 3 * MIB),
        name="backward",
    )(
        *[cots[step] for step in range(1, ranks)],
        own,
        soft,
        att,
        att_t,
        pre,
        q_heads,
        k_t,
        v_full,
        after,
        before,
        conv_weight,
    )

    back = {step: swap(blocks[step], step) for step in order}
    copies = lax.axis_size("dp")
    others = {}
    for step in range(ranks):
        others[step] = own_taps
        for shift in range(1, copies):
            pairs = [
                (one * ranks + rank, (one + shift) % copies * ranks + (rank ^ step))
                for one in range(copies)
                for rank in range(ranks)
            ]
            others[step] = lax.ppermute(own_taps, ("dp", "seq"), pairs)

    mixed, grad_q, grad_k, grad_v, grad_taps = pl.pallas_call(
        functools.partial(spread_kernel, ranks, frames),
        out_shape=[struct(queries.shape, bf16)] * 4 + [struct(conv_weight.shape, f32)],
        in_specs=[vmem] * (2 * ranks),
        out_specs=[vmem] * 5,
        compiler_params=params,
        name="spread",
    )(
        blocks[0],
        *[back[step] for step in range(1, ranks)],
        *[others[step] for step in range(ranks)],
    )
    return (mixed, grad_q, grad_k, grad_v, grad_taps)


def on_device_any(queries, keys, values, cotangent, conv_weight, rec_lengths):
    ranks = lax.axis_size("seq")
    frames, channels = queries.shape[1], queries.shape[2]
    fits = channels == ranks * LANES and ranks & (ranks - 1) == 0 and frames % LANES == 0
    if fits and ranks > 1 and ranks * frames <= 1024 and lax.axis_size("dp") == 2:
        return on_device_heads(queries, keys, values, cotangent, conv_weight, rec_lengths)
    return on_device(queries, keys, values, cotangent, conv_weight, rec_lengths)


def solution(mesh):
    placed = (
        P(("groups", "dp"), "seq", "mp"),
        P(("groups", "dp"), "seq", "mp"),
        P(("groups", "dp"), "seq", "mp"),
        P(("groups", "dp"), "seq", "mp"),
        P(None, "mp"),
        P(("groups", "dp"), None),
    )
    return jax.shard_map(
        on_device_any,
        mesh=mesh,
        in_specs=placed,
        out_specs=(
            P(("groups", "dp"), "seq", "mp"),
            P(("groups", "dp"), "seq", "mp"),
            P(("groups", "dp"), "seq", "mp"),
            P(("groups", "dp"), "seq", "mp"),
            P("groups", "mp"),
        ),
        check_vma=False,
    )
```

```python
import functools
import math

import jax
import jax.numpy as jnp
from jax import lax
from jax.experimental import pallas as pl
from jax.experimental.pallas import tpu as pltpu
from jax.sharding import PartitionSpec as P

HDIM = 64
KERNEL = 31
HALF = 15


NEGATIVE_FILL = -1e30


def extended(block, sides, width):
    for axis, dim in sides:
        count = lax.axis_size(axis)
        forward = [(i, i + 1) for i in range(count - 1)]
        backward = [(target, source) for source, target in forward]
        low = lax.ppermute(
            lax.slice_in_dim(block, block.shape[dim] - width, None, axis=dim), axis, forward
        )
        high = lax.ppermute(lax.slice_in_dim(block, 0, width, axis=dim), axis, backward)
        block = jnp.concatenate([low, block, high], axis=dim)
    return block


def pick_block(total_rows):
    for candidate in (512, 256, 128):
        return candidate
    return total_rows


def over_blocks(total_rows, advance, initial):
    block_rows = pick_block(total_rows)
    block_count = total_rows // block_rows
    if block_count == 1:
        return advance(initial, 0, block_rows)
    return lax.fori_loop(
        0,
        block_count,
        lambda number, running: advance(running, number * block_rows, block_rows),
        initial,
    )


def when_shared(compute, running):
    result = compute(running)
    return result


def on_device(queries, keys, values, cotangent, conv_weight, rec_lengths):
    frames = queries.shape[1]
    channels = queries.shape[2]
    local_heads = channels // HDIM
    score_scale = 1.0 / math.sqrt(HDIM)
    length_all = frames * lax.axis_size("seq")
    offset = lax.axis_index("seq") * frames
    record_ends = jnp.cumsum(rec_lengths[0], dtype=jnp.int32)

    def segment_of(positions):
        return jnp.sum((record_ends[None, :] <= positions[:, None]).astype(jnp.int32), axis=1)

    own_seg = segment_of(offset + jnp.arange(frames, dtype=jnp.int32))

    def to_heads(array):
        return array.reshape(array.shape[0], local_heads, HDIM).transpose(1, 0, 2)

    def from_heads(array):
        return array.transpose(1, 0, 2).reshape(array.shape[1], channels)

    q_heads = to_heads(queries[0])
    k_heads = to_heads(keys[0])
    v_heads = to_heads(values[0])

    def over_rows(advance, initial, members, first_row):
        total_rows = members[0].shape[1]

        def one_block(running, block_start, block_rows):
            sliced = tuple(
                (lax.dynamic_slice_in_dim(member, block_start, block_rows, 1) for member in members)
            )
            other_seg = segment_of(
                first_row + block_start + jnp.arange(block_rows, dtype=jnp.int32)
            )
            return when_shared(lambda current: advance(current, sliced, other_seg), running)

        return over_blocks(total_rows, one_block, initial)

    def query_scores(key_block, key_seg):
        raw_scores = (
            jnp.einsum("hqd,hkd->hqk", q_heads, key_block, preferred_element_type=jnp.float32)
            * score_scale
        )
        return jnp.where((own_seg[:, None] == key_seg[None, :])[None], raw_scores, NEGATIVE_FILL)

    def stats_step(running, sliced, key_seg):
        top_now, total_now = running
        scores = query_scores(sliced[0], key_seg)
        top_new = jnp.maximum(top_now, jnp.max(scores, axis=2))
        total_new = total_now * jnp.exp(top_now - top_new) + jnp.sum(
            jnp.exp(scores - top_new[:, :, None]), axis=2
        )
        return (top_new, total_new)

    stats_init = (
        jnp.full((local_heads, frames), NEGATIVE_FILL, jnp.float32),
        jnp.zeros((local_heads, frames), jnp.float32),
    )
    gathered = (
        lax.all_gather(keys, "seq", axis=1, tiled=True),
        lax.all_gather(values, "seq", axis=1, tiled=True),
    )
    key_whole = to_heads(gathered[0][0])
    value_whole = to_heads(gathered[1][0])
    row_stats = over_rows(stats_step, stats_init, (key_whole,), 0)
    log_total = row_stats[0] + jnp.log(row_stats[1])

    def output_step(running, sliced, key_seg):
        scores = query_scores(sliced[0], key_seg)
        soft_rounded = jnp.exp(scores - log_total[:, :, None]).astype(jnp.bfloat16)
        return running + jnp.einsum(
            "hqk,hkd->hqd", soft_rounded, sliced[1], preferred_element_type=jnp.float32
        )

    frame_zeros = jnp.zeros((local_heads, frames, HDIM), jnp.float32)
    attended_sum = over_rows(output_step, frame_zeros, (key_whole, value_whole), 0)
    attended_heads = attended_sum.astype(jnp.bfloat16)
    attended = from_heads(attended_heads)
    padded = extended(attended[None], (("seq", 1),), HALF)
    padded_wide = padded[0].astype(jnp.float32)
    pad_positions = offset - HALF + jnp.arange(frames + 2 * HALF, dtype=jnp.int32)
    inside = jnp.logical_and(pad_positions >= 0, pad_positions < length_all)
    pad_seg = jnp.where(inside, segment_of(pad_positions), -1)
    conv_pre = jnp.zeros((frames, channels), jnp.float32)
    for tap_index in range(KERNEL):
        tap_mask = (pad_seg[tap_index : tap_index + frames] == own_seg)[:, None]
        conv_pre = conv_pre + jnp.where(
            tap_mask, conv_weight[tap_index] * padded_wide[tap_index : tap_index + frames], 0.0
        )
    gate_value = jax.nn.sigmoid(conv_pre)
    mixed = (conv_pre * gate_value).astype(jnp.bfloat16)
    conv_grad = (
        cotangent[0].astype(jnp.float32) * gate_value * (1.0 + conv_pre * (1.0 - gate_value))
    ).astype(jnp.bfloat16)
    padded_grad = extended(conv_grad[None], (("seq", 1),), HALF)
    grad_wide = padded_grad[0].astype(jnp.float32)
    conv_grad_wide = conv_grad.astype(jnp.float32)
    grad_attended = jnp.zeros((frames, channels), jnp.float32)
    kernel_rows = []
    for tap_index in range(KERNEL):
        back_start = 2 * HALF - tap_index
        back_mask = (pad_seg[back_start : back_start + frames] == own_seg)[:, None]
        grad_attended = grad_attended + jnp.where(
            back_mask, conv_weight[tap_index] * grad_wide[back_start : back_start + frames], 0.0
        )
        tap_mask = (pad_seg[tap_index : tap_index + frames] == own_seg)[:, None]
        product = conv_grad_wide * padded_wide[tap_index : tap_index + frames]
        kernel_rows.append(jnp.sum(jnp.where(tap_mask, product, 0.0), axis=0))
    grad_kernel = lax.psum(jnp.stack(kernel_rows), ("dp", "seq"))
    grad_attended = grad_attended.astype(jnp.bfloat16)
    g_heads = to_heads(grad_attended)
    row_delta = jnp.sum(g_heads.astype(jnp.float32) * attended_heads.astype(jnp.float32), axis=2)

    def query_grad_step(running, sliced, key_seg):
        key_block = sliced[0]
        value_block = sliced[1]
        soft_weights = jnp.exp(query_scores(key_block, key_seg) - log_total[:, :, None])
        slopes = jnp.einsum(
            "hqd,hkd->hqk", g_heads, value_block, preferred_element_type=jnp.float32
        )
        mixed_grad = (soft_weights * (slopes - row_delta[:, :, None])).astype(jnp.bfloat16)
        return running + jnp.einsum(
            "hqk,hkd->hqd", mixed_grad, key_block, preferred_element_type=jnp.float32
        )

    grad_query = over_rows(query_grad_step, frame_zeros, (key_whole, value_whole), 0)

    def key_grad_step(running, sliced, query_seg):
        grad_key_now, grad_value_now = running
        query_block = sliced[0]
        grad_block = sliced[1]
        total_block = sliced[2]
        delta_block = sliced[3]
        raw_scores = (
            jnp.einsum("hqd,hkd->hqk", query_block, k_heads, preferred_element_type=jnp.float32)
            * score_scale
        )
        scores = jnp.where(
            (query_seg[:, None] == own_seg[None, :])[None], raw_scores, NEGATIVE_FILL
        )
        soft_weights = jnp.exp(scores - total_block[:, :, None])
        grad_value_new = grad_value_now + jnp.einsum(
            "hqk,hqd->hkd",
            soft_weights.astype(jnp.bfloat16),
            grad_block,
            preferred_element_type=jnp.float32,
        )
        slopes = jnp.einsum("hqd,hkd->hqk", grad_block, v_heads, preferred_element_type=jnp.float32)
        mixed_grad = (soft_weights * (slopes - delta_block[:, :, None])).astype(jnp.bfloat16)
        grad_key_new = grad_key_now + jnp.einsum(
            "hqk,hqd->hkd", mixed_grad, query_block, preferred_element_type=jnp.float32
        )
        return (grad_key_new, grad_value_new)

    all_totals, all_deltas = (
        lax.all_gather(log_total[None], "seq", axis=2, tiled=True),
        lax.all_gather(row_delta[None], "seq", axis=2, tiled=True),
    )
    member = (
        lax.all_gather(queries, "seq", axis=1, tiled=True),
        lax.all_gather(grad_attended[None], "seq", axis=1, tiled=True),
    )
    totals_piece = all_totals[0]
    deltas_piece = all_deltas[0]
    grad_key, grad_value = over_rows(
        key_grad_step,
        (frame_zeros, frame_zeros),
        (to_heads(member[0][0]), to_heads(member[1][0]), totals_piece, deltas_piece),
        jnp.int32(0),
    )
    grad_queries = from_heads(grad_query * score_scale).astype(jnp.bfloat16)[None]
    grad_keys = from_heads(grad_key * score_scale).astype(jnp.bfloat16)[None]
    grad_values = from_heads(grad_value).astype(jnp.bfloat16)[None]
    return (mixed[None], grad_queries, grad_keys, grad_values, grad_kernel)


LANES = 128
PAD = 16
VMEM = pltpu.VMEM
MIB = 1024 * 1024


def mm(left, right):
    return lax.dot_general(
        left, right, (((1,), (0,)), ((), ())), preferred_element_type=jnp.float32
    )


def mm_nt(left, right):
    return lax.dot_general(
        left, right, (((1,), (1,)), ((), ())), preferred_element_type=jnp.float32
    )


def rows_at(block, frames):
    return pl.ds(pl.multiple_of(block * frames, frames), frames)


def lanes_at(block):
    return pl.ds(pl.multiple_of(block * LANES, LANES), LANES)


def pack_kernel(ranks, q_ref, k_ref, v_ref, *rest):
    outs, sems = rest[:-1], rest[-1]
    me = lax.axis_index("seq")
    copies = []
    for step in range(ranks - 1, 0, -1):
        for place, source in enumerate((q_ref, k_ref, v_ref)):
            copies.append((source.at[0, :, lanes_at(me ^ step)], outs[step - 1].at[place]))
    run_copies(copies, sems)


def run_copies(pairs, sems, meanwhile=None):
    copies = [
        pltpu.make_async_copy(source, target, sems.at[number])
        for number, (source, target) in enumerate(pairs)
    ]
    for copy in copies:
        copy.start()
    if meanwhile is not None:
        meanwhile()
    for copy in copies:
        copy.wait()


def mask_kernel(ranks, length, lens_ref, q_ref, k_ref, v_ref, c_ref, *refs):
    cot_refs = refs[: ranks - 1]
    own_ref, col_ref, row_ref, after_ref, before_ref, sems = refs[ranks - 1 :]
    me = lax.axis_index("seq")
    pairs = [(c_ref.at[0, :, lanes_at(me ^ step)], cot_refs[step - 1]) for step in range(1, ranks)]
    for place, source in enumerate((q_ref, k_ref, v_ref, c_ref)):
        pairs.append((source.at[0, :, lanes_at(me)], own_ref.at[place]))

    def extents():
        ends = []
        running = jnp.int32(0)
        for number in range(lens_ref.shape[1]):
            running = running + lens_ref[0, number]
            ends.append(running)
        row_time = lax.broadcasted_iota(jnp.int32, row_ref.shape, 1)
        row_first = jnp.zeros(row_ref.shape, jnp.int32)
        for end in ends:
            row_first = jnp.where(row_time >= end, end, row_first)
        row_ref[...] = row_first
        chunk = 64

        def some_rows(number, carry):
            base = pl.multiple_of(number * chunk, chunk)
            time = base + lax.broadcasted_iota(jnp.int32, (chunk, LANES), 0)
            first = jnp.zeros((chunk, LANES), jnp.int32)
            last = jnp.full((chunk, LANES), length, jnp.int32)
            for end in ends:
                first = jnp.where(time >= end, end, first)
            for end in reversed(ends):
                last = jnp.where(time < end, end, last)
            rows = pl.ds(base, chunk)
            col_ref[rows, :] = first
            after_ref[rows, :] = last - 1 - time
            before_ref[rows, :] = time - first
            return carry

        lax.fori_loop(0, length // chunk, some_rows, 0)

    run_copies(pairs, sems, extents)


def forward_kernel(ranks, frames, *refs):
    recvs = refs[: ranks - 1]
    own_ref, col_ref, row_ref, after_ref, before_ref, w_ref = refs[ranks - 1 : ranks + 5]
    soft_ref, att_ref, pre_ref, q_ref, k_t_ref, v_ref = refs[ranks + 5 : ranks + 11]
    att_t_ref, k_full, q_full, w_own, w_sem = refs[ranks + 11 :]
    me = lax.axis_index("seq")
    length = ranks * frames
    copy = pltpu.make_async_copy(w_ref.at[:, lanes_at(me)], w_own, w_sem)
    copy.start()
    for place, target in enumerate((q_full, k_full, v_ref)):
        target[rows_at(me, frames), :] = own_ref[place]
        for step in range(1, ranks):
            target[rows_at(me ^ step, frames), :] = recvs[ranks - 1 - step][place]
    heads = LANES // HDIM
    lane_head = lax.broadcasted_iota(jnp.int32, (1, LANES), 1) // HDIM
    scaled = q_full[...].astype(jnp.float32) * (1.0 / math.sqrt(HDIM))
    for head in range(heads):
        q_ref[head] = jnp.where(lane_head == head, scaled, 0.0).astype(jnp.bfloat16)
    k_t_ref[...] = k_full[...].astype(jnp.float32).T.astype(jnp.bfloat16)
    v_t = v_ref[...].astype(jnp.float32).T.astype(jnp.bfloat16)
    wide = 256
    for head in range(heads):
        for start in range(0, length, wide):
            cols = slice(start, start + wide)
            raw = mm_nt(k_full[...], q_ref[head, cols, :])
            same = jnp.concatenate([col_ref[...]] * (wide // LANES), axis=1) == row_ref[0:1, cols]
            scores = jnp.where(same, raw, NEGATIVE_FILL)
            top = jnp.max(scores, axis=0, keepdims=True)
            powers = jnp.exp(scores - top)
            share = 1.0 / jnp.sum(powers, axis=0, keepdims=True)
            soft = (powers * share).astype(jnp.bfloat16)
            soft_ref[head, :, cols] = soft
            rows = slice(head * HDIM, (head + 1) * HDIM)
            att_t_ref[rows, cols] = mm(v_t[rows], soft).astype(jnp.bfloat16).astype(jnp.float32)
    zeros = jnp.zeros((PAD, LANES), jnp.float32)
    att_ref[0:PAD, :] = zeros
    att_ref[PAD : PAD + length, :] = att_t_ref[...].T
    att_ref[PAD + length :, :] = zeros
    copy.wait()

    chunk = 64

    def some_rows(number, carry):
        base = pl.multiple_of(number * chunk, chunk)
        rows = pl.ds(base, chunk)
        after, before = after_ref[rows, :], before_ref[rows, :]
        total = jnp.zeros((chunk, LANES), jnp.float32)
        for tap in range(KERNEL):
            off = tap - HALF
            piece = att_ref[pl.ds(base + (PAD + off), chunk), :]
            if off > 0:
                piece = jnp.where(after >= off, piece, 0.0)
            if off < 0:
                piece = jnp.where(before >= -off, piece, 0.0)
            total = total + w_own[tap : tap + 1, :] * piece
        pre_ref[rows, :] = total
        return carry

    lax.fori_loop(0, length // chunk, some_rows, 0)


def conv_back_kernel(ranks, frames, *refs):
    cots = refs[: ranks - 1]
    own_ref, att_ref, pre_ref, after_ref, before_ref, w_ref = refs[ranks - 1 : ranks + 5]
    mixed_ref, g_att, taps_ref, cot, grad_pad, tap_sum, w_own, w_sem = refs[ranks + 5 :]
    me = lax.axis_index("seq")
    length = ranks * frames
    copy = pltpu.make_async_copy(w_ref.at[:, lanes_at(me)], w_own, w_sem)
    copy.start()
    cot[rows_at(me, frames), :] = own_ref[3]
    for step in range(1, ranks):
        cot[rows_at(me ^ step, frames), :] = cots[ranks - 1 - step][...]
    zeros = jnp.zeros((PAD, LANES), jnp.float32)
    grad_pad[0:PAD, :] = zeros
    grad_pad[PAD + length :, :] = zeros
    pre = pre_ref[...]
    gate = jax.nn.sigmoid(pre)
    mixed_ref[...] = (pre * gate).astype(jnp.bfloat16)
    conv_grad = cot[...].astype(jnp.float32) * gate * (1.0 + pre * (1.0 - gate))
    grad_pad[PAD : PAD + length, :] = conv_grad.astype(jnp.bfloat16).astype(jnp.float32)
    tap_sum[...] = jnp.zeros(tap_sum.shape, jnp.float32)
    copy.wait()

    chunk = 64

    def some_rows(number, carry):
        base = pl.multiple_of(number * chunk, chunk)
        rows = pl.ds(base, chunk)
        after, before = after_ref[rows, :], before_ref[rows, :]
        own_att = att_ref[pl.ds(base + PAD, chunk), :]
        total = jnp.zeros((chunk, LANES), jnp.float32)
        for tap in range(KERNEL):
            off = tap - HALF
            piece = grad_pad[pl.ds(base + (PAD - off), chunk), :]
            if off > 0:
                piece = jnp.where(before >= off, piece, 0.0)
            if off < 0:
                piece = jnp.where(after >= -off, piece, 0.0)
            total = total + w_own[tap : tap + 1, :] * piece
            part = (own_att * piece).reshape(chunk // 8, 8, LANES)
            tap_sum[tap] = tap_sum[tap] + jnp.sum(part, axis=0)
        g_att[rows, :] = total.astype(jnp.bfloat16)
        return carry

    lax.fori_loop(0, length // chunk, some_rows, 0)
    taps_ref[...] = jnp.sum(tap_sum[...], axis=1)


def backward_kernel(soft_ref, att_ref, g_att, q_ref, k_t_ref, v_ref, res_q, res_k, res_v, grad_t):
    length = v_ref.shape[0]
    heads = LANES // HDIM
    lane_head = lax.broadcasted_iota(jnp.int32, (1, LANES), 1) // HDIM
    g_wide = g_att[...].astype(jnp.float32)
    products_t = (g_wide * att_ref[PAD : PAD + length, :]).T
    g_heads = [jnp.where(lane_head == head, g_wide, 0.0).astype(jnp.bfloat16) for head in range(heads)]
    wide = 256
    grad_v = jnp.zeros((length, LANES), jnp.float32)
    grad_k = jnp.zeros((length, LANES), jnp.float32)
    for head in range(heads):
        rows = slice(head * HDIM, (head + 1) * HDIM)
        delta = jnp.sum(products_t[rows], axis=0, keepdims=True)
        for start in range(0, length, wide):
            cols = slice(start, start + wide)
            soft = soft_ref[head, :, cols]
            slopes = mm_nt(v_ref[...], g_heads[head][cols])
            mixed_grad = (soft.astype(jnp.float32) * (slopes - delta[:, cols])).astype(jnp.bfloat16)
            grad_v = grad_v + mm(soft, g_heads[head][cols])
            grad_k = grad_k + mm(mixed_grad, q_ref[head, cols, :])
            grad_t[rows, cols] = mm(k_t_ref[rows, :], mixed_grad) * (1.0 / math.sqrt(HDIM))
    res_k[...] = grad_k.astype(jnp.bfloat16)
    res_v[...] = grad_v.astype(jnp.bfloat16)
    res_q[...] = grad_t[...].T.astype(jnp.bfloat16)


def block_kernel(steps, frames, *refs):
    sources, tap_refs, outs = refs[:4], refs[4 : -len(steps)], refs[-len(steps) :]
    me = lax.axis_index("seq")
    taps = tap_refs[0][...]
    for other in tap_refs[1:]:
        taps = taps + other[...]
    for step, out in zip(steps, outs):
        rows = rows_at(me ^ step, frames)
        for place, source in enumerate(sources):
            out[place * frames : (place + 1) * frames, :] = source[rows, :]
        out[4 * frames :, :] = taps.astype(jnp.bfloat16)


def spread_kernel(ranks, frames, *refs):
    blocks = refs[:ranks]
    targets, taps_ref = refs[ranks : ranks + 4], refs[ranks + 4]
    sems = refs[-1]
    me = lax.axis_index("seq")
    pairs = []
    for step in range(ranks):
        for place, target in enumerate(targets):
            pairs.append(
                (blocks[step].at[place * frames : (place + 1) * frames, :], target.at[0, :, lanes_at(me ^ step)])
            )

    def tap_grads():
        for step in range(ranks):
            taps = blocks[step][4 * frames :, :].astype(jnp.float32)
            taps_ref[:, lanes_at(me ^ step)] = taps[:KERNEL]

    run_copies(pairs, sems, tap_grads)


def cost(flops, moved):
    return pl.CostEstimate(flops=flops, bytes_accessed=moved, transcendentals=0)


def on_device_heads(queries, keys, values, cotangent, conv_weight, rec_lengths):
    ranks = lax.axis_size("seq")
    frames = queries.shape[1]
    length = ranks * frames
    heads = LANES // HDIM
    bf16, f32, i32 = jnp.bfloat16, jnp.float32, jnp.int32
    struct = jax.ShapeDtypeStruct
    hbm = pl.BlockSpec(memory_space=pltpu.HBM)
    anywhere = pl.BlockSpec(memory_space=pl.ANY)
    vmem = pl.BlockSpec(memory_space=VMEM)
    smem = pl.BlockSpec(memory_space=pltpu.SMEM)
    params = pltpu.CompilerParams(vmem_limit_bytes=24 * MIB)
    taps = KERNEL + 1

    sends = pl.pallas_call(
        functools.partial(pack_kernel, ranks),
        out_shape=[struct((3, frames, LANES), bf16)] * (ranks - 1),
        in_specs=[hbm] * 3,
        out_specs=[hbm] * (ranks - 1),
        scratch_shapes=[pltpu.SemaphoreType.DMA((3 * (ranks - 1),))],
        name="pack",
    )(queries, keys, values)

    def swap(array, step):
        return lax.ppermute(array, "seq", [(rank, rank ^ step) for rank in range(ranks)])

    order = list(range(ranks - 1, 0, -1))
    received = {step: swap(sends[step - 1], step) for step in order}

    *cot_sends, own, col, row, after, before = pl.pallas_call(
        functools.partial(mask_kernel, ranks, length),
        out_shape=[struct((frames, LANES), bf16)] * (ranks - 1)
        + [
            struct((4, frames, LANES), bf16),
            struct((length, LANES), i32),
            struct((8, length), i32),
            struct((length, LANES), i32),
            struct((length, LANES), i32),
        ],
        in_specs=[smem] + [hbm] * 4,
        out_specs=[vmem] * (ranks + 4),
        scratch_shapes=[pltpu.SemaphoreType.DMA((ranks + 3,))],
        compiler_params=params,
        cost_estimate=cost(4 * MIB, MIB),
        name="masks",
    )(rec_lengths, queries, keys, values, cotangent)
    cots = {step: swap(cot_sends[step - 1], step) for step in order}

    soft, att, pre, q_heads, k_t, v_full = pl.pallas_call(
        functools.partial(forward_kernel, ranks, frames),
        out_shape=[
            struct((heads, length, length), bf16),
            struct((length + 2 * PAD, LANES), f32),
            struct((length, LANES), f32),
            struct((heads, length, LANES), bf16),
            struct((LANES, length), bf16),
            struct((length, LANES), bf16),
        ],
        in_specs=[vmem] * (ranks + 4) + [anywhere],
        out_specs=[vmem] * 6,
        scratch_shapes=[
            VMEM((LANES, length), f32),
            VMEM((length, LANES), bf16),
            VMEM((length, LANES), bf16),
            VMEM((KERNEL, LANES), f32),
            pltpu.SemaphoreType.DMA,
        ],
        compiler_params=params,
        cost_estimate=cost(400 * MIB, 3 * MIB),
        name="forward",
    )(*[received[step] for step in order], own, col, row, after, before, conv_weight)

    mixed, g_att, own_taps = pl.pallas_call(
        functools.partial(conv_back_kernel, ranks, frames),
        out_shape=[struct((length, LANES), bf16)] * 2 + [struct((taps, LANES), f32)],
        in_specs=[vmem] * (ranks + 4) + [anywhere],
        out_specs=[vmem] * 3,
        scratch_shapes=[
            VMEM((length, LANES), bf16),
            VMEM((length + 2 * PAD, LANES), f32),
            VMEM((taps, 8, LANES), f32),
            VMEM((KERNEL, LANES), f32),
            pltpu.SemaphoreType.DMA,
        ],
        compiler_params=params,
        cost_estimate=cost(400 * MIB, 3 * MIB),
        name="conv_back",
    )(*[cots[step] for step in order], own, att, pre, after, before, conv_weight)

    copies = lax.axis_size("dp")
    part_taps = [own_taps] + [
        lax.ppermute(own_taps, "dp", [(one, (one + shift) % copies) for one in range(copies)])
        for shift in range(1, copies)
    ]

    results = pl.pallas_call(
        backward_kernel,
        out_shape=[struct((length, LANES), bf16)] * 3,
        in_specs=[vmem] * 6,
        out_specs=[vmem] * 3,
        scratch_shapes=[VMEM((LANES, length), f32)],
        compiler_params=params,
        cost_estimate=cost(800 * MIB, 3 * MIB),
        name="backward",
    )(soft, att, g_att, q_heads, k_t, v_full)

    def blocks_of(steps):
        return pl.pallas_call(
            functools.partial(block_kernel, steps, frames),
            out_shape=[struct((4 * frames + taps, LANES), bf16)] * len(steps),
            in_specs=[vmem] * (4 + copies),
            out_specs=[vmem] * len(steps),
            compiler_params=params,
            cost_estimate=cost(MIB, MIB),
            name="blocks",
        )(mixed, *results, *part_taps)

    half = ranks // 2
    far = blocks_of(list(range(half, ranks)))
    near = blocks_of(list(range(half)))
    back = {step: swap(far[step - half], step) for step in range(half, ranks)}
    back |= {step: swap(near[step], step) for step in range(1, half)}
    back[0] = near[0]

    return pl.pallas_call(
        functools.partial(spread_kernel, ranks, frames),
        out_shape=[struct(queries.shape, bf16)] * 4 + [struct(conv_weight.shape, f32)],
        in_specs=[vmem] * ranks,
        out_specs=[hbm] * 4 + [vmem],
        scratch_shapes=[pltpu.SemaphoreType.DMA((4 * ranks,))],
        compiler_params=params,
        name="spread",
    )(*[back[step] for step in range(ranks)])


def on_device_any(queries, keys, values, cotangent, conv_weight, rec_lengths):
    ranks = lax.axis_size("seq")
    frames, channels = queries.shape[1], queries.shape[2]
    fits = channels == ranks * LANES and ranks & (ranks - 1) == 0 and frames % LANES == 0
    if fits and ranks > 1 and ranks * frames <= 1024 and lax.axis_size("dp") == 2:
        return on_device_heads(queries, keys, values, cotangent, conv_weight, rec_lengths)
    return on_device(queries, keys, values, cotangent, conv_weight, rec_lengths)


def solution(mesh):
    placed = (
        P(("groups", "dp"), "seq", "mp"),
        P(("groups", "dp"), "seq", "mp"),
        P(("groups", "dp"), "seq", "mp"),
        P(("groups", "dp"), "seq", "mp"),
        P(None, "mp"),
        P(("groups", "dp"), None),
    )
    return jax.shard_map(
        on_device_any,
        mesh=mesh,
        in_specs=placed,
        out_specs=(
            P(("groups", "dp"), "seq", "mp"),
            P(("groups", "dp"), "seq", "mp"),
            P(("groups", "dp"), "seq", "mp"),
            P(("groups", "dp"), "seq", "mp"),
            P("groups", "mp"),
        ),
        check_vma=False,
    )
```

```python
import functools
import math

import jax
import jax.numpy as jnp
from jax import lax
from jax.experimental import pallas as pl
from jax.experimental.pallas import tpu as pltpu
from jax.sharding import PartitionSpec as P

HDIM = 64
KERNEL = 31
HALF = 15


NEGATIVE_FILL = -1e30


def extended(block, sides, width):
    for axis, dim in sides:
        count = lax.axis_size(axis)
        forward = [(i, i + 1) for i in range(count - 1)]
        backward = [(target, source) for source, target in forward]
        low = lax.ppermute(
            lax.slice_in_dim(block, block.shape[dim] - width, None, axis=dim), axis, forward
        )
        high = lax.ppermute(lax.slice_in_dim(block, 0, width, axis=dim), axis, backward)
        block = jnp.concatenate([low, block, high], axis=dim)
    return block


def pick_block(total_rows):
    for candidate in (512, 256, 128):
        return candidate
    return total_rows


def over_blocks(total_rows, advance, initial):
    block_rows = pick_block(total_rows)
    block_count = total_rows // block_rows
    if block_count == 1:
        return advance(initial, 0, block_rows)
    return lax.fori_loop(
        0,
        block_count,
        lambda number, running: advance(running, number * block_rows, block_rows),
        initial,
    )


def when_shared(compute, running):
    result = compute(running)
    return result


def on_device(queries, keys, values, cotangent, conv_weight, rec_lengths):
    frames = queries.shape[1]
    channels = queries.shape[2]
    local_heads = channels // HDIM
    score_scale = 1.0 / math.sqrt(HDIM)
    length_all = frames * lax.axis_size("seq")
    offset = lax.axis_index("seq") * frames
    record_ends = jnp.cumsum(rec_lengths[0], dtype=jnp.int32)

    def segment_of(positions):
        return jnp.sum((record_ends[None, :] <= positions[:, None]).astype(jnp.int32), axis=1)

    own_seg = segment_of(offset + jnp.arange(frames, dtype=jnp.int32))

    def to_heads(array):
        return array.reshape(array.shape[0], local_heads, HDIM).transpose(1, 0, 2)

    def from_heads(array):
        return array.transpose(1, 0, 2).reshape(array.shape[1], channels)

    q_heads = to_heads(queries[0])
    k_heads = to_heads(keys[0])
    v_heads = to_heads(values[0])

    def over_rows(advance, initial, members, first_row):
        total_rows = members[0].shape[1]

        def one_block(running, block_start, block_rows):
            sliced = tuple(
                (lax.dynamic_slice_in_dim(member, block_start, block_rows, 1) for member in members)
            )
            other_seg = segment_of(
                first_row + block_start + jnp.arange(block_rows, dtype=jnp.int32)
            )
            return when_shared(lambda current: advance(current, sliced, other_seg), running)

        return over_blocks(total_rows, one_block, initial)

    def query_scores(key_block, key_seg):
        raw_scores = (
            jnp.einsum("hqd,hkd->hqk", q_heads, key_block, preferred_element_type=jnp.float32)
            * score_scale
        )
        return jnp.where((own_seg[:, None] == key_seg[None, :])[None], raw_scores, NEGATIVE_FILL)

    def stats_step(running, sliced, key_seg):
        top_now, total_now = running
        scores = query_scores(sliced[0], key_seg)
        top_new = jnp.maximum(top_now, jnp.max(scores, axis=2))
        total_new = total_now * jnp.exp(top_now - top_new) + jnp.sum(
            jnp.exp(scores - top_new[:, :, None]), axis=2
        )
        return (top_new, total_new)

    stats_init = (
        jnp.full((local_heads, frames), NEGATIVE_FILL, jnp.float32),
        jnp.zeros((local_heads, frames), jnp.float32),
    )
    gathered = (
        lax.all_gather(keys, "seq", axis=1, tiled=True),
        lax.all_gather(values, "seq", axis=1, tiled=True),
    )
    key_whole = to_heads(gathered[0][0])
    value_whole = to_heads(gathered[1][0])
    row_stats = over_rows(stats_step, stats_init, (key_whole,), 0)
    log_total = row_stats[0] + jnp.log(row_stats[1])

    def output_step(running, sliced, key_seg):
        scores = query_scores(sliced[0], key_seg)
        soft_rounded = jnp.exp(scores - log_total[:, :, None]).astype(jnp.bfloat16)
        return running + jnp.einsum(
            "hqk,hkd->hqd", soft_rounded, sliced[1], preferred_element_type=jnp.float32
        )

    frame_zeros = jnp.zeros((local_heads, frames, HDIM), jnp.float32)
    attended_sum = over_rows(output_step, frame_zeros, (key_whole, value_whole), 0)
    attended_heads = attended_sum.astype(jnp.bfloat16)
    attended = from_heads(attended_heads)
    padded = extended(attended[None], (("seq", 1),), HALF)
    padded_wide = padded[0].astype(jnp.float32)
    pad_positions = offset - HALF + jnp.arange(frames + 2 * HALF, dtype=jnp.int32)
    inside = jnp.logical_and(pad_positions >= 0, pad_positions < length_all)
    pad_seg = jnp.where(inside, segment_of(pad_positions), -1)
    conv_pre = jnp.zeros((frames, channels), jnp.float32)
    for tap_index in range(KERNEL):
        tap_mask = (pad_seg[tap_index : tap_index + frames] == own_seg)[:, None]
        conv_pre = conv_pre + jnp.where(
            tap_mask, conv_weight[tap_index] * padded_wide[tap_index : tap_index + frames], 0.0
        )
    gate_value = jax.nn.sigmoid(conv_pre)
    mixed = (conv_pre * gate_value).astype(jnp.bfloat16)
    conv_grad = (
        cotangent[0].astype(jnp.float32) * gate_value * (1.0 + conv_pre * (1.0 - gate_value))
    ).astype(jnp.bfloat16)
    padded_grad = extended(conv_grad[None], (("seq", 1),), HALF)
    grad_wide = padded_grad[0].astype(jnp.float32)
    conv_grad_wide = conv_grad.astype(jnp.float32)
    grad_attended = jnp.zeros((frames, channels), jnp.float32)
    kernel_rows = []
    for tap_index in range(KERNEL):
        back_start = 2 * HALF - tap_index
        back_mask = (pad_seg[back_start : back_start + frames] == own_seg)[:, None]
        grad_attended = grad_attended + jnp.where(
            back_mask, conv_weight[tap_index] * grad_wide[back_start : back_start + frames], 0.0
        )
        tap_mask = (pad_seg[tap_index : tap_index + frames] == own_seg)[:, None]
        product = conv_grad_wide * padded_wide[tap_index : tap_index + frames]
        kernel_rows.append(jnp.sum(jnp.where(tap_mask, product, 0.0), axis=0))
    grad_kernel = lax.psum(jnp.stack(kernel_rows), ("dp", "seq"))
    grad_attended = grad_attended.astype(jnp.bfloat16)
    g_heads = to_heads(grad_attended)
    row_delta = jnp.sum(g_heads.astype(jnp.float32) * attended_heads.astype(jnp.float32), axis=2)

    def query_grad_step(running, sliced, key_seg):
        key_block = sliced[0]
        value_block = sliced[1]
        soft_weights = jnp.exp(query_scores(key_block, key_seg) - log_total[:, :, None])
        slopes = jnp.einsum(
            "hqd,hkd->hqk", g_heads, value_block, preferred_element_type=jnp.float32
        )
        mixed_grad = (soft_weights * (slopes - row_delta[:, :, None])).astype(jnp.bfloat16)
        return running + jnp.einsum(
            "hqk,hkd->hqd", mixed_grad, key_block, preferred_element_type=jnp.float32
        )

    grad_query = over_rows(query_grad_step, frame_zeros, (key_whole, value_whole), 0)

    def key_grad_step(running, sliced, query_seg):
        grad_key_now, grad_value_now = running
        query_block = sliced[0]
        grad_block = sliced[1]
        total_block = sliced[2]
        delta_block = sliced[3]
        raw_scores = (
            jnp.einsum("hqd,hkd->hqk", query_block, k_heads, preferred_element_type=jnp.float32)
            * score_scale
        )
        scores = jnp.where(
            (query_seg[:, None] == own_seg[None, :])[None], raw_scores, NEGATIVE_FILL
        )
        soft_weights = jnp.exp(scores - total_block[:, :, None])
        grad_value_new = grad_value_now + jnp.einsum(
            "hqk,hqd->hkd",
            soft_weights.astype(jnp.bfloat16),
            grad_block,
            preferred_element_type=jnp.float32,
        )
        slopes = jnp.einsum("hqd,hkd->hqk", grad_block, v_heads, preferred_element_type=jnp.float32)
        mixed_grad = (soft_weights * (slopes - delta_block[:, :, None])).astype(jnp.bfloat16)
        grad_key_new = grad_key_now + jnp.einsum(
            "hqk,hqd->hkd", mixed_grad, query_block, preferred_element_type=jnp.float32
        )
        return (grad_key_new, grad_value_new)

    all_totals, all_deltas = (
        lax.all_gather(log_total[None], "seq", axis=2, tiled=True),
        lax.all_gather(row_delta[None], "seq", axis=2, tiled=True),
    )
    member = (
        lax.all_gather(queries, "seq", axis=1, tiled=True),
        lax.all_gather(grad_attended[None], "seq", axis=1, tiled=True),
    )
    totals_piece = all_totals[0]
    deltas_piece = all_deltas[0]
    grad_key, grad_value = over_rows(
        key_grad_step,
        (frame_zeros, frame_zeros),
        (to_heads(member[0][0]), to_heads(member[1][0]), totals_piece, deltas_piece),
        jnp.int32(0),
    )
    grad_queries = from_heads(grad_query * score_scale).astype(jnp.bfloat16)[None]
    grad_keys = from_heads(grad_key * score_scale).astype(jnp.bfloat16)[None]
    grad_values = from_heads(grad_value).astype(jnp.bfloat16)[None]
    return (mixed[None], grad_queries, grad_keys, grad_values, grad_kernel)


LANES = 128
PAD = 16
VMEM = pltpu.VMEM
MIB = 1024 * 1024


def mm(left, right):
    return lax.dot_general(
        left, right, (((1,), (0,)), ((), ())), preferred_element_type=jnp.float32
    )


def mm_nt(left, right):
    return lax.dot_general(
        left, right, (((1,), (1,)), ((), ())), preferred_element_type=jnp.float32
    )


def rows_at(block, frames):
    return pl.ds(pl.multiple_of(block * frames, frames), frames)


def lanes_at(block):
    return pl.ds(pl.multiple_of(block * LANES, LANES), LANES)


def pack_kernel(ranks, q_ref, k_ref, v_ref, *rest):
    outs, (whole, sems) = rest[:-2], rest[-2:]
    me = lax.axis_index("seq")
    sources = (q_ref, k_ref, v_ref)
    run_copies([(source.at[0], whole.at[place]) for place, source in enumerate(sources)], sems)
    for step in range(ranks - 1, 0, -1):
        for place in range(len(sources)):
            outs[step - 1][place] = whole[place, :, lanes_at(me ^ step)]


def run_copies(pairs, sems, meanwhile=None):
    copies = [
        pltpu.make_async_copy(source, target, sems.at[number])
        for number, (source, target) in enumerate(pairs)
    ]
    for copy in copies:
        copy.start()
    if meanwhile is not None:
        meanwhile()
    for copy in copies:
        copy.wait()


def mask_kernel(ranks, length, lens_ref, q_ref, k_ref, v_ref, c_ref, *refs):
    cot_refs = refs[: ranks - 1]
    own_ref, col_ref, row_ref, after_ref, before_ref, sems = refs[ranks - 1 :]
    me = lax.axis_index("seq")
    pairs = [(c_ref.at[0, :, lanes_at(me ^ step)], cot_refs[step - 1]) for step in range(1, ranks)]
    for place, source in enumerate((q_ref, k_ref, v_ref, c_ref)):
        pairs.append((source.at[0, :, lanes_at(me)], own_ref.at[place]))

    def extents():
        ends = []
        running = jnp.int32(0)
        for number in range(lens_ref.shape[1]):
            running = running + lens_ref[0, number]
            ends.append(running)
        row_time = lax.broadcasted_iota(jnp.int32, row_ref.shape, 1)
        row_first = jnp.zeros(row_ref.shape, jnp.int32)
        for end in ends:
            row_first = jnp.where(row_time >= end, end, row_first)
        row_ref[...] = row_first
        chunk = 64

        def some_rows(number, carry):
            base = pl.multiple_of(number * chunk, chunk)
            time = base + lax.broadcasted_iota(jnp.int32, (chunk, LANES), 0)
            first = jnp.zeros((chunk, LANES), jnp.int32)
            last = jnp.full((chunk, LANES), length, jnp.int32)
            for end in ends:
                first = jnp.where(time >= end, end, first)
            for end in reversed(ends):
                last = jnp.where(time < end, end, last)
            rows = pl.ds(base, chunk)
            col_ref[rows, :] = first
            after_ref[rows, :] = last - 1 - time
            before_ref[rows, :] = time - first
            return carry

        lax.fori_loop(0, length // chunk, some_rows, 0)

    run_copies(pairs, sems, extents)


def forward_kernel(ranks, frames, *refs):
    recvs = refs[: ranks - 1]
    own_ref, col_ref, row_ref, after_ref, before_ref, w_ref = refs[ranks - 1 : ranks + 5]
    soft_ref, att_ref, pre_ref, q_ref, k_t_ref, v_ref = refs[ranks + 5 : ranks + 11]
    att_t_ref, k_full, q_full, w_own, w_sem = refs[ranks + 11 :]
    me = lax.axis_index("seq")
    length = ranks * frames
    copy = pltpu.make_async_copy(w_ref.at[:, lanes_at(me)], w_own, w_sem)
    copy.start()
    for place, target in enumerate((q_full, k_full, v_ref)):
        target[rows_at(me, frames), :] = own_ref[place]
        for step in range(1, ranks):
            target[rows_at(me ^ step, frames), :] = recvs[ranks - 1 - step][place]
    heads = LANES // HDIM
    lane_head = lax.broadcasted_iota(jnp.int32, (1, LANES), 1) // HDIM
    scaled = q_full[...].astype(jnp.float32) * (1.0 / math.sqrt(HDIM))
    for head in range(heads):
        q_ref[head] = jnp.where(lane_head == head, scaled, 0.0).astype(jnp.bfloat16)
    k_t_ref[...] = k_full[...].astype(jnp.float32).T.astype(jnp.bfloat16)
    v_t = v_ref[...].astype(jnp.float32).T.astype(jnp.bfloat16)
    wide = 256
    for head in range(heads):
        for start in range(0, length, wide):
            cols = slice(start, start + wide)
            raw = mm_nt(k_full[...], q_ref[head, cols, :])
            same = jnp.concatenate([col_ref[...]] * (wide // LANES), axis=1) == row_ref[0:1, cols]
            scores = jnp.where(same, raw, NEGATIVE_FILL)
            top = jnp.max(scores, axis=0, keepdims=True)
            powers = jnp.exp(scores - top)
            share = 1.0 / jnp.sum(powers, axis=0, keepdims=True)
            soft = (powers * share).astype(jnp.bfloat16)
            soft_ref[head, :, cols] = soft
            rows = slice(head * HDIM, (head + 1) * HDIM)
            att_t_ref[rows, cols] = mm(v_t[rows], soft).astype(jnp.bfloat16).astype(jnp.float32)
    zeros = jnp.zeros((PAD, LANES), jnp.float32)
    att_ref[0:PAD, :] = zeros
    att_ref[PAD : PAD + length, :] = att_t_ref[...].T
    att_ref[PAD + length :, :] = zeros
    copy.wait()

    chunk = 64

    def some_rows(number, carry):
        base = pl.multiple_of(number * chunk, chunk)
        rows = pl.ds(base, chunk)
        after, before = after_ref[rows, :], before_ref[rows, :]
        total = jnp.zeros((chunk, LANES), jnp.float32)
        for tap in range(KERNEL):
            off = tap - HALF
            piece = att_ref[pl.ds(base + (PAD + off), chunk), :]
            if off > 0:
                piece = jnp.where(after >= off, piece, 0.0)
            if off < 0:
                piece = jnp.where(before >= -off, piece, 0.0)
            total = total + w_own[tap : tap + 1, :] * piece
        pre_ref[rows, :] = total
        return carry

    lax.fori_loop(0, length // chunk, some_rows, 0)


def conv_back_kernel(ranks, frames, *refs):
    cots = refs[: ranks - 1]
    own_ref, att_ref, pre_ref, after_ref, before_ref, w_ref = refs[ranks - 1 : ranks + 5]
    mixed_ref, g_att, taps_ref, cot, grad_pad, tap_sum, w_own, w_sem = refs[ranks + 5 :]
    me = lax.axis_index("seq")
    length = ranks * frames
    copy = pltpu.make_async_copy(w_ref.at[:, lanes_at(me)], w_own, w_sem)
    copy.start()
    cot[rows_at(me, frames), :] = own_ref[3]
    for step in range(1, ranks):
        cot[rows_at(me ^ step, frames), :] = cots[ranks - 1 - step][...]
    zeros = jnp.zeros((PAD, LANES), jnp.float32)
    grad_pad[0:PAD, :] = zeros
    grad_pad[PAD + length :, :] = zeros
    pre = pre_ref[...]
    gate = jax.nn.sigmoid(pre)
    mixed_ref[...] = (pre * gate).astype(jnp.bfloat16)
    conv_grad = cot[...].astype(jnp.float32) * gate * (1.0 + pre * (1.0 - gate))
    grad_pad[PAD : PAD + length, :] = conv_grad.astype(jnp.bfloat16).astype(jnp.float32)
    tap_sum[...] = jnp.zeros(tap_sum.shape, jnp.float32)
    copy.wait()

    chunk = 64

    def some_rows(number, carry):
        base = pl.multiple_of(number * chunk, chunk)
        rows = pl.ds(base, chunk)
        after, before = after_ref[rows, :], before_ref[rows, :]
        own_att = att_ref[pl.ds(base + PAD, chunk), :]
        total = jnp.zeros((chunk, LANES), jnp.float32)
        for tap in range(KERNEL):
            off = tap - HALF
            piece = grad_pad[pl.ds(base + (PAD - off), chunk), :]
            if off > 0:
                piece = jnp.where(before >= off, piece, 0.0)
            if off < 0:
                piece = jnp.where(after >= -off, piece, 0.0)
            total = total + w_own[tap : tap + 1, :] * piece
            part = (own_att * piece).reshape(chunk // 8, 8, LANES)
            tap_sum[tap] = tap_sum[tap] + jnp.sum(part, axis=0)
        g_att[rows, :] = total.astype(jnp.bfloat16)
        return carry

    lax.fori_loop(0, length // chunk, some_rows, 0)
    taps_ref[...] = jnp.sum(tap_sum[...], axis=1)


def backward_kernel(soft_ref, att_ref, g_att, q_ref, k_t_ref, v_ref, res_q, res_k, res_v, grad_t):
    length = v_ref.shape[0]
    heads = LANES // HDIM
    lane_head = lax.broadcasted_iota(jnp.int32, (1, LANES), 1) // HDIM
    g_wide = g_att[...].astype(jnp.float32)
    products_t = (g_wide * att_ref[PAD : PAD + length, :]).T
    g_heads = [jnp.where(lane_head == head, g_wide, 0.0).astype(jnp.bfloat16) for head in range(heads)]
    wide = 256
    grad_v = jnp.zeros((length, LANES), jnp.float32)
    grad_k = jnp.zeros((length, LANES), jnp.float32)
    for head in range(heads):
        rows = slice(head * HDIM, (head + 1) * HDIM)
        delta = jnp.sum(products_t[rows], axis=0, keepdims=True)
        for start in range(0, length, wide):
            cols = slice(start, start + wide)
            soft = soft_ref[head, :, cols]
            slopes = mm_nt(v_ref[...], g_heads[head][cols])
            mixed_grad = (soft.astype(jnp.float32) * (slopes - delta[:, cols])).astype(jnp.bfloat16)
            grad_v = grad_v + mm(soft, g_heads[head][cols])
            grad_k = grad_k + mm(mixed_grad, q_ref[head, cols, :])
            grad_t[rows, cols] = mm(k_t_ref[rows, :], mixed_grad) * (1.0 / math.sqrt(HDIM))
    res_k[...] = grad_k.astype(jnp.bfloat16)
    res_v[...] = grad_v.astype(jnp.bfloat16)
    res_q[...] = grad_t[...].T.astype(jnp.bfloat16)


def block_kernel(steps, frames, *refs):
    sources, tap_refs, outs = refs[:4], refs[4 : -len(steps)], refs[-len(steps) :]
    me = lax.axis_index("seq")
    taps = tap_refs[0][...]
    for other in tap_refs[1:]:
        taps = taps + other[...]
    for step, out in zip(steps, outs):
        rows = rows_at(me ^ step, frames)
        for place, source in enumerate(sources):
            out[place * frames : (place + 1) * frames, :] = source[rows, :]
        out[4 * frames :, :] = taps.astype(jnp.bfloat16)


def spread_kernel(ranks, frames, *refs):
    blocks = refs[:ranks]
    targets, taps_ref = refs[ranks : ranks + 4], refs[ranks + 4]
    me = lax.axis_index("seq")
    for step in range(ranks):
        lanes = lanes_at(me ^ step)
        for place, target in enumerate(targets):
            target[0, :, lanes] = blocks[step][place * frames : (place + 1) * frames, :]
        taps = blocks[step][4 * frames :, :].astype(jnp.float32)
        taps_ref[:, lanes] = taps[:KERNEL]


def cost(flops, moved):
    return pl.CostEstimate(flops=flops, bytes_accessed=moved, transcendentals=0)


def on_device_heads(queries, keys, values, cotangent, conv_weight, rec_lengths):
    ranks = lax.axis_size("seq")
    frames = queries.shape[1]
    length = ranks * frames
    heads = LANES // HDIM
    bf16, f32, i32 = jnp.bfloat16, jnp.float32, jnp.int32
    struct = jax.ShapeDtypeStruct
    hbm = pl.BlockSpec(memory_space=pltpu.HBM)
    anywhere = pl.BlockSpec(memory_space=pl.ANY)
    vmem = pl.BlockSpec(memory_space=VMEM)
    smem = pl.BlockSpec(memory_space=pltpu.SMEM)
    params = pltpu.CompilerParams(vmem_limit_bytes=24 * MIB)
    taps = KERNEL + 1

    sends = pl.pallas_call(
        functools.partial(pack_kernel, ranks),
        out_shape=[struct((3, frames, LANES), bf16)] * (ranks - 1),
        in_specs=[hbm] * 3,
        out_specs=[vmem] * (ranks - 1),
        scratch_shapes=[VMEM((3,) + queries.shape[1:], bf16), pltpu.SemaphoreType.DMA((3,))],
        compiler_params=pltpu.CompilerParams(vmem_limit_bytes=54912 * 1024),
        name="pack",
    )(queries, keys, values)

    def swap(array, step):
        return lax.ppermute(array, "seq", [(rank, rank ^ step) for rank in range(ranks)])

    order = list(range(ranks - 1, 0, -1))
    received = {step: swap(sends[step - 1], step) for step in order}

    *cot_sends, own, col, row, after, before = pl.pallas_call(
        functools.partial(mask_kernel, ranks, length),
        out_shape=[struct((frames, LANES), bf16)] * (ranks - 1)
        + [
            struct((4, frames, LANES), bf16),
            struct((length, LANES), i32),
            struct((8, length), i32),
            struct((length, LANES), i32),
            struct((length, LANES), i32),
        ],
        in_specs=[smem] + [hbm] * 4,
        out_specs=[vmem] * (ranks + 4),
        scratch_shapes=[pltpu.SemaphoreType.DMA((ranks + 3,))],
        compiler_params=params,
        cost_estimate=cost(4 * MIB, MIB),
        name="masks",
    )(rec_lengths, queries, keys, values, cotangent)
    cots = {step: swap(cot_sends[step - 1], step) for step in order}

    soft, att, pre, q_heads, k_t, v_full = pl.pallas_call(
        functools.partial(forward_kernel, ranks, frames),
        out_shape=[
            struct((heads, length, length), bf16),
            struct((length + 2 * PAD, LANES), f32),
            struct((length, LANES), f32),
            struct((heads, length, LANES), bf16),
            struct((LANES, length), bf16),
            struct((length, LANES), bf16),
        ],
        in_specs=[vmem] * (ranks + 4) + [anywhere],
        out_specs=[vmem] * 6,
        scratch_shapes=[
            VMEM((LANES, length), f32),
            VMEM((length, LANES), bf16),
            VMEM((length, LANES), bf16),
            VMEM((KERNEL, LANES), f32),
            pltpu.SemaphoreType.DMA,
        ],
        compiler_params=params,
        cost_estimate=cost(400 * MIB, 3 * MIB),
        name="forward",
    )(*[received[step] for step in order], own, col, row, after, before, conv_weight)

    mixed, g_att, own_taps = pl.pallas_call(
        functools.partial(conv_back_kernel, ranks, frames),
        out_shape=[struct((length, LANES), bf16)] * 2 + [struct((taps, LANES), f32)],
        in_specs=[vmem] * (ranks + 4) + [anywhere],
        out_specs=[vmem] * 3,
        scratch_shapes=[
            VMEM((length, LANES), bf16),
            VMEM((length + 2 * PAD, LANES), f32),
            VMEM((taps, 8, LANES), f32),
            VMEM((KERNEL, LANES), f32),
            pltpu.SemaphoreType.DMA,
        ],
        compiler_params=params,
        cost_estimate=cost(400 * MIB, 3 * MIB),
        name="conv_back",
    )(*[cots[step] for step in order], own, att, pre, after, before, conv_weight)

    copies = lax.axis_size("dp")
    part_taps = [own_taps] + [
        lax.ppermute(own_taps, "dp", [(one, (one + shift) % copies) for one in range(copies)])
        for shift in range(1, copies)
    ]

    results = pl.pallas_call(
        backward_kernel,
        out_shape=[struct((length, LANES), bf16)] * 3,
        in_specs=[vmem] * 6,
        out_specs=[vmem] * 3,
        scratch_shapes=[VMEM((LANES, length), f32)],
        compiler_params=params,
        cost_estimate=cost(800 * MIB, 3 * MIB),
        name="backward",
    )(soft, att, g_att, q_heads, k_t, v_full)

    def blocks_of(steps):
        return pl.pallas_call(
            functools.partial(block_kernel, steps, frames),
            out_shape=[struct((4 * frames + taps, LANES), bf16)] * len(steps),
            in_specs=[vmem] * (4 + copies),
            out_specs=[vmem] * len(steps),
            compiler_params=params,
            cost_estimate=cost(MIB, MIB),
            name="blocks",
        )(mixed, *results, *part_taps)

    half = ranks // 2
    far = blocks_of(list(range(half, ranks)))
    near = blocks_of(list(range(half)))
    back = {step: swap(far[step - half], step) for step in range(half, ranks)}
    back |= {step: swap(near[step], step) for step in range(1, half)}
    back[0] = near[0]

    return pl.pallas_call(
        functools.partial(spread_kernel, ranks, frames),
        out_shape=[struct(queries.shape, bf16)] * 4 + [struct(conv_weight.shape, f32)],
        in_specs=[vmem] * ranks,
        out_specs=[vmem] * 5,
        compiler_params=params,
        name="spread",
    )(*[back[step] for step in range(ranks)])


def on_device_any(queries, keys, values, cotangent, conv_weight, rec_lengths):
    ranks = lax.axis_size("seq")
    frames, channels = queries.shape[1], queries.shape[2]
    fits = channels == ranks * LANES and ranks & (ranks - 1) == 0 and frames % LANES == 0
    if fits and ranks > 1 and ranks * frames <= 1024 and lax.axis_size("dp") == 2:
        return on_device_heads(queries, keys, values, cotangent, conv_weight, rec_lengths)
    return on_device(queries, keys, values, cotangent, conv_weight, rec_lengths)


def solution(mesh):
    placed = (
        P(("groups", "dp"), "seq", "mp"),
        P(("groups", "dp"), "seq", "mp"),
        P(("groups", "dp"), "seq", "mp"),
        P(("groups", "dp"), "seq", "mp"),
        P(None, "mp"),
        P(("groups", "dp"), None),
    )
    return jax.shard_map(
        on_device_any,
        mesh=mesh,
        in_specs=placed,
        out_specs=(
            P(("groups", "dp"), "seq", "mp"),
            P(("groups", "dp"), "seq", "mp"),
            P(("groups", "dp"), "seq", "mp"),
            P(("groups", "dp"), "seq", "mp"),
            P("groups", "mp"),
        ),
        check_vma=False,
    )
```

```python
import functools
import math

import jax
import jax.numpy as jnp
from jax import lax
from jax.experimental import pallas as pl
from jax.experimental.pallas import tpu as pltpu
from jax.sharding import PartitionSpec as P

HDIM = 64
KERNEL = 31
HALF = 15


NEGATIVE_FILL = -1e30


def extended(block, sides, width):
    for axis, dim in sides:
        count = lax.axis_size(axis)
        forward = [(i, i + 1) for i in range(count - 1)]
        backward = [(target, source) for source, target in forward]
        low = lax.ppermute(
            lax.slice_in_dim(block, block.shape[dim] - width, None, axis=dim), axis, forward
        )
        high = lax.ppermute(lax.slice_in_dim(block, 0, width, axis=dim), axis, backward)
        block = jnp.concatenate([low, block, high], axis=dim)
    return block


def pick_block(total_rows):
    for candidate in (512, 256, 128):
        return candidate
    return total_rows


def over_blocks(total_rows, advance, initial):
    block_rows = pick_block(total_rows)
    block_count = total_rows // block_rows
    if block_count == 1:
        return advance(initial, 0, block_rows)
    return lax.fori_loop(
        0,
        block_count,
        lambda number, running: advance(running, number * block_rows, block_rows),
        initial,
    )


def when_shared(compute, running):
    result = compute(running)
    return result


def on_device(queries, keys, values, cotangent, conv_weight, rec_lengths):
    frames = queries.shape[1]
    channels = queries.shape[2]
    local_heads = channels // HDIM
    score_scale = 1.0 / math.sqrt(HDIM)
    length_all = frames * lax.axis_size("seq")
    offset = lax.axis_index("seq") * frames
    record_ends = jnp.cumsum(rec_lengths[0], dtype=jnp.int32)

    def segment_of(positions):
        return jnp.sum((record_ends[None, :] <= positions[:, None]).astype(jnp.int32), axis=1)

    own_seg = segment_of(offset + jnp.arange(frames, dtype=jnp.int32))

    def to_heads(array):
        return array.reshape(array.shape[0], local_heads, HDIM).transpose(1, 0, 2)

    def from_heads(array):
        return array.transpose(1, 0, 2).reshape(array.shape[1], channels)

    q_heads = to_heads(queries[0])
    k_heads = to_heads(keys[0])
    v_heads = to_heads(values[0])

    def over_rows(advance, initial, members, first_row):
        total_rows = members[0].shape[1]

        def one_block(running, block_start, block_rows):
            sliced = tuple(
                (lax.dynamic_slice_in_dim(member, block_start, block_rows, 1) for member in members)
            )
            other_seg = segment_of(
                first_row + block_start + jnp.arange(block_rows, dtype=jnp.int32)
            )
            return when_shared(lambda current: advance(current, sliced, other_seg), running)

        return over_blocks(total_rows, one_block, initial)

    def query_scores(key_block, key_seg):
        raw_scores = (
            jnp.einsum("hqd,hkd->hqk", q_heads, key_block, preferred_element_type=jnp.float32)
            * score_scale
        )
        return jnp.where((own_seg[:, None] == key_seg[None, :])[None], raw_scores, NEGATIVE_FILL)

    def stats_step(running, sliced, key_seg):
        top_now, total_now = running
        scores = query_scores(sliced[0], key_seg)
        top_new = jnp.maximum(top_now, jnp.max(scores, axis=2))
        total_new = total_now * jnp.exp(top_now - top_new) + jnp.sum(
            jnp.exp(scores - top_new[:, :, None]), axis=2
        )
        return (top_new, total_new)

    stats_init = (
        jnp.full((local_heads, frames), NEGATIVE_FILL, jnp.float32),
        jnp.zeros((local_heads, frames), jnp.float32),
    )
    gathered = (
        lax.all_gather(keys, "seq", axis=1, tiled=True),
        lax.all_gather(values, "seq", axis=1, tiled=True),
    )
    key_whole = to_heads(gathered[0][0])
    value_whole = to_heads(gathered[1][0])
    row_stats = over_rows(stats_step, stats_init, (key_whole,), 0)
    log_total = row_stats[0] + jnp.log(row_stats[1])

    def output_step(running, sliced, key_seg):
        scores = query_scores(sliced[0], key_seg)
        soft_rounded = jnp.exp(scores - log_total[:, :, None]).astype(jnp.bfloat16)
        return running + jnp.einsum(
            "hqk,hkd->hqd", soft_rounded, sliced[1], preferred_element_type=jnp.float32
        )

    frame_zeros = jnp.zeros((local_heads, frames, HDIM), jnp.float32)
    attended_sum = over_rows(output_step, frame_zeros, (key_whole, value_whole), 0)
    attended_heads = attended_sum.astype(jnp.bfloat16)
    attended = from_heads(attended_heads)
    padded = extended(attended[None], (("seq", 1),), HALF)
    padded_wide = padded[0].astype(jnp.float32)
    pad_positions = offset - HALF + jnp.arange(frames + 2 * HALF, dtype=jnp.int32)
    inside = jnp.logical_and(pad_positions >= 0, pad_positions < length_all)
    pad_seg = jnp.where(inside, segment_of(pad_positions), -1)
    conv_pre = jnp.zeros((frames, channels), jnp.float32)
    for tap_index in range(KERNEL):
        tap_mask = (pad_seg[tap_index : tap_index + frames] == own_seg)[:, None]
        conv_pre = conv_pre + jnp.where(
            tap_mask, conv_weight[tap_index] * padded_wide[tap_index : tap_index + frames], 0.0
        )
    gate_value = jax.nn.sigmoid(conv_pre)
    mixed = (conv_pre * gate_value).astype(jnp.bfloat16)
    conv_grad = (
        cotangent[0].astype(jnp.float32) * gate_value * (1.0 + conv_pre * (1.0 - gate_value))
    ).astype(jnp.bfloat16)
    padded_grad = extended(conv_grad[None], (("seq", 1),), HALF)
    grad_wide = padded_grad[0].astype(jnp.float32)
    conv_grad_wide = conv_grad.astype(jnp.float32)
    grad_attended = jnp.zeros((frames, channels), jnp.float32)
    kernel_rows = []
    for tap_index in range(KERNEL):
        back_start = 2 * HALF - tap_index
        back_mask = (pad_seg[back_start : back_start + frames] == own_seg)[:, None]
        grad_attended = grad_attended + jnp.where(
            back_mask, conv_weight[tap_index] * grad_wide[back_start : back_start + frames], 0.0
        )
        tap_mask = (pad_seg[tap_index : tap_index + frames] == own_seg)[:, None]
        product = conv_grad_wide * padded_wide[tap_index : tap_index + frames]
        kernel_rows.append(jnp.sum(jnp.where(tap_mask, product, 0.0), axis=0))
    grad_kernel = lax.psum(jnp.stack(kernel_rows), ("dp", "seq"))
    grad_attended = grad_attended.astype(jnp.bfloat16)
    g_heads = to_heads(grad_attended)
    row_delta = jnp.sum(g_heads.astype(jnp.float32) * attended_heads.astype(jnp.float32), axis=2)

    def query_grad_step(running, sliced, key_seg):
        key_block = sliced[0]
        value_block = sliced[1]
        soft_weights = jnp.exp(query_scores(key_block, key_seg) - log_total[:, :, None])
        slopes = jnp.einsum(
            "hqd,hkd->hqk", g_heads, value_block, preferred_element_type=jnp.float32
        )
        mixed_grad = (soft_weights * (slopes - row_delta[:, :, None])).astype(jnp.bfloat16)
        return running + jnp.einsum(
            "hqk,hkd->hqd", mixed_grad, key_block, preferred_element_type=jnp.float32
        )

    grad_query = over_rows(query_grad_step, frame_zeros, (key_whole, value_whole), 0)

    def key_grad_step(running, sliced, query_seg):
        grad_key_now, grad_value_now = running
        query_block = sliced[0]
        grad_block = sliced[1]
        total_block = sliced[2]
        delta_block = sliced[3]
        raw_scores = (
            jnp.einsum("hqd,hkd->hqk", query_block, k_heads, preferred_element_type=jnp.float32)
            * score_scale
        )
        scores = jnp.where(
            (query_seg[:, None] == own_seg[None, :])[None], raw_scores, NEGATIVE_FILL
        )
        soft_weights = jnp.exp(scores - total_block[:, :, None])
        grad_value_new = grad_value_now + jnp.einsum(
            "hqk,hqd->hkd",
            soft_weights.astype(jnp.bfloat16),
            grad_block,
            preferred_element_type=jnp.float32,
        )
        slopes = jnp.einsum("hqd,hkd->hqk", grad_block, v_heads, preferred_element_type=jnp.float32)
        mixed_grad = (soft_weights * (slopes - delta_block[:, :, None])).astype(jnp.bfloat16)
        grad_key_new = grad_key_now + jnp.einsum(
            "hqk,hqd->hkd", mixed_grad, query_block, preferred_element_type=jnp.float32
        )
        return (grad_key_new, grad_value_new)

    all_totals, all_deltas = (
        lax.all_gather(log_total[None], "seq", axis=2, tiled=True),
        lax.all_gather(row_delta[None], "seq", axis=2, tiled=True),
    )
    member = (
        lax.all_gather(queries, "seq", axis=1, tiled=True),
        lax.all_gather(grad_attended[None], "seq", axis=1, tiled=True),
    )
    totals_piece = all_totals[0]
    deltas_piece = all_deltas[0]
    grad_key, grad_value = over_rows(
        key_grad_step,
        (frame_zeros, frame_zeros),
        (to_heads(member[0][0]), to_heads(member[1][0]), totals_piece, deltas_piece),
        jnp.int32(0),
    )
    grad_queries = from_heads(grad_query * score_scale).astype(jnp.bfloat16)[None]
    grad_keys = from_heads(grad_key * score_scale).astype(jnp.bfloat16)[None]
    grad_values = from_heads(grad_value).astype(jnp.bfloat16)[None]
    return (mixed[None], grad_queries, grad_keys, grad_values, grad_kernel)


LANES = 128
PAD = 16
VMEM = pltpu.VMEM
MIB = 1024 * 1024


def mm(left, right):
    return lax.dot_general(
        left, right, (((1,), (0,)), ((), ())), preferred_element_type=jnp.float32
    )


def mm_nt(left, right):
    return lax.dot_general(
        left, right, (((1,), (1,)), ((), ())), preferred_element_type=jnp.float32
    )


def rows_at(block, frames):
    return pl.ds(pl.multiple_of(block * frames, frames), frames)


def lanes_at(block):
    return pl.ds(pl.multiple_of(block * LANES, LANES), LANES)


def pack_kernel(ranks, q_ref, k_ref, v_ref, *rest):
    outs, (whole, sems) = rest[:-2], rest[-2:]
    me = lax.axis_index("seq")
    sources = (q_ref, k_ref, v_ref)
    run_copies([(source.at[0], whole.at[place]) for place, source in enumerate(sources)], sems)
    for step in range(ranks - 1, 0, -1):
        for place in range(len(sources)):
            outs[step - 1][place] = whole[place, :, lanes_at(me ^ step)]


def run_copies(pairs, sems, meanwhile=None):
    copies = [
        pltpu.make_async_copy(source, target, sems.at[number])
        for number, (source, target) in enumerate(pairs)
    ]
    for copy in copies:
        copy.start()
    if meanwhile is not None:
        meanwhile()
    for copy in copies:
        copy.wait()


def mask_kernel(ranks, length, lens_ref, q_ref, k_ref, v_ref, c_ref, *refs):
    cot_refs = refs[: ranks - 1]
    own_ref, col_ref, row_ref, after_ref, before_ref, sems = refs[ranks - 1 :]
    me = lax.axis_index("seq")
    pairs = [(c_ref.at[0, :, lanes_at(me ^ step)], cot_refs[step - 1]) for step in range(1, ranks)]
    for place, source in enumerate((q_ref, k_ref, v_ref, c_ref)):
        pairs.append((source.at[0, :, lanes_at(me)], own_ref.at[place]))

    def extents():
        ends = []
        running = jnp.int32(0)
        for number in range(lens_ref.shape[1]):
            running = running + lens_ref[0, number]
            ends.append(running)
        row_time = lax.broadcasted_iota(jnp.int32, row_ref.shape, 1)
        row_first = jnp.zeros(row_ref.shape, jnp.int32)
        for end in ends:
            row_first = jnp.where(row_time >= end, end, row_first)
        row_ref[...] = row_first
        chunk = 64

        def some_rows(number, carry):
            base = pl.multiple_of(number * chunk, chunk)
            time = base + lax.broadcasted_iota(jnp.int32, (chunk, LANES), 0)
            first = jnp.zeros((chunk, LANES), jnp.int32)
            last = jnp.full((chunk, LANES), length, jnp.int32)
            for end in ends:
                first = jnp.where(time >= end, end, first)
            for end in reversed(ends):
                last = jnp.where(time < end, end, last)
            rows = pl.ds(base, chunk)
            col_ref[rows, :] = first
            after_ref[rows, :] = last - 1 - time
            before_ref[rows, :] = time - first
            return carry

        lax.fori_loop(0, length // chunk, some_rows, 0)

    run_copies(pairs, sems, extents)


def forward_kernel(ranks, frames, *refs):
    recvs = refs[: ranks - 1]
    own_ref, col_ref, row_ref, after_ref, before_ref, w_ref = refs[ranks - 1 : ranks + 5]
    soft_ref, att_ref, pre_ref, q_ref, k_t_ref, v_ref = refs[ranks + 5 : ranks + 11]
    att_t_ref, k_full, q_full, w_own, w_sem = refs[ranks + 11 :]
    me = lax.axis_index("seq")
    length = ranks * frames
    copy = pltpu.make_async_copy(w_ref.at[:, lanes_at(me)], w_own, w_sem)
    copy.start()
    for place, target in enumerate((q_full, k_full, v_ref)):
        target[rows_at(me, frames), :] = own_ref[place]
        for step in range(1, ranks):
            target[rows_at(me ^ step, frames), :] = recvs[ranks - 1 - step][place]
    heads = LANES // HDIM
    lane_head = lax.broadcasted_iota(jnp.int32, (1, LANES), 1) // HDIM
    scaled = q_full[...].astype(jnp.float32) * (1.0 / math.sqrt(HDIM))
    for head in range(heads):
        q_ref[head] = jnp.where(lane_head == head, scaled, 0.0).astype(jnp.bfloat16)
    k_t_ref[...] = k_full[...].astype(jnp.float32).T.astype(jnp.bfloat16)
    v_t = v_ref[...].astype(jnp.float32).T.astype(jnp.bfloat16)
    wide = 256
    for head in range(heads):
        for start in range(0, length, wide):
            cols = slice(start, start + wide)
            raw = mm_nt(k_full[...], q_ref[head, cols, :])
            same = jnp.concatenate([col_ref[...]] * (wide // LANES), axis=1) == row_ref[0:1, cols]
            scores = jnp.where(same, raw, NEGATIVE_FILL)
            top = jnp.max(scores, axis=0, keepdims=True)
            powers = jnp.exp(scores - top)
            share = 1.0 / jnp.sum(powers, axis=0, keepdims=True)
            soft = (powers * share).astype(jnp.bfloat16)
            soft_ref[head, :, cols] = soft
            rows = slice(head * HDIM, (head + 1) * HDIM)
            att_t_ref[rows, cols] = mm(v_t[rows], soft).astype(jnp.bfloat16).astype(jnp.float32)
    zeros = jnp.zeros((PAD, LANES), jnp.float32)
    att_ref[0:PAD, :] = zeros
    att_ref[PAD : PAD + length, :] = att_t_ref[...].T
    att_ref[PAD + length :, :] = zeros
    copy.wait()

    chunk = 64

    def some_rows(number, carry):
        base = pl.multiple_of(number * chunk, chunk)
        rows = pl.ds(base, chunk)
        after, before = after_ref[rows, :], before_ref[rows, :]
        total = jnp.zeros((chunk, LANES), jnp.float32)
        for tap in range(KERNEL):
            off = tap - HALF
            piece = att_ref[pl.ds(base + (PAD + off), chunk), :]
            if off > 0:
                piece = jnp.where(after >= off, piece, 0.0)
            if off < 0:
                piece = jnp.where(before >= -off, piece, 0.0)
            total = total + w_own[tap : tap + 1, :] * piece
        pre_ref[rows, :] = total
        return carry

    lax.fori_loop(0, length // chunk, some_rows, 0)


def split_heads(wide):
    lane_head = lax.broadcasted_iota(jnp.int32, (1, LANES), 1) // HDIM
    return [jnp.where(lane_head == head, wide, 0.0).astype(jnp.bfloat16) for head in range(LANES // HDIM)]


def conv_back_kernel(ranks, frames, *refs):
    half = ranks // 2
    cots = refs[: ranks - 1]
    own_ref, pre_ref, after_ref, before_ref, soft_ref, w_ref = refs[ranks - 1 : ranks + 5]
    mixed_ref, g_att, res_v, grad_pad = refs[ranks + 5 : ranks + 9]
    early = refs[ranks + 9 : ranks + 9 + half]
    cot, w_own, w_sem = refs[ranks + 9 + half :]
    me = lax.axis_index("seq")
    length = ranks * frames
    copy = pltpu.make_async_copy(w_ref.at[:, lanes_at(me)], w_own, w_sem)
    copy.start()
    cot[rows_at(me, frames), :] = own_ref[3]
    for step in range(1, ranks):
        cot[rows_at(me ^ step, frames), :] = cots[ranks - 1 - step][...]
    zeros = jnp.zeros((PAD, LANES), jnp.float32)
    grad_pad[0:PAD, :] = zeros
    grad_pad[PAD + length :, :] = zeros
    pre = pre_ref[...]
    gate = jax.nn.sigmoid(pre)
    mixed_ref[...] = (pre * gate).astype(jnp.bfloat16)
    conv_grad = cot[...].astype(jnp.float32) * gate * (1.0 + pre * (1.0 - gate))
    grad_pad[PAD : PAD + length, :] = conv_grad.astype(jnp.bfloat16).astype(jnp.float32)
    copy.wait()
    chunk = 64

    def some_rows(number, carry):
        base = pl.multiple_of(number * chunk, chunk)
        rows = pl.ds(base, chunk)
        after, before = after_ref[rows, :], before_ref[rows, :]
        total = jnp.zeros((chunk, LANES), jnp.float32)
        for tap in range(KERNEL):
            off = tap - HALF
            piece = grad_pad[pl.ds(base + (PAD - off), chunk), :]
            if off > 0:
                piece = jnp.where(before >= off, piece, 0.0)
            if off < 0:
                piece = jnp.where(after >= -off, piece, 0.0)
            total = total + w_own[tap : tap + 1, :] * piece
        g_att[rows, :] = total.astype(jnp.bfloat16)
        return carry

    lax.fori_loop(0, length // chunk, some_rows, 0)
    g_heads = split_heads(g_att[...].astype(jnp.float32))
    grad_v = mm(soft_ref[0], g_heads[0])
    for head in range(1, LANES // HDIM):
        grad_v = grad_v + mm(soft_ref[head], g_heads[head])
    res_v[...] = grad_v.astype(jnp.bfloat16)
    for step, out in zip(range(half, ranks), early):
        rows = rows_at(me ^ step, frames)
        out[0:frames, :] = mixed_ref[rows, :]
        out[frames:, :] = res_v[rows, :]


def taps_kernel(att_ref, grad_pad, after_ref, before_ref, taps_ref, tap_sum):
    length = after_ref.shape[0]
    tap_sum[...] = jnp.zeros(tap_sum.shape, jnp.float32)
    chunk = 64

    def some_rows(number, carry):
        base = pl.multiple_of(number * chunk, chunk)
        rows = pl.ds(base, chunk)
        after, before = after_ref[rows, :], before_ref[rows, :]
        own_grad = grad_pad[pl.ds(base + PAD, chunk), :]
        for tap in range(KERNEL):
            off = tap - HALF
            piece = att_ref[pl.ds(base + (PAD + off), chunk), :]
            if off > 0:
                piece = jnp.where(after >= off, piece, 0.0)
            if off < 0:
                piece = jnp.where(before >= -off, piece, 0.0)
            part = (own_grad * piece).reshape(chunk // 8, 8, LANES)
            tap_sum[tap] = tap_sum[tap] + jnp.sum(part, axis=0)
        return carry

    lax.fori_loop(0, length // chunk, some_rows, 0)
    taps_ref[...] = jnp.sum(tap_sum[...], axis=1)


def backward_kernel(soft_ref, att_ref, g_att, q_ref, k_t_ref, v_ref, res_q, res_k, grad_t):
    length = v_ref.shape[0]
    g_wide = g_att[...].astype(jnp.float32)
    products_t = (g_wide * att_ref[PAD : PAD + length, :]).T
    g_heads = split_heads(g_wide)
    wide = 256
    grad_k = jnp.zeros((length, LANES), jnp.float32)
    for head in range(LANES // HDIM):
        rows = slice(head * HDIM, (head + 1) * HDIM)
        delta = jnp.sum(products_t[rows], axis=0, keepdims=True)
        for start in range(0, length, wide):
            cols = slice(start, start + wide)
            slopes = mm_nt(v_ref[...], g_heads[head][cols])
            soft = soft_ref[head, :, cols].astype(jnp.float32)
            mixed_grad = (soft * (slopes - delta[:, cols])).astype(jnp.bfloat16)
            grad_k = grad_k + mm(mixed_grad, q_ref[head, cols, :])
            grad_t[rows, cols] = mm(k_t_ref[rows, :], mixed_grad) * (1.0 / math.sqrt(HDIM))
    res_k[...] = grad_k.astype(jnp.bfloat16)
    res_q[...] = grad_t[...].T.astype(jnp.bfloat16)


def block_kernel(steps, frames, count, *refs):
    sources, tap_refs, outs = refs[:count], refs[count : -len(steps)], refs[-len(steps) :]
    me = lax.axis_index("seq")
    taps = tap_refs[0][...]
    for other in tap_refs[1:]:
        taps = taps + other[...]
    for step, out in zip(steps, outs):
        rows = rows_at(me ^ step, frames)
        for place, source in enumerate(sources):
            out[place * frames : (place + 1) * frames, :] = source[rows, :]
        out[count * frames :, :] = taps.astype(jnp.bfloat16)


def stage_kernel(*refs):
    half = len(refs) // 2
    for source, target in zip(refs[:half], refs[half:]):
        target[...] = source[...]


def spread_kernel(ranks, frames, *refs):
    half = ranks // 2
    near, far, early = refs[:half], refs[half:ranks], refs[ranks : ranks + half]
    targets, taps_ref = refs[ranks + half : ranks + half + 4], refs[ranks + half + 4]
    me = lax.axis_index("seq")
    for step in range(ranks):
        lanes = lanes_at(me ^ step)
        if step < half:
            parts = [(near[step], place) for place in range(4)]
            last = near[step], 4
        else:
            late, soon = far[step - half], early[step - half]
            parts = [(late, 0), (late, 1), (soon, 0), (soon, 1)]
            last = late, 2
        for target, (source, place) in zip(targets, parts):
            target[0, :, lanes] = source[place * frames : (place + 1) * frames, :]
        taps = last[0][last[1] * frames :, :].astype(jnp.float32)
        taps_ref[:, lanes] = taps[:KERNEL]


def cost(flops, moved):
    return pl.CostEstimate(flops=flops, bytes_accessed=moved, transcendentals=0)


def on_device_heads(queries, keys, values, cotangent, conv_weight, rec_lengths):
    ranks = lax.axis_size("seq")
    frames = queries.shape[1]
    length = ranks * frames
    heads = LANES // HDIM
    bf16, f32, i32 = jnp.bfloat16, jnp.float32, jnp.int32
    struct = jax.ShapeDtypeStruct
    hbm = pl.BlockSpec(memory_space=pltpu.HBM)
    anywhere = pl.BlockSpec(memory_space=pl.ANY)
    vmem = pl.BlockSpec(memory_space=VMEM)
    smem = pl.BlockSpec(memory_space=pltpu.SMEM)
    params = pltpu.CompilerParams(vmem_limit_bytes=24 * MIB)
    taps = KERNEL + 1

    sends = pl.pallas_call(
        functools.partial(pack_kernel, ranks),
        out_shape=[struct((3, frames, LANES), bf16)] * (ranks - 1),
        in_specs=[hbm] * 3,
        out_specs=[vmem] * (ranks - 1),
        scratch_shapes=[VMEM((3,) + queries.shape[1:], bf16), pltpu.SemaphoreType.DMA((3,))],
        compiler_params=pltpu.CompilerParams(vmem_limit_bytes=54912 * 1024),
        name="pack",
    )(queries, keys, values)

    def swap(array, step):
        return lax.ppermute(array, "seq", [(rank, rank ^ step) for rank in range(ranks)])

    order = list(range(ranks - 1, 0, -1))
    received = {step: swap(sends[step - 1], step) for step in order}

    *cot_sends, own, col, row, after, before = pl.pallas_call(
        functools.partial(mask_kernel, ranks, length),
        out_shape=[struct((frames, LANES), bf16)] * (ranks - 1)
        + [
            struct((4, frames, LANES), bf16),
            struct((length, LANES), i32),
            struct((8, length), i32),
            struct((length, LANES), i32),
            struct((length, LANES), i32),
        ],
        in_specs=[smem] + [hbm] * 4,
        out_specs=[vmem] * (ranks + 4),
        scratch_shapes=[pltpu.SemaphoreType.DMA((ranks + 3,))],
        compiler_params=params,
        cost_estimate=cost(4 * MIB, MIB),
        name="masks",
    )(rec_lengths, queries, keys, values, cotangent)
    cots = {step: swap(cot_sends[step - 1], step) for step in order}

    soft, att, pre, q_heads, k_t, v_full = pl.pallas_call(
        functools.partial(forward_kernel, ranks, frames),
        out_shape=[
            struct((heads, length, length), bf16),
            struct((length + 2 * PAD, LANES), f32),
            struct((length, LANES), f32),
            struct((heads, length, LANES), bf16),
            struct((LANES, length), bf16),
            struct((length, LANES), bf16),
        ],
        in_specs=[vmem] * (ranks + 4) + [anywhere],
        out_specs=[vmem] * 6,
        scratch_shapes=[
            VMEM((LANES, length), f32),
            VMEM((length, LANES), bf16),
            VMEM((length, LANES), bf16),
            VMEM((KERNEL, LANES), f32),
            pltpu.SemaphoreType.DMA,
        ],
        compiler_params=params,
        cost_estimate=cost(400 * MIB, 3 * MIB),
        name="forward",
    )(*[received[step] for step in order], own, col, row, after, before, conv_weight)

    half = ranks // 2
    wide = struct((length, LANES), bf16)
    mixed, g_att, grad_v, grad_pad, *early = pl.pallas_call(
        functools.partial(conv_back_kernel, ranks, frames),
        out_shape=[wide] * 3
        + [struct((length + 2 * PAD, LANES), f32)]
        + [struct((2 * frames, LANES), bf16)] * half,
        in_specs=[vmem] * (ranks + 4) + [anywhere],
        out_specs=[vmem] * (4 + half),
        scratch_shapes=[
            VMEM((length, LANES), bf16),
            VMEM((KERNEL, LANES), f32),
            pltpu.SemaphoreType.DMA,
        ],
        compiler_params=params,
        cost_estimate=cost(400 * MIB, 3 * MIB),
        name="conv_back",
    )(*[cots[step] for step in order], own, pre, after, before, soft, conv_weight)
    early = [swap(early[step - half], step) for step in range(half, ranks)]

    own_taps = pl.pallas_call(
        taps_kernel,
        out_shape=struct((taps, LANES), f32),
        in_specs=[vmem] * 4,
        out_specs=vmem,
        scratch_shapes=[VMEM((taps, 8, LANES), f32)],
        compiler_params=params,
        cost_estimate=cost(MIB, MIB // 64),
        name="taps",
    )(att, grad_pad, after, before)
    copies = lax.axis_size("dp")
    part_taps = [own_taps] + [
        lax.ppermute(own_taps, "dp", [(one, (one + shift) % copies) for one in range(copies)])
        for shift in range(1, copies)
    ]

    grad_q, grad_k = pl.pallas_call(
        backward_kernel,
        out_shape=[wide] * 2,
        in_specs=[vmem] * 6,
        out_specs=[vmem] * 2,
        scratch_shapes=[VMEM((LANES, length), f32)],
        compiler_params=params,
        cost_estimate=cost(MIB, MIB // 64),
        name="backward",
    )(soft, att, g_att, q_heads, k_t, v_full)

    def blocks_of(steps, *sources):
        rows = len(sources) * frames + taps
        return pl.pallas_call(
            functools.partial(block_kernel, steps, frames, len(sources)),
            out_shape=[struct((rows, LANES), bf16)] * len(steps),
            in_specs=[vmem] * (len(sources) + copies),
            out_specs=[vmem] * len(steps),
            compiler_params=params,
            cost_estimate=cost(MIB, MIB // 64),
            name="blocks",
        )(*sources, *part_taps)

    far = blocks_of(range(half, ranks), grad_q, grad_k)
    near = blocks_of(range(half), grad_q, grad_k, mixed, grad_v)
    far = [swap(far[step - half], step) for step in range(half, ranks)]
    near = [near[0]] + [swap(near[step], step) for step in range(1, half)]

    early = pl.pallas_call(
        stage_kernel,
        out_shape=[struct((2 * frames, LANES), bf16)] * half,
        in_specs=[vmem] * half,
        out_specs=[vmem] * half,
        compiler_params=params,
        cost_estimate=cost(16384 * MIB, 64 * MIB),
        name="stage",
    )(*early)

    grad_q, grad_k, mixed, grad_v, grad_taps = pl.pallas_call(
        functools.partial(spread_kernel, ranks, frames),
        out_shape=[struct(queries.shape, bf16)] * 4 + [struct(conv_weight.shape, f32)],
        in_specs=[vmem] * (ranks + half),
        out_specs=[vmem] * 5,
        compiler_params=params,
        name="spread",
    )(*near, *far, *early)
    return (mixed, grad_q, grad_k, grad_v, grad_taps)


def on_device_any(queries, keys, values, cotangent, conv_weight, rec_lengths):
    ranks = lax.axis_size("seq")
    frames, channels = queries.shape[1], queries.shape[2]
    fits = channels == ranks * LANES and ranks & (ranks - 1) == 0 and frames % LANES == 0
    if fits and ranks > 1 and ranks * frames <= 1024 and lax.axis_size("dp") == 2:
        return on_device_heads(queries, keys, values, cotangent, conv_weight, rec_lengths)
    return on_device(queries, keys, values, cotangent, conv_weight, rec_lengths)


def solution(mesh):
    placed = (
        P(("groups", "dp"), "seq", "mp"),
        P(("groups", "dp"), "seq", "mp"),
        P(("groups", "dp"), "seq", "mp"),
        P(("groups", "dp"), "seq", "mp"),
        P(None, "mp"),
        P(("groups", "dp"), None),
    )
    return jax.shard_map(
        on_device_any,
        mesh=mesh,
        in_specs=placed,
        out_specs=(
            P(("groups", "dp"), "seq", "mp"),
            P(("groups", "dp"), "seq", "mp"),
            P(("groups", "dp"), "seq", "mp"),
            P(("groups", "dp"), "seq", "mp"),
            P("groups", "mp"),
        ),
        check_vma=False,
    )
```

```python
import functools
import math

import jax
import jax.numpy as jnp
from jax import lax
from jax.experimental import pallas as pl
from jax.experimental.pallas import tpu as pltpu
from jax.sharding import PartitionSpec as P

HDIM = 64
KERNEL = 31
HALF = 15


NEGATIVE_FILL = -1e30


def extended(block, sides, width):
    for axis, dim in sides:
        count = lax.axis_size(axis)
        forward = [(i, i + 1) for i in range(count - 1)]
        backward = [(target, source) for source, target in forward]
        low = lax.ppermute(
            lax.slice_in_dim(block, block.shape[dim] - width, None, axis=dim), axis, forward
        )
        high = lax.ppermute(lax.slice_in_dim(block, 0, width, axis=dim), axis, backward)
        block = jnp.concatenate([low, block, high], axis=dim)
    return block


def pick_block(total_rows):
    for candidate in (512, 256, 128):
        return candidate
    return total_rows


def over_blocks(total_rows, advance, initial):
    block_rows = pick_block(total_rows)
    block_count = total_rows // block_rows
    if block_count == 1:
        return advance(initial, 0, block_rows)
    return lax.fori_loop(
        0,
        block_count,
        lambda number, running: advance(running, number * block_rows, block_rows),
        initial,
    )


def when_shared(compute, running):
    result = compute(running)
    return result


def on_device(queries, keys, values, cotangent, conv_weight, rec_lengths):
    frames = queries.shape[1]
    channels = queries.shape[2]
    local_heads = channels // HDIM
    score_scale = 1.0 / math.sqrt(HDIM)
    length_all = frames * lax.axis_size("seq")
    offset = lax.axis_index("seq") * frames
    record_ends = jnp.cumsum(rec_lengths[0], dtype=jnp.int32)

    def segment_of(positions):
        return jnp.sum((record_ends[None, :] <= positions[:, None]).astype(jnp.int32), axis=1)

    own_seg = segment_of(offset + jnp.arange(frames, dtype=jnp.int32))

    def to_heads(array):
        return array.reshape(array.shape[0], local_heads, HDIM).transpose(1, 0, 2)

    def from_heads(array):
        return array.transpose(1, 0, 2).reshape(array.shape[1], channels)

    q_heads = to_heads(queries[0])
    k_heads = to_heads(keys[0])
    v_heads = to_heads(values[0])

    def over_rows(advance, initial, members, first_row):
        total_rows = members[0].shape[1]

        def one_block(running, block_start, block_rows):
            sliced = tuple(
                (lax.dynamic_slice_in_dim(member, block_start, block_rows, 1) for member in members)
            )
            other_seg = segment_of(
                first_row + block_start + jnp.arange(block_rows, dtype=jnp.int32)
            )
            return when_shared(lambda current: advance(current, sliced, other_seg), running)

        return over_blocks(total_rows, one_block, initial)

    def query_scores(key_block, key_seg):
        raw_scores = (
            jnp.einsum("hqd,hkd->hqk", q_heads, key_block, preferred_element_type=jnp.float32)
            * score_scale
        )
        return jnp.where((own_seg[:, None] == key_seg[None, :])[None], raw_scores, NEGATIVE_FILL)

    def stats_step(running, sliced, key_seg):
        top_now, total_now = running
        scores = query_scores(sliced[0], key_seg)
        top_new = jnp.maximum(top_now, jnp.max(scores, axis=2))
        total_new = total_now * jnp.exp(top_now - top_new) + jnp.sum(
            jnp.exp(scores - top_new[:, :, None]), axis=2
        )
        return (top_new, total_new)

    stats_init = (
        jnp.full((local_heads, frames), NEGATIVE_FILL, jnp.float32),
        jnp.zeros((local_heads, frames), jnp.float32),
    )
    gathered = (
        lax.all_gather(keys, "seq", axis=1, tiled=True),
        lax.all_gather(values, "seq", axis=1, tiled=True),
    )
    key_whole = to_heads(gathered[0][0])
    value_whole = to_heads(gathered[1][0])
    row_stats = over_rows(stats_step, stats_init, (key_whole,), 0)
    log_total = row_stats[0] + jnp.log(row_stats[1])

    def output_step(running, sliced, key_seg):
        scores = query_scores(sliced[0], key_seg)
        soft_rounded = jnp.exp(scores - log_total[:, :, None]).astype(jnp.bfloat16)
        return running + jnp.einsum(
            "hqk,hkd->hqd", soft_rounded, sliced[1], preferred_element_type=jnp.float32
        )

    frame_zeros = jnp.zeros((local_heads, frames, HDIM), jnp.float32)
    attended_sum = over_rows(output_step, frame_zeros, (key_whole, value_whole), 0)
    attended_heads = attended_sum.astype(jnp.bfloat16)
    attended = from_heads(attended_heads)
    padded = extended(attended[None], (("seq", 1),), HALF)
    padded_wide = padded[0].astype(jnp.float32)
    pad_positions = offset - HALF + jnp.arange(frames + 2 * HALF, dtype=jnp.int32)
    inside = jnp.logical_and(pad_positions >= 0, pad_positions < length_all)
    pad_seg = jnp.where(inside, segment_of(pad_positions), -1)
    conv_pre = jnp.zeros((frames, channels), jnp.float32)
    for tap_index in range(KERNEL):
        tap_mask = (pad_seg[tap_index : tap_index + frames] == own_seg)[:, None]
        conv_pre = conv_pre + jnp.where(
            tap_mask, conv_weight[tap_index] * padded_wide[tap_index : tap_index + frames], 0.0
        )
    gate_value = jax.nn.sigmoid(conv_pre)
    mixed = (conv_pre * gate_value).astype(jnp.bfloat16)
    conv_grad = (
        cotangent[0].astype(jnp.float32) * gate_value * (1.0 + conv_pre * (1.0 - gate_value))
    ).astype(jnp.bfloat16)
    padded_grad = extended(conv_grad[None], (("seq", 1),), HALF)
    grad_wide = padded_grad[0].astype(jnp.float32)
    conv_grad_wide = conv_grad.astype(jnp.float32)
    grad_attended = jnp.zeros((frames, channels), jnp.float32)
    kernel_rows = []
    for tap_index in range(KERNEL):
        back_start = 2 * HALF - tap_index
        back_mask = (pad_seg[back_start : back_start + frames] == own_seg)[:, None]
        grad_attended = grad_attended + jnp.where(
            back_mask, conv_weight[tap_index] * grad_wide[back_start : back_start + frames], 0.0
        )
        tap_mask = (pad_seg[tap_index : tap_index + frames] == own_seg)[:, None]
        product = conv_grad_wide * padded_wide[tap_index : tap_index + frames]
        kernel_rows.append(jnp.sum(jnp.where(tap_mask, product, 0.0), axis=0))
    grad_kernel = lax.psum(jnp.stack(kernel_rows), ("dp", "seq"))
    grad_attended = grad_attended.astype(jnp.bfloat16)
    g_heads = to_heads(grad_attended)
    row_delta = jnp.sum(g_heads.astype(jnp.float32) * attended_heads.astype(jnp.float32), axis=2)

    def query_grad_step(running, sliced, key_seg):
        key_block = sliced[0]
        value_block = sliced[1]
        soft_weights = jnp.exp(query_scores(key_block, key_seg) - log_total[:, :, None])
        slopes = jnp.einsum(
            "hqd,hkd->hqk", g_heads, value_block, preferred_element_type=jnp.float32
        )
        mixed_grad = (soft_weights * (slopes - row_delta[:, :, None])).astype(jnp.bfloat16)
        return running + jnp.einsum(
            "hqk,hkd->hqd", mixed_grad, key_block, preferred_element_type=jnp.float32
        )

    grad_query = over_rows(query_grad_step, frame_zeros, (key_whole, value_whole), 0)

    def key_grad_step(running, sliced, query_seg):
        grad_key_now, grad_value_now = running
        query_block = sliced[0]
        grad_block = sliced[1]
        total_block = sliced[2]
        delta_block = sliced[3]
        raw_scores = (
            jnp.einsum("hqd,hkd->hqk", query_block, k_heads, preferred_element_type=jnp.float32)
            * score_scale
        )
        scores = jnp.where(
            (query_seg[:, None] == own_seg[None, :])[None], raw_scores, NEGATIVE_FILL
        )
        soft_weights = jnp.exp(scores - total_block[:, :, None])
        grad_value_new = grad_value_now + jnp.einsum(
            "hqk,hqd->hkd",
            soft_weights.astype(jnp.bfloat16),
            grad_block,
            preferred_element_type=jnp.float32,
        )
        slopes = jnp.einsum("hqd,hkd->hqk", grad_block, v_heads, preferred_element_type=jnp.float32)
        mixed_grad = (soft_weights * (slopes - delta_block[:, :, None])).astype(jnp.bfloat16)
        grad_key_new = grad_key_now + jnp.einsum(
            "hqk,hqd->hkd", mixed_grad, query_block, preferred_element_type=jnp.float32
        )
        return (grad_key_new, grad_value_new)

    all_totals, all_deltas = (
        lax.all_gather(log_total[None], "seq", axis=2, tiled=True),
        lax.all_gather(row_delta[None], "seq", axis=2, tiled=True),
    )
    member = (
        lax.all_gather(queries, "seq", axis=1, tiled=True),
        lax.all_gather(grad_attended[None], "seq", axis=1, tiled=True),
    )
    totals_piece = all_totals[0]
    deltas_piece = all_deltas[0]
    grad_key, grad_value = over_rows(
        key_grad_step,
        (frame_zeros, frame_zeros),
        (to_heads(member[0][0]), to_heads(member[1][0]), totals_piece, deltas_piece),
        jnp.int32(0),
    )
    grad_queries = from_heads(grad_query * score_scale).astype(jnp.bfloat16)[None]
    grad_keys = from_heads(grad_key * score_scale).astype(jnp.bfloat16)[None]
    grad_values = from_heads(grad_value).astype(jnp.bfloat16)[None]
    return (mixed[None], grad_queries, grad_keys, grad_values, grad_kernel)


LANES = 128
PAD = 16
VMEM = pltpu.VMEM
MIB = 1024 * 1024


def mm(left, right):
    return lax.dot_general(
        left, right, (((1,), (0,)), ((), ())), preferred_element_type=jnp.float32
    )


def mm_nt(left, right):
    return lax.dot_general(
        left, right, (((1,), (1,)), ((), ())), preferred_element_type=jnp.float32
    )


def rows_at(block, frames):
    return pl.ds(pl.multiple_of(block * frames, frames), frames)


def lanes_at(block):
    return pl.ds(pl.multiple_of(block * LANES, LANES), LANES)


def partners(ranks):
    middle = ranks // 2
    return [middle] + [step for step in range(ranks - 1, 0, -1) if step != middle]


def pack_kernel(ranks, q_ref, k_ref, v_ref, c_ref, *rest):
    outs, whole, sems = rest[: ranks - 1], *rest[ranks - 1 :]
    me = lax.axis_index("seq")
    sources = (q_ref, k_ref, v_ref, c_ref)
    run_copies([(source.at[0], whole.at[place]) for place, source in enumerate(sources)], sems)
    for step in range(1, ranks):
        lanes = lanes_at(me ^ step)
        for place in range(outs[step - 1].shape[0]):
            outs[step - 1][place] = whole[place, :, lanes]


def run_copies(pairs, sems, meanwhile=None):
    copies = [
        pltpu.make_async_copy(source, target, sems.at[number])
        for number, (source, target) in enumerate(pairs)
    ]
    for copy in copies:
        copy.start()
    if meanwhile is not None:
        meanwhile()
    for copy in copies:
        copy.wait()


def mask_kernel(ranks, length, lens_ref, q_ref, k_ref, v_ref, c_ref, *refs):
    late_ref, own_ref, col_ref, row_ref, after_ref, before_ref, sems = refs
    me = lax.axis_index("seq")
    lanes = lanes_at(me)
    pairs = [
        (source.at[0, :, lanes], own_ref.at[place])
        for place, source in enumerate((q_ref, k_ref, v_ref, c_ref))
    ]
    pairs.append((c_ref.at[0, :, lanes_at(me ^ (ranks // 2))], late_ref))

    def extents():
        ends = []
        running = jnp.int32(0)
        for number in range(lens_ref.shape[1]):
            running = running + lens_ref[0, number]
            ends.append(running)
        row_time = lax.broadcasted_iota(jnp.int32, row_ref.shape, 1)
        row_first = jnp.zeros(row_ref.shape, jnp.int32)
        for end in ends:
            row_first = jnp.where(row_time >= end, end, row_first)
        row_ref[...] = row_first
        chunk = 64

        def some_rows(number, carry):
            base = pl.multiple_of(number * chunk, chunk)
            time = base + lax.broadcasted_iota(jnp.int32, (chunk, LANES), 0)
            first = jnp.zeros((chunk, LANES), jnp.int32)
            last = jnp.full((chunk, LANES), length, jnp.int32)
            for end in ends:
                first = jnp.where(time >= end, end, first)
            for end in reversed(ends):
                last = jnp.where(time < end, end, last)
            rows = pl.ds(base, chunk)
            col_ref[rows, :] = first
            after_ref[rows, :] = last - 1 - time
            before_ref[rows, :] = time - first
            return carry

        lax.fori_loop(0, length // chunk, some_rows, 0)

    run_copies(pairs, sems, extents)


def forward_kernel(ranks, frames, *refs):
    recvs = dict(zip(partners(ranks), refs))
    own_ref, col_ref, row_ref, after_ref, before_ref, w_ref = refs[ranks - 1 : ranks + 5]
    soft_ref, att_ref, pre_ref, q_ref, k_t_ref, v_ref = refs[ranks + 5 : ranks + 11]
    att_t_ref, k_full, q_full, w_own, w_sem = refs[ranks + 11 :]
    me = lax.axis_index("seq")
    length = ranks * frames
    copy = pltpu.make_async_copy(w_ref.at[:, lanes_at(me)], w_own, w_sem)
    copy.start()
    for place, target in enumerate((q_full, k_full, v_ref)):
        target[rows_at(me, frames), :] = own_ref[place]
        for step in range(1, ranks):
            target[rows_at(me ^ step, frames), :] = recvs[step][place]
    heads = LANES // HDIM
    lane_head = lax.broadcasted_iota(jnp.int32, (1, LANES), 1) // HDIM
    scaled = q_full[...].astype(jnp.float32) * (1.0 / math.sqrt(HDIM))
    for head in range(heads):
        q_ref[head] = jnp.where(lane_head == head, scaled, 0.0).astype(jnp.bfloat16)
    k_t_ref[...] = k_full[...].astype(jnp.float32).T.astype(jnp.bfloat16)
    v_t = v_ref[...].astype(jnp.float32).T.astype(jnp.bfloat16)
    wide = 256
    for head in range(heads):
        for start in range(0, length, wide):
            cols = slice(start, start + wide)
            raw = mm_nt(k_full[...], q_ref[head, cols, :])
            same = jnp.concatenate([col_ref[...]] * (wide // LANES), axis=1) == row_ref[0:1, cols]
            scores = jnp.where(same, raw, NEGATIVE_FILL)
            top = jnp.max(scores, axis=0, keepdims=True)
            powers = jnp.exp(scores - top)
            share = 1.0 / jnp.sum(powers, axis=0, keepdims=True)
            soft = (powers * share).astype(jnp.bfloat16)
            soft_ref[head, :, cols] = soft
            rows = slice(head * HDIM, (head + 1) * HDIM)
            att_t_ref[rows, cols] = mm(v_t[rows], soft).astype(jnp.bfloat16).astype(jnp.float32)
    zeros = jnp.zeros((PAD, LANES), jnp.float32)
    att_ref[0:PAD, :] = zeros
    att_ref[PAD : PAD + length, :] = att_t_ref[...].T
    att_ref[PAD + length :, :] = zeros
    copy.wait()

    chunk = 64

    def some_rows(number, carry):
        base = pl.multiple_of(number * chunk, chunk)
        rows = pl.ds(base, chunk)
        after, before = after_ref[rows, :], before_ref[rows, :]
        total = jnp.zeros((chunk, LANES), jnp.float32)
        for tap in range(KERNEL):
            off = tap - HALF
            piece = att_ref[pl.ds(base + (PAD + off), chunk), :]
            if off > 0:
                piece = jnp.where(after >= off, piece, 0.0)
            if off < 0:
                piece = jnp.where(before >= -off, piece, 0.0)
            total = total + w_own[tap : tap + 1, :] * piece
        pre_ref[rows, :] = total
        return carry

    lax.fori_loop(0, length // chunk, some_rows, 0)


def split_heads(wide):
    lane_head = lax.broadcasted_iota(jnp.int32, (1, LANES), 1) // HDIM
    return [jnp.where(lane_head == head, wide, 0.0).astype(jnp.bfloat16) for head in range(LANES // HDIM)]


def conv_back_kernel(ranks, frames, *refs):
    cots = refs[: ranks - 1]
    own_ref, pre_ref, after_ref, before_ref, soft_ref, w_ref = refs[ranks - 1 : ranks + 5]
    mixed_ref, g_att, res_v, grad_pad, early = refs[ranks + 5 : ranks + 10]
    cot, w_own, w_sem = refs[ranks + 10 :]
    me = lax.axis_index("seq")
    length = ranks * frames
    copy = pltpu.make_async_copy(w_ref.at[:, lanes_at(me)], w_own, w_sem)
    copy.start()
    cot[rows_at(me, frames), :] = own_ref[3]
    for step in range(1, ranks):
        block = cots[step - 1]
        cot[rows_at(me ^ step, frames), :] = block[...] if step == ranks // 2 else block[3]
    zeros = jnp.zeros((PAD, LANES), jnp.float32)
    grad_pad[0:PAD, :] = zeros
    grad_pad[PAD + length :, :] = zeros
    pre = pre_ref[...]
    gate = jax.nn.sigmoid(pre)
    mixed_ref[...] = (pre * gate).astype(jnp.bfloat16)
    conv_grad = cot[...].astype(jnp.float32) * gate * (1.0 + pre * (1.0 - gate))
    grad_pad[PAD : PAD + length, :] = conv_grad.astype(jnp.bfloat16).astype(jnp.float32)
    copy.wait()
    chunk = 64

    def some_rows(number, carry):
        base = pl.multiple_of(number * chunk, chunk)
        rows = pl.ds(base, chunk)
        after, before = after_ref[rows, :], before_ref[rows, :]
        total = jnp.zeros((chunk, LANES), jnp.float32)
        for tap in range(KERNEL):
            off = tap - HALF
            piece = grad_pad[pl.ds(base + (PAD - off), chunk), :]
            if off > 0:
                piece = jnp.where(before >= off, piece, 0.0)
            if off < 0:
                piece = jnp.where(after >= -off, piece, 0.0)
            total = total + w_own[tap : tap + 1, :] * piece
        g_att[rows, :] = total.astype(jnp.bfloat16)
        return carry

    lax.fori_loop(0, length // chunk, some_rows, 0)
    g_heads = split_heads(g_att[...].astype(jnp.float32))
    grad_v = mm(soft_ref[0], g_heads[0])
    for head in range(1, LANES // HDIM):
        grad_v = grad_v + mm(soft_ref[head], g_heads[head])
    res_v[...] = grad_v.astype(jnp.bfloat16)
    rows = rows_at(me ^ (ranks // 2), frames)
    early[0:frames, :] = mixed_ref[rows, :]
    early[frames:, :] = res_v[rows, :]


def taps_kernel(att_ref, grad_pad, after_ref, before_ref, taps_ref, tap_sum):
    length = after_ref.shape[0]
    tap_sum[...] = jnp.zeros(tap_sum.shape, jnp.float32)
    chunk = 64

    def some_rows(number, carry):
        base = pl.multiple_of(number * chunk, chunk)
        rows = pl.ds(base, chunk)
        after, before = after_ref[rows, :], before_ref[rows, :]
        own_grad = grad_pad[pl.ds(base + PAD, chunk), :]
        for tap in range(KERNEL):
            off = tap - HALF
            piece = att_ref[pl.ds(base + (PAD + off), chunk), :]
            if off > 0:
                piece = jnp.where(after >= off, piece, 0.0)
            if off < 0:
                piece = jnp.where(before >= -off, piece, 0.0)
            part = (own_grad * piece).reshape(chunk // 8, 8, LANES)
            tap_sum[tap] = tap_sum[tap] + jnp.sum(part, axis=0)
        return carry

    lax.fori_loop(0, length // chunk, some_rows, 0)
    taps_ref[...] = jnp.sum(tap_sum[...], axis=1)


def backward_kernel(soft_ref, att_ref, g_att, q_ref, k_t_ref, v_ref, res_q, res_k, grad_t):
    length = v_ref.shape[0]
    g_wide = g_att[...].astype(jnp.float32)
    products_t = (g_wide * att_ref[PAD : PAD + length, :]).T
    g_heads = split_heads(g_wide)
    wide = 256
    grad_k = jnp.zeros((length, LANES), jnp.float32)
    for head in range(LANES // HDIM):
        rows = slice(head * HDIM, (head + 1) * HDIM)
        delta = jnp.sum(products_t[rows], axis=0, keepdims=True)
        for start in range(0, length, wide):
            cols = slice(start, start + wide)
            slopes = mm_nt(v_ref[...], g_heads[head][cols])
            soft = soft_ref[head, :, cols].astype(jnp.float32)
            mixed_grad = (soft * (slopes - delta[:, cols])).astype(jnp.bfloat16)
            grad_k = grad_k + mm(mixed_grad, q_ref[head, cols, :])
            grad_t[rows, cols] = mm(k_t_ref[rows, :], mixed_grad) * (1.0 / math.sqrt(HDIM))
    res_k[...] = grad_k.astype(jnp.bfloat16)
    res_q[...] = grad_t[...].T.astype(jnp.bfloat16)


def block_kernel(steps, frames, count, *refs):
    sources, tap_refs, outs = refs[:count], refs[count : -len(steps)], refs[-len(steps) :]
    me = lax.axis_index("seq")
    taps = tap_refs[0][...]
    for other in tap_refs[1:]:
        taps = taps + other[...]
    for step, out in zip(steps, outs):
        rows = rows_at(me ^ step, frames)
        for place, source in enumerate(sources):
            out[place * frames : (place + 1) * frames, :] = source[rows, :]
        out[count * frames :, :] = taps.astype(jnp.bfloat16)


def stage_kernel(source, target):
    target[...] = source[...]


def spread_kernel(ranks, frames, *refs):
    blocks, early = refs[:ranks], refs[ranks]
    targets, taps_ref = refs[ranks + 1 : ranks + 5], refs[ranks + 5]
    me = lax.axis_index("seq")
    for step in range(ranks):
        lanes = lanes_at(me ^ step)
        parts = [(blocks[step], place) for place in range(4)]
        if step == ranks // 2:
            parts[2:] = [(early, 0), (early, 1)]
        for target, (source, place) in zip(targets, parts):
            target[0, :, lanes] = source[place * frames : (place + 1) * frames, :]
        taps = blocks[step][-(KERNEL + 1) :, :].astype(jnp.float32)
        taps_ref[:, lanes] = taps[:KERNEL]


def cost(flops, moved):
    return pl.CostEstimate(flops=flops, bytes_accessed=moved, transcendentals=0)


def on_device_heads(queries, keys, values, cotangent, conv_weight, rec_lengths):
    ranks = lax.axis_size("seq")
    frames = queries.shape[1]
    length = ranks * frames
    heads = LANES // HDIM
    bf16, f32, i32 = jnp.bfloat16, jnp.float32, jnp.int32
    struct = jax.ShapeDtypeStruct
    hbm = pl.BlockSpec(memory_space=pltpu.HBM)
    anywhere = pl.BlockSpec(memory_space=pl.ANY)
    vmem = pl.BlockSpec(memory_space=VMEM)
    smem = pl.BlockSpec(memory_space=pltpu.SMEM)
    params = pltpu.CompilerParams(vmem_limit_bytes=24 * MIB)
    taps = KERNEL + 1

    middle = ranks // 2
    light = partners(ranks)[1:]

    sends = pl.pallas_call(
        functools.partial(pack_kernel, ranks),
        out_shape=[
            struct((3 if step == middle else 4, frames, LANES), bf16) for step in range(1, ranks)
        ],
        in_specs=[hbm] * 4,
        out_specs=[vmem] * (ranks - 1),
        scratch_shapes=[VMEM((4,) + queries.shape[1:], bf16), pltpu.SemaphoreType.DMA((4,))],
        compiler_params=pltpu.CompilerParams(vmem_limit_bytes=54832 * 1024),
        name="pack",
    )(queries, keys, values, cotangent)

    def swap(array, step):
        return lax.ppermute(array, "seq", [(rank, rank ^ step) for rank in range(ranks)])

    order = partners(ranks)
    received = {step: swap(sends[step - 1], step) for step in order}

    late_send, own, col, row, after, before = pl.pallas_call(
        functools.partial(mask_kernel, ranks, length),
        out_shape=[
            struct((frames, LANES), bf16),
            struct((4, frames, LANES), bf16),
            struct((length, LANES), i32),
            struct((8, length), i32),
            struct((length, LANES), i32),
            struct((length, LANES), i32),
        ],
        in_specs=[smem] + [hbm] * 4,
        out_specs=[vmem] * 6,
        scratch_shapes=[pltpu.SemaphoreType.DMA((5,))],
        compiler_params=params,
        cost_estimate=cost(16384 * MIB, 64 * MIB),
        name="masks",
    )(rec_lengths, queries, keys, values, cotangent)
    cots = received | {middle: swap(late_send, middle)}

    soft, att, pre, q_heads, k_t, v_full = pl.pallas_call(
        functools.partial(forward_kernel, ranks, frames),
        out_shape=[
            struct((heads, length, length), bf16),
            struct((length + 2 * PAD, LANES), f32),
            struct((length, LANES), f32),
            struct((heads, length, LANES), bf16),
            struct((LANES, length), bf16),
            struct((length, LANES), bf16),
        ],
        in_specs=[vmem] * (ranks + 4) + [anywhere],
        out_specs=[vmem] * 6,
        scratch_shapes=[
            VMEM((LANES, length), f32),
            VMEM((length, LANES), bf16),
            VMEM((length, LANES), bf16),
            VMEM((KERNEL, LANES), f32),
            pltpu.SemaphoreType.DMA,
        ],
        compiler_params=params,
        cost_estimate=cost(400 * MIB, 3 * MIB),
        name="forward",
    )(*[received[step] for step in order], own, col, row, after, before, conv_weight)

    wide = struct((length, LANES), bf16)
    mixed, g_att, grad_v, grad_pad, early = pl.pallas_call(
        functools.partial(conv_back_kernel, ranks, frames),
        out_shape=[wide] * 3
        + [struct((length + 2 * PAD, LANES), f32)]
        + [struct((2 * frames, LANES), bf16)],
        in_specs=[vmem] * (ranks + 4) + [anywhere],
        out_specs=[vmem] * 5,
        scratch_shapes=[
            VMEM((length, LANES), bf16),
            VMEM((KERNEL, LANES), f32),
            pltpu.SemaphoreType.DMA,
        ],
        compiler_params=params,
        cost_estimate=cost(400 * MIB, 3 * MIB),
        name="conv_back",
    )(*[cots[step] for step in range(1, ranks)], own, pre, after, before, soft, conv_weight)
    early = swap(early, middle)

    own_taps = pl.pallas_call(
        taps_kernel,
        out_shape=struct((taps, LANES), f32),
        in_specs=[vmem] * 4,
        out_specs=vmem,
        scratch_shapes=[VMEM((taps, 8, LANES), f32)],
        compiler_params=params,
        cost_estimate=cost(MIB, MIB // 64),
        name="taps",
    )(att, grad_pad, after, before)
    copies = lax.axis_size("dp")
    part_taps = [own_taps] + [
        lax.ppermute(own_taps, "dp", [(one, (one + shift) % copies) for one in range(copies)])
        for shift in range(1, copies)
    ]

    grad_q, grad_k = pl.pallas_call(
        backward_kernel,
        out_shape=[wide] * 2,
        in_specs=[vmem] * 6,
        out_specs=[vmem] * 2,
        scratch_shapes=[VMEM((LANES, length), f32)],
        compiler_params=params,
        cost_estimate=cost(MIB, MIB // 64),
        name="backward",
    )(soft, att, g_att, q_heads, k_t, v_full)

    def blocks_of(steps, *sources):
        rows = len(sources) * frames + taps
        return pl.pallas_call(
            functools.partial(block_kernel, steps, frames, len(sources)),
            out_shape=[struct((rows, LANES), bf16)] * len(steps),
            in_specs=[vmem] * (len(sources) + copies),
            out_specs=[vmem] * len(steps),
            compiler_params=params,
            cost_estimate=cost(MIB, MIB // 64),
            name="blocks",
        )(*sources, *part_taps)

    (blocks,) = blocks_of([middle], grad_q, grad_k)
    rest = blocks_of([0] + light, grad_q, grad_k, mixed, grad_v)
    blocks = {middle: swap(blocks, middle), 0: rest[0]}
    blocks |= {step: swap(rest[1 + number], step) for number, step in enumerate(light)}

    early = pl.pallas_call(
        stage_kernel,
        out_shape=struct((2 * frames, LANES), bf16),
        in_specs=[vmem],
        out_specs=vmem,
        compiler_params=params,
        cost_estimate=cost(16384 * MIB, 64 * MIB),
        name="stage",
    )(early)

    grad_q, grad_k, mixed, grad_v, grad_taps = pl.pallas_call(
        functools.partial(spread_kernel, ranks, frames),
        out_shape=[struct(queries.shape, bf16)] * 4 + [struct(conv_weight.shape, f32)],
        in_specs=[vmem] * (ranks + 1),
        out_specs=[vmem] * 5,
        compiler_params=params,
        name="spread",
    )(*[blocks[step] for step in range(ranks)], early)
    return (mixed, grad_q, grad_k, grad_v, grad_taps)


def on_device_any(queries, keys, values, cotangent, conv_weight, rec_lengths):
    ranks = lax.axis_size("seq")
    frames, channels = queries.shape[1], queries.shape[2]
    fits = channels == ranks * LANES and ranks & (ranks - 1) == 0 and frames % LANES == 0
    if fits and ranks > 1 and ranks * frames <= 1024 and lax.axis_size("dp") == 2:
        return on_device_heads(queries, keys, values, cotangent, conv_weight, rec_lengths)
    return on_device(queries, keys, values, cotangent, conv_weight, rec_lengths)


def solution(mesh):
    placed = (
        P(("groups", "dp"), "seq", "mp"),
        P(("groups", "dp"), "seq", "mp"),
        P(("groups", "dp"), "seq", "mp"),
        P(("groups", "dp"), "seq", "mp"),
        P(None, "mp"),
        P(("groups", "dp"), None),
    )
    return jax.shard_map(
        on_device_any,
        mesh=mesh,
        in_specs=placed,
        out_specs=(
            P(("groups", "dp"), "seq", "mp"),
            P(("groups", "dp"), "seq", "mp"),
            P(("groups", "dp"), "seq", "mp"),
            P(("groups", "dp"), "seq", "mp"),
            P("groups", "mp"),
        ),
        check_vma=False,
    )
```

```python
import functools
import math

import jax
import jax.numpy as jnp
from jax import lax
from jax.experimental import pallas as pl
from jax.experimental.pallas import tpu as pltpu
from jax.sharding import PartitionSpec as P

HDIM = 64
KERNEL = 31
HALF = 15


NEGATIVE_FILL = -1e30


def extended(block, sides, width):
    for axis, dim in sides:
        count = lax.axis_size(axis)
        forward = [(i, i + 1) for i in range(count - 1)]
        backward = [(target, source) for source, target in forward]
        low = lax.ppermute(
            lax.slice_in_dim(block, block.shape[dim] - width, None, axis=dim), axis, forward
        )
        high = lax.ppermute(lax.slice_in_dim(block, 0, width, axis=dim), axis, backward)
        block = jnp.concatenate([low, block, high], axis=dim)
    return block


def pick_block(total_rows):
    for candidate in (512, 256, 128):
        return candidate
    return total_rows


def over_blocks(total_rows, advance, initial):
    block_rows = pick_block(total_rows)
    block_count = total_rows // block_rows
    if block_count == 1:
        return advance(initial, 0, block_rows)
    return lax.fori_loop(
        0,
        block_count,
        lambda number, running: advance(running, number * block_rows, block_rows),
        initial,
    )


def when_shared(compute, running):
    result = compute(running)
    return result


def on_device(queries, keys, values, cotangent, conv_weight, rec_lengths):
    frames = queries.shape[1]
    channels = queries.shape[2]
    local_heads = channels // HDIM
    score_scale = 1.0 / math.sqrt(HDIM)
    length_all = frames * lax.axis_size("seq")
    offset = lax.axis_index("seq") * frames
    record_ends = jnp.cumsum(rec_lengths[0], dtype=jnp.int32)

    def segment_of(positions):
        return jnp.sum((record_ends[None, :] <= positions[:, None]).astype(jnp.int32), axis=1)

    own_seg = segment_of(offset + jnp.arange(frames, dtype=jnp.int32))

    def to_heads(array):
        return array.reshape(array.shape[0], local_heads, HDIM).transpose(1, 0, 2)

    def from_heads(array):
        return array.transpose(1, 0, 2).reshape(array.shape[1], channels)

    q_heads = to_heads(queries[0])
    k_heads = to_heads(keys[0])
    v_heads = to_heads(values[0])

    def over_rows(advance, initial, members, first_row):
        total_rows = members[0].shape[1]

        def one_block(running, block_start, block_rows):
            sliced = tuple(
                (lax.dynamic_slice_in_dim(member, block_start, block_rows, 1) for member in members)
            )
            other_seg = segment_of(
                first_row + block_start + jnp.arange(block_rows, dtype=jnp.int32)
            )
            return when_shared(lambda current: advance(current, sliced, other_seg), running)

        return over_blocks(total_rows, one_block, initial)

    def query_scores(key_block, key_seg):
        raw_scores = (
            jnp.einsum("hqd,hkd->hqk", q_heads, key_block, preferred_element_type=jnp.float32)
            * score_scale
        )
        return jnp.where((own_seg[:, None] == key_seg[None, :])[None], raw_scores, NEGATIVE_FILL)

    def stats_step(running, sliced, key_seg):
        top_now, total_now = running
        scores = query_scores(sliced[0], key_seg)
        top_new = jnp.maximum(top_now, jnp.max(scores, axis=2))
        total_new = total_now * jnp.exp(top_now - top_new) + jnp.sum(
            jnp.exp(scores - top_new[:, :, None]), axis=2
        )
        return (top_new, total_new)

    stats_init = (
        jnp.full((local_heads, frames), NEGATIVE_FILL, jnp.float32),
        jnp.zeros((local_heads, frames), jnp.float32),
    )
    gathered = (
        lax.all_gather(keys, "seq", axis=1, tiled=True),
        lax.all_gather(values, "seq", axis=1, tiled=True),
    )
    key_whole = to_heads(gathered[0][0])
    value_whole = to_heads(gathered[1][0])
    row_stats = over_rows(stats_step, stats_init, (key_whole,), 0)
    log_total = row_stats[0] + jnp.log(row_stats[1])

    def output_step(running, sliced, key_seg):
        scores = query_scores(sliced[0], key_seg)
        soft_rounded = jnp.exp(scores - log_total[:, :, None]).astype(jnp.bfloat16)
        return running + jnp.einsum(
            "hqk,hkd->hqd", soft_rounded, sliced[1], preferred_element_type=jnp.float32
        )

    frame_zeros = jnp.zeros((local_heads, frames, HDIM), jnp.float32)
    attended_sum = over_rows(output_step, frame_zeros, (key_whole, value_whole), 0)
    attended_heads = attended_sum.astype(jnp.bfloat16)
    attended = from_heads(attended_heads)
    padded = extended(attended[None], (("seq", 1),), HALF)
    padded_wide = padded[0].astype(jnp.float32)
    pad_positions = offset - HALF + jnp.arange(frames + 2 * HALF, dtype=jnp.int32)
    inside = jnp.logical_and(pad_positions >= 0, pad_positions < length_all)
    pad_seg = jnp.where(inside, segment_of(pad_positions), -1)
    conv_pre = jnp.zeros((frames, channels), jnp.float32)
    for tap_index in range(KERNEL):
        tap_mask = (pad_seg[tap_index : tap_index + frames] == own_seg)[:, None]
        conv_pre = conv_pre + jnp.where(
            tap_mask, conv_weight[tap_index] * padded_wide[tap_index : tap_index + frames], 0.0
        )
    gate_value = jax.nn.sigmoid(conv_pre)
    mixed = (conv_pre * gate_value).astype(jnp.bfloat16)
    conv_grad = (
        cotangent[0].astype(jnp.float32) * gate_value * (1.0 + conv_pre * (1.0 - gate_value))
    ).astype(jnp.bfloat16)
    padded_grad = extended(conv_grad[None], (("seq", 1),), HALF)
    grad_wide = padded_grad[0].astype(jnp.float32)
    conv_grad_wide = conv_grad.astype(jnp.float32)
    grad_attended = jnp.zeros((frames, channels), jnp.float32)
    kernel_rows = []
    for tap_index in range(KERNEL):
        back_start = 2 * HALF - tap_index
        back_mask = (pad_seg[back_start : back_start + frames] == own_seg)[:, None]
        grad_attended = grad_attended + jnp.where(
            back_mask, conv_weight[tap_index] * grad_wide[back_start : back_start + frames], 0.0
        )
        tap_mask = (pad_seg[tap_index : tap_index + frames] == own_seg)[:, None]
        product = conv_grad_wide * padded_wide[tap_index : tap_index + frames]
        kernel_rows.append(jnp.sum(jnp.where(tap_mask, product, 0.0), axis=0))
    grad_kernel = lax.psum(jnp.stack(kernel_rows), ("dp", "seq"))
    grad_attended = grad_attended.astype(jnp.bfloat16)
    g_heads = to_heads(grad_attended)
    row_delta = jnp.sum(g_heads.astype(jnp.float32) * attended_heads.astype(jnp.float32), axis=2)

    def query_grad_step(running, sliced, key_seg):
        key_block = sliced[0]
        value_block = sliced[1]
        soft_weights = jnp.exp(query_scores(key_block, key_seg) - log_total[:, :, None])
        slopes = jnp.einsum(
            "hqd,hkd->hqk", g_heads, value_block, preferred_element_type=jnp.float32
        )
        mixed_grad = (soft_weights * (slopes - row_delta[:, :, None])).astype(jnp.bfloat16)
        return running + jnp.einsum(
            "hqk,hkd->hqd", mixed_grad, key_block, preferred_element_type=jnp.float32
        )

    grad_query = over_rows(query_grad_step, frame_zeros, (key_whole, value_whole), 0)

    def key_grad_step(running, sliced, query_seg):
        grad_key_now, grad_value_now = running
        query_block = sliced[0]
        grad_block = sliced[1]
        total_block = sliced[2]
        delta_block = sliced[3]
        raw_scores = (
            jnp.einsum("hqd,hkd->hqk", query_block, k_heads, preferred_element_type=jnp.float32)
            * score_scale
        )
        scores = jnp.where(
            (query_seg[:, None] == own_seg[None, :])[None], raw_scores, NEGATIVE_FILL
        )
        soft_weights = jnp.exp(scores - total_block[:, :, None])
        grad_value_new = grad_value_now + jnp.einsum(
            "hqk,hqd->hkd",
            soft_weights.astype(jnp.bfloat16),
            grad_block,
            preferred_element_type=jnp.float32,
        )
        slopes = jnp.einsum("hqd,hkd->hqk", grad_block, v_heads, preferred_element_type=jnp.float32)
        mixed_grad = (soft_weights * (slopes - delta_block[:, :, None])).astype(jnp.bfloat16)
        grad_key_new = grad_key_now + jnp.einsum(
            "hqk,hqd->hkd", mixed_grad, query_block, preferred_element_type=jnp.float32
        )
        return (grad_key_new, grad_value_new)

    all_totals, all_deltas = (
        lax.all_gather(log_total[None], "seq", axis=2, tiled=True),
        lax.all_gather(row_delta[None], "seq", axis=2, tiled=True),
    )
    member = (
        lax.all_gather(queries, "seq", axis=1, tiled=True),
        lax.all_gather(grad_attended[None], "seq", axis=1, tiled=True),
    )
    totals_piece = all_totals[0]
    deltas_piece = all_deltas[0]
    grad_key, grad_value = over_rows(
        key_grad_step,
        (frame_zeros, frame_zeros),
        (to_heads(member[0][0]), to_heads(member[1][0]), totals_piece, deltas_piece),
        jnp.int32(0),
    )
    grad_queries = from_heads(grad_query * score_scale).astype(jnp.bfloat16)[None]
    grad_keys = from_heads(grad_key * score_scale).astype(jnp.bfloat16)[None]
    grad_values = from_heads(grad_value).astype(jnp.bfloat16)[None]
    return (mixed[None], grad_queries, grad_keys, grad_values, grad_kernel)


LANES = 128
PAD = 16
VMEM = pltpu.VMEM
MIB = 1024 * 1024


def mm(left, right):
    return lax.dot_general(
        left, right, (((1,), (0,)), ((), ())), preferred_element_type=jnp.float32
    )


def mm_nt(left, right):
    return lax.dot_general(
        left, right, (((1,), (1,)), ((), ())), preferred_element_type=jnp.float32
    )


def rows_at(block, frames):
    return pl.ds(pl.multiple_of(block * frames, frames), frames)


def lanes_at(block):
    return pl.ds(pl.multiple_of(block * LANES, LANES), LANES)


def pack_kernel(ranks, q_ref, k_ref, v_ref, c_ref, *rest):
    outs, (whole, sems) = rest[:-2], rest[-2:]
    me = lax.axis_index("seq")
    sources = (q_ref, k_ref, v_ref, c_ref)
    run_copies([(source.at[0], whole.at[place]) for place, source in enumerate(sources)], sems)
    for step in range(ranks - 1, 0, -1):
        for place in range(len(sources)):
            outs[step - 1][place] = whole[place, :, lanes_at(me ^ step)]


def run_copies(pairs, sems, meanwhile=None):
    copies = [
        pltpu.make_async_copy(source, target, sems.at[number])
        for number, (source, target) in enumerate(pairs)
    ]
    for copy in copies:
        copy.start()
    if meanwhile is not None:
        meanwhile()
    for copy in copies:
        copy.wait()


def mask_kernel(length, lens_ref, q_ref, k_ref, v_ref, c_ref, *refs):
    own_ref, col_ref, row_ref, after_ref, before_ref, sems = refs
    lanes = lanes_at(lax.axis_index("seq"))
    pairs = [
        (source.at[0, :, lanes], own_ref.at[place])
        for place, source in enumerate((q_ref, k_ref, v_ref, c_ref))
    ]

    def extents():
        ends = []
        running = jnp.int32(0)
        for number in range(lens_ref.shape[1]):
            running = running + lens_ref[0, number]
            ends.append(running)
        row_time = lax.broadcasted_iota(jnp.int32, row_ref.shape, 1)
        row_first = jnp.zeros(row_ref.shape, jnp.int32)
        for end in ends:
            row_first = jnp.where(row_time >= end, end, row_first)
        row_ref[...] = row_first
        chunk = 64

        def some_rows(number, carry):
            base = pl.multiple_of(number * chunk, chunk)
            time = base + lax.broadcasted_iota(jnp.int32, (chunk, LANES), 0)
            first = jnp.zeros((chunk, LANES), jnp.int32)
            last = jnp.full((chunk, LANES), length, jnp.int32)
            for end in ends:
                first = jnp.where(time >= end, end, first)
            for end in reversed(ends):
                last = jnp.where(time < end, end, last)
            rows = pl.ds(base, chunk)
            col_ref[rows, :] = first
            after_ref[rows, :] = last - 1 - time
            before_ref[rows, :] = time - first
            return carry

        lax.fori_loop(0, length // chunk, some_rows, 0)

    run_copies(pairs, sems, extents)


def forward_kernel(ranks, frames, *refs):
    recvs = dict(zip(range(ranks - 1, 0, -1), refs))
    own_ref, col_ref, row_ref, after_ref, before_ref, w_ref = refs[ranks - 1 : ranks + 5]
    soft_ref, att_ref, q_ref, k_t_ref, v_ref, mixed_ref, g_att, taps_ref = refs[ranks + 5 : ranks + 13]
    att_t_ref, k_full, q_full, cot, grad_pad, tap_sum, w_own, w_sem = refs[ranks + 13 :]
    me = lax.axis_index("seq")
    length = ranks * frames
    copy = pltpu.make_async_copy(w_ref.at[:, lanes_at(me)], w_own, w_sem)
    copy.start()
    for place, target in enumerate((q_full, k_full, v_ref, cot)):
        target[rows_at(me, frames), :] = own_ref[place]
        for step in range(1, ranks):
            target[rows_at(me ^ step, frames), :] = recvs[step][place]
    zeros = jnp.zeros((PAD, LANES), jnp.float32)
    for padded in (att_ref, grad_pad):
        padded[0:PAD, :] = zeros
        padded[PAD + length :, :] = zeros
    tap_sum[...] = jnp.zeros(tap_sum.shape, jnp.float32)
    heads = LANES // HDIM
    lane_head = lax.broadcasted_iota(jnp.int32, (1, LANES), 1) // HDIM
    scaled = q_full[...].astype(jnp.float32) * (1.0 / math.sqrt(HDIM))
    for head in range(heads):
        q_ref[head] = jnp.where(lane_head == head, scaled, 0.0).astype(jnp.bfloat16)
    k_t_ref[...] = k_full[...].astype(jnp.float32).T.astype(jnp.bfloat16)
    v_t = v_ref[...].astype(jnp.float32).T.astype(jnp.bfloat16)
    wide = 256
    for head in range(heads):
        for start in range(0, length, wide):
            cols = slice(start, start + wide)
            raw = mm_nt(k_full[...], q_ref[head, cols, :])
            same = jnp.concatenate([col_ref[...]] * (wide // LANES), axis=1) == row_ref[0:1, cols]
            scores = jnp.where(same, raw, NEGATIVE_FILL)
            top = jnp.max(scores, axis=0, keepdims=True)
            powers = jnp.exp(scores - top)
            share = 1.0 / jnp.sum(powers, axis=0, keepdims=True)
            soft = (powers * share).astype(jnp.bfloat16)
            soft_ref[head, :, cols] = soft
            rows = slice(head * HDIM, (head + 1) * HDIM)
            att_t_ref[rows, cols] = mm(v_t[rows], soft).astype(jnp.bfloat16).astype(jnp.float32)
    att_ref[PAD : PAD + length, :] = att_t_ref[...].T
    copy.wait()
    chunk = 64

    def masked(source, base, off, low, high):
        piece = source[pl.ds(base + (PAD + off), chunk), :]
        if off > 0:
            piece = jnp.where(high >= off, piece, 0.0)
        if off < 0:
            piece = jnp.where(low >= -off, piece, 0.0)
        return piece

    def conv_rows(number, carry):
        base = pl.multiple_of(number * chunk, chunk)
        rows = pl.ds(base, chunk)
        after, before = after_ref[rows, :], before_ref[rows, :]
        pre = jnp.zeros((chunk, LANES), jnp.float32)
        for tap in range(KERNEL):
            pre = pre + w_own[tap : tap + 1, :] * masked(att_ref, base, tap - HALF, before, after)
        gate = jax.nn.sigmoid(pre)
        mixed_ref[rows, :] = (pre * gate).astype(jnp.bfloat16)
        conv_grad = cot[rows, :].astype(jnp.float32) * gate * (1.0 + pre * (1.0 - gate))
        grad_pad[pl.ds(base + PAD, chunk), :] = conv_grad.astype(jnp.bfloat16).astype(jnp.float32)
        return carry

    lax.fori_loop(0, length // chunk, conv_rows, 0)

    def back_rows(number, carry):
        base = pl.multiple_of(number * chunk, chunk)
        rows = pl.ds(base, chunk)
        after, before = after_ref[rows, :], before_ref[rows, :]
        own_att = att_ref[pl.ds(base + PAD, chunk), :]
        total = jnp.zeros((chunk, LANES), jnp.float32)
        for tap in range(KERNEL):
            piece = masked(grad_pad, base, HALF - tap, before, after)
            total = total + w_own[tap : tap + 1, :] * piece
            part = (own_att * piece).reshape(chunk // 8, 8, LANES)
            tap_sum[tap] = tap_sum[tap] + jnp.sum(part, axis=0)
        g_att[rows, :] = total.astype(jnp.bfloat16)
        return carry

    lax.fori_loop(0, length // chunk, back_rows, 0)
    taps_ref[...] = jnp.sum(tap_sum[...], axis=1)


def backward_kernel(soft_ref, att_ref, g_att, q_ref, k_t_ref, v_ref, res_q, res_k, res_v, grad_t):
    length = v_ref.shape[0]
    heads = LANES // HDIM
    lane_head = lax.broadcasted_iota(jnp.int32, (1, LANES), 1) // HDIM
    g_wide = g_att[...].astype(jnp.float32)
    products_t = (g_wide * att_ref[PAD : PAD + length, :]).T
    g_heads = [jnp.where(lane_head == head, g_wide, 0.0).astype(jnp.bfloat16) for head in range(heads)]
    wide = 256
    grad_v = jnp.zeros((length, LANES), jnp.float32)
    grad_k = jnp.zeros((length, LANES), jnp.float32)
    for head in range(heads):
        rows = slice(head * HDIM, (head + 1) * HDIM)
        delta = jnp.sum(products_t[rows], axis=0, keepdims=True)
        for start in range(0, length, wide):
            cols = slice(start, start + wide)
            soft = soft_ref[head, :, cols]
            slopes = mm_nt(v_ref[...], g_heads[head][cols])
            mixed_grad = (soft.astype(jnp.float32) * (slopes - delta[:, cols])).astype(jnp.bfloat16)
            grad_v = grad_v + mm(soft, g_heads[head][cols])
            grad_k = grad_k + mm(mixed_grad, q_ref[head, cols, :])
            grad_t[rows, cols] = mm(k_t_ref[rows, :], mixed_grad) * (1.0 / math.sqrt(HDIM))
    res_k[...] = grad_k.astype(jnp.bfloat16)
    res_v[...] = grad_v.astype(jnp.bfloat16)
    res_q[...] = grad_t[...].T.astype(jnp.bfloat16)


def block_kernel(steps, frames, *refs):
    sources, tap_refs, outs = refs[:4], refs[4 : -len(steps)], refs[-len(steps) :]
    me = lax.axis_index("seq")
    taps = tap_refs[0][...]
    for other in tap_refs[1:]:
        taps = taps + other[...]
    for step, out in zip(steps, outs):
        rows = rows_at(me ^ step, frames)
        for place, source in enumerate(sources):
            out[place * frames : (place + 1) * frames, :] = source[rows, :]
        out[4 * frames :, :] = taps.astype(jnp.bfloat16)


def spread_kernel(ranks, frames, *refs):
    blocks = refs[:ranks][::-1]
    targets, taps_ref = refs[ranks : ranks + 4], refs[ranks + 4]
    me = lax.axis_index("seq")
    for step in range(ranks):
        lanes = lanes_at(me ^ step)
        for place, target in enumerate(targets):
            target[0, :, lanes] = blocks[step][place * frames : (place + 1) * frames, :]
        taps = blocks[step][4 * frames :, :].astype(jnp.float32)
        taps_ref[:, lanes] = taps[:KERNEL]


def cost(flops, moved):
    return pl.CostEstimate(flops=flops, bytes_accessed=moved, transcendentals=0)


def on_device_heads(queries, keys, values, cotangent, conv_weight, rec_lengths):
    ranks = lax.axis_size("seq")
    frames = queries.shape[1]
    length = ranks * frames
    heads = LANES // HDIM
    bf16, f32, i32 = jnp.bfloat16, jnp.float32, jnp.int32
    struct = jax.ShapeDtypeStruct
    hbm = pl.BlockSpec(memory_space=pltpu.HBM)
    anywhere = pl.BlockSpec(memory_space=pl.ANY)
    vmem = pl.BlockSpec(memory_space=VMEM)
    smem = pl.BlockSpec(memory_space=pltpu.SMEM)
    params = pltpu.CompilerParams(vmem_limit_bytes=24 * MIB)
    taps = KERNEL + 1

    sends = pl.pallas_call(
        functools.partial(pack_kernel, ranks),
        out_shape=[struct((4, frames, LANES), bf16)] * (ranks - 1),
        in_specs=[hbm] * 4,
        out_specs=[vmem] * (ranks - 1),
        scratch_shapes=[VMEM((4,) + queries.shape[1:], bf16), pltpu.SemaphoreType.DMA((4,))],
        compiler_params=pltpu.CompilerParams(vmem_limit_bytes=54784 * 1024),
        name="pack",
    )(queries, keys, values, cotangent)

    def swap(array, step):
        return lax.ppermute(array, "seq", [(rank, rank ^ step) for rank in range(ranks)])

    received = [swap(sends[step - 1], step) for step in range(ranks - 1, 0, -1)]

    own, col, row, after, before = pl.pallas_call(
        functools.partial(mask_kernel, length),
        out_shape=[
            struct((4, frames, LANES), bf16),
            struct((length, LANES), i32),
            struct((8, length), i32),
            struct((length, LANES), i32),
            struct((length, LANES), i32),
        ],
        in_specs=[smem] + [hbm] * 4,
        out_specs=[vmem] * 5,
        scratch_shapes=[pltpu.SemaphoreType.DMA((4,))],
        compiler_params=params,
        cost_estimate=cost(16384 * MIB, 64 * MIB),
        name="masks",
    )(rec_lengths, queries, keys, values, cotangent)

    wide = struct((length, LANES), bf16)
    padded = (length + 2 * PAD, LANES)
    soft, att, q_heads, k_t, v_full, mixed, g_att, own_taps = pl.pallas_call(
        functools.partial(forward_kernel, ranks, frames),
        out_shape=[
            struct((heads, length, length), bf16),
            struct(padded, f32),
            struct((heads, length, LANES), bf16),
            struct((LANES, length), bf16),
            wide,
            wide,
            wide,
            struct((taps, LANES), f32),
        ],
        in_specs=[vmem] * (ranks + 4) + [anywhere],
        out_specs=[vmem] * 8,
        scratch_shapes=[
            VMEM((LANES, length), f32),
            VMEM((length, LANES), bf16),
            VMEM((length, LANES), bf16),
            VMEM((length, LANES), bf16),
            VMEM(padded, f32),
            VMEM((taps, 8, LANES), f32),
            VMEM((KERNEL, LANES), f32),
            pltpu.SemaphoreType.DMA,
        ],
        compiler_params=params,
        cost_estimate=cost(800 * MIB, 3 * MIB),
        name="forward",
    )(*received, own, col, row, after, before, conv_weight)

    copies = lax.axis_size("dp")
    part_taps = [own_taps] + [
        lax.ppermute(own_taps, "dp", [(one, (one + shift) % copies) for one in range(copies)])
        for shift in range(1, copies)
    ]

    results = pl.pallas_call(
        backward_kernel,
        out_shape=[struct((length, LANES), bf16)] * 3,
        in_specs=[vmem] * 6,
        out_specs=[vmem] * 3,
        scratch_shapes=[VMEM((LANES, length), f32)],
        compiler_params=params,
        cost_estimate=cost(800 * MIB, 3 * MIB),
        name="backward",
    )(soft, att, g_att, q_heads, k_t, v_full)

    steps = list(range(ranks - 1, -1, -1))
    blocks = pl.pallas_call(
        functools.partial(block_kernel, steps, frames),
        out_shape=[struct((4 * frames + taps, LANES), bf16)] * ranks,
        in_specs=[vmem] * (4 + copies),
        out_specs=[vmem] * ranks,
        compiler_params=params,
        cost_estimate=cost(MIB, MIB),
        name="blocks",
    )(mixed, *results, *part_taps)
    back = [swap(block, step) if step else block for block, step in zip(blocks, steps)]

    return pl.pallas_call(
        functools.partial(spread_kernel, ranks, frames),
        out_shape=[struct(queries.shape, bf16)] * 4 + [struct(conv_weight.shape, f32)],
        in_specs=[vmem] * ranks,
        out_specs=[vmem] * 5,
        compiler_params=params,
        name="spread",
    )(*back)


def on_device_any(queries, keys, values, cotangent, conv_weight, rec_lengths):
    ranks = lax.axis_size("seq")
    frames, channels = queries.shape[1], queries.shape[2]
    fits = channels == ranks * LANES and ranks & (ranks - 1) == 0 and frames % LANES == 0
    if fits and ranks > 1 and ranks * frames <= 1024 and lax.axis_size("dp") == 2:
        return on_device_heads(queries, keys, values, cotangent, conv_weight, rec_lengths)
    return on_device(queries, keys, values, cotangent, conv_weight, rec_lengths)


def solution(mesh):
    placed = (
        P(("groups", "dp"), "seq", "mp"),
        P(("groups", "dp"), "seq", "mp"),
        P(("groups", "dp"), "seq", "mp"),
        P(("groups", "dp"), "seq", "mp"),
        P(None, "mp"),
        P(("groups", "dp"), None),
    )
    return jax.shard_map(
        on_device_any,
        mesh=mesh,
        in_specs=placed,
        out_specs=(
            P(("groups", "dp"), "seq", "mp"),
            P(("groups", "dp"), "seq", "mp"),
            P(("groups", "dp"), "seq", "mp"),
            P(("groups", "dp"), "seq", "mp"),
            P("groups", "mp"),
        ),
        check_vma=False,
    )
```

```python
import functools
import math

import jax
import jax.numpy as jnp
from jax import lax
from jax.experimental import pallas as pl
from jax.experimental.pallas import tpu as pltpu
from jax.sharding import PartitionSpec as P

HDIM = 64
KERNEL = 31
HALF = 15


NEGATIVE_FILL = -1e30


def extended(block, sides, width):
    for axis, dim in sides:
        count = lax.axis_size(axis)
        forward = [(i, i + 1) for i in range(count - 1)]
        backward = [(target, source) for source, target in forward]
        low = lax.ppermute(
            lax.slice_in_dim(block, block.shape[dim] - width, None, axis=dim), axis, forward
        )
        high = lax.ppermute(lax.slice_in_dim(block, 0, width, axis=dim), axis, backward)
        block = jnp.concatenate([low, block, high], axis=dim)
    return block


def pick_block(total_rows):
    for candidate in (512, 256, 128):
        return candidate
    return total_rows


def over_blocks(total_rows, advance, initial):
    block_rows = pick_block(total_rows)
    block_count = total_rows // block_rows
    if block_count == 1:
        return advance(initial, 0, block_rows)
    return lax.fori_loop(
        0,
        block_count,
        lambda number, running: advance(running, number * block_rows, block_rows),
        initial,
    )


def when_shared(compute, running):
    result = compute(running)
    return result


def on_device(queries, keys, values, cotangent, conv_weight, rec_lengths):
    frames = queries.shape[1]
    channels = queries.shape[2]
    local_heads = channels // HDIM
    score_scale = 1.0 / math.sqrt(HDIM)
    length_all = frames * lax.axis_size("seq")
    offset = lax.axis_index("seq") * frames
    record_ends = jnp.cumsum(rec_lengths[0], dtype=jnp.int32)

    def segment_of(positions):
        return jnp.sum((record_ends[None, :] <= positions[:, None]).astype(jnp.int32), axis=1)

    own_seg = segment_of(offset + jnp.arange(frames, dtype=jnp.int32))

    def to_heads(array):
        return array.reshape(array.shape[0], local_heads, HDIM).transpose(1, 0, 2)

    def from_heads(array):
        return array.transpose(1, 0, 2).reshape(array.shape[1], channels)

    q_heads = to_heads(queries[0])
    k_heads = to_heads(keys[0])
    v_heads = to_heads(values[0])

    def over_rows(advance, initial, members, first_row):
        total_rows = members[0].shape[1]

        def one_block(running, block_start, block_rows):
            sliced = tuple(
                (lax.dynamic_slice_in_dim(member, block_start, block_rows, 1) for member in members)
            )
            other_seg = segment_of(
                first_row + block_start + jnp.arange(block_rows, dtype=jnp.int32)
            )
            return when_shared(lambda current: advance(current, sliced, other_seg), running)

        return over_blocks(total_rows, one_block, initial)

    def query_scores(key_block, key_seg):
        raw_scores = (
            jnp.einsum("hqd,hkd->hqk", q_heads, key_block, preferred_element_type=jnp.float32)
            * score_scale
        )
        return jnp.where((own_seg[:, None] == key_seg[None, :])[None], raw_scores, NEGATIVE_FILL)

    def stats_step(running, sliced, key_seg):
        top_now, total_now = running
        scores = query_scores(sliced[0], key_seg)
        top_new = jnp.maximum(top_now, jnp.max(scores, axis=2))
        total_new = total_now * jnp.exp(top_now - top_new) + jnp.sum(
            jnp.exp(scores - top_new[:, :, None]), axis=2
        )
        return (top_new, total_new)

    stats_init = (
        jnp.full((local_heads, frames), NEGATIVE_FILL, jnp.float32),
        jnp.zeros((local_heads, frames), jnp.float32),
    )
    gathered = (
        lax.all_gather(keys, "seq", axis=1, tiled=True),
        lax.all_gather(values, "seq", axis=1, tiled=True),
    )
    key_whole = to_heads(gathered[0][0])
    value_whole = to_heads(gathered[1][0])
    row_stats = over_rows(stats_step, stats_init, (key_whole,), 0)
    log_total = row_stats[0] + jnp.log(row_stats[1])

    def output_step(running, sliced, key_seg):
        scores = query_scores(sliced[0], key_seg)
        soft_rounded = jnp.exp(scores - log_total[:, :, None]).astype(jnp.bfloat16)
        return running + jnp.einsum(
            "hqk,hkd->hqd", soft_rounded, sliced[1], preferred_element_type=jnp.float32
        )

    frame_zeros = jnp.zeros((local_heads, frames, HDIM), jnp.float32)
    attended_sum = over_rows(output_step, frame_zeros, (key_whole, value_whole), 0)
    attended_heads = attended_sum.astype(jnp.bfloat16)
    attended = from_heads(attended_heads)
    padded = extended(attended[None], (("seq", 1),), HALF)
    padded_wide = padded[0].astype(jnp.float32)
    pad_positions = offset - HALF + jnp.arange(frames + 2 * HALF, dtype=jnp.int32)
    inside = jnp.logical_and(pad_positions >= 0, pad_positions < length_all)
    pad_seg = jnp.where(inside, segment_of(pad_positions), -1)
    conv_pre = jnp.zeros((frames, channels), jnp.float32)
    for tap_index in range(KERNEL):
        tap_mask = (pad_seg[tap_index : tap_index + frames] == own_seg)[:, None]
        conv_pre = conv_pre + jnp.where(
            tap_mask, conv_weight[tap_index] * padded_wide[tap_index : tap_index + frames], 0.0
        )
    gate_value = jax.nn.sigmoid(conv_pre)
    mixed = (conv_pre * gate_value).astype(jnp.bfloat16)
    conv_grad = (
        cotangent[0].astype(jnp.float32) * gate_value * (1.0 + conv_pre * (1.0 - gate_value))
    ).astype(jnp.bfloat16)
    padded_grad = extended(conv_grad[None], (("seq", 1),), HALF)
    grad_wide = padded_grad[0].astype(jnp.float32)
    conv_grad_wide = conv_grad.astype(jnp.float32)
    grad_attended = jnp.zeros((frames, channels), jnp.float32)
    kernel_rows = []
    for tap_index in range(KERNEL):
        back_start = 2 * HALF - tap_index
        back_mask = (pad_seg[back_start : back_start + frames] == own_seg)[:, None]
        grad_attended = grad_attended + jnp.where(
            back_mask, conv_weight[tap_index] * grad_wide[back_start : back_start + frames], 0.0
        )
        tap_mask = (pad_seg[tap_index : tap_index + frames] == own_seg)[:, None]
        product = conv_grad_wide * padded_wide[tap_index : tap_index + frames]
        kernel_rows.append(jnp.sum(jnp.where(tap_mask, product, 0.0), axis=0))
    grad_kernel = lax.psum(jnp.stack(kernel_rows), ("dp", "seq"))
    grad_attended = grad_attended.astype(jnp.bfloat16)
    g_heads = to_heads(grad_attended)
    row_delta = jnp.sum(g_heads.astype(jnp.float32) * attended_heads.astype(jnp.float32), axis=2)

    def query_grad_step(running, sliced, key_seg):
        key_block = sliced[0]
        value_block = sliced[1]
        soft_weights = jnp.exp(query_scores(key_block, key_seg) - log_total[:, :, None])
        slopes = jnp.einsum(
            "hqd,hkd->hqk", g_heads, value_block, preferred_element_type=jnp.float32
        )
        mixed_grad = (soft_weights * (slopes - row_delta[:, :, None])).astype(jnp.bfloat16)
        return running + jnp.einsum(
            "hqk,hkd->hqd", mixed_grad, key_block, preferred_element_type=jnp.float32
        )

    grad_query = over_rows(query_grad_step, frame_zeros, (key_whole, value_whole), 0)

    def key_grad_step(running, sliced, query_seg):
        grad_key_now, grad_value_now = running
        query_block = sliced[0]
        grad_block = sliced[1]
        total_block = sliced[2]
        delta_block = sliced[3]
        raw_scores = (
            jnp.einsum("hqd,hkd->hqk", query_block, k_heads, preferred_element_type=jnp.float32)
            * score_scale
        )
        scores = jnp.where(
            (query_seg[:, None] == own_seg[None, :])[None], raw_scores, NEGATIVE_FILL
        )
        soft_weights = jnp.exp(scores - total_block[:, :, None])
        grad_value_new = grad_value_now + jnp.einsum(
            "hqk,hqd->hkd",
            soft_weights.astype(jnp.bfloat16),
            grad_block,
            preferred_element_type=jnp.float32,
        )
        slopes = jnp.einsum("hqd,hkd->hqk", grad_block, v_heads, preferred_element_type=jnp.float32)
        mixed_grad = (soft_weights * (slopes - delta_block[:, :, None])).astype(jnp.bfloat16)
        grad_key_new = grad_key_now + jnp.einsum(
            "hqk,hqd->hkd", mixed_grad, query_block, preferred_element_type=jnp.float32
        )
        return (grad_key_new, grad_value_new)

    all_totals, all_deltas = (
        lax.all_gather(log_total[None], "seq", axis=2, tiled=True),
        lax.all_gather(row_delta[None], "seq", axis=2, tiled=True),
    )
    member = (
        lax.all_gather(queries, "seq", axis=1, tiled=True),
        lax.all_gather(grad_attended[None], "seq", axis=1, tiled=True),
    )
    totals_piece = all_totals[0]
    deltas_piece = all_deltas[0]
    grad_key, grad_value = over_rows(
        key_grad_step,
        (frame_zeros, frame_zeros),
        (to_heads(member[0][0]), to_heads(member[1][0]), totals_piece, deltas_piece),
        jnp.int32(0),
    )
    grad_queries = from_heads(grad_query * score_scale).astype(jnp.bfloat16)[None]
    grad_keys = from_heads(grad_key * score_scale).astype(jnp.bfloat16)[None]
    grad_values = from_heads(grad_value).astype(jnp.bfloat16)[None]
    return (mixed[None], grad_queries, grad_keys, grad_values, grad_kernel)


LANES = 128
PAD = 16
VMEM = pltpu.VMEM
MIB = 1024 * 1024


def mm(left, right):
    return lax.dot_general(
        left, right, (((1,), (0,)), ((), ())), preferred_element_type=jnp.float32
    )


def mm_nt(left, right):
    return lax.dot_general(
        left, right, (((1,), (1,)), ((), ())), preferred_element_type=jnp.float32
    )


def rows_at(block, frames):
    return pl.ds(pl.multiple_of(block * frames, frames), frames)


def lanes_at(block):
    return pl.ds(pl.multiple_of(block * LANES, LANES), LANES)


def pack_kernel(ranks, q_ref, k_ref, v_ref, *rest):
    outs, (whole, sems) = rest[:-2], rest[-2:]
    me = lax.axis_index("seq")
    sources = (q_ref, k_ref, v_ref)
    run_copies([(source.at[0], whole.at[place]) for place, source in enumerate(sources)], sems)
    for step in range(ranks - 1, 0, -1):
        for place in range(len(sources)):
            outs[step - 1][place] = whole[place, :, lanes_at(me ^ step)]


def run_copies(pairs, sems, meanwhile=None):
    copies = [
        pltpu.make_async_copy(source, target, sems.at[number])
        for number, (source, target) in enumerate(pairs)
    ]
    for copy in copies:
        copy.start()
    if meanwhile is not None:
        meanwhile()
    for copy in copies:
        copy.wait()


def mask_kernel(ranks, length, lens_ref, q_ref, k_ref, v_ref, c_ref, *refs):
    cot_refs = refs[: ranks - 1]
    own_ref, col_ref, row_ref, after_ref, before_ref, sems = refs[ranks - 1 :]
    me = lax.axis_index("seq")
    pairs = [(c_ref.at[0, :, lanes_at(me ^ step)], cot_refs[step - 1]) for step in range(1, ranks)]
    for place, source in enumerate((q_ref, k_ref, v_ref, c_ref)):
        pairs.append((source.at[0, :, lanes_at(me)], own_ref.at[place]))

    def extents():
        ends = []
        running = jnp.int32(0)
        for number in range(lens_ref.shape[1]):
            running = running + lens_ref[0, number]
            ends.append(running)
        row_time = lax.broadcasted_iota(jnp.int32, row_ref.shape, 1)
        row_first = jnp.zeros(row_ref.shape, jnp.int32)
        for end in ends:
            row_first = jnp.where(row_time >= end, end, row_first)
        row_ref[...] = row_first
        chunk = 64

        def some_rows(number, carry):
            base = pl.multiple_of(number * chunk, chunk)
            time = base + lax.broadcasted_iota(jnp.int32, (chunk, LANES), 0)
            first = jnp.zeros((chunk, LANES), jnp.int32)
            last = jnp.full((chunk, LANES), length, jnp.int32)
            for end in ends:
                first = jnp.where(time >= end, end, first)
            for end in reversed(ends):
                last = jnp.where(time < end, end, last)
            rows = pl.ds(base, chunk)
            col_ref[rows, :] = first
            after_ref[rows, :] = last - 1 - time
            before_ref[rows, :] = time - first
            return carry

        lax.fori_loop(0, length // chunk, some_rows, 0)

    run_copies(pairs, sems, extents)


def forward_kernel(ranks, frames, *refs):
    recvs = refs[: ranks - 1]
    own_ref, col_ref, row_ref, after_ref, before_ref, w_ref = refs[ranks - 1 : ranks + 5]
    soft_ref, att_ref, pre_ref, q_ref, k_t_ref, v_ref = refs[ranks + 5 : ranks + 11]
    att_t_ref, k_full, q_full, w_own, w_sem = refs[ranks + 11 :]
    me = lax.axis_index("seq")
    length = ranks * frames
    copy = pltpu.make_async_copy(w_ref.at[:, lanes_at(me)], w_own, w_sem)
    copy.start()
    for place, target in enumerate((q_full, k_full, v_ref)):
        target[rows_at(me, frames), :] = own_ref[place]
        for step in range(1, ranks):
            target[rows_at(me ^ step, frames), :] = recvs[ranks - 1 - step][place]
    heads = LANES // HDIM
    lane_head = lax.broadcasted_iota(jnp.int32, (1, LANES), 1) // HDIM
    scaled = q_full[...].astype(jnp.float32) * (1.0 / math.sqrt(HDIM))
    for head in range(heads):
        q_ref[head] = jnp.where(lane_head == head, scaled, 0.0).astype(jnp.bfloat16)
    k_t_ref[...] = k_full[...].astype(jnp.float32).T.astype(jnp.bfloat16)
    v_t = v_ref[...].astype(jnp.float32).T.astype(jnp.bfloat16)
    wide = 512
    for head in range(heads):
        for start in range(0, length, wide):
            cols = slice(start, start + wide)
            raw = mm_nt(k_full[...], q_ref[head, cols, :])
            same = jnp.concatenate([col_ref[...]] * (wide // LANES), axis=1) == row_ref[0:1, cols]
            scores = jnp.where(same, raw, NEGATIVE_FILL)
            top = jnp.max(scores, axis=0, keepdims=True)
            powers = jnp.exp(scores - top)
            share = 1.0 / jnp.sum(powers, axis=0, keepdims=True)
            soft = (powers * share).astype(jnp.bfloat16)
            soft_ref[head, :, cols] = soft
            rows = slice(head * HDIM, (head + 1) * HDIM)
            att_t_ref[rows, cols] = mm(v_t[rows], soft).astype(jnp.bfloat16).astype(jnp.float32)
    zeros = jnp.zeros((PAD, LANES), jnp.float32)
    att_ref[0:PAD, :] = zeros
    att_ref[PAD : PAD + length, :] = att_t_ref[...].T
    att_ref[PAD + length :, :] = zeros
    copy.wait()

    chunk = 64

    def some_rows(number, carry):
        base = pl.multiple_of(number * chunk, chunk)
        rows = pl.ds(base, chunk)
        after, before = after_ref[rows, :], before_ref[rows, :]
        total = jnp.zeros((chunk, LANES), jnp.float32)
        for tap in range(KERNEL):
            off = tap - HALF
            piece = att_ref[pl.ds(base + (PAD + off), chunk), :]
            if off > 0:
                piece = jnp.where(after >= off, piece, 0.0)
            if off < 0:
                piece = jnp.where(before >= -off, piece, 0.0)
            total = total + w_own[tap : tap + 1, :] * piece
        pre_ref[rows, :] = total
        return carry

    lax.fori_loop(0, length // chunk, some_rows, 0)


def conv_back_kernel(ranks, frames, *refs):
    cots = refs[: ranks - 1]
    own_ref, att_ref, pre_ref, after_ref, before_ref, w_ref = refs[ranks - 1 : ranks + 5]
    mixed_ref, g_att, taps_ref, cot, grad_pad, tap_sum, w_own, w_sem = refs[ranks + 5 :]
    me = lax.axis_index("seq")
    length = ranks * frames
    copy = pltpu.make_async_copy(w_ref.at[:, lanes_at(me)], w_own, w_sem)
    copy.start()
    cot[rows_at(me, frames), :] = own_ref[3]
    for step in range(1, ranks):
        cot[rows_at(me ^ step, frames), :] = cots[ranks - 1 - step][...]
    zeros = jnp.zeros((PAD, LANES), jnp.float32)
    grad_pad[0:PAD, :] = zeros
    grad_pad[PAD + length :, :] = zeros
    pre = pre_ref[...]
    gate = jax.nn.sigmoid(pre)
    mixed_ref[...] = (pre * gate).astype(jnp.bfloat16)
    conv_grad = cot[...].astype(jnp.float32) * gate * (1.0 + pre * (1.0 - gate))
    grad_pad[PAD : PAD + length, :] = conv_grad.astype(jnp.bfloat16).astype(jnp.float32)
    tap_sum[...] = jnp.zeros(tap_sum.shape, jnp.float32)
    copy.wait()

    chunk = 64

    def some_rows(number, carry):
        base = pl.multiple_of(number * chunk, chunk)
        rows = pl.ds(base, chunk)
        after, before = after_ref[rows, :], before_ref[rows, :]
        own_att = att_ref[pl.ds(base + PAD, chunk), :]
        total = jnp.zeros((chunk, LANES), jnp.float32)
        for tap in range(KERNEL):
            off = tap - HALF
            piece = grad_pad[pl.ds(base + (PAD - off), chunk), :]
            if off > 0:
                piece = jnp.where(before >= off, piece, 0.0)
            if off < 0:
                piece = jnp.where(after >= -off, piece, 0.0)
            total = total + w_own[tap : tap + 1, :] * piece
            part = (own_att * piece).reshape(chunk // 8, 8, LANES)
            tap_sum[tap] = tap_sum[tap] + jnp.sum(part, axis=0)
        g_att[rows, :] = total.astype(jnp.bfloat16)
        return carry

    lax.fori_loop(0, length // chunk, some_rows, 0)
    taps_ref[...] = jnp.sum(tap_sum[...], axis=1)


def backward_kernel(soft_ref, att_ref, g_att, q_ref, k_t_ref, v_ref, res_q, res_k, res_v, grad_t):
    length = v_ref.shape[0]
    heads = LANES // HDIM
    lane_head = lax.broadcasted_iota(jnp.int32, (1, LANES), 1) // HDIM
    g_wide = g_att[...].astype(jnp.float32)
    products_t = (g_wide * att_ref[PAD : PAD + length, :]).T
    g_heads = [jnp.where(lane_head == head, g_wide, 0.0).astype(jnp.bfloat16) for head in range(heads)]
    wide = 512
    grad_v = jnp.zeros((length, LANES), jnp.float32)
    grad_k = jnp.zeros((length, LANES), jnp.float32)
    for head in range(heads):
        rows = slice(head * HDIM, (head + 1) * HDIM)
        delta = jnp.sum(products_t[rows], axis=0, keepdims=True)
        for start in range(0, length, wide):
            cols = slice(start, start + wide)
            soft = soft_ref[head, :, cols]
            slopes = mm_nt(v_ref[...], g_heads[head][cols])
            mixed_grad = (soft.astype(jnp.float32) * (slopes - delta[:, cols])).astype(jnp.bfloat16)
            grad_v = grad_v + mm(soft, g_heads[head][cols])
            grad_k = grad_k + mm(mixed_grad, q_ref[head, cols, :])
            grad_t[rows, cols] = mm(k_t_ref[rows, :], mixed_grad) * (1.0 / math.sqrt(HDIM))
    res_k[...] = grad_k.astype(jnp.bfloat16)
    res_v[...] = grad_v.astype(jnp.bfloat16)
    res_q[...] = grad_t[...].T.astype(jnp.bfloat16)


def block_kernel(steps, frames, *refs):
    sources, tap_refs, outs = refs[:4], refs[4 : -len(steps)], refs[-len(steps) :]
    me = lax.axis_index("seq")
    taps = tap_refs[0][...]
    for other in tap_refs[1:]:
        taps = taps + other[...]
    for step, out in zip(steps, outs):
        rows = rows_at(me ^ step, frames)
        for place, source in enumerate(sources):
            out[place * frames : (place + 1) * frames, :] = source[rows, :]
        out[4 * frames :, :] = taps.astype(jnp.bfloat16)


def spread_kernel(ranks, frames, *refs):
    blocks = refs[:ranks]
    targets, taps_ref = refs[ranks : ranks + 4], refs[ranks + 4]
    me = lax.axis_index("seq")
    for step in range(ranks):
        lanes = lanes_at(me ^ step)
        for place, target in enumerate(targets):
            target[0, :, lanes] = blocks[step][place * frames : (place + 1) * frames, :]
        taps = blocks[step][4 * frames :, :].astype(jnp.float32)
        taps_ref[:, lanes] = taps[:KERNEL]


def cost(flops, moved):
    return pl.CostEstimate(flops=flops, bytes_accessed=moved, transcendentals=0)


def on_device_heads(queries, keys, values, cotangent, conv_weight, rec_lengths):
    ranks = lax.axis_size("seq")
    frames = queries.shape[1]
    length = ranks * frames
    heads = LANES // HDIM
    bf16, f32, i32 = jnp.bfloat16, jnp.float32, jnp.int32
    struct = jax.ShapeDtypeStruct
    hbm = pl.BlockSpec(memory_space=pltpu.HBM)
    anywhere = pl.BlockSpec(memory_space=pl.ANY)
    vmem = pl.BlockSpec(memory_space=VMEM)
    smem = pl.BlockSpec(memory_space=pltpu.SMEM)
    params = pltpu.CompilerParams(vmem_limit_bytes=24 * MIB)
    taps = KERNEL + 1

    sends = pl.pallas_call(
        functools.partial(pack_kernel, ranks),
        out_shape=[struct((3, frames, LANES), bf16)] * (ranks - 1),
        in_specs=[hbm] * 3,
        out_specs=[vmem] * (ranks - 1),
        scratch_shapes=[VMEM((3,) + queries.shape[1:], bf16), pltpu.SemaphoreType.DMA((3,))],
        compiler_params=pltpu.CompilerParams(vmem_limit_bytes=54912 * 1024),
        name="pack",
    )(queries, keys, values)

    def swap(array, step):
        return lax.ppermute(array, "seq", [(rank, rank ^ step) for rank in range(ranks)])

    order = list(range(ranks - 1, 0, -1))
    received = {step: swap(sends[step - 1], step) for step in order}

    *cot_sends, own, col, row, after, before = pl.pallas_call(
        functools.partial(mask_kernel, ranks, length),
        out_shape=[struct((frames, LANES), bf16)] * (ranks - 1)
        + [
            struct((4, frames, LANES), bf16),
            struct((length, LANES), i32),
            struct((8, length), i32),
            struct((length, LANES), i32),
            struct((length, LANES), i32),
        ],
        in_specs=[smem] + [hbm] * 4,
        out_specs=[vmem] * (ranks + 4),
        scratch_shapes=[pltpu.SemaphoreType.DMA((ranks + 3,))],
        compiler_params=params,
        cost_estimate=cost(4 * MIB, MIB),
        name="masks",
    )(rec_lengths, queries, keys, values, cotangent)
    cots = {step: swap(cot_sends[step - 1], step) for step in order}

    soft, att, pre, q_heads, k_t, v_full = pl.pallas_call(
        functools.partial(forward_kernel, ranks, frames),
        out_shape=[
            struct((heads, length, length), bf16),
            struct((length + 2 * PAD, LANES), f32),
            struct((length, LANES), f32),
            struct((heads, length, LANES), bf16),
            struct((LANES, length), bf16),
            struct((length, LANES), bf16),
        ],
        in_specs=[vmem] * (ranks + 4) + [anywhere],
        out_specs=[vmem] * 6,
        scratch_shapes=[
            VMEM((LANES, length), f32),
            VMEM((length, LANES), bf16),
            VMEM((length, LANES), bf16),
            VMEM((KERNEL, LANES), f32),
            pltpu.SemaphoreType.DMA,
        ],
        compiler_params=params,
        cost_estimate=cost(400 * MIB, 3 * MIB),
        name="forward",
    )(*[received[step] for step in order], own, col, row, after, before, conv_weight)

    mixed, g_att, own_taps = pl.pallas_call(
        functools.partial(conv_back_kernel, ranks, frames),
        out_shape=[struct((length, LANES), bf16)] * 2 + [struct((taps, LANES), f32)],
        in_specs=[vmem] * (ranks + 4) + [anywhere],
        out_specs=[vmem] * 3,
        scratch_shapes=[
            VMEM((length, LANES), bf16),
            VMEM((length + 2 * PAD, LANES), f32),
            VMEM((taps, 8, LANES), f32),
            VMEM((KERNEL, LANES), f32),
            pltpu.SemaphoreType.DMA,
        ],
        compiler_params=params,
        cost_estimate=cost(400 * MIB, 3 * MIB),
        name="conv_back",
    )(*[cots[step] for step in order], own, att, pre, after, before, conv_weight)

    copies = lax.axis_size("dp")
    part_taps = [own_taps] + [
        lax.ppermute(own_taps, "dp", [(one, (one + shift) % copies) for one in range(copies)])
        for shift in range(1, copies)
    ]

    results = pl.pallas_call(
        backward_kernel,
        out_shape=[struct((length, LANES), bf16)] * 3,
        in_specs=[vmem] * 6,
        out_specs=[vmem] * 3,
        scratch_shapes=[VMEM((LANES, length), f32)],
        compiler_params=params,
        cost_estimate=cost(800 * MIB, 3 * MIB),
        name="backward",
    )(soft, att, g_att, q_heads, k_t, v_full)

    def blocks_of(steps):
        return pl.pallas_call(
            functools.partial(block_kernel, steps, frames),
            out_shape=[struct((4 * frames + taps, LANES), bf16)] * len(steps),
            in_specs=[vmem] * (4 + copies),
            out_specs=[vmem] * len(steps),
            compiler_params=params,
            cost_estimate=cost(MIB, MIB),
            name="blocks",
        )(mixed, *results, *part_taps)

    half = ranks // 2
    far = blocks_of(list(range(half, ranks)))
    near = blocks_of(list(range(half)))
    back = {step: swap(far[step - half], step) for step in range(half, ranks)}
    back |= {step: swap(near[step], step) for step in range(1, half)}
    back[0] = near[0]

    return pl.pallas_call(
        functools.partial(spread_kernel, ranks, frames),
        out_shape=[struct(queries.shape, bf16)] * 4 + [struct(conv_weight.shape, f32)],
        in_specs=[vmem] * ranks,
        out_specs=[vmem] * 5,
        compiler_params=params,
        name="spread",
    )(*[back[step] for step in range(ranks)])


def on_device_any(queries, keys, values, cotangent, conv_weight, rec_lengths):
    ranks = lax.axis_size("seq")
    frames, channels = queries.shape[1], queries.shape[2]
    fits = channels == ranks * LANES and ranks & (ranks - 1) == 0 and frames % LANES == 0
    if fits and ranks > 1 and ranks * frames <= 1024 and lax.axis_size("dp") == 2:
        return on_device_heads(queries, keys, values, cotangent, conv_weight, rec_lengths)
    return on_device(queries, keys, values, cotangent, conv_weight, rec_lengths)


def solution(mesh):
    placed = (
        P(("groups", "dp"), "seq", "mp"),
        P(("groups", "dp"), "seq", "mp"),
        P(("groups", "dp"), "seq", "mp"),
        P(("groups", "dp"), "seq", "mp"),
        P(None, "mp"),
        P(("groups", "dp"), None),
    )
    return jax.shard_map(
        on_device_any,
        mesh=mesh,
        in_specs=placed,
        out_specs=(
            P(("groups", "dp"), "seq", "mp"),
            P(("groups", "dp"), "seq", "mp"),
            P(("groups", "dp"), "seq", "mp"),
            P(("groups", "dp"), "seq", "mp"),
            P("groups", "mp"),
        ),
        check_vma=False,
    )
```

```python
import functools
import math

import jax
import jax.numpy as jnp
from jax import lax
from jax.experimental import pallas as pl
from jax.experimental.pallas import tpu as pltpu
from jax.sharding import PartitionSpec as P

HDIM = 64
KERNEL = 31
HALF = 15


NEGATIVE_FILL = -1e30


def extended(block, sides, width):
    for axis, dim in sides:
        count = lax.axis_size(axis)
        forward = [(i, i + 1) for i in range(count - 1)]
        backward = [(target, source) for source, target in forward]
        low = lax.ppermute(
            lax.slice_in_dim(block, block.shape[dim] - width, None, axis=dim), axis, forward
        )
        high = lax.ppermute(lax.slice_in_dim(block, 0, width, axis=dim), axis, backward)
        block = jnp.concatenate([low, block, high], axis=dim)
    return block


def pick_block(total_rows):
    for candidate in (512, 256, 128):
        return candidate
    return total_rows


def over_blocks(total_rows, advance, initial):
    block_rows = pick_block(total_rows)
    block_count = total_rows // block_rows
    if block_count == 1:
        return advance(initial, 0, block_rows)
    return lax.fori_loop(
        0,
        block_count,
        lambda number, running: advance(running, number * block_rows, block_rows),
        initial,
    )


def when_shared(compute, running):
    result = compute(running)
    return result


def on_device(queries, keys, values, cotangent, conv_weight, rec_lengths):
    frames = queries.shape[1]
    channels = queries.shape[2]
    local_heads = channels // HDIM
    score_scale = 1.0 / math.sqrt(HDIM)
    length_all = frames * lax.axis_size("seq")
    offset = lax.axis_index("seq") * frames
    record_ends = jnp.cumsum(rec_lengths[0], dtype=jnp.int32)

    def segment_of(positions):
        return jnp.sum((record_ends[None, :] <= positions[:, None]).astype(jnp.int32), axis=1)

    own_seg = segment_of(offset + jnp.arange(frames, dtype=jnp.int32))

    def to_heads(array):
        return array.reshape(array.shape[0], local_heads, HDIM).transpose(1, 0, 2)

    def from_heads(array):
        return array.transpose(1, 0, 2).reshape(array.shape[1], channels)

    q_heads = to_heads(queries[0])
    k_heads = to_heads(keys[0])
    v_heads = to_heads(values[0])

    def over_rows(advance, initial, members, first_row):
        total_rows = members[0].shape[1]

        def one_block(running, block_start, block_rows):
            sliced = tuple(
                (lax.dynamic_slice_in_dim(member, block_start, block_rows, 1) for member in members)
            )
            other_seg = segment_of(
                first_row + block_start + jnp.arange(block_rows, dtype=jnp.int32)
            )
            return when_shared(lambda current: advance(current, sliced, other_seg), running)

        return over_blocks(total_rows, one_block, initial)

    def query_scores(key_block, key_seg):
        raw_scores = (
            jnp.einsum("hqd,hkd->hqk", q_heads, key_block, preferred_element_type=jnp.float32)
            * score_scale
        )
        return jnp.where((own_seg[:, None] == key_seg[None, :])[None], raw_scores, NEGATIVE_FILL)

    def stats_step(running, sliced, key_seg):
        top_now, total_now = running
        scores = query_scores(sliced[0], key_seg)
        top_new = jnp.maximum(top_now, jnp.max(scores, axis=2))
        total_new = total_now * jnp.exp(top_now - top_new) + jnp.sum(
            jnp.exp(scores - top_new[:, :, None]), axis=2
        )
        return (top_new, total_new)

    stats_init = (
        jnp.full((local_heads, frames), NEGATIVE_FILL, jnp.float32),
        jnp.zeros((local_heads, frames), jnp.float32),
    )
    gathered = (
        lax.all_gather(keys, "seq", axis=1, tiled=True),
        lax.all_gather(values, "seq", axis=1, tiled=True),
    )
    key_whole = to_heads(gathered[0][0])
    value_whole = to_heads(gathered[1][0])
    row_stats = over_rows(stats_step, stats_init, (key_whole,), 0)
    log_total = row_stats[0] + jnp.log(row_stats[1])

    def output_step(running, sliced, key_seg):
        scores = query_scores(sliced[0], key_seg)
        soft_rounded = jnp.exp(scores - log_total[:, :, None]).astype(jnp.bfloat16)
        return running + jnp.einsum(
            "hqk,hkd->hqd", soft_rounded, sliced[1], preferred_element_type=jnp.float32
        )

    frame_zeros = jnp.zeros((local_heads, frames, HDIM), jnp.float32)
    attended_sum = over_rows(output_step, frame_zeros, (key_whole, value_whole), 0)
    attended_heads = attended_sum.astype(jnp.bfloat16)
    attended = from_heads(attended_heads)
    padded = extended(attended[None], (("seq", 1),), HALF)
    padded_wide = padded[0].astype(jnp.float32)
    pad_positions = offset - HALF + jnp.arange(frames + 2 * HALF, dtype=jnp.int32)
    inside = jnp.logical_and(pad_positions >= 0, pad_positions < length_all)
    pad_seg = jnp.where(inside, segment_of(pad_positions), -1)
    conv_pre = jnp.zeros((frames, channels), jnp.float32)
    for tap_index in range(KERNEL):
        tap_mask = (pad_seg[tap_index : tap_index + frames] == own_seg)[:, None]
        conv_pre = conv_pre + jnp.where(
            tap_mask, conv_weight[tap_index] * padded_wide[tap_index : tap_index + frames], 0.0
        )
    gate_value = jax.nn.sigmoid(conv_pre)
    mixed = (conv_pre * gate_value).astype(jnp.bfloat16)
    conv_grad = (
        cotangent[0].astype(jnp.float32) * gate_value * (1.0 + conv_pre * (1.0 - gate_value))
    ).astype(jnp.bfloat16)
    padded_grad = extended(conv_grad[None], (("seq", 1),), HALF)
    grad_wide = padded_grad[0].astype(jnp.float32)
    conv_grad_wide = conv_grad.astype(jnp.float32)
    grad_attended = jnp.zeros((frames, channels), jnp.float32)
    kernel_rows = []
    for tap_index in range(KERNEL):
        back_start = 2 * HALF - tap_index
        back_mask = (pad_seg[back_start : back_start + frames] == own_seg)[:, None]
        grad_attended = grad_attended + jnp.where(
            back_mask, conv_weight[tap_index] * grad_wide[back_start : back_start + frames], 0.0
        )
        tap_mask = (pad_seg[tap_index : tap_index + frames] == own_seg)[:, None]
        product = conv_grad_wide * padded_wide[tap_index : tap_index + frames]
        kernel_rows.append(jnp.sum(jnp.where(tap_mask, product, 0.0), axis=0))
    grad_kernel = lax.psum(jnp.stack(kernel_rows), ("dp", "seq"))
    grad_attended = grad_attended.astype(jnp.bfloat16)
    g_heads = to_heads(grad_attended)
    row_delta = jnp.sum(g_heads.astype(jnp.float32) * attended_heads.astype(jnp.float32), axis=2)

    def query_grad_step(running, sliced, key_seg):
        key_block = sliced[0]
        value_block = sliced[1]
        soft_weights = jnp.exp(query_scores(key_block, key_seg) - log_total[:, :, None])
        slopes = jnp.einsum(
            "hqd,hkd->hqk", g_heads, value_block, preferred_element_type=jnp.float32
        )
        mixed_grad = (soft_weights * (slopes - row_delta[:, :, None])).astype(jnp.bfloat16)
        return running + jnp.einsum(
            "hqk,hkd->hqd", mixed_grad, key_block, preferred_element_type=jnp.float32
        )

    grad_query = over_rows(query_grad_step, frame_zeros, (key_whole, value_whole), 0)

    def key_grad_step(running, sliced, query_seg):
        grad_key_now, grad_value_now = running
        query_block = sliced[0]
        grad_block = sliced[1]
        total_block = sliced[2]
        delta_block = sliced[3]
        raw_scores = (
            jnp.einsum("hqd,hkd->hqk", query_block, k_heads, preferred_element_type=jnp.float32)
            * score_scale
        )
        scores = jnp.where(
            (query_seg[:, None] == own_seg[None, :])[None], raw_scores, NEGATIVE_FILL
        )
        soft_weights = jnp.exp(scores - total_block[:, :, None])
        grad_value_new = grad_value_now + jnp.einsum(
            "hqk,hqd->hkd",
            soft_weights.astype(jnp.bfloat16),
            grad_block,
            preferred_element_type=jnp.float32,
        )
        slopes = jnp.einsum("hqd,hkd->hqk", grad_block, v_heads, preferred_element_type=jnp.float32)
        mixed_grad = (soft_weights * (slopes - delta_block[:, :, None])).astype(jnp.bfloat16)
        grad_key_new = grad_key_now + jnp.einsum(
            "hqk,hqd->hkd", mixed_grad, query_block, preferred_element_type=jnp.float32
        )
        return (grad_key_new, grad_value_new)

    all_totals, all_deltas = (
        lax.all_gather(log_total[None], "seq", axis=2, tiled=True),
        lax.all_gather(row_delta[None], "seq", axis=2, tiled=True),
    )
    member = (
        lax.all_gather(queries, "seq", axis=1, tiled=True),
        lax.all_gather(grad_attended[None], "seq", axis=1, tiled=True),
    )
    totals_piece = all_totals[0]
    deltas_piece = all_deltas[0]
    grad_key, grad_value = over_rows(
        key_grad_step,
        (frame_zeros, frame_zeros),
        (to_heads(member[0][0]), to_heads(member[1][0]), totals_piece, deltas_piece),
        jnp.int32(0),
    )
    grad_queries = from_heads(grad_query * score_scale).astype(jnp.bfloat16)[None]
    grad_keys = from_heads(grad_key * score_scale).astype(jnp.bfloat16)[None]
    grad_values = from_heads(grad_value).astype(jnp.bfloat16)[None]
    return (mixed[None], grad_queries, grad_keys, grad_values, grad_kernel)


LANES = 128
PAD = 16
VMEM = pltpu.VMEM
MIB = 1024 * 1024


def mm(left, right):
    return lax.dot_general(
        left, right, (((1,), (0,)), ((), ())), preferred_element_type=jnp.float32
    )


def mm_nt(left, right):
    return lax.dot_general(
        left, right, (((1,), (1,)), ((), ())), preferred_element_type=jnp.float32
    )


def rows_at(block, frames):
    return pl.ds(pl.multiple_of(block * frames, frames), frames)


def lanes_at(block):
    return pl.ds(pl.multiple_of(block * LANES, LANES), LANES)


def pack_kernel(ranks, q_ref, k_ref, v_ref, *rest):
    outs, (whole, sems) = rest[:-2], rest[-2:]
    me = lax.axis_index("seq")
    sources = (q_ref, k_ref, v_ref)
    run_copies([(source.at[0], whole.at[place]) for place, source in enumerate(sources)], sems)
    for step in range(ranks - 1, 0, -1):
        for place in range(len(sources)):
            outs[step - 1][place] = whole[place, :, lanes_at(me ^ step)]


def run_copies(pairs, sems, meanwhile=None):
    copies = [
        pltpu.make_async_copy(source, target, sems.at[number])
        for number, (source, target) in enumerate(pairs)
    ]
    for copy in copies:
        copy.start()
    if meanwhile is not None:
        meanwhile()
    for copy in copies:
        copy.wait()


def mask_kernel(ranks, length, lens_ref, q_ref, k_ref, v_ref, c_ref, *refs):
    cot_refs = refs[: ranks - 1]
    own_ref, col_ref, row_ref, after_ref, before_ref, sems = refs[ranks - 1 :]
    me = lax.axis_index("seq")
    pairs = [(c_ref.at[0, :, lanes_at(me ^ step)], cot_refs[step - 1]) for step in range(1, ranks)]
    for place, source in enumerate((q_ref, k_ref, v_ref, c_ref)):
        pairs.append((source.at[0, :, lanes_at(me)], own_ref.at[place]))

    def extents():
        ends = []
        running = jnp.int32(0)
        for number in range(lens_ref.shape[1]):
            running = running + lens_ref[0, number]
            ends.append(running)
        row_time = lax.broadcasted_iota(jnp.int32, row_ref.shape, 1)
        row_first = jnp.zeros(row_ref.shape, jnp.int32)
        for end in ends:
            row_first = jnp.where(row_time >= end, end, row_first)
        row_ref[...] = row_first
        chunk = 64

        def some_rows(number, carry):
            base = pl.multiple_of(number * chunk, chunk)
            time = base + lax.broadcasted_iota(jnp.int32, (chunk, LANES), 0)
            first = jnp.zeros((chunk, LANES), jnp.int32)
            last = jnp.full((chunk, LANES), length, jnp.int32)
            for end in ends:
                first = jnp.where(time >= end, end, first)
            for end in reversed(ends):
                last = jnp.where(time < end, end, last)
            rows = pl.ds(base, chunk)
            col_ref[rows, :] = first
            after_ref[rows, :] = last - 1 - time
            before_ref[rows, :] = time - first
            return carry

        lax.fori_loop(0, length // chunk, some_rows, 0)

    run_copies(pairs, sems, extents)


def forward_kernel(ranks, frames, *refs):
    recvs = refs[: ranks - 1]
    own_ref, col_ref, row_ref, after_ref, before_ref, w_ref = refs[ranks - 1 : ranks + 5]
    soft_ref, att_ref, pre_ref, q_ref, k_t_ref, v_ref = refs[ranks + 5 : ranks + 11]
    att_t_ref, k_full, q_full, w_own, w_sem = refs[ranks + 11 :]
    me = lax.axis_index("seq")
    length = ranks * frames
    copy = pltpu.make_async_copy(w_ref.at[:, lanes_at(me)], w_own, w_sem)
    copy.start()
    for place, target in enumerate((q_full, k_full, v_ref)):
        target[rows_at(me, frames), :] = own_ref[place]
        for step in range(1, ranks):
            target[rows_at(me ^ step, frames), :] = recvs[ranks - 1 - step][place]
    heads = LANES // HDIM
    lane_head = lax.broadcasted_iota(jnp.int32, (1, LANES), 1) // HDIM
    scaled = q_full[...].astype(jnp.float32) * (1.0 / math.sqrt(HDIM))
    for head in range(heads):
        q_ref[head] = jnp.where(lane_head == head, scaled, 0.0).astype(jnp.bfloat16)
    k_t_ref[...] = k_full[...].astype(jnp.float32).T.astype(jnp.bfloat16)
    v_t = v_ref[...].astype(jnp.float32).T.astype(jnp.bfloat16)
    wide = 512
    for head in range(heads):
        for start in range(0, length, wide):
            cols = slice(start, start + wide)
            raw = mm_nt(k_full[...], q_ref[head, cols, :])
            same = jnp.concatenate([col_ref[...]] * (wide // LANES), axis=1) == row_ref[0:1, cols]
            scores = jnp.where(same, raw, NEGATIVE_FILL)
            top = jnp.max(scores, axis=0, keepdims=True)
            powers = jnp.exp(scores - top)
            share = 1.0 / jnp.sum(powers, axis=0, keepdims=True)
            soft = (powers * share).astype(jnp.bfloat16)
            soft_ref[head, :, cols] = soft
            rows = slice(head * HDIM, (head + 1) * HDIM)
            att_t_ref[rows, cols] = mm(v_t[rows], soft).astype(jnp.bfloat16).astype(jnp.float32)
    zeros = jnp.zeros((PAD, LANES), jnp.float32)
    att_ref[0:PAD, :] = zeros
    att_ref[PAD : PAD + length, :] = att_t_ref[...].T
    att_ref[PAD + length :, :] = zeros
    copy.wait()

    chunk = 64

    def some_rows(number, carry):
        base = pl.multiple_of(number * chunk, chunk)
        rows = pl.ds(base, chunk)
        after, before = after_ref[rows, :], before_ref[rows, :]
        total = jnp.zeros((chunk, LANES), jnp.float32)
        for tap in range(KERNEL):
            off = tap - HALF
            piece = att_ref[pl.ds(base + (PAD + off), chunk), :]
            if off > 0:
                piece = jnp.where(after >= off, piece, 0.0)
            if off < 0:
                piece = jnp.where(before >= -off, piece, 0.0)
            total = total + w_own[tap : tap + 1, :] * piece
        pre_ref[rows, :] = total
        return carry

    lax.fori_loop(0, length // chunk, some_rows, 0)


def conv_back_kernel(ranks, frames, *refs):
    cots = refs[: ranks - 1]
    own_ref, att_ref, pre_ref, after_ref, before_ref, w_ref = refs[ranks - 1 : ranks + 5]
    mixed_ref, g_att, taps_ref, cot, grad_pad, tap_sum, w_own, w_sem = refs[ranks + 5 :]
    me = lax.axis_index("seq")
    length = ranks * frames
    copy = pltpu.make_async_copy(w_ref.at[:, lanes_at(me)], w_own, w_sem)
    copy.start()
    cot[rows_at(me, frames), :] = own_ref[3]
    for step in range(1, ranks):
        cot[rows_at(me ^ step, frames), :] = cots[ranks - 1 - step][...]
    zeros = jnp.zeros((PAD, LANES), jnp.float32)
    grad_pad[0:PAD, :] = zeros
    grad_pad[PAD + length :, :] = zeros
    pre = pre_ref[...]
    gate = jax.nn.sigmoid(pre)
    mixed_ref[...] = (pre * gate).astype(jnp.bfloat16)
    conv_grad = cot[...].astype(jnp.float32) * gate * (1.0 + pre * (1.0 - gate))
    grad_pad[PAD : PAD + length, :] = conv_grad.astype(jnp.bfloat16).astype(jnp.float32)
    tap_sum[...] = jnp.zeros(tap_sum.shape, jnp.float32)
    copy.wait()

    chunk = 64

    def some_rows(number, carry):
        base = pl.multiple_of(number * chunk, chunk)
        rows = pl.ds(base, chunk)
        after, before = after_ref[rows, :], before_ref[rows, :]
        own_att = att_ref[pl.ds(base + PAD, chunk), :]
        total = jnp.zeros((chunk, LANES), jnp.float32)
        for tap in range(KERNEL):
            off = tap - HALF
            piece = grad_pad[pl.ds(base + (PAD - off), chunk), :]
            if off > 0:
                piece = jnp.where(before >= off, piece, 0.0)
            if off < 0:
                piece = jnp.where(after >= -off, piece, 0.0)
            total = total + w_own[tap : tap + 1, :] * piece
            part = (own_att * piece).reshape(chunk // 8, 8, LANES)
            tap_sum[tap] = tap_sum[tap] + jnp.sum(part, axis=0)
        g_att[rows, :] = total.astype(jnp.bfloat16)
        return carry

    lax.fori_loop(0, length // chunk, some_rows, 0)
    taps_ref[...] = jnp.sum(tap_sum[...], axis=1)


def backward_kernel(soft_ref, att_ref, g_att, q_ref, k_t_ref, v_ref, res_q, res_k, res_v, grad_t):
    length = v_ref.shape[0]
    heads = LANES // HDIM
    lane_head = lax.broadcasted_iota(jnp.int32, (1, LANES), 1) // HDIM
    g_wide = g_att[...].astype(jnp.float32)
    products_t = (g_wide * att_ref[PAD : PAD + length, :]).T
    g_heads = [jnp.where(lane_head == head, g_wide, 0.0).astype(jnp.bfloat16) for head in range(heads)]
    wide = 512
    grad_v = jnp.zeros((length, LANES), jnp.float32)
    grad_k = jnp.zeros((length, LANES), jnp.float32)
    for head in range(heads):
        rows = slice(head * HDIM, (head + 1) * HDIM)
        delta = jnp.sum(products_t[rows], axis=0, keepdims=True)
        for start in range(0, length, wide):
            cols = slice(start, start + wide)
            soft = soft_ref[head, :, cols]
            slopes = mm_nt(v_ref[...], g_heads[head][cols])
            mixed_grad = (soft.astype(jnp.float32) * (slopes - delta[:, cols])).astype(jnp.bfloat16)
            grad_v = grad_v + mm(soft, g_heads[head][cols])
            grad_k = grad_k + mm(mixed_grad, q_ref[head, cols, :])
            grad_t[rows, cols] = mm(k_t_ref[rows, :], mixed_grad) * (1.0 / math.sqrt(HDIM))
    res_k[...] = grad_k.astype(jnp.bfloat16)
    res_v[...] = grad_v.astype(jnp.bfloat16)
    res_q[...] = grad_t[...].T.astype(jnp.bfloat16)


def block_kernel(steps, frames, *refs):
    sources, tap_refs, outs = refs[:4], refs[4 : -len(steps)], refs[-len(steps) :]
    me = lax.axis_index("seq")
    taps = tap_refs[0][...]
    for other in tap_refs[1:]:
        taps = taps + other[...]
    for step, out in zip(steps, outs):
        rows = rows_at(me ^ step, frames)
        for place, source in enumerate(sources):
            out[place * frames : (place + 1) * frames, :] = source[rows, :]
        out[4 * frames :, :] = taps.astype(jnp.bfloat16)


def spread_kernel(ranks, frames, *refs):
    blocks = refs[:ranks][::-1]
    targets, taps_ref = refs[ranks : ranks + 4], refs[ranks + 4]
    me = lax.axis_index("seq")
    for step in range(ranks):
        lanes = lanes_at(me ^ step)
        for place, target in enumerate(targets):
            target[0, :, lanes] = blocks[step][place * frames : (place + 1) * frames, :]
        taps = blocks[step][4 * frames :, :].astype(jnp.float32)
        taps_ref[:, lanes] = taps[:KERNEL]


def cost(flops, moved):
    return pl.CostEstimate(flops=flops, bytes_accessed=moved, transcendentals=0)


def on_device_heads(queries, keys, values, cotangent, conv_weight, rec_lengths):
    ranks = lax.axis_size("seq")
    frames = queries.shape[1]
    length = ranks * frames
    heads = LANES // HDIM
    bf16, f32, i32 = jnp.bfloat16, jnp.float32, jnp.int32
    struct = jax.ShapeDtypeStruct
    hbm = pl.BlockSpec(memory_space=pltpu.HBM)
    anywhere = pl.BlockSpec(memory_space=pl.ANY)
    vmem = pl.BlockSpec(memory_space=VMEM)
    smem = pl.BlockSpec(memory_space=pltpu.SMEM)
    params = pltpu.CompilerParams(vmem_limit_bytes=24 * MIB)
    taps = KERNEL + 1

    sends = pl.pallas_call(
        functools.partial(pack_kernel, ranks),
        out_shape=[struct((3, frames, LANES), bf16)] * (ranks - 1),
        in_specs=[hbm] * 3,
        out_specs=[vmem] * (ranks - 1),
        scratch_shapes=[VMEM((3,) + queries.shape[1:], bf16), pltpu.SemaphoreType.DMA((3,))],
        compiler_params=pltpu.CompilerParams(vmem_limit_bytes=54912 * 1024),
        name="pack",
    )(queries, keys, values)

    def swap(array, step):
        return lax.ppermute(array, "seq", [(rank, rank ^ step) for rank in range(ranks)])

    order = list(range(ranks - 1, 0, -1))
    received = {step: swap(sends[step - 1], step) for step in order}

    *cot_sends, own, col, row, after, before = pl.pallas_call(
        functools.partial(mask_kernel, ranks, length),
        out_shape=[struct((frames, LANES), bf16)] * (ranks - 1)
        + [
            struct((4, frames, LANES), bf16),
            struct((length, LANES), i32),
            struct((8, length), i32),
            struct((length, LANES), i32),
            struct((length, LANES), i32),
        ],
        in_specs=[smem] + [hbm] * 4,
        out_specs=[vmem] * (ranks + 4),
        scratch_shapes=[pltpu.SemaphoreType.DMA((ranks + 3,))],
        compiler_params=params,
        cost_estimate=cost(4 * MIB, MIB),
        name="masks",
    )(rec_lengths, queries, keys, values, cotangent)
    cots = {step: swap(cot_sends[step - 1], step) for step in order}

    soft, att, pre, q_heads, k_t, v_full = pl.pallas_call(
        functools.partial(forward_kernel, ranks, frames),
        out_shape=[
            struct((heads, length, length), bf16),
            struct((length + 2 * PAD, LANES), f32),
            struct((length, LANES), f32),
            struct((heads, length, LANES), bf16),
            struct((LANES, length), bf16),
            struct((length, LANES), bf16),
        ],
        in_specs=[vmem] * (ranks + 4) + [anywhere],
        out_specs=[vmem] * 6,
        scratch_shapes=[
            VMEM((LANES, length), f32),
            VMEM((length, LANES), bf16),
            VMEM((length, LANES), bf16),
            VMEM((KERNEL, LANES), f32),
            pltpu.SemaphoreType.DMA,
        ],
        compiler_params=params,
        cost_estimate=cost(400 * MIB, 3 * MIB),
        name="forward",
    )(*[received[step] for step in order], own, col, row, after, before, conv_weight)

    mixed, g_att, own_taps = pl.pallas_call(
        functools.partial(conv_back_kernel, ranks, frames),
        out_shape=[struct((length, LANES), bf16)] * 2 + [struct((taps, LANES), f32)],
        in_specs=[vmem] * (ranks + 4) + [anywhere],
        out_specs=[vmem] * 3,
        scratch_shapes=[
            VMEM((length, LANES), bf16),
            VMEM((length + 2 * PAD, LANES), f32),
            VMEM((taps, 8, LANES), f32),
            VMEM((KERNEL, LANES), f32),
            pltpu.SemaphoreType.DMA,
        ],
        compiler_params=params,
        cost_estimate=cost(400 * MIB, 3 * MIB),
        name="conv_back",
    )(*[cots[step] for step in order], own, att, pre, after, before, conv_weight)

    copies = lax.axis_size("dp")
    part_taps = [own_taps] + [
        lax.ppermute(own_taps, "dp", [(one, (one + shift) % copies) for one in range(copies)])
        for shift in range(1, copies)
    ]

    results = pl.pallas_call(
        backward_kernel,
        out_shape=[struct((length, LANES), bf16)] * 3,
        in_specs=[vmem] * 6,
        out_specs=[vmem] * 3,
        scratch_shapes=[VMEM((LANES, length), f32)],
        compiler_params=params,
        cost_estimate=cost(800 * MIB, 3 * MIB),
        name="backward",
    )(soft, att, g_att, q_heads, k_t, v_full)

    steps = list(range(ranks - 1, -1, -1))
    blocks = pl.pallas_call(
        functools.partial(block_kernel, steps, frames),
        out_shape=[struct((4 * frames + taps, LANES), bf16)] * ranks,
        in_specs=[vmem] * (4 + copies),
        out_specs=[vmem] * ranks,
        compiler_params=params,
        cost_estimate=cost(MIB, MIB),
        name="blocks",
    )(mixed, *results, *part_taps)
    back = [swap(block, step) if step else block for block, step in zip(blocks, steps)]

    return pl.pallas_call(
        functools.partial(spread_kernel, ranks, frames),
        out_shape=[struct(queries.shape, bf16)] * 4 + [struct(conv_weight.shape, f32)],
        in_specs=[vmem] * ranks,
        out_specs=[vmem] * 5,
        compiler_params=params,
        name="spread",
    )(*back)


def on_device_any(queries, keys, values, cotangent, conv_weight, rec_lengths):
    ranks = lax.axis_size("seq")
    frames, channels = queries.shape[1], queries.shape[2]
    fits = channels == ranks * LANES and ranks & (ranks - 1) == 0 and frames % LANES == 0
    if fits and ranks > 1 and ranks * frames <= 1024 and lax.axis_size("dp") == 2:
        return on_device_heads(queries, keys, values, cotangent, conv_weight, rec_lengths)
    return on_device(queries, keys, values, cotangent, conv_weight, rec_lengths)


def solution(mesh):
    placed = (
        P(("groups", "dp"), "seq", "mp"),
        P(("groups", "dp"), "seq", "mp"),
        P(("groups", "dp"), "seq", "mp"),
        P(("groups", "dp"), "seq", "mp"),
        P(None, "mp"),
        P(("groups", "dp"), None),
    )
    return jax.shard_map(
        on_device_any,
        mesh=mesh,
        in_specs=placed,
        out_specs=(
            P(("groups", "dp"), "seq", "mp"),
            P(("groups", "dp"), "seq", "mp"),
            P(("groups", "dp"), "seq", "mp"),
            P(("groups", "dp"), "seq", "mp"),
            P("groups", "mp"),
        ),
        check_vma=False,
    )
```

```python
import functools
import math

import jax
import jax.numpy as jnp
from jax import lax
from jax.experimental import pallas as pl
from jax.experimental.pallas import tpu as pltpu
from jax.sharding import PartitionSpec as P

HDIM = 64
KERNEL = 31
HALF = 15


NEGATIVE_FILL = -1e30


def extended(block, sides, width):
    for axis, dim in sides:
        count = lax.axis_size(axis)
        forward = [(i, i + 1) for i in range(count - 1)]
        backward = [(target, source) for source, target in forward]
        low = lax.ppermute(
            lax.slice_in_dim(block, block.shape[dim] - width, None, axis=dim), axis, forward
        )
        high = lax.ppermute(lax.slice_in_dim(block, 0, width, axis=dim), axis, backward)
        block = jnp.concatenate([low, block, high], axis=dim)
    return block


def pick_block(total_rows):
    for candidate in (512, 256, 128):
        return candidate
    return total_rows


def over_blocks(total_rows, advance, initial):
    block_rows = pick_block(total_rows)
    block_count = total_rows // block_rows
    if block_count == 1:
        return advance(initial, 0, block_rows)
    return lax.fori_loop(
        0,
        block_count,
        lambda number, running: advance(running, number * block_rows, block_rows),
        initial,
    )


def when_shared(compute, running):
    result = compute(running)
    return result


def on_device(queries, keys, values, cotangent, conv_weight, rec_lengths):
    frames = queries.shape[1]
    channels = queries.shape[2]
    local_heads = channels // HDIM
    score_scale = 1.0 / math.sqrt(HDIM)
    length_all = frames * lax.axis_size("seq")
    offset = lax.axis_index("seq") * frames
    record_ends = jnp.cumsum(rec_lengths[0], dtype=jnp.int32)

    def segment_of(positions):
        return jnp.sum((record_ends[None, :] <= positions[:, None]).astype(jnp.int32), axis=1)

    own_seg = segment_of(offset + jnp.arange(frames, dtype=jnp.int32))

    def to_heads(array):
        return array.reshape(array.shape[0], local_heads, HDIM).transpose(1, 0, 2)

    def from_heads(array):
        return array.transpose(1, 0, 2).reshape(array.shape[1], channels)

    q_heads = to_heads(queries[0])
    k_heads = to_heads(keys[0])
    v_heads = to_heads(values[0])

    def over_rows(advance, initial, members, first_row):
        total_rows = members[0].shape[1]

        def one_block(running, block_start, block_rows):
            sliced = tuple(
                (lax.dynamic_slice_in_dim(member, block_start, block_rows, 1) for member in members)
            )
            other_seg = segment_of(
                first_row + block_start + jnp.arange(block_rows, dtype=jnp.int32)
            )
            return when_shared(lambda current: advance(current, sliced, other_seg), running)

        return over_blocks(total_rows, one_block, initial)

    def query_scores(key_block, key_seg):
        raw_scores = (
            jnp.einsum("hqd,hkd->hqk", q_heads, key_block, preferred_element_type=jnp.float32)
            * score_scale
        )
        return jnp.where((own_seg[:, None] == key_seg[None, :])[None], raw_scores, NEGATIVE_FILL)

    def stats_step(running, sliced, key_seg):
        top_now, total_now = running
        scores = query_scores(sliced[0], key_seg)
        top_new = jnp.maximum(top_now, jnp.max(scores, axis=2))
        total_new = total_now * jnp.exp(top_now - top_new) + jnp.sum(
            jnp.exp(scores - top_new[:, :, None]), axis=2
        )
        return (top_new, total_new)

    stats_init = (
        jnp.full((local_heads, frames), NEGATIVE_FILL, jnp.float32),
        jnp.zeros((local_heads, frames), jnp.float32),
    )
    gathered = (
        lax.all_gather(keys, "seq", axis=1, tiled=True),
        lax.all_gather(values, "seq", axis=1, tiled=True),
    )
    key_whole = to_heads(gathered[0][0])
    value_whole = to_heads(gathered[1][0])
    row_stats = over_rows(stats_step, stats_init, (key_whole,), 0)
    log_total = row_stats[0] + jnp.log(row_stats[1])

    def output_step(running, sliced, key_seg):
        scores = query_scores(sliced[0], key_seg)
        soft_rounded = jnp.exp(scores - log_total[:, :, None]).astype(jnp.bfloat16)
        return running + jnp.einsum(
            "hqk,hkd->hqd", soft_rounded, sliced[1], preferred_element_type=jnp.float32
        )

    frame_zeros = jnp.zeros((local_heads, frames, HDIM), jnp.float32)
    attended_sum = over_rows(output_step, frame_zeros, (key_whole, value_whole), 0)
    attended_heads = attended_sum.astype(jnp.bfloat16)
    attended = from_heads(attended_heads)
    padded = extended(attended[None], (("seq", 1),), HALF)
    padded_wide = padded[0].astype(jnp.float32)
    pad_positions = offset - HALF + jnp.arange(frames + 2 * HALF, dtype=jnp.int32)
    inside = jnp.logical_and(pad_positions >= 0, pad_positions < length_all)
    pad_seg = jnp.where(inside, segment_of(pad_positions), -1)
    conv_pre = jnp.zeros((frames, channels), jnp.float32)
    for tap_index in range(KERNEL):
        tap_mask = (pad_seg[tap_index : tap_index + frames] == own_seg)[:, None]
        conv_pre = conv_pre + jnp.where(
            tap_mask, conv_weight[tap_index] * padded_wide[tap_index : tap_index + frames], 0.0
        )
    gate_value = jax.nn.sigmoid(conv_pre)
    mixed = (conv_pre * gate_value).astype(jnp.bfloat16)
    conv_grad = (
        cotangent[0].astype(jnp.float32) * gate_value * (1.0 + conv_pre * (1.0 - gate_value))
    ).astype(jnp.bfloat16)
    padded_grad = extended(conv_grad[None], (("seq", 1),), HALF)
    grad_wide = padded_grad[0].astype(jnp.float32)
    conv_grad_wide = conv_grad.astype(jnp.float32)
    grad_attended = jnp.zeros((frames, channels), jnp.float32)
    kernel_rows = []
    for tap_index in range(KERNEL):
        back_start = 2 * HALF - tap_index
        back_mask = (pad_seg[back_start : back_start + frames] == own_seg)[:, None]
        grad_attended = grad_attended + jnp.where(
            back_mask, conv_weight[tap_index] * grad_wide[back_start : back_start + frames], 0.0
        )
        tap_mask = (pad_seg[tap_index : tap_index + frames] == own_seg)[:, None]
        product = conv_grad_wide * padded_wide[tap_index : tap_index + frames]
        kernel_rows.append(jnp.sum(jnp.where(tap_mask, product, 0.0), axis=0))
    grad_kernel = lax.psum(jnp.stack(kernel_rows), ("dp", "seq"))
    grad_attended = grad_attended.astype(jnp.bfloat16)
    g_heads = to_heads(grad_attended)
    row_delta = jnp.sum(g_heads.astype(jnp.float32) * attended_heads.astype(jnp.float32), axis=2)

    def query_grad_step(running, sliced, key_seg):
        key_block = sliced[0]
        value_block = sliced[1]
        soft_weights = jnp.exp(query_scores(key_block, key_seg) - log_total[:, :, None])
        slopes = jnp.einsum(
            "hqd,hkd->hqk", g_heads, value_block, preferred_element_type=jnp.float32
        )
        mixed_grad = (soft_weights * (slopes - row_delta[:, :, None])).astype(jnp.bfloat16)
        return running + jnp.einsum(
            "hqk,hkd->hqd", mixed_grad, key_block, preferred_element_type=jnp.float32
        )

    grad_query = over_rows(query_grad_step, frame_zeros, (key_whole, value_whole), 0)

    def key_grad_step(running, sliced, query_seg):
        grad_key_now, grad_value_now = running
        query_block = sliced[0]
        grad_block = sliced[1]
        total_block = sliced[2]
        delta_block = sliced[3]
        raw_scores = (
            jnp.einsum("hqd,hkd->hqk", query_block, k_heads, preferred_element_type=jnp.float32)
            * score_scale
        )
        scores = jnp.where(
            (query_seg[:, None] == own_seg[None, :])[None], raw_scores, NEGATIVE_FILL
        )
        soft_weights = jnp.exp(scores - total_block[:, :, None])
        grad_value_new = grad_value_now + jnp.einsum(
            "hqk,hqd->hkd",
            soft_weights.astype(jnp.bfloat16),
            grad_block,
            preferred_element_type=jnp.float32,
        )
        slopes = jnp.einsum("hqd,hkd->hqk", grad_block, v_heads, preferred_element_type=jnp.float32)
        mixed_grad = (soft_weights * (slopes - delta_block[:, :, None])).astype(jnp.bfloat16)
        grad_key_new = grad_key_now + jnp.einsum(
            "hqk,hqd->hkd", mixed_grad, query_block, preferred_element_type=jnp.float32
        )
        return (grad_key_new, grad_value_new)

    all_totals, all_deltas = (
        lax.all_gather(log_total[None], "seq", axis=2, tiled=True),
        lax.all_gather(row_delta[None], "seq", axis=2, tiled=True),
    )
    member = (
        lax.all_gather(queries, "seq", axis=1, tiled=True),
        lax.all_gather(grad_attended[None], "seq", axis=1, tiled=True),
    )
    totals_piece = all_totals[0]
    deltas_piece = all_deltas[0]
    grad_key, grad_value = over_rows(
        key_grad_step,
        (frame_zeros, frame_zeros),
        (to_heads(member[0][0]), to_heads(member[1][0]), totals_piece, deltas_piece),
        jnp.int32(0),
    )
    grad_queries = from_heads(grad_query * score_scale).astype(jnp.bfloat16)[None]
    grad_keys = from_heads(grad_key * score_scale).astype(jnp.bfloat16)[None]
    grad_values = from_heads(grad_value).astype(jnp.bfloat16)[None]
    return (mixed[None], grad_queries, grad_keys, grad_values, grad_kernel)


LANES = 128
PAD = 16
VMEM = pltpu.VMEM
MIB = 1024 * 1024


def mm(left, right):
    return lax.dot_general(
        left, right, (((1,), (0,)), ((), ())), preferred_element_type=jnp.float32
    )


def mm_nt(left, right):
    return lax.dot_general(
        left, right, (((1,), (1,)), ((), ())), preferred_element_type=jnp.float32
    )


def rows_at(block, frames):
    return pl.ds(pl.multiple_of(block * frames, frames), frames)


def lanes_at(block):
    return pl.ds(pl.multiple_of(block * LANES, LANES), LANES)


def partners(ranks):
    middle = ranks // 2
    return [middle] + [step for step in range(ranks - 1, 0, -1) if step != middle]


def pack_kernel(ranks, q_ref, k_ref, v_ref, *rest):
    outs, (whole, sems) = rest[:-2], rest[-2:]
    me = lax.axis_index("seq")
    sources = (q_ref, k_ref, v_ref)
    run_copies([(source.at[0], whole.at[place]) for place, source in enumerate(sources)], sems)
    for step in range(ranks - 1, 0, -1):
        for place in range(len(sources)):
            outs[step - 1][place] = whole[place, :, lanes_at(me ^ step)]


def run_copies(pairs, sems, meanwhile=None):
    copies = [
        pltpu.make_async_copy(source, target, sems.at[number])
        for number, (source, target) in enumerate(pairs)
    ]
    for copy in copies:
        copy.start()
    if meanwhile is not None:
        meanwhile()
    for copy in copies:
        copy.wait()


def mask_kernel(ranks, length, lens_ref, q_ref, k_ref, v_ref, c_ref, *refs):
    cot_refs = refs[: ranks - 1]
    own_ref, col_ref, row_ref, after_ref, before_ref, sems = refs[ranks - 1 :]
    me = lax.axis_index("seq")
    pairs = [(c_ref.at[0, :, lanes_at(me ^ step)], cot_refs[step - 1]) for step in range(1, ranks)]
    for place, source in enumerate((q_ref, k_ref, v_ref, c_ref)):
        pairs.append((source.at[0, :, lanes_at(me)], own_ref.at[place]))

    def extents():
        ends = []
        running = jnp.int32(0)
        for number in range(lens_ref.shape[1]):
            running = running + lens_ref[0, number]
            ends.append(running)
        row_time = lax.broadcasted_iota(jnp.int32, row_ref.shape, 1)
        row_first = jnp.zeros(row_ref.shape, jnp.int32)
        for end in ends:
            row_first = jnp.where(row_time >= end, end, row_first)
        row_ref[...] = row_first
        chunk = 64

        def some_rows(number, carry):
            base = pl.multiple_of(number * chunk, chunk)
            time = base + lax.broadcasted_iota(jnp.int32, (chunk, LANES), 0)
            first = jnp.zeros((chunk, LANES), jnp.int32)
            last = jnp.full((chunk, LANES), length, jnp.int32)
            for end in ends:
                first = jnp.where(time >= end, end, first)
            for end in reversed(ends):
                last = jnp.where(time < end, end, last)
            rows = pl.ds(base, chunk)
            col_ref[rows, :] = first
            after_ref[rows, :] = last - 1 - time
            before_ref[rows, :] = time - first
            return carry

        lax.fori_loop(0, length // chunk, some_rows, 0)

    run_copies(pairs, sems, extents)


def forward_kernel(ranks, frames, *refs):
    recvs = dict(zip(partners(ranks), refs))
    own_ref, col_ref, row_ref, after_ref, before_ref, w_ref = refs[ranks - 1 : ranks + 5]
    soft_ref, att_ref, pre_ref, q_ref, k_t_ref, v_ref = refs[ranks + 5 : ranks + 11]
    att_t_ref, k_full, q_full, w_own, w_sem = refs[ranks + 11 :]
    me = lax.axis_index("seq")
    length = ranks * frames
    copy = pltpu.make_async_copy(w_ref.at[:, lanes_at(me)], w_own, w_sem)
    copy.start()
    for place, target in enumerate((q_full, k_full, v_ref)):
        target[rows_at(me, frames), :] = own_ref[place]
        for step in range(1, ranks):
            target[rows_at(me ^ step, frames), :] = recvs[step][place]
    heads = LANES // HDIM
    lane_head = lax.broadcasted_iota(jnp.int32, (1, LANES), 1) // HDIM
    scaled = q_full[...].astype(jnp.float32) * (1.0 / math.sqrt(HDIM))
    for head in range(heads):
        q_ref[head] = jnp.where(lane_head == head, scaled, 0.0).astype(jnp.bfloat16)
    k_t_ref[...] = k_full[...].astype(jnp.float32).T.astype(jnp.bfloat16)
    v_t = v_ref[...].astype(jnp.float32).T.astype(jnp.bfloat16)
    wide = 512
    for head in range(heads):
        for start in range(0, length, wide):
            cols = slice(start, start + wide)
            raw = mm_nt(k_full[...], q_ref[head, cols, :])
            same = jnp.concatenate([col_ref[...]] * (wide // LANES), axis=1) == row_ref[0:1, cols]
            scores = jnp.where(same, raw, NEGATIVE_FILL)
            top = jnp.max(scores, axis=0, keepdims=True)
            powers = jnp.exp(scores - top)
            share = 1.0 / jnp.sum(powers, axis=0, keepdims=True)
            soft = (powers * share).astype(jnp.bfloat16)
            soft_ref[head, :, cols] = soft
            rows = slice(head * HDIM, (head + 1) * HDIM)
            att_t_ref[rows, cols] = mm(v_t[rows], soft).astype(jnp.bfloat16).astype(jnp.float32)
    zeros = jnp.zeros((PAD, LANES), jnp.float32)
    att_ref[0:PAD, :] = zeros
    att_ref[PAD : PAD + length, :] = att_t_ref[...].T
    att_ref[PAD + length :, :] = zeros
    copy.wait()

    chunk = 64

    def some_rows(number, carry):
        base = pl.multiple_of(number * chunk, chunk)
        rows = pl.ds(base, chunk)
        after, before = after_ref[rows, :], before_ref[rows, :]
        total = jnp.zeros((chunk, LANES), jnp.float32)
        for tap in range(KERNEL):
            off = tap - HALF
            piece = att_ref[pl.ds(base + (PAD + off), chunk), :]
            if off > 0:
                piece = jnp.where(after >= off, piece, 0.0)
            if off < 0:
                piece = jnp.where(before >= -off, piece, 0.0)
            total = total + w_own[tap : tap + 1, :] * piece
        pre_ref[rows, :] = total
        return carry

    lax.fori_loop(0, length // chunk, some_rows, 0)


def conv_back_kernel(ranks, frames, *refs):
    cots = dict(zip(partners(ranks), refs))
    own_ref, att_ref, pre_ref, after_ref, before_ref, w_ref = refs[ranks - 1 : ranks + 5]
    mixed_ref, g_att, taps_ref, cot, grad_pad, tap_sum, w_own, w_sem = refs[ranks + 5 :]
    me = lax.axis_index("seq")
    length = ranks * frames
    copy = pltpu.make_async_copy(w_ref.at[:, lanes_at(me)], w_own, w_sem)
    copy.start()
    cot[rows_at(me, frames), :] = own_ref[3]
    for step in range(1, ranks):
        cot[rows_at(me ^ step, frames), :] = cots[step][...]
    zeros = jnp.zeros((PAD, LANES), jnp.float32)
    grad_pad[0:PAD, :] = zeros
    grad_pad[PAD + length :, :] = zeros
    pre = pre_ref[...]
    gate = jax.nn.sigmoid(pre)
    mixed_ref[...] = (pre * gate).astype(jnp.bfloat16)
    conv_grad = cot[...].astype(jnp.float32) * gate * (1.0 + pre * (1.0 - gate))
    grad_pad[PAD : PAD + length, :] = conv_grad.astype(jnp.bfloat16).astype(jnp.float32)
    tap_sum[...] = jnp.zeros(tap_sum.shape, jnp.float32)
    copy.wait()

    chunk = 64

    def some_rows(number, carry):
        base = pl.multiple_of(number * chunk, chunk)
        rows = pl.ds(base, chunk)
        after, before = after_ref[rows, :], before_ref[rows, :]
        own_att = att_ref[pl.ds(base + PAD, chunk), :]
        total = jnp.zeros((chunk, LANES), jnp.float32)
        for tap in range(KERNEL):
            off = tap - HALF
            piece = grad_pad[pl.ds(base + (PAD - off), chunk), :]
            if off > 0:
                piece = jnp.where(before >= off, piece, 0.0)
            if off < 0:
                piece = jnp.where(after >= -off, piece, 0.0)
            total = total + w_own[tap : tap + 1, :] * piece
            part = (own_att * piece).reshape(chunk // 8, 8, LANES)
            tap_sum[tap] = tap_sum[tap] + jnp.sum(part, axis=0)
        g_att[rows, :] = total.astype(jnp.bfloat16)
        return carry

    lax.fori_loop(0, length // chunk, some_rows, 0)
    taps_ref[...] = jnp.sum(tap_sum[...], axis=1)


def backward_kernel(soft_ref, att_ref, g_att, q_ref, k_t_ref, v_ref, res_q, res_k, res_v, grad_t):
    length = v_ref.shape[0]
    heads = LANES // HDIM
    lane_head = lax.broadcasted_iota(jnp.int32, (1, LANES), 1) // HDIM
    g_wide = g_att[...].astype(jnp.float32)
    products_t = (g_wide * att_ref[PAD : PAD + length, :]).T
    g_heads = [jnp.where(lane_head == head, g_wide, 0.0).astype(jnp.bfloat16) for head in range(heads)]
    wide = 512
    grad_v = jnp.zeros((length, LANES), jnp.float32)
    grad_k = jnp.zeros((length, LANES), jnp.float32)
    for head in range(heads):
        rows = slice(head * HDIM, (head + 1) * HDIM)
        delta = jnp.sum(products_t[rows], axis=0, keepdims=True)
        for start in range(0, length, wide):
            cols = slice(start, start + wide)
            soft = soft_ref[head, :, cols]
            slopes = mm_nt(v_ref[...], g_heads[head][cols])
            mixed_grad = (soft.astype(jnp.float32) * (slopes - delta[:, cols])).astype(jnp.bfloat16)
            grad_v = grad_v + mm(soft, g_heads[head][cols])
            grad_k = grad_k + mm(mixed_grad, q_ref[head, cols, :])
            grad_t[rows, cols] = mm(k_t_ref[rows, :], mixed_grad) * (1.0 / math.sqrt(HDIM))
    res_k[...] = grad_k.astype(jnp.bfloat16)
    res_v[...] = grad_v.astype(jnp.bfloat16)
    res_q[...] = grad_t[...].T.astype(jnp.bfloat16)


def block_kernel(steps, frames, *refs):
    sources, tap_refs, outs = refs[:4], refs[4 : -len(steps)], refs[-len(steps) :]
    me = lax.axis_index("seq")
    taps = tap_refs[0][...]
    for other in tap_refs[1:]:
        taps = taps + other[...]
    for step, out in zip(steps, outs):
        rows = rows_at(me ^ step, frames)
        for place, source in enumerate(sources):
            out[place * frames : (place + 1) * frames, :] = source[rows, :]
        out[4 * frames :, :] = taps.astype(jnp.bfloat16)


def spread_kernel(ranks, frames, *refs):
    blocks = refs[:ranks]
    targets, taps_ref = refs[ranks : ranks + 4], refs[ranks + 4]
    me = lax.axis_index("seq")
    for step in range(ranks):
        lanes = lanes_at(me ^ step)
        for place, target in enumerate(targets):
            target[0, :, lanes] = blocks[step][place * frames : (place + 1) * frames, :]
        taps = blocks[step][4 * frames :, :].astype(jnp.float32)
        taps_ref[:, lanes] = taps[:KERNEL]


def cost(flops, moved):
    return pl.CostEstimate(flops=flops, bytes_accessed=moved, transcendentals=0)


def on_device_heads(queries, keys, values, cotangent, conv_weight, rec_lengths):
    ranks = lax.axis_size("seq")
    frames = queries.shape[1]
    length = ranks * frames
    heads = LANES // HDIM
    bf16, f32, i32 = jnp.bfloat16, jnp.float32, jnp.int32
    struct = jax.ShapeDtypeStruct
    hbm = pl.BlockSpec(memory_space=pltpu.HBM)
    anywhere = pl.BlockSpec(memory_space=pl.ANY)
    vmem = pl.BlockSpec(memory_space=VMEM)
    smem = pl.BlockSpec(memory_space=pltpu.SMEM)
    params = pltpu.CompilerParams(vmem_limit_bytes=24 * MIB)
    taps = KERNEL + 1

    sends = pl.pallas_call(
        functools.partial(pack_kernel, ranks),
        out_shape=[struct((3, frames, LANES), bf16)] * (ranks - 1),
        in_specs=[hbm] * 3,
        out_specs=[vmem] * (ranks - 1),
        scratch_shapes=[VMEM((3,) + queries.shape[1:], bf16), pltpu.SemaphoreType.DMA((3,))],
        compiler_params=pltpu.CompilerParams(vmem_limit_bytes=54912 * 1024),
        name="pack",
    )(queries, keys, values)

    def swap(array, step):
        return lax.ppermute(array, "seq", [(rank, rank ^ step) for rank in range(ranks)])

    order = partners(ranks)
    received = {step: swap(sends[step - 1], step) for step in order}

    *cot_sends, own, col, row, after, before = pl.pallas_call(
        functools.partial(mask_kernel, ranks, length),
        out_shape=[struct((frames, LANES), bf16)] * (ranks - 1)
        + [
            struct((4, frames, LANES), bf16),
            struct((length, LANES), i32),
            struct((8, length), i32),
            struct((length, LANES), i32),
            struct((length, LANES), i32),
        ],
        in_specs=[smem] + [hbm] * 4,
        out_specs=[vmem] * (ranks + 4),
        scratch_shapes=[pltpu.SemaphoreType.DMA((ranks + 3,))],
        compiler_params=params,
        cost_estimate=cost(4 * MIB, MIB),
        name="masks",
    )(rec_lengths, queries, keys, values, cotangent)
    cots = {step: swap(cot_sends[step - 1], step) for step in order}

    soft, att, pre, q_heads, k_t, v_full = pl.pallas_call(
        functools.partial(forward_kernel, ranks, frames),
        out_shape=[
            struct((heads, length, length), bf16),
            struct((length + 2 * PAD, LANES), f32),
            struct((length, LANES), f32),
            struct((heads, length, LANES), bf16),
            struct((LANES, length), bf16),
            struct((length, LANES), bf16),
        ],
        in_specs=[vmem] * (ranks + 4) + [anywhere],
        out_specs=[vmem] * 6,
        scratch_shapes=[
            VMEM((LANES, length), f32),
            VMEM((length, LANES), bf16),
            VMEM((length, LANES), bf16),
            VMEM((KERNEL, LANES), f32),
            pltpu.SemaphoreType.DMA,
        ],
        compiler_params=params,
        cost_estimate=cost(400 * MIB, 3 * MIB),
        name="forward",
    )(*[received[step] for step in order], own, col, row, after, before, conv_weight)

    mixed, g_att, own_taps = pl.pallas_call(
        functools.partial(conv_back_kernel, ranks, frames),
        out_shape=[struct((length, LANES), bf16)] * 2 + [struct((taps, LANES), f32)],
        in_specs=[vmem] * (ranks + 4) + [anywhere],
        out_specs=[vmem] * 3,
        scratch_shapes=[
            VMEM((length, LANES), bf16),
            VMEM((length + 2 * PAD, LANES), f32),
            VMEM((taps, 8, LANES), f32),
            VMEM((KERNEL, LANES), f32),
            pltpu.SemaphoreType.DMA,
        ],
        compiler_params=params,
        cost_estimate=cost(400 * MIB, 3 * MIB),
        name="conv_back",
    )(*[cots[step] for step in order], own, att, pre, after, before, conv_weight)

    copies = lax.axis_size("dp")
    part_taps = [own_taps] + [
        lax.ppermute(own_taps, "dp", [(one, (one + shift) % copies) for one in range(copies)])
        for shift in range(1, copies)
    ]

    results = pl.pallas_call(
        backward_kernel,
        out_shape=[struct((length, LANES), bf16)] * 3,
        in_specs=[vmem] * 6,
        out_specs=[vmem] * 3,
        scratch_shapes=[VMEM((LANES, length), f32)],
        compiler_params=params,
        cost_estimate=cost(800 * MIB, 3 * MIB),
        name="backward",
    )(soft, att, g_att, q_heads, k_t, v_full)

    def blocks_of(steps):
        return pl.pallas_call(
            functools.partial(block_kernel, steps, frames),
            out_shape=[struct((4 * frames + taps, LANES), bf16)] * len(steps),
            in_specs=[vmem] * (4 + copies),
            out_specs=[vmem] * len(steps),
            compiler_params=params,
            cost_estimate=cost(MIB, MIB),
            name="blocks",
        )(mixed, *results, *part_taps)

    half = ranks // 2
    far = blocks_of(list(range(half, ranks)))
    near = blocks_of(list(range(half)))
    back = {step: swap(far[step - half], step) for step in range(half, ranks)}
    back |= {step: swap(near[step], step) for step in range(1, half)}
    back[0] = near[0]

    return pl.pallas_call(
        functools.partial(spread_kernel, ranks, frames),
        out_shape=[struct(queries.shape, bf16)] * 4 + [struct(conv_weight.shape, f32)],
        in_specs=[vmem] * ranks,
        out_specs=[vmem] * 5,
        compiler_params=params,
        name="spread",
    )(*[back[step] for step in range(ranks)])


def on_device_any(queries, keys, values, cotangent, conv_weight, rec_lengths):
    ranks = lax.axis_size("seq")
    frames, channels = queries.shape[1], queries.shape[2]
    fits = channels == ranks * LANES and ranks & (ranks - 1) == 0 and frames % LANES == 0
    if fits and ranks > 1 and ranks * frames <= 1024 and lax.axis_size("dp") == 2:
        return on_device_heads(queries, keys, values, cotangent, conv_weight, rec_lengths)
    return on_device(queries, keys, values, cotangent, conv_weight, rec_lengths)


def solution(mesh):
    placed = (
        P(("groups", "dp"), "seq", "mp"),
        P(("groups", "dp"), "seq", "mp"),
        P(("groups", "dp"), "seq", "mp"),
        P(("groups", "dp"), "seq", "mp"),
        P(None, "mp"),
        P(("groups", "dp"), None),
    )
    return jax.shard_map(
        on_device_any,
        mesh=mesh,
        in_specs=placed,
        out_specs=(
            P(("groups", "dp"), "seq", "mp"),
            P(("groups", "dp"), "seq", "mp"),
            P(("groups", "dp"), "seq", "mp"),
            P(("groups", "dp"), "seq", "mp"),
            P("groups", "mp"),
        ),
        check_vma=False,
    )
```

```python
import functools
import math

import jax
import jax.numpy as jnp
from jax import lax
from jax.experimental import pallas as pl
from jax.experimental.pallas import tpu as pltpu
from jax.sharding import PartitionSpec as P

HDIM = 64
KERNEL = 31
HALF = 15


NEGATIVE_FILL = -1e30


def extended(block, sides, width):
    for axis, dim in sides:
        count = lax.axis_size(axis)
        forward = [(i, i + 1) for i in range(count - 1)]
        backward = [(target, source) for source, target in forward]
        low = lax.ppermute(
            lax.slice_in_dim(block, block.shape[dim] - width, None, axis=dim), axis, forward
        )
        high = lax.ppermute(lax.slice_in_dim(block, 0, width, axis=dim), axis, backward)
        block = jnp.concatenate([low, block, high], axis=dim)
    return block


def pick_block(total_rows):
    for candidate in (512, 256, 128):
        return candidate
    return total_rows


def over_blocks(total_rows, advance, initial):
    block_rows = pick_block(total_rows)
    block_count = total_rows // block_rows
    if block_count == 1:
        return advance(initial, 0, block_rows)
    return lax.fori_loop(
        0,
        block_count,
        lambda number, running: advance(running, number * block_rows, block_rows),
        initial,
    )


def when_shared(compute, running):
    result = compute(running)
    return result


def on_device(queries, keys, values, cotangent, conv_weight, rec_lengths):
    frames = queries.shape[1]
    channels = queries.shape[2]
    local_heads = channels // HDIM
    score_scale = 1.0 / math.sqrt(HDIM)
    length_all = frames * lax.axis_size("seq")
    offset = lax.axis_index("seq") * frames
    record_ends = jnp.cumsum(rec_lengths[0], dtype=jnp.int32)

    def segment_of(positions):
        return jnp.sum((record_ends[None, :] <= positions[:, None]).astype(jnp.int32), axis=1)

    own_seg = segment_of(offset + jnp.arange(frames, dtype=jnp.int32))

    def to_heads(array):
        return array.reshape(array.shape[0], local_heads, HDIM).transpose(1, 0, 2)

    def from_heads(array):
        return array.transpose(1, 0, 2).reshape(array.shape[1], channels)

    q_heads = to_heads(queries[0])
    k_heads = to_heads(keys[0])
    v_heads = to_heads(values[0])

    def over_rows(advance, initial, members, first_row):
        total_rows = members[0].shape[1]

        def one_block(running, block_start, block_rows):
            sliced = tuple(
                (lax.dynamic_slice_in_dim(member, block_start, block_rows, 1) for member in members)
            )
            other_seg = segment_of(
                first_row + block_start + jnp.arange(block_rows, dtype=jnp.int32)
            )
            return when_shared(lambda current: advance(current, sliced, other_seg), running)

        return over_blocks(total_rows, one_block, initial)

    def query_scores(key_block, key_seg):
        raw_scores = (
            jnp.einsum("hqd,hkd->hqk", q_heads, key_block, preferred_element_type=jnp.float32)
            * score_scale
        )
        return jnp.where((own_seg[:, None] == key_seg[None, :])[None], raw_scores, NEGATIVE_FILL)

    def stats_step(running, sliced, key_seg):
        top_now, total_now = running
        scores = query_scores(sliced[0], key_seg)
        top_new = jnp.maximum(top_now, jnp.max(scores, axis=2))
        total_new = total_now * jnp.exp(top_now - top_new) + jnp.sum(
            jnp.exp(scores - top_new[:, :, None]), axis=2
        )
        return (top_new, total_new)

    stats_init = (
        jnp.full((local_heads, frames), NEGATIVE_FILL, jnp.float32),
        jnp.zeros((local_heads, frames), jnp.float32),
    )
    gathered = (
        lax.all_gather(keys, "seq", axis=1, tiled=True),
        lax.all_gather(values, "seq", axis=1, tiled=True),
    )
    key_whole = to_heads(gathered[0][0])
    value_whole = to_heads(gathered[1][0])
    row_stats = over_rows(stats_step, stats_init, (key_whole,), 0)
    log_total = row_stats[0] + jnp.log(row_stats[1])

    def output_step(running, sliced, key_seg):
        scores = query_scores(sliced[0], key_seg)
        soft_rounded = jnp.exp(scores - log_total[:, :, None]).astype(jnp.bfloat16)
        return running + jnp.einsum(
            "hqk,hkd->hqd", soft_rounded, sliced[1], preferred_element_type=jnp.float32
        )

    frame_zeros = jnp.zeros((local_heads, frames, HDIM), jnp.float32)
    attended_sum = over_rows(output_step, frame_zeros, (key_whole, value_whole), 0)
    attended_heads = attended_sum.astype(jnp.bfloat16)
    attended = from_heads(attended_heads)
    padded = extended(attended[None], (("seq", 1),), HALF)
    padded_wide = padded[0].astype(jnp.float32)
    pad_positions = offset - HALF + jnp.arange(frames + 2 * HALF, dtype=jnp.int32)
    inside = jnp.logical_and(pad_positions >= 0, pad_positions < length_all)
    pad_seg = jnp.where(inside, segment_of(pad_positions), -1)
    conv_pre = jnp.zeros((frames, channels), jnp.float32)
    for tap_index in range(KERNEL):
        tap_mask = (pad_seg[tap_index : tap_index + frames] == own_seg)[:, None]
        conv_pre = conv_pre + jnp.where(
            tap_mask, conv_weight[tap_index] * padded_wide[tap_index : tap_index + frames], 0.0
        )
    gate_value = jax.nn.sigmoid(conv_pre)
    mixed = (conv_pre * gate_value).astype(jnp.bfloat16)
    conv_grad = (
        cotangent[0].astype(jnp.float32) * gate_value * (1.0 + conv_pre * (1.0 - gate_value))
    ).astype(jnp.bfloat16)
    padded_grad = extended(conv_grad[None], (("seq", 1),), HALF)
    grad_wide = padded_grad[0].astype(jnp.float32)
    conv_grad_wide = conv_grad.astype(jnp.float32)
    grad_attended = jnp.zeros((frames, channels), jnp.float32)
    kernel_rows = []
    for tap_index in range(KERNEL):
        back_start = 2 * HALF - tap_index
        back_mask = (pad_seg[back_start : back_start + frames] == own_seg)[:, None]
        grad_attended = grad_attended + jnp.where(
            back_mask, conv_weight[tap_index] * grad_wide[back_start : back_start + frames], 0.0
        )
        tap_mask = (pad_seg[tap_index : tap_index + frames] == own_seg)[:, None]
        product = conv_grad_wide * padded_wide[tap_index : tap_index + frames]
        kernel_rows.append(jnp.sum(jnp.where(tap_mask, product, 0.0), axis=0))
    grad_kernel = lax.psum(jnp.stack(kernel_rows), ("dp", "seq"))
    grad_attended = grad_attended.astype(jnp.bfloat16)
    g_heads = to_heads(grad_attended)
    row_delta = jnp.sum(g_heads.astype(jnp.float32) * attended_heads.astype(jnp.float32), axis=2)

    def query_grad_step(running, sliced, key_seg):
        key_block = sliced[0]
        value_block = sliced[1]
        soft_weights = jnp.exp(query_scores(key_block, key_seg) - log_total[:, :, None])
        slopes = jnp.einsum(
            "hqd,hkd->hqk", g_heads, value_block, preferred_element_type=jnp.float32
        )
        mixed_grad = (soft_weights * (slopes - row_delta[:, :, None])).astype(jnp.bfloat16)
        return running + jnp.einsum(
            "hqk,hkd->hqd", mixed_grad, key_block, preferred_element_type=jnp.float32
        )

    grad_query = over_rows(query_grad_step, frame_zeros, (key_whole, value_whole), 0)

    def key_grad_step(running, sliced, query_seg):
        grad_key_now, grad_value_now = running
        query_block = sliced[0]
        grad_block = sliced[1]
        total_block = sliced[2]
        delta_block = sliced[3]
        raw_scores = (
            jnp.einsum("hqd,hkd->hqk", query_block, k_heads, preferred_element_type=jnp.float32)
            * score_scale
        )
        scores = jnp.where(
            (query_seg[:, None] == own_seg[None, :])[None], raw_scores, NEGATIVE_FILL
        )
        soft_weights = jnp.exp(scores - total_block[:, :, None])
        grad_value_new = grad_value_now + jnp.einsum(
            "hqk,hqd->hkd",
            soft_weights.astype(jnp.bfloat16),
            grad_block,
            preferred_element_type=jnp.float32,
        )
        slopes = jnp.einsum("hqd,hkd->hqk", grad_block, v_heads, preferred_element_type=jnp.float32)
        mixed_grad = (soft_weights * (slopes - delta_block[:, :, None])).astype(jnp.bfloat16)
        grad_key_new = grad_key_now + jnp.einsum(
            "hqk,hqd->hkd", mixed_grad, query_block, preferred_element_type=jnp.float32
        )
        return (grad_key_new, grad_value_new)

    all_totals, all_deltas = (
        lax.all_gather(log_total[None], "seq", axis=2, tiled=True),
        lax.all_gather(row_delta[None], "seq", axis=2, tiled=True),
    )
    member = (
        lax.all_gather(queries, "seq", axis=1, tiled=True),
        lax.all_gather(grad_attended[None], "seq", axis=1, tiled=True),
    )
    totals_piece = all_totals[0]
    deltas_piece = all_deltas[0]
    grad_key, grad_value = over_rows(
        key_grad_step,
        (frame_zeros, frame_zeros),
        (to_heads(member[0][0]), to_heads(member[1][0]), totals_piece, deltas_piece),
        jnp.int32(0),
    )
    grad_queries = from_heads(grad_query * score_scale).astype(jnp.bfloat16)[None]
    grad_keys = from_heads(grad_key * score_scale).astype(jnp.bfloat16)[None]
    grad_values = from_heads(grad_value).astype(jnp.bfloat16)[None]
    return (mixed[None], grad_queries, grad_keys, grad_values, grad_kernel)


LANES = 128
PAD = 16
VMEM = pltpu.VMEM
MIB = 1024 * 1024


def mm(left, right):
    return lax.dot_general(
        left, right, (((1,), (0,)), ((), ())), preferred_element_type=jnp.float32
    )


def mm_nt(left, right):
    return lax.dot_general(
        left, right, (((1,), (1,)), ((), ())), preferred_element_type=jnp.float32
    )


def rows_at(block, frames):
    return pl.ds(pl.multiple_of(block * frames, frames), frames)


def lanes_at(block):
    return pl.ds(pl.multiple_of(block * LANES, LANES), LANES)


def pack_kernel(ranks, q_ref, k_ref, v_ref, *rest):
    outs, sems = rest[:-1], rest[-1]
    me = lax.axis_index("seq")
    pairs = []
    for step in range(ranks - 1, 0, -1):
        for place, source in enumerate((q_ref, k_ref, v_ref)):
            pairs.append((source.at[0, :, lanes_at(me ^ step)], outs[step - 1].at[place]))
    run_copies(pairs, sems)


def run_copies(pairs, sems, meanwhile=None):
    copies = [
        pltpu.make_async_copy(source, target, sems.at[number])
        for number, (source, target) in enumerate(pairs)
    ]
    for copy in copies:
        copy.start()
    if meanwhile is not None:
        meanwhile()
    for copy in copies:
        copy.wait()


def mask_kernel(ranks, length, lens_ref, q_ref, k_ref, v_ref, c_ref, *refs):
    cot_refs = refs[: ranks - 1]
    own_ref, col_ref, row_ref, after_ref, before_ref, sems = refs[ranks - 1 :]
    me = lax.axis_index("seq")
    pairs = [(c_ref.at[0, :, lanes_at(me ^ step)], cot_refs[step - 1]) for step in range(1, ranks)]
    for place, source in enumerate((q_ref, k_ref, v_ref, c_ref)):
        pairs.append((source.at[0, :, lanes_at(me)], own_ref.at[place]))

    def extents():
        ends = []
        running = jnp.int32(0)
        for number in range(lens_ref.shape[1]):
            running = running + lens_ref[0, number]
            ends.append(running)
        row_time = lax.broadcasted_iota(jnp.int32, row_ref.shape, 1)
        row_first = jnp.zeros(row_ref.shape, jnp.int32)
        for end in ends:
            row_first = jnp.where(row_time >= end, end, row_first)
        row_ref[...] = row_first
        chunk = 64

        def some_rows(number, carry):
            base = pl.multiple_of(number * chunk, chunk)
            time = base + lax.broadcasted_iota(jnp.int32, (chunk, LANES), 0)
            first = jnp.zeros((chunk, LANES), jnp.int32)
            last = jnp.full((chunk, LANES), length, jnp.int32)
            for end in ends:
                first = jnp.where(time >= end, end, first)
            for end in reversed(ends):
                last = jnp.where(time < end, end, last)
            rows = pl.ds(base, chunk)
            col_ref[rows, :] = first
            after_ref[rows, :] = last - 1 - time
            before_ref[rows, :] = time - first
            return carry

        lax.fori_loop(0, length // chunk, some_rows, 0)

    run_copies(pairs, sems, extents)


def forward_kernel(ranks, frames, *refs):
    recvs = refs[: ranks - 1]
    own_ref, col_ref, row_ref, after_ref, before_ref, w_ref = refs[ranks - 1 : ranks + 5]
    soft_ref, att_ref, pre_ref, q_ref, k_t_ref, v_ref = refs[ranks + 5 : ranks + 11]
    att_t_ref, k_full, q_full, w_own, w_sem = refs[ranks + 11 :]
    me = lax.axis_index("seq")
    length = ranks * frames
    copy = pltpu.make_async_copy(w_ref.at[:, lanes_at(me)], w_own, w_sem)
    copy.start()
    for place, target in enumerate((q_full, k_full, v_ref)):
        target[rows_at(me, frames), :] = own_ref[place]
        for step in range(1, ranks):
            target[rows_at(me ^ step, frames), :] = recvs[ranks - 1 - step][place]
    heads = LANES // HDIM
    lane_head = lax.broadcasted_iota(jnp.int32, (1, LANES), 1) // HDIM
    scaled = q_full[...].astype(jnp.float32) * (1.0 / math.sqrt(HDIM))
    for head in range(heads):
        q_ref[head] = jnp.where(lane_head == head, scaled, 0.0).astype(jnp.bfloat16)
    k_t_ref[...] = k_full[...].astype(jnp.float32).T.astype(jnp.bfloat16)
    v_t = v_ref[...].astype(jnp.float32).T.astype(jnp.bfloat16)
    wide = 512
    for head in range(heads):
        for start in range(0, length, wide):
            cols = slice(start, start + wide)
            raw = mm_nt(k_full[...], q_ref[head, cols, :])
            same = jnp.concatenate([col_ref[...]] * (wide // LANES), axis=1) == row_ref[0:1, cols]
            scores = jnp.where(same, raw, NEGATIVE_FILL)
            top = jnp.max(scores, axis=0, keepdims=True)
            powers = jnp.exp(scores - top)
            share = 1.0 / jnp.sum(powers, axis=0, keepdims=True)
            soft = (powers * share).astype(jnp.bfloat16)
            soft_ref[head, :, cols] = soft
            rows = slice(head * HDIM, (head + 1) * HDIM)
            att_t_ref[rows, cols] = mm(v_t[rows], soft).astype(jnp.bfloat16).astype(jnp.float32)
    zeros = jnp.zeros((PAD, LANES), jnp.float32)
    att_ref[0:PAD, :] = zeros
    att_ref[PAD : PAD + length, :] = att_t_ref[...].T
    att_ref[PAD + length :, :] = zeros
    copy.wait()

    chunk = 64

    def some_rows(number, carry):
        base = pl.multiple_of(number * chunk, chunk)
        rows = pl.ds(base, chunk)
        after, before = after_ref[rows, :], before_ref[rows, :]
        total = jnp.zeros((chunk, LANES), jnp.float32)
        for tap in range(KERNEL):
            off = tap - HALF
            piece = att_ref[pl.ds(base + (PAD + off), chunk), :]
            if off > 0:
                piece = jnp.where(after >= off, piece, 0.0)
            if off < 0:
                piece = jnp.where(before >= -off, piece, 0.0)
            total = total + w_own[tap : tap + 1, :] * piece
        pre_ref[rows, :] = total
        return carry

    lax.fori_loop(0, length // chunk, some_rows, 0)


def masked(source, base, chunk, off, before, after):
    piece = source[pl.ds(base + (PAD + off), chunk), :]
    if off > 0:
        piece = jnp.where(after >= off, piece, 0.0)
    if off < 0:
        piece = jnp.where(before >= -off, piece, 0.0)
    return piece


def taps_kernel(ranks, frames, *refs):
    cots = refs[: ranks - 1]
    own_ref, att_ref, pre_ref, after_ref, before_ref = refs[ranks - 1 : ranks + 4]
    mixed_ref, grad_pad, taps_ref, cot, tap_sum = refs[ranks + 4 :]
    me = lax.axis_index("seq")
    length = ranks * frames
    cot[rows_at(me, frames), :] = own_ref[3]
    for step in range(1, ranks):
        cot[rows_at(me ^ step, frames), :] = cots[ranks - 1 - step][...]
    zeros = jnp.zeros((PAD, LANES), jnp.float32)
    grad_pad[0:PAD, :] = zeros
    grad_pad[PAD + length :, :] = zeros
    tap_sum[...] = jnp.zeros(tap_sum.shape, jnp.float32)
    chunk = 64

    def some_rows(number, carry):
        base = pl.multiple_of(number * chunk, chunk)
        rows = pl.ds(base, chunk)
        pre = pre_ref[rows, :]
        gate = jax.nn.sigmoid(pre)
        mixed_ref[rows, :] = (pre * gate).astype(jnp.bfloat16)
        conv_grad = cot[rows, :].astype(jnp.float32) * gate * (1.0 + pre * (1.0 - gate))
        conv_grad = conv_grad.astype(jnp.bfloat16).astype(jnp.float32)
        grad_pad[pl.ds(base + PAD, chunk), :] = conv_grad
        after, before = after_ref[rows, :], before_ref[rows, :]
        for tap in range(KERNEL):
            part = conv_grad * masked(att_ref, base, chunk, tap - HALF, before, after)
            tap_sum[tap] = tap_sum[tap] + jnp.sum(part.reshape(chunk // 8, 8, LANES), axis=0)
        return carry

    lax.fori_loop(0, length // chunk, some_rows, 0)
    taps_ref[...] = jnp.sum(tap_sum[...], axis=1)


def backward_kernel(soft_ref, att_ref, grad_pad, after_ref, before_ref, q_ref, k_t_ref, v_ref, w_ref, *refs):
    res_q, res_k, res_v, g_att, grad_t, w_own, w_sem = refs
    length = v_ref.shape[0]
    copy = pltpu.make_async_copy(w_ref.at[:, lanes_at(lax.axis_index("seq"))], w_own, w_sem)
    copy.start()
    copy.wait()
    chunk = 64

    def some_rows(number, carry):
        base = pl.multiple_of(number * chunk, chunk)
        rows = pl.ds(base, chunk)
        after, before = after_ref[rows, :], before_ref[rows, :]
        total = jnp.zeros((chunk, LANES), jnp.float32)
        for tap in range(KERNEL):
            total = total + w_own[tap : tap + 1, :] * masked(grad_pad, base, chunk, HALF - tap, before, after)
        g_att[rows, :] = total.astype(jnp.bfloat16)
        return carry

    lax.fori_loop(0, length // chunk, some_rows, 0)
    heads = LANES // HDIM
    lane_head = lax.broadcasted_iota(jnp.int32, (1, LANES), 1) // HDIM
    g_wide = g_att[...].astype(jnp.float32)
    products_t = (g_wide * att_ref[PAD : PAD + length, :]).T
    grad_v = jnp.zeros((length, LANES), jnp.float32)
    grad_k = jnp.zeros((length, LANES), jnp.float32)
    for head in range(heads):
        rows = slice(head * HDIM, (head + 1) * HDIM)
        g_head = jnp.where(lane_head == head, g_wide, 0.0).astype(jnp.bfloat16)
        delta = jnp.sum(products_t[rows], axis=0, keepdims=True)
        soft = soft_ref[head]
        slopes = mm_nt(v_ref[...], g_head)
        mixed_grad = (soft.astype(jnp.float32) * (slopes - delta)).astype(jnp.bfloat16)
        grad_v = grad_v + mm(soft, g_head)
        grad_k = grad_k + mm(mixed_grad, q_ref[head])
        grad_t[rows, :] = mm(k_t_ref[rows, :], mixed_grad) * (1.0 / math.sqrt(HDIM))
    res_k[...] = grad_k.astype(jnp.bfloat16)
    res_v[...] = grad_v.astype(jnp.bfloat16)
    res_q[...] = grad_t[...].T.astype(jnp.bfloat16)


def block_kernel(steps, frames, *refs):
    sources, tap_refs, outs = refs[:4], refs[4 : -len(steps)], refs[-len(steps) :]
    me = lax.axis_index("seq")
    taps = tap_refs[0][...]
    for other in tap_refs[1:]:
        taps = taps + other[...]
    for step, out in zip(steps, outs):
        rows = rows_at(me ^ step, frames)
        for place, source in enumerate(sources):
            out[place * frames : (place + 1) * frames, :] = source[rows, :]
        out[4 * frames :, :] = taps.astype(jnp.bfloat16)


def spread_kernel(ranks, frames, *refs):
    blocks = refs[:ranks]
    targets, taps_ref = refs[ranks : ranks + 4], refs[ranks + 4]
    me = lax.axis_index("seq")
    for step in range(ranks):
        lanes = lanes_at(me ^ step)
        for place, target in enumerate(targets):
            target[0, :, lanes] = blocks[step][place * frames : (place + 1) * frames, :]
        taps = blocks[step][4 * frames :, :].astype(jnp.float32)
        taps_ref[:, lanes] = taps[:KERNEL]


def cost(flops, moved):
    return pl.CostEstimate(flops=flops, bytes_accessed=moved, transcendentals=0)


def on_device_heads(queries, keys, values, cotangent, conv_weight, rec_lengths):
    ranks = lax.axis_size("seq")
    frames = queries.shape[1]
    length = ranks * frames
    heads = LANES // HDIM
    bf16, f32, i32 = jnp.bfloat16, jnp.float32, jnp.int32
    struct = jax.ShapeDtypeStruct
    hbm = pl.BlockSpec(memory_space=pltpu.HBM)
    anywhere = pl.BlockSpec(memory_space=pl.ANY)
    vmem = pl.BlockSpec(memory_space=VMEM)
    smem = pl.BlockSpec(memory_space=pltpu.SMEM)
    params = pltpu.CompilerParams(vmem_limit_bytes=24 * MIB)
    taps = KERNEL + 1

    sends = pl.pallas_call(
        functools.partial(pack_kernel, ranks),
        out_shape=[struct((3, frames, LANES), bf16)] * (ranks - 1),
        in_specs=[hbm] * 3,
        out_specs=[vmem] * (ranks - 1),
        scratch_shapes=[pltpu.SemaphoreType.DMA((3 * (ranks - 1),))],
        compiler_params=pltpu.CompilerParams(vmem_limit_bytes=54912 * 1024),
        name="pack",
    )(queries, keys, values)

    def swap(array, step):
        return lax.ppermute(array, "seq", [(rank, rank ^ step) for rank in range(ranks)])

    order = list(range(ranks - 1, 0, -1))
    received = {step: swap(sends[step - 1], step) for step in order}

    *cot_sends, own, col, row, after, before = pl.pallas_call(
        functools.partial(mask_kernel, ranks, length),
        out_shape=[struct((frames, LANES), bf16)] * (ranks - 1)
        + [
            struct((4, frames, LANES), bf16),
            struct((length, LANES), i32),
            struct((8, length), i32),
            struct((length, LANES), i32),
            struct((length, LANES), i32),
        ],
        in_specs=[smem] + [hbm] * 4,
        out_specs=[vmem] * (ranks + 4),
        scratch_shapes=[pltpu.SemaphoreType.DMA((ranks + 3,))],
        compiler_params=params,
        cost_estimate=cost(4 * MIB, MIB),
        name="masks",
    )(rec_lengths, queries, keys, values, cotangent)
    cots = {step: swap(cot_sends[step - 1], step) for step in order}

    soft, att, pre, q_heads, k_t, v_full = pl.pallas_call(
        functools.partial(forward_kernel, ranks, frames),
        out_shape=[
            struct((heads, length, length), bf16),
            struct((length + 2 * PAD, LANES), f32),
            struct((length, LANES), f32),
            struct((heads, length, LANES), bf16),
            struct((LANES, length), bf16),
            struct((length, LANES), bf16),
        ],
        in_specs=[vmem] * (ranks + 4) + [anywhere],
        out_specs=[vmem] * 6,
        scratch_shapes=[
            VMEM((LANES, length), f32),
            VMEM((length, LANES), bf16),
            VMEM((length, LANES), bf16),
            VMEM((KERNEL, LANES), f32),
            pltpu.SemaphoreType.DMA,
        ],
        compiler_params=params,
        cost_estimate=cost(400 * MIB, 3 * MIB),
        name="forward",
    )(*[received[step] for step in order], own, col, row, after, before, conv_weight)

    mixed, grad_pad, own_taps = pl.pallas_call(
        functools.partial(taps_kernel, ranks, frames),
        out_shape=[
            struct((length, LANES), bf16),
            struct((length + 2 * PAD, LANES), f32),
            struct((taps, LANES), f32),
        ],
        in_specs=[vmem] * (ranks + 4),
        out_specs=[vmem] * 3,
        scratch_shapes=[VMEM((length, LANES), bf16), VMEM((taps, 8, LANES), f32)],
        compiler_params=params,
        cost_estimate=cost(400 * MIB, 3 * MIB),
        name="taps",
    )(*[cots[step] for step in order], own, att, pre, after, before)

    copies = lax.axis_size("dp")
    part_taps = [own_taps] + [
        lax.ppermute(own_taps, "dp", [(one, (one + shift) % copies) for one in range(copies)])
        for shift in range(1, copies)
    ]

    results = pl.pallas_call(
        backward_kernel,
        out_shape=[struct((length, LANES), bf16)] * 3,
        in_specs=[vmem] * 8 + [anywhere],
        out_specs=[vmem] * 3,
        scratch_shapes=[
            VMEM((length, LANES), bf16),
            VMEM((LANES, length), f32),
            VMEM((KERNEL, LANES), f32),
            pltpu.SemaphoreType.DMA,
        ],
        compiler_params=params,
        cost_estimate=cost(800 * MIB, 3 * MIB),
        name="backward",
    )(soft, att, grad_pad, after, before, q_heads, k_t, v_full, conv_weight)

    def blocks_of(steps):
        return pl.pallas_call(
            functools.partial(block_kernel, steps, frames),
            out_shape=[struct((4 * frames + taps, LANES), bf16)] * len(steps),
            in_specs=[vmem] * (4 + copies),
            out_specs=[vmem] * len(steps),
            compiler_params=params,
            cost_estimate=cost(MIB, MIB),
            name="blocks",
        )(mixed, *results, *part_taps)

    half = ranks // 2
    far = blocks_of(list(range(half, ranks)))
    near = blocks_of(list(range(half)))
    back = {step: swap(far[step - half], step) for step in range(half, ranks)}
    back |= {step: swap(near[step], step) for step in range(1, half)}
    back[0] = near[0]

    return pl.pallas_call(
        functools.partial(spread_kernel, ranks, frames),
        out_shape=[struct(queries.shape, bf16)] * 4 + [struct(conv_weight.shape, f32)],
        in_specs=[vmem] * ranks,
        out_specs=[vmem] * 5,
        compiler_params=params,
        name="spread",
    )(*[back[step] for step in range(ranks)])


def on_device_any(queries, keys, values, cotangent, conv_weight, rec_lengths):
    ranks = lax.axis_size("seq")
    frames, channels = queries.shape[1], queries.shape[2]
    fits = channels == ranks * LANES and ranks & (ranks - 1) == 0 and frames % LANES == 0
    if fits and ranks > 1 and ranks * frames <= 1024 and lax.axis_size("dp") == 2:
        return on_device_heads(queries, keys, values, cotangent, conv_weight, rec_lengths)
    return on_device(queries, keys, values, cotangent, conv_weight, rec_lengths)


def solution(mesh):
    placed = (
        P(("groups", "dp"), "seq", "mp"),
        P(("groups", "dp"), "seq", "mp"),
        P(("groups", "dp"), "seq", "mp"),
        P(("groups", "dp"), "seq", "mp"),
        P(None, "mp"),
        P(("groups", "dp"), None),
    )
    return jax.shard_map(
        on_device_any,
        mesh=mesh,
        in_specs=placed,
        out_specs=(
            P(("groups", "dp"), "seq", "mp"),
            P(("groups", "dp"), "seq", "mp"),
            P(("groups", "dp"), "seq", "mp"),
            P(("groups", "dp"), "seq", "mp"),
            P("groups", "mp"),
        ),
        check_vma=False,
    )
```

```python
import functools
import math

import jax
import jax.numpy as jnp
from jax import lax
from jax.experimental import pallas as pl
from jax.experimental.pallas import tpu as pltpu
from jax.sharding import PartitionSpec as P

HDIM = 64
KERNEL = 31
HALF = 15


NEGATIVE_FILL = -1e30


def extended(block, sides, width):
    for axis, dim in sides:
        count = lax.axis_size(axis)
        forward = [(i, i + 1) for i in range(count - 1)]
        backward = [(target, source) for source, target in forward]
        low = lax.ppermute(
            lax.slice_in_dim(block, block.shape[dim] - width, None, axis=dim), axis, forward
        )
        high = lax.ppermute(lax.slice_in_dim(block, 0, width, axis=dim), axis, backward)
        block = jnp.concatenate([low, block, high], axis=dim)
    return block


def pick_block(total_rows):
    for candidate in (512, 256, 128):
        return candidate
    return total_rows


def over_blocks(total_rows, advance, initial):
    block_rows = pick_block(total_rows)
    block_count = total_rows // block_rows
    if block_count == 1:
        return advance(initial, 0, block_rows)
    return lax.fori_loop(
        0,
        block_count,
        lambda number, running: advance(running, number * block_rows, block_rows),
        initial,
    )


def when_shared(compute, running):
    result = compute(running)
    return result


def on_device(queries, keys, values, cotangent, conv_weight, rec_lengths):
    frames = queries.shape[1]
    channels = queries.shape[2]
    local_heads = channels // HDIM
    score_scale = 1.0 / math.sqrt(HDIM)
    length_all = frames * lax.axis_size("seq")
    offset = lax.axis_index("seq") * frames
    record_ends = jnp.cumsum(rec_lengths[0], dtype=jnp.int32)

    def segment_of(positions):
        return jnp.sum((record_ends[None, :] <= positions[:, None]).astype(jnp.int32), axis=1)

    own_seg = segment_of(offset + jnp.arange(frames, dtype=jnp.int32))

    def to_heads(array):
        return array.reshape(array.shape[0], local_heads, HDIM).transpose(1, 0, 2)

    def from_heads(array):
        return array.transpose(1, 0, 2).reshape(array.shape[1], channels)

    q_heads = to_heads(queries[0])
    k_heads = to_heads(keys[0])
    v_heads = to_heads(values[0])

    def over_rows(advance, initial, members, first_row):
        total_rows = members[0].shape[1]

        def one_block(running, block_start, block_rows):
            sliced = tuple(
                (lax.dynamic_slice_in_dim(member, block_start, block_rows, 1) for member in members)
            )
            other_seg = segment_of(
                first_row + block_start + jnp.arange(block_rows, dtype=jnp.int32)
            )
            return when_shared(lambda current: advance(current, sliced, other_seg), running)

        return over_blocks(total_rows, one_block, initial)

    def query_scores(key_block, key_seg):
        raw_scores = (
            jnp.einsum("hqd,hkd->hqk", q_heads, key_block, preferred_element_type=jnp.float32)
            * score_scale
        )
        return jnp.where((own_seg[:, None] == key_seg[None, :])[None], raw_scores, NEGATIVE_FILL)

    def stats_step(running, sliced, key_seg):
        top_now, total_now = running
        scores = query_scores(sliced[0], key_seg)
        top_new = jnp.maximum(top_now, jnp.max(scores, axis=2))
        total_new = total_now * jnp.exp(top_now - top_new) + jnp.sum(
            jnp.exp(scores - top_new[:, :, None]), axis=2
        )
        return (top_new, total_new)

    stats_init = (
        jnp.full((local_heads, frames), NEGATIVE_FILL, jnp.float32),
        jnp.zeros((local_heads, frames), jnp.float32),
    )
    gathered = (
        lax.all_gather(keys, "seq", axis=1, tiled=True),
        lax.all_gather(values, "seq", axis=1, tiled=True),
    )
    key_whole = to_heads(gathered[0][0])
    value_whole = to_heads(gathered[1][0])
    row_stats = over_rows(stats_step, stats_init, (key_whole,), 0)
    log_total = row_stats[0] + jnp.log(row_stats[1])

    def output_step(running, sliced, key_seg):
        scores = query_scores(sliced[0], key_seg)
        soft_rounded = jnp.exp(scores - log_total[:, :, None]).astype(jnp.bfloat16)
        return running + jnp.einsum(
            "hqk,hkd->hqd", soft_rounded, sliced[1], preferred_element_type=jnp.float32
        )

    frame_zeros = jnp.zeros((local_heads, frames, HDIM), jnp.float32)
    attended_sum = over_rows(output_step, frame_zeros, (key_whole, value_whole), 0)
    attended_heads = attended_sum.astype(jnp.bfloat16)
    attended = from_heads(attended_heads)
    padded = extended(attended[None], (("seq", 1),), HALF)
    padded_wide = padded[0].astype(jnp.float32)
    pad_positions = offset - HALF + jnp.arange(frames + 2 * HALF, dtype=jnp.int32)
    inside = jnp.logical_and(pad_positions >= 0, pad_positions < length_all)
    pad_seg = jnp.where(inside, segment_of(pad_positions), -1)
    conv_pre = jnp.zeros((frames, channels), jnp.float32)
    for tap_index in range(KERNEL):
        tap_mask = (pad_seg[tap_index : tap_index + frames] == own_seg)[:, None]
        conv_pre = conv_pre + jnp.where(
            tap_mask, conv_weight[tap_index] * padded_wide[tap_index : tap_index + frames], 0.0
        )
    gate_value = jax.nn.sigmoid(conv_pre)
    mixed = (conv_pre * gate_value).astype(jnp.bfloat16)
    conv_grad = (
        cotangent[0].astype(jnp.float32) * gate_value * (1.0 + conv_pre * (1.0 - gate_value))
    ).astype(jnp.bfloat16)
    padded_grad = extended(conv_grad[None], (("seq", 1),), HALF)
    grad_wide = padded_grad[0].astype(jnp.float32)
    conv_grad_wide = conv_grad.astype(jnp.float32)
    grad_attended = jnp.zeros((frames, channels), jnp.float32)
    kernel_rows = []
    for tap_index in range(KERNEL):
        back_start = 2 * HALF - tap_index
        back_mask = (pad_seg[back_start : back_start + frames] == own_seg)[:, None]
        grad_attended = grad_attended + jnp.where(
            back_mask, conv_weight[tap_index] * grad_wide[back_start : back_start + frames], 0.0
        )
        tap_mask = (pad_seg[tap_index : tap_index + frames] == own_seg)[:, None]
        product = conv_grad_wide * padded_wide[tap_index : tap_index + frames]
        kernel_rows.append(jnp.sum(jnp.where(tap_mask, product, 0.0), axis=0))
    grad_kernel = lax.psum(jnp.stack(kernel_rows), ("dp", "seq"))
    grad_attended = grad_attended.astype(jnp.bfloat16)
    g_heads = to_heads(grad_attended)
    row_delta = jnp.sum(g_heads.astype(jnp.float32) * attended_heads.astype(jnp.float32), axis=2)

    def query_grad_step(running, sliced, key_seg):
        key_block = sliced[0]
        value_block = sliced[1]
        soft_weights = jnp.exp(query_scores(key_block, key_seg) - log_total[:, :, None])
        slopes = jnp.einsum(
            "hqd,hkd->hqk", g_heads, value_block, preferred_element_type=jnp.float32
        )
        mixed_grad = (soft_weights * (slopes - row_delta[:, :, None])).astype(jnp.bfloat16)
        return running + jnp.einsum(
            "hqk,hkd->hqd", mixed_grad, key_block, preferred_element_type=jnp.float32
        )

    grad_query = over_rows(query_grad_step, frame_zeros, (key_whole, value_whole), 0)

    def key_grad_step(running, sliced, query_seg):
        grad_key_now, grad_value_now = running
        query_block = sliced[0]
        grad_block = sliced[1]
        total_block = sliced[2]
        delta_block = sliced[3]
        raw_scores = (
            jnp.einsum("hqd,hkd->hqk", query_block, k_heads, preferred_element_type=jnp.float32)
            * score_scale
        )
        scores = jnp.where(
            (query_seg[:, None] == own_seg[None, :])[None], raw_scores, NEGATIVE_FILL
        )
        soft_weights = jnp.exp(scores - total_block[:, :, None])
        grad_value_new = grad_value_now + jnp.einsum(
            "hqk,hqd->hkd",
            soft_weights.astype(jnp.bfloat16),
            grad_block,
            preferred_element_type=jnp.float32,
        )
        slopes = jnp.einsum("hqd,hkd->hqk", grad_block, v_heads, preferred_element_type=jnp.float32)
        mixed_grad = (soft_weights * (slopes - delta_block[:, :, None])).astype(jnp.bfloat16)
        grad_key_new = grad_key_now + jnp.einsum(
            "hqk,hqd->hkd", mixed_grad, query_block, preferred_element_type=jnp.float32
        )
        return (grad_key_new, grad_value_new)

    all_totals, all_deltas = (
        lax.all_gather(log_total[None], "seq", axis=2, tiled=True),
        lax.all_gather(row_delta[None], "seq", axis=2, tiled=True),
    )
    member = (
        lax.all_gather(queries, "seq", axis=1, tiled=True),
        lax.all_gather(grad_attended[None], "seq", axis=1, tiled=True),
    )
    totals_piece = all_totals[0]
    deltas_piece = all_deltas[0]
    grad_key, grad_value = over_rows(
        key_grad_step,
        (frame_zeros, frame_zeros),
        (to_heads(member[0][0]), to_heads(member[1][0]), totals_piece, deltas_piece),
        jnp.int32(0),
    )
    grad_queries = from_heads(grad_query * score_scale).astype(jnp.bfloat16)[None]
    grad_keys = from_heads(grad_key * score_scale).astype(jnp.bfloat16)[None]
    grad_values = from_heads(grad_value).astype(jnp.bfloat16)[None]
    return (mixed[None], grad_queries, grad_keys, grad_values, grad_kernel)


LANES = 128
PAD = 16
VMEM = pltpu.VMEM
MIB = 1024 * 1024


def mm(left, right):
    return lax.dot_general(
        left, right, (((1,), (0,)), ((), ())), preferred_element_type=jnp.float32
    )


def mm_nt(left, right):
    return lax.dot_general(
        left, right, (((1,), (1,)), ((), ())), preferred_element_type=jnp.float32
    )


def rows_at(block, frames):
    return pl.ds(pl.multiple_of(block * frames, frames), frames)


def lanes_at(block):
    return pl.ds(pl.multiple_of(block * LANES, LANES), LANES)


def late_order(ranks):
    middle = ranks // 2
    return [step for step in range(ranks - 1, 0, -1) if step != middle] + [middle]


def pack_kernel(ranks, q_ref, k_ref, v_ref, *rest):
    outs, sems = rest[:-1], rest[-1]
    me = lax.axis_index("seq")
    pairs = []
    for step in range(ranks - 1, 0, -1):
        for place, source in enumerate((q_ref, k_ref, v_ref)):
            pairs.append((source.at[0, :, lanes_at(me ^ step)], outs[step - 1].at[place]))
    run_copies(pairs, sems)


def run_copies(pairs, sems, meanwhile=None):
    copies = [
        pltpu.make_async_copy(source, target, sems.at[number])
        for number, (source, target) in enumerate(pairs)
    ]
    for copy in copies:
        copy.start()
    if meanwhile is not None:
        meanwhile()
    for copy in copies:
        copy.wait()


def mask_kernel(ranks, length, lens_ref, q_ref, k_ref, v_ref, c_ref, *refs):
    cot_refs = refs[: ranks - 1]
    own_ref, col_ref, row_ref, after_ref, before_ref, sems = refs[ranks - 1 :]
    me = lax.axis_index("seq")
    pairs = [(c_ref.at[0, :, lanes_at(me ^ step)], cot_refs[step - 1]) for step in range(1, ranks)]
    for place, source in enumerate((q_ref, k_ref, v_ref, c_ref)):
        pairs.append((source.at[0, :, lanes_at(me)], own_ref.at[place]))

    def extents():
        ends = []
        running = jnp.int32(0)
        for number in range(lens_ref.shape[1]):
            running = running + lens_ref[0, number]
            ends.append(running)
        row_time = lax.broadcasted_iota(jnp.int32, row_ref.shape, 1)
        row_first = jnp.zeros(row_ref.shape, jnp.int32)
        for end in ends:
            row_first = jnp.where(row_time >= end, end, row_first)
        row_ref[...] = row_first
        chunk = 64

        def some_rows(number, carry):
            base = pl.multiple_of(number * chunk, chunk)
            time = base + lax.broadcasted_iota(jnp.int32, (chunk, LANES), 0)
            first = jnp.zeros((chunk, LANES), jnp.int32)
            last = jnp.full((chunk, LANES), length, jnp.int32)
            for end in ends:
                first = jnp.where(time >= end, end, first)
            for end in reversed(ends):
                last = jnp.where(time < end, end, last)
            rows = pl.ds(base, chunk)
            col_ref[rows, :] = first
            after_ref[rows, :] = last - 1 - time
            before_ref[rows, :] = time - first
            return carry

        lax.fori_loop(0, length // chunk, some_rows, 0)

    run_copies(pairs, sems, extents)


def forward_kernel(ranks, frames, *refs):
    recvs = refs[: ranks - 1]
    own_ref, col_ref, row_ref, after_ref, before_ref, w_ref = refs[ranks - 1 : ranks + 5]
    soft_ref, att_ref, pre_ref, q_ref, k_t_ref, v_ref = refs[ranks + 5 : ranks + 11]
    att_t_ref, k_full, q_full, w_own, w_sem = refs[ranks + 11 :]
    me = lax.axis_index("seq")
    length = ranks * frames
    copy = pltpu.make_async_copy(w_ref.at[:, lanes_at(me)], w_own, w_sem)
    copy.start()
    for place, target in enumerate((q_full, k_full, v_ref)):
        target[rows_at(me, frames), :] = own_ref[place]
        for step in range(1, ranks):
            target[rows_at(me ^ step, frames), :] = recvs[ranks - 1 - step][place]
    heads = LANES // HDIM
    lane_head = lax.broadcasted_iota(jnp.int32, (1, LANES), 1) // HDIM
    scaled = q_full[...].astype(jnp.float32) * (1.0 / math.sqrt(HDIM))
    for head in range(heads):
        q_ref[head] = jnp.where(lane_head == head, scaled, 0.0).astype(jnp.bfloat16)
    k_t_ref[...] = k_full[...].astype(jnp.float32).T.astype(jnp.bfloat16)
    v_t = v_ref[...].astype(jnp.float32).T.astype(jnp.bfloat16)
    wide = 512
    for head in range(heads):
        for start in range(0, length, wide):
            cols = slice(start, start + wide)
            raw = mm_nt(k_full[...], q_ref[head, cols, :])
            same = jnp.concatenate([col_ref[...]] * (wide // LANES), axis=1) == row_ref[0:1, cols]
            scores = jnp.where(same, raw, NEGATIVE_FILL)
            top = jnp.max(scores, axis=0, keepdims=True)
            powers = jnp.exp(scores - top)
            share = 1.0 / jnp.sum(powers, axis=0, keepdims=True)
            soft = (powers * share).astype(jnp.bfloat16)
            soft_ref[head, :, cols] = soft
            rows = slice(head * HDIM, (head + 1) * HDIM)
            att_t_ref[rows, cols] = mm(v_t[rows], soft).astype(jnp.bfloat16).astype(jnp.float32)
    zeros = jnp.zeros((PAD, LANES), jnp.float32)
    att_ref[0:PAD, :] = zeros
    att_ref[PAD : PAD + length, :] = att_t_ref[...].T
    att_ref[PAD + length :, :] = zeros
    copy.wait()

    chunk = 64

    def some_rows(number, carry):
        base = pl.multiple_of(number * chunk, chunk)
        rows = pl.ds(base, chunk)
        after, before = after_ref[rows, :], before_ref[rows, :]
        total = jnp.zeros((chunk, LANES), jnp.float32)
        for tap in range(KERNEL):
            off = tap - HALF
            piece = att_ref[pl.ds(base + (PAD + off), chunk), :]
            if off > 0:
                piece = jnp.where(after >= off, piece, 0.0)
            if off < 0:
                piece = jnp.where(before >= -off, piece, 0.0)
            total = total + w_own[tap : tap + 1, :] * piece
        pre_ref[rows, :] = total
        return carry

    lax.fori_loop(0, length // chunk, some_rows, 0)


def masked(source, base, chunk, off, before, after):
    piece = source[pl.ds(base + (PAD + off), chunk), :]
    if off > 0:
        piece = jnp.where(after >= off, piece, 0.0)
    if off < 0:
        piece = jnp.where(before >= -off, piece, 0.0)
    return piece


def taps_kernel(ranks, frames, *refs):
    cots = dict(zip(late_order(ranks), refs))
    own_ref, att_ref, pre_ref, after_ref, before_ref = refs[ranks - 1 : ranks + 4]
    mixed_ref, grad_pad, taps_ref, cot, tap_sum = refs[ranks + 4 :]
    me = lax.axis_index("seq")
    length = ranks * frames
    cot[rows_at(me, frames), :] = own_ref[3]
    for step in range(1, ranks):
        cot[rows_at(me ^ step, frames), :] = cots[step][...]
    zeros = jnp.zeros((PAD, LANES), jnp.float32)
    grad_pad[0:PAD, :] = zeros
    grad_pad[PAD + length :, :] = zeros
    tap_sum[...] = jnp.zeros(tap_sum.shape, jnp.float32)
    chunk = 64

    def some_rows(number, carry):
        base = pl.multiple_of(number * chunk, chunk)
        rows = pl.ds(base, chunk)
        pre = pre_ref[rows, :]
        gate = jax.nn.sigmoid(pre)
        mixed_ref[rows, :] = (pre * gate).astype(jnp.bfloat16)
        conv_grad = cot[rows, :].astype(jnp.float32) * gate * (1.0 + pre * (1.0 - gate))
        conv_grad = conv_grad.astype(jnp.bfloat16).astype(jnp.float32)
        grad_pad[pl.ds(base + PAD, chunk), :] = conv_grad
        after, before = after_ref[rows, :], before_ref[rows, :]
        for tap in range(KERNEL):
            part = conv_grad * masked(att_ref, base, chunk, tap - HALF, before, after)
            tap_sum[tap] = tap_sum[tap] + jnp.sum(part.reshape(chunk // 8, 8, LANES), axis=0)
        return carry

    lax.fori_loop(0, length // chunk, some_rows, 0)
    taps_ref[...] = jnp.sum(tap_sum[...], axis=1)


def backward_kernel(soft_ref, att_ref, grad_pad, after_ref, before_ref, q_ref, k_t_ref, v_ref, w_ref, *refs):
    res_q, res_k, res_v, g_att, grad_t, w_own, w_sem = refs
    length = v_ref.shape[0]
    copy = pltpu.make_async_copy(w_ref.at[:, lanes_at(lax.axis_index("seq"))], w_own, w_sem)
    copy.start()
    copy.wait()
    chunk = 64

    def some_rows(number, carry):
        base = pl.multiple_of(number * chunk, chunk)
        rows = pl.ds(base, chunk)
        after, before = after_ref[rows, :], before_ref[rows, :]
        total = jnp.zeros((chunk, LANES), jnp.float32)
        for tap in range(KERNEL):
            total = total + w_own[tap : tap + 1, :] * masked(grad_pad, base, chunk, HALF - tap, before, after)
        g_att[rows, :] = total.astype(jnp.bfloat16)
        return carry

    lax.fori_loop(0, length // chunk, some_rows, 0)
    heads = LANES // HDIM
    lane_head = lax.broadcasted_iota(jnp.int32, (1, LANES), 1) // HDIM
    g_wide = g_att[...].astype(jnp.float32)
    products_t = (g_wide * att_ref[PAD : PAD + length, :]).T
    grad_v = jnp.zeros((length, LANES), jnp.float32)
    grad_k = jnp.zeros((length, LANES), jnp.float32)
    for head in range(heads):
        rows = slice(head * HDIM, (head + 1) * HDIM)
        g_head = jnp.where(lane_head == head, g_wide, 0.0).astype(jnp.bfloat16)
        delta = jnp.sum(products_t[rows], axis=0, keepdims=True)
        soft = soft_ref[head]
        slopes = mm_nt(v_ref[...], g_head)
        mixed_grad = (soft.astype(jnp.float32) * (slopes - delta)).astype(jnp.bfloat16)
        grad_v = grad_v + mm(soft, g_head)
        grad_k = grad_k + mm(mixed_grad, q_ref[head])
        grad_t[rows, :] = mm(k_t_ref[rows, :], mixed_grad) * (1.0 / math.sqrt(HDIM))
    res_k[...] = grad_k.astype(jnp.bfloat16)
    res_v[...] = grad_v.astype(jnp.bfloat16)
    res_q[...] = grad_t[...].T.astype(jnp.bfloat16)


def block_kernel(steps, frames, *refs):
    sources, tap_refs, outs = refs[:4], refs[4 : -len(steps)], refs[-len(steps) :]
    me = lax.axis_index("seq")
    taps = tap_refs[0][...]
    for other in tap_refs[1:]:
        taps = taps + other[...]
    for step, out in zip(steps, outs):
        rows = rows_at(me ^ step, frames)
        for place, source in enumerate(sources):
            out[place * frames : (place + 1) * frames, :] = source[rows, :]
        out[4 * frames :, :] = taps.astype(jnp.bfloat16)


def spread_kernel(ranks, frames, *refs):
    blocks = refs[:ranks]
    targets, taps_ref = refs[ranks : ranks + 4], refs[ranks + 4]
    me = lax.axis_index("seq")
    for step in range(ranks):
        lanes = lanes_at(me ^ step)
        for place, target in enumerate(targets):
            target[0, :, lanes] = blocks[step][place * frames : (place + 1) * frames, :]
        taps = blocks[step][4 * frames :, :].astype(jnp.float32)
        taps_ref[:, lanes] = taps[:KERNEL]


def cost(flops, moved):
    return pl.CostEstimate(flops=flops, bytes_accessed=moved, transcendentals=0)


def on_device_heads(queries, keys, values, cotangent, conv_weight, rec_lengths):
    ranks = lax.axis_size("seq")
    frames = queries.shape[1]
    length = ranks * frames
    heads = LANES // HDIM
    bf16, f32, i32 = jnp.bfloat16, jnp.float32, jnp.int32
    struct = jax.ShapeDtypeStruct
    hbm = pl.BlockSpec(memory_space=pltpu.HBM)
    anywhere = pl.BlockSpec(memory_space=pl.ANY)
    vmem = pl.BlockSpec(memory_space=VMEM)
    smem = pl.BlockSpec(memory_space=pltpu.SMEM)
    params = pltpu.CompilerParams(vmem_limit_bytes=24 * MIB)
    taps = KERNEL + 1

    sends = pl.pallas_call(
        functools.partial(pack_kernel, ranks),
        out_shape=[struct((3, frames, LANES), bf16)] * (ranks - 1),
        in_specs=[hbm] * 3,
        out_specs=[vmem] * (ranks - 1),
        scratch_shapes=[pltpu.SemaphoreType.DMA((3 * (ranks - 1),))],
        compiler_params=pltpu.CompilerParams(vmem_limit_bytes=54912 * 1024),
        name="pack",
    )(queries, keys, values)

    def swap(array, step):
        return lax.ppermute(array, "seq", [(rank, rank ^ step) for rank in range(ranks)])

    order = list(range(ranks - 1, 0, -1))
    received = {step: swap(sends[step - 1], step) for step in order}

    *cot_sends, own, col, row, after, before = pl.pallas_call(
        functools.partial(mask_kernel, ranks, length),
        out_shape=[struct((frames, LANES), bf16)] * (ranks - 1)
        + [
            struct((4, frames, LANES), bf16),
            struct((length, LANES), i32),
            struct((8, length), i32),
            struct((length, LANES), i32),
            struct((length, LANES), i32),
        ],
        in_specs=[smem] + [hbm] * 4,
        out_specs=[vmem] * (ranks + 4),
        scratch_shapes=[pltpu.SemaphoreType.DMA((ranks + 3,))],
        compiler_params=params,
        cost_estimate=cost(4 * MIB, MIB),
        name="masks",
    )(rec_lengths, queries, keys, values, cotangent)
    cots = {step: swap(cot_sends[step - 1], step) for step in order}

    soft, att, pre, q_heads, k_t, v_full = pl.pallas_call(
        functools.partial(forward_kernel, ranks, frames),
        out_shape=[
            struct((heads, length, length), bf16),
            struct((length + 2 * PAD, LANES), f32),
            struct((length, LANES), f32),
            struct((heads, length, LANES), bf16),
            struct((LANES, length), bf16),
            struct((length, LANES), bf16),
        ],
        in_specs=[vmem] * (ranks + 4) + [anywhere],
        out_specs=[vmem] * 6,
        scratch_shapes=[
            VMEM((LANES, length), f32),
            VMEM((length, LANES), bf16),
            VMEM((length, LANES), bf16),
            VMEM((KERNEL, LANES), f32),
            pltpu.SemaphoreType.DMA,
        ],
        compiler_params=params,
        cost_estimate=cost(400 * MIB, 3 * MIB),
        name="forward",
    )(*[received[step] for step in order], own, col, row, after, before, conv_weight)

    mixed, grad_pad, own_taps = pl.pallas_call(
        functools.partial(taps_kernel, ranks, frames),
        out_shape=[
            struct((length, LANES), bf16),
            struct((length + 2 * PAD, LANES), f32),
            struct((taps, LANES), f32),
        ],
        in_specs=[vmem] * (ranks + 4),
        out_specs=[vmem] * 3,
        scratch_shapes=[VMEM((length, LANES), bf16), VMEM((taps, 8, LANES), f32)],
        compiler_params=params,
        cost_estimate=cost(400 * MIB, 3 * MIB),
        name="taps",
    )(*[cots[step] for step in late_order(ranks)], own, att, pre, after, before)

    copies = lax.axis_size("dp")
    part_taps = [own_taps] + [
        lax.ppermute(own_taps, "dp", [(one, (one + shift) % copies) for one in range(copies)])
        for shift in range(1, copies)
    ]

    results = pl.pallas_call(
        backward_kernel,
        out_shape=[struct((length, LANES), bf16)] * 3,
        in_specs=[vmem] * 8 + [anywhere],
        out_specs=[vmem] * 3,
        scratch_shapes=[
            VMEM((length, LANES), bf16),
            VMEM((LANES, length), f32),
            VMEM((KERNEL, LANES), f32),
            pltpu.SemaphoreType.DMA,
        ],
        compiler_params=params,
        cost_estimate=cost(800 * MIB, 3 * MIB),
        name="backward",
    )(soft, att, grad_pad, after, before, q_heads, k_t, v_full, conv_weight)

    def blocks_of(steps):
        return pl.pallas_call(
            functools.partial(block_kernel, steps, frames),
            out_shape=[struct((4 * frames + taps, LANES), bf16)] * len(steps),
            in_specs=[vmem] * (4 + copies),
            out_specs=[vmem] * len(steps),
            compiler_params=params,
            cost_estimate=cost(MIB, MIB),
            name="blocks",
        )(mixed, *results, *part_taps)

    half = ranks // 2
    far = blocks_of(list(range(half, ranks)))
    near = blocks_of(list(range(half)))
    back = {step: swap(far[step - half], step) for step in range(half, ranks)}
    back |= {step: swap(near[step], step) for step in range(1, half)}
    back[0] = near[0]

    return pl.pallas_call(
        functools.partial(spread_kernel, ranks, frames),
        out_shape=[struct(queries.shape, bf16)] * 4 + [struct(conv_weight.shape, f32)],
        in_specs=[vmem] * ranks,
        out_specs=[vmem] * 5,
        compiler_params=params,
        name="spread",
    )(*[back[step] for step in range(ranks)])


def on_device_any(queries, keys, values, cotangent, conv_weight, rec_lengths):
    ranks = lax.axis_size("seq")
    frames, channels = queries.shape[1], queries.shape[2]
    fits = channels == ranks * LANES and ranks & (ranks - 1) == 0 and frames % LANES == 0
    if fits and ranks > 1 and ranks * frames <= 1024 and lax.axis_size("dp") == 2:
        return on_device_heads(queries, keys, values, cotangent, conv_weight, rec_lengths)
    return on_device(queries, keys, values, cotangent, conv_weight, rec_lengths)


def solution(mesh):
    placed = (
        P(("groups", "dp"), "seq", "mp"),
        P(("groups", "dp"), "seq", "mp"),
        P(("groups", "dp"), "seq", "mp"),
        P(("groups", "dp"), "seq", "mp"),
        P(None, "mp"),
        P(("groups", "dp"), None),
    )
    return jax.shard_map(
        on_device_any,
        mesh=mesh,
        in_specs=placed,
        out_specs=(
            P(("groups", "dp"), "seq", "mp"),
            P(("groups", "dp"), "seq", "mp"),
            P(("groups", "dp"), "seq", "mp"),
            P(("groups", "dp"), "seq", "mp"),
            P("groups", "mp"),
        ),
        check_vma=False,
    )
```

```python
import functools
import math

import jax
import jax.numpy as jnp
from jax import lax
from jax.experimental import pallas as pl
from jax.experimental.pallas import tpu as pltpu
from jax.sharding import PartitionSpec as P

HDIM = 64
KERNEL = 31
HALF = 15


NEGATIVE_FILL = -1e30


def extended(block, sides, width):
    for axis, dim in sides:
        count = lax.axis_size(axis)
        forward = [(i, i + 1) for i in range(count - 1)]
        backward = [(target, source) for source, target in forward]
        low = lax.ppermute(
            lax.slice_in_dim(block, block.shape[dim] - width, None, axis=dim), axis, forward
        )
        high = lax.ppermute(lax.slice_in_dim(block, 0, width, axis=dim), axis, backward)
        block = jnp.concatenate([low, block, high], axis=dim)
    return block


def pick_block(total_rows):
    for candidate in (512, 256, 128):
        return candidate
    return total_rows


def over_blocks(total_rows, advance, initial):
    block_rows = pick_block(total_rows)
    block_count = total_rows // block_rows
    if block_count == 1:
        return advance(initial, 0, block_rows)
    return lax.fori_loop(
        0,
        block_count,
        lambda number, running: advance(running, number * block_rows, block_rows),
        initial,
    )


def when_shared(compute, running):
    result = compute(running)
    return result


def on_device(queries, keys, values, cotangent, conv_weight, rec_lengths):
    frames = queries.shape[1]
    channels = queries.shape[2]
    local_heads = channels // HDIM
    score_scale = 1.0 / math.sqrt(HDIM)
    length_all = frames * lax.axis_size("seq")
    offset = lax.axis_index("seq") * frames
    record_ends = jnp.cumsum(rec_lengths[0], dtype=jnp.int32)

    def segment_of(positions):
        return jnp.sum((record_ends[None, :] <= positions[:, None]).astype(jnp.int32), axis=1)

    own_seg = segment_of(offset + jnp.arange(frames, dtype=jnp.int32))

    def to_heads(array):
        return array.reshape(array.shape[0], local_heads, HDIM).transpose(1, 0, 2)

    def from_heads(array):
        return array.transpose(1, 0, 2).reshape(array.shape[1], channels)

    q_heads = to_heads(queries[0])
    k_heads = to_heads(keys[0])
    v_heads = to_heads(values[0])

    def over_rows(advance, initial, members, first_row):
        total_rows = members[0].shape[1]

        def one_block(running, block_start, block_rows):
            sliced = tuple(
                (lax.dynamic_slice_in_dim(member, block_start, block_rows, 1) for member in members)
            )
            other_seg = segment_of(
                first_row + block_start + jnp.arange(block_rows, dtype=jnp.int32)
            )
            return when_shared(lambda current: advance(current, sliced, other_seg), running)

        return over_blocks(total_rows, one_block, initial)

    def query_scores(key_block, key_seg):
        raw_scores = (
            jnp.einsum("hqd,hkd->hqk", q_heads, key_block, preferred_element_type=jnp.float32)
            * score_scale
        )
        return jnp.where((own_seg[:, None] == key_seg[None, :])[None], raw_scores, NEGATIVE_FILL)

    def stats_step(running, sliced, key_seg):
        top_now, total_now = running
        scores = query_scores(sliced[0], key_seg)
        top_new = jnp.maximum(top_now, jnp.max(scores, axis=2))
        total_new = total_now * jnp.exp(top_now - top_new) + jnp.sum(
            jnp.exp(scores - top_new[:, :, None]), axis=2
        )
        return (top_new, total_new)

    stats_init = (
        jnp.full((local_heads, frames), NEGATIVE_FILL, jnp.float32),
        jnp.zeros((local_heads, frames), jnp.float32),
    )
    gathered = (
        lax.all_gather(keys, "seq", axis=1, tiled=True),
        lax.all_gather(values, "seq", axis=1, tiled=True),
    )
    key_whole = to_heads(gathered[0][0])
    value_whole = to_heads(gathered[1][0])
    row_stats = over_rows(stats_step, stats_init, (key_whole,), 0)
    log_total = row_stats[0] + jnp.log(row_stats[1])

    def output_step(running, sliced, key_seg):
        scores = query_scores(sliced[0], key_seg)
        soft_rounded = jnp.exp(scores - log_total[:, :, None]).astype(jnp.bfloat16)
        return running + jnp.einsum(
            "hqk,hkd->hqd", soft_rounded, sliced[1], preferred_element_type=jnp.float32
        )

    frame_zeros = jnp.zeros((local_heads, frames, HDIM), jnp.float32)
    attended_sum = over_rows(output_step, frame_zeros, (key_whole, value_whole), 0)
    attended_heads = attended_sum.astype(jnp.bfloat16)
    attended = from_heads(attended_heads)
    padded = extended(attended[None], (("seq", 1),), HALF)
    padded_wide = padded[0].astype(jnp.float32)
    pad_positions = offset - HALF + jnp.arange(frames + 2 * HALF, dtype=jnp.int32)
    inside = jnp.logical_and(pad_positions >= 0, pad_positions < length_all)
    pad_seg = jnp.where(inside, segment_of(pad_positions), -1)
    conv_pre = jnp.zeros((frames, channels), jnp.float32)
    for tap_index in range(KERNEL):
        tap_mask = (pad_seg[tap_index : tap_index + frames] == own_seg)[:, None]
        conv_pre = conv_pre + jnp.where(
            tap_mask, conv_weight[tap_index] * padded_wide[tap_index : tap_index + frames], 0.0
        )
    gate_value = jax.nn.sigmoid(conv_pre)
    mixed = (conv_pre * gate_value).astype(jnp.bfloat16)
    conv_grad = (
        cotangent[0].astype(jnp.float32) * gate_value * (1.0 + conv_pre * (1.0 - gate_value))
    ).astype(jnp.bfloat16)
    padded_grad = extended(conv_grad[None], (("seq", 1),), HALF)
    grad_wide = padded_grad[0].astype(jnp.float32)
    conv_grad_wide = conv_grad.astype(jnp.float32)
    grad_attended = jnp.zeros((frames, channels), jnp.float32)
    kernel_rows = []
    for tap_index in range(KERNEL):
        back_start = 2 * HALF - tap_index
        back_mask = (pad_seg[back_start : back_start + frames] == own_seg)[:, None]
        grad_attended = grad_attended + jnp.where(
            back_mask, conv_weight[tap_index] * grad_wide[back_start : back_start + frames], 0.0
        )
        tap_mask = (pad_seg[tap_index : tap_index + frames] == own_seg)[:, None]
        product = conv_grad_wide * padded_wide[tap_index : tap_index + frames]
        kernel_rows.append(jnp.sum(jnp.where(tap_mask, product, 0.0), axis=0))
    grad_kernel = lax.psum(jnp.stack(kernel_rows), ("dp", "seq"))
    grad_attended = grad_attended.astype(jnp.bfloat16)
    g_heads = to_heads(grad_attended)
    row_delta = jnp.sum(g_heads.astype(jnp.float32) * attended_heads.astype(jnp.float32), axis=2)

    def query_grad_step(running, sliced, key_seg):
        key_block = sliced[0]
        value_block = sliced[1]
        soft_weights = jnp.exp(query_scores(key_block, key_seg) - log_total[:, :, None])
        slopes = jnp.einsum(
            "hqd,hkd->hqk", g_heads, value_block, preferred_element_type=jnp.float32
        )
        mixed_grad = (soft_weights * (slopes - row_delta[:, :, None])).astype(jnp.bfloat16)
        return running + jnp.einsum(
            "hqk,hkd->hqd", mixed_grad, key_block, preferred_element_type=jnp.float32
        )

    grad_query = over_rows(query_grad_step, frame_zeros, (key_whole, value_whole), 0)

    def key_grad_step(running, sliced, query_seg):
        grad_key_now, grad_value_now = running
        query_block = sliced[0]
        grad_block = sliced[1]
        total_block = sliced[2]
        delta_block = sliced[3]
        raw_scores = (
            jnp.einsum("hqd,hkd->hqk", query_block, k_heads, preferred_element_type=jnp.float32)
            * score_scale
        )
        scores = jnp.where(
            (query_seg[:, None] == own_seg[None, :])[None], raw_scores, NEGATIVE_FILL
        )
        soft_weights = jnp.exp(scores - total_block[:, :, None])
        grad_value_new = grad_value_now + jnp.einsum(
            "hqk,hqd->hkd",
            soft_weights.astype(jnp.bfloat16),
            grad_block,
            preferred_element_type=jnp.float32,
        )
        slopes = jnp.einsum("hqd,hkd->hqk", grad_block, v_heads, preferred_element_type=jnp.float32)
        mixed_grad = (soft_weights * (slopes - delta_block[:, :, None])).astype(jnp.bfloat16)
        grad_key_new = grad_key_now + jnp.einsum(
            "hqk,hqd->hkd", mixed_grad, query_block, preferred_element_type=jnp.float32
        )
        return (grad_key_new, grad_value_new)

    all_totals, all_deltas = (
        lax.all_gather(log_total[None], "seq", axis=2, tiled=True),
        lax.all_gather(row_delta[None], "seq", axis=2, tiled=True),
    )
    member = (
        lax.all_gather(queries, "seq", axis=1, tiled=True),
        lax.all_gather(grad_attended[None], "seq", axis=1, tiled=True),
    )
    totals_piece = all_totals[0]
    deltas_piece = all_deltas[0]
    grad_key, grad_value = over_rows(
        key_grad_step,
        (frame_zeros, frame_zeros),
        (to_heads(member[0][0]), to_heads(member[1][0]), totals_piece, deltas_piece),
        jnp.int32(0),
    )
    grad_queries = from_heads(grad_query * score_scale).astype(jnp.bfloat16)[None]
    grad_keys = from_heads(grad_key * score_scale).astype(jnp.bfloat16)[None]
    grad_values = from_heads(grad_value).astype(jnp.bfloat16)[None]
    return (mixed[None], grad_queries, grad_keys, grad_values, grad_kernel)


LANES = 128
PAD = 16
VMEM = pltpu.VMEM
MIB = 1024 * 1024


def mm(left, right):
    return lax.dot_general(
        left, right, (((1,), (0,)), ((), ())), preferred_element_type=jnp.float32
    )


def mm_nt(left, right):
    return lax.dot_general(
        left, right, (((1,), (1,)), ((), ())), preferred_element_type=jnp.float32
    )


def rows_at(block, frames):
    return pl.ds(pl.multiple_of(block * frames, frames), frames)


def lanes_at(block):
    return pl.ds(pl.multiple_of(block * LANES, LANES), LANES)


def turns(ranks):
    middle = ranks // 2
    even = [middle] + [step for step in range(ranks - 1, 0, -1) if step != middle]
    return list(zip(even, even[1:] + even[:1]))


def step_of(turn):
    even, odd = turn
    return jnp.where(lax.axis_index("mp") % 2 == 0, even, odd)


def pack_kernel(ranks, q_ref, k_ref, v_ref, *rest):
    outs, sems = rest[:-1], rest[-1]
    me = lax.axis_index("seq")
    pairs = []
    for step in range(ranks - 1, 0, -1):
        for place, source in enumerate((q_ref, k_ref, v_ref)):
            pairs.append((source.at[0, :, lanes_at(me ^ step)], outs[step - 1].at[place]))
    run_copies(pairs, sems)


def run_copies(pairs, sems, meanwhile=None):
    copies = [
        pltpu.make_async_copy(source, target, sems.at[number])
        for number, (source, target) in enumerate(pairs)
    ]
    for copy in copies:
        copy.start()
    if meanwhile is not None:
        meanwhile()
    for copy in copies:
        copy.wait()


def mask_kernel(ranks, length, lens_ref, q_ref, k_ref, v_ref, c_ref, *refs):
    cot_refs = refs[: ranks - 1]
    own_ref, col_ref, row_ref, after_ref, before_ref, sems = refs[ranks - 1 :]
    me = lax.axis_index("seq")
    pairs = [(c_ref.at[0, :, lanes_at(me ^ step)], cot_refs[step - 1]) for step in range(1, ranks)]
    for place, source in enumerate((q_ref, k_ref, v_ref, c_ref)):
        pairs.append((source.at[0, :, lanes_at(me)], own_ref.at[place]))

    def extents():
        ends = []
        running = jnp.int32(0)
        for number in range(lens_ref.shape[1]):
            running = running + lens_ref[0, number]
            ends.append(running)
        row_time = lax.broadcasted_iota(jnp.int32, row_ref.shape, 1)
        row_first = jnp.zeros(row_ref.shape, jnp.int32)
        for end in ends:
            row_first = jnp.where(row_time >= end, end, row_first)
        row_ref[...] = row_first
        chunk = 64

        def some_rows(number, carry):
            base = pl.multiple_of(number * chunk, chunk)
            time = base + lax.broadcasted_iota(jnp.int32, (chunk, LANES), 0)
            first = jnp.zeros((chunk, LANES), jnp.int32)
            last = jnp.full((chunk, LANES), length, jnp.int32)
            for end in ends:
                first = jnp.where(time >= end, end, first)
            for end in reversed(ends):
                last = jnp.where(time < end, end, last)
            rows = pl.ds(base, chunk)
            col_ref[rows, :] = first
            after_ref[rows, :] = last - 1 - time
            before_ref[rows, :] = time - first
            return carry

        lax.fori_loop(0, length // chunk, some_rows, 0)

    run_copies(pairs, sems, extents)


def forward_kernel(ranks, frames, *refs):
    recvs = refs[: ranks - 1]
    own_ref, col_ref, row_ref, after_ref, before_ref, w_ref = refs[ranks - 1 : ranks + 5]
    soft_ref, att_ref, pre_ref, q_ref, k_t_ref, v_ref = refs[ranks + 5 : ranks + 11]
    att_t_ref, k_full, q_full, w_own, w_sem = refs[ranks + 11 :]
    me = lax.axis_index("seq")
    length = ranks * frames
    copy = pltpu.make_async_copy(w_ref.at[:, lanes_at(me)], w_own, w_sem)
    copy.start()
    for place, target in enumerate((q_full, k_full, v_ref)):
        target[rows_at(me, frames), :] = own_ref[place]
        for step in range(1, ranks):
            target[rows_at(me ^ step, frames), :] = recvs[ranks - 1 - step][place]
    heads = LANES // HDIM
    lane_head = lax.broadcasted_iota(jnp.int32, (1, LANES), 1) // HDIM
    scaled = q_full[...].astype(jnp.float32) * (1.0 / math.sqrt(HDIM))
    for head in range(heads):
        q_ref[head] = jnp.where(lane_head == head, scaled, 0.0).astype(jnp.bfloat16)
    k_t_ref[...] = k_full[...].astype(jnp.float32).T.astype(jnp.bfloat16)
    v_t = v_ref[...].astype(jnp.float32).T.astype(jnp.bfloat16)
    wide = 512
    for head in range(heads):
        for start in range(0, length, wide):
            cols = slice(start, start + wide)
            raw = mm_nt(k_full[...], q_ref[head, cols, :])
            same = jnp.concatenate([col_ref[...]] * (wide // LANES), axis=1) == row_ref[0:1, cols]
            scores = jnp.where(same, raw, NEGATIVE_FILL)
            top = jnp.max(scores, axis=0, keepdims=True)
            powers = jnp.exp(scores - top)
            share = 1.0 / jnp.sum(powers, axis=0, keepdims=True)
            soft = (powers * share).astype(jnp.bfloat16)
            soft_ref[head, :, cols] = soft
            rows = slice(head * HDIM, (head + 1) * HDIM)
            att_t_ref[rows, cols] = mm(v_t[rows], soft).astype(jnp.bfloat16).astype(jnp.float32)
    zeros = jnp.zeros((PAD, LANES), jnp.float32)
    att_ref[0:PAD, :] = zeros
    att_ref[PAD : PAD + length, :] = att_t_ref[...].T
    att_ref[PAD + length :, :] = zeros
    copy.wait()

    chunk = 64

    def some_rows(number, carry):
        base = pl.multiple_of(number * chunk, chunk)
        rows = pl.ds(base, chunk)
        after, before = after_ref[rows, :], before_ref[rows, :]
        total = jnp.zeros((chunk, LANES), jnp.float32)
        for tap in range(KERNEL):
            off = tap - HALF
            piece = att_ref[pl.ds(base + (PAD + off), chunk), :]
            if off > 0:
                piece = jnp.where(after >= off, piece, 0.0)
            if off < 0:
                piece = jnp.where(before >= -off, piece, 0.0)
            total = total + w_own[tap : tap + 1, :] * piece
        pre_ref[rows, :] = total
        return carry

    lax.fori_loop(0, length // chunk, some_rows, 0)


def masked(source, base, chunk, off, before, after):
    piece = source[pl.ds(base + (PAD + off), chunk), :]
    if off > 0:
        piece = jnp.where(after >= off, piece, 0.0)
    if off < 0:
        piece = jnp.where(before >= -off, piece, 0.0)
    return piece


def taps_kernel(ranks, frames, *refs):
    cots = refs[: ranks - 1]
    own_ref, att_ref, pre_ref, after_ref, before_ref = refs[ranks - 1 : ranks + 4]
    mixed_ref, grad_pad, taps_ref, cot, tap_sum = refs[ranks + 4 :]
    me = lax.axis_index("seq")
    length = ranks * frames
    cot[rows_at(me, frames), :] = own_ref[3]
    for step in range(1, ranks):
        cot[rows_at(me ^ step, frames), :] = cots[ranks - 1 - step][...]
    zeros = jnp.zeros((PAD, LANES), jnp.float32)
    grad_pad[0:PAD, :] = zeros
    grad_pad[PAD + length :, :] = zeros
    tap_sum[...] = jnp.zeros(tap_sum.shape, jnp.float32)
    chunk = 64

    def some_rows(number, carry):
        base = pl.multiple_of(number * chunk, chunk)
        rows = pl.ds(base, chunk)
        pre = pre_ref[rows, :]
        gate = jax.nn.sigmoid(pre)
        mixed_ref[rows, :] = (pre * gate).astype(jnp.bfloat16)
        conv_grad = cot[rows, :].astype(jnp.float32) * gate * (1.0 + pre * (1.0 - gate))
        conv_grad = conv_grad.astype(jnp.bfloat16).astype(jnp.float32)
        grad_pad[pl.ds(base + PAD, chunk), :] = conv_grad
        after, before = after_ref[rows, :], before_ref[rows, :]
        for tap in range(KERNEL):
            part = conv_grad * masked(att_ref, base, chunk, tap - HALF, before, after)
            tap_sum[tap] = tap_sum[tap] + jnp.sum(part.reshape(chunk // 8, 8, LANES), axis=0)
        return carry

    lax.fori_loop(0, length // chunk, some_rows, 0)
    taps_ref[...] = jnp.sum(tap_sum[...], axis=1)


def backward_kernel(soft_ref, att_ref, grad_pad, after_ref, before_ref, q_ref, k_t_ref, v_ref, w_ref, *refs):
    res_q, res_k, res_v, g_att, grad_t, w_own, w_sem = refs
    length = v_ref.shape[0]
    copy = pltpu.make_async_copy(w_ref.at[:, lanes_at(lax.axis_index("seq"))], w_own, w_sem)
    copy.start()
    copy.wait()
    chunk = 64

    def some_rows(number, carry):
        base = pl.multiple_of(number * chunk, chunk)
        rows = pl.ds(base, chunk)
        after, before = after_ref[rows, :], before_ref[rows, :]
        total = jnp.zeros((chunk, LANES), jnp.float32)
        for tap in range(KERNEL):
            total = total + w_own[tap : tap + 1, :] * masked(grad_pad, base, chunk, HALF - tap, before, after)
        g_att[rows, :] = total.astype(jnp.bfloat16)
        return carry

    lax.fori_loop(0, length // chunk, some_rows, 0)
    heads = LANES // HDIM
    lane_head = lax.broadcasted_iota(jnp.int32, (1, LANES), 1) // HDIM
    g_wide = g_att[...].astype(jnp.float32)
    products_t = (g_wide * att_ref[PAD : PAD + length, :]).T
    grad_v = jnp.zeros((length, LANES), jnp.float32)
    grad_k = jnp.zeros((length, LANES), jnp.float32)
    for head in range(heads):
        rows = slice(head * HDIM, (head + 1) * HDIM)
        g_head = jnp.where(lane_head == head, g_wide, 0.0).astype(jnp.bfloat16)
        delta = jnp.sum(products_t[rows], axis=0, keepdims=True)
        soft = soft_ref[head]
        slopes = mm_nt(v_ref[...], g_head)
        mixed_grad = (soft.astype(jnp.float32) * (slopes - delta)).astype(jnp.bfloat16)
        grad_v = grad_v + mm(soft, g_head)
        grad_k = grad_k + mm(mixed_grad, q_ref[head])
        grad_t[rows, :] = mm(k_t_ref[rows, :], mixed_grad) * (1.0 / math.sqrt(HDIM))
    res_k[...] = grad_k.astype(jnp.bfloat16)
    res_v[...] = grad_v.astype(jnp.bfloat16)
    res_q[...] = grad_t[...].T.astype(jnp.bfloat16)


def block_kernel(steps, frames, *refs):
    sources, tap_refs, outs = refs[:4], refs[4 : -len(steps)], refs[-len(steps) :]
    me = lax.axis_index("seq")
    taps = tap_refs[0][...]
    for other in tap_refs[1:]:
        taps = taps + other[...]
    for turn, out in zip(steps, outs):
        rows = rows_at(me ^ step_of(turn), frames)
        for place, source in enumerate(sources):
            out[place * frames : (place + 1) * frames, :] = source[rows, :]
        out[4 * frames :, :] = taps.astype(jnp.bfloat16)


def spread_kernel(steps, frames, *refs):
    ranks = len(steps)
    blocks = refs[:ranks]
    targets, taps_ref = refs[ranks : ranks + 4], refs[ranks + 4]
    me = lax.axis_index("seq")
    for turn, block in zip(steps, blocks):
        lanes = lanes_at(me ^ step_of(turn))
        for place, target in enumerate(targets):
            target[0, :, lanes] = block[place * frames : (place + 1) * frames, :]
        taps = block[4 * frames :, :].astype(jnp.float32)
        taps_ref[:, lanes] = taps[:KERNEL]


def cost(flops, moved):
    return pl.CostEstimate(flops=flops, bytes_accessed=moved, transcendentals=0)


def on_device_heads(queries, keys, values, cotangent, conv_weight, rec_lengths):
    ranks = lax.axis_size("seq")
    frames = queries.shape[1]
    length = ranks * frames
    heads = LANES // HDIM
    bf16, f32, i32 = jnp.bfloat16, jnp.float32, jnp.int32
    struct = jax.ShapeDtypeStruct
    hbm = pl.BlockSpec(memory_space=pltpu.HBM)
    anywhere = pl.BlockSpec(memory_space=pl.ANY)
    vmem = pl.BlockSpec(memory_space=VMEM)
    smem = pl.BlockSpec(memory_space=pltpu.SMEM)
    params = pltpu.CompilerParams(vmem_limit_bytes=24 * MIB)
    taps = KERNEL + 1

    sends = pl.pallas_call(
        functools.partial(pack_kernel, ranks),
        out_shape=[struct((3, frames, LANES), bf16)] * (ranks - 1),
        in_specs=[hbm] * 3,
        out_specs=[vmem] * (ranks - 1),
        scratch_shapes=[pltpu.SemaphoreType.DMA((3 * (ranks - 1),))],
        compiler_params=pltpu.CompilerParams(vmem_limit_bytes=54912 * 1024),
        name="pack",
    )(queries, keys, values)

    def swap(array, step):
        return lax.ppermute(array, "seq", [(rank, rank ^ step) for rank in range(ranks)])

    order = list(range(ranks - 1, 0, -1))
    received = {step: swap(sends[step - 1], step) for step in order}

    *cot_sends, own, col, row, after, before = pl.pallas_call(
        functools.partial(mask_kernel, ranks, length),
        out_shape=[struct((frames, LANES), bf16)] * (ranks - 1)
        + [
            struct((4, frames, LANES), bf16),
            struct((length, LANES), i32),
            struct((8, length), i32),
            struct((length, LANES), i32),
            struct((length, LANES), i32),
        ],
        in_specs=[smem] + [hbm] * 4,
        out_specs=[vmem] * (ranks + 4),
        scratch_shapes=[pltpu.SemaphoreType.DMA((ranks + 3,))],
        compiler_params=params,
        cost_estimate=cost(4 * MIB, MIB),
        name="masks",
    )(rec_lengths, queries, keys, values, cotangent)
    cots = {step: swap(cot_sends[step - 1], step) for step in order}

    soft, att, pre, q_heads, k_t, v_full = pl.pallas_call(
        functools.partial(forward_kernel, ranks, frames),
        out_shape=[
            struct((heads, length, length), bf16),
            struct((length + 2 * PAD, LANES), f32),
            struct((length, LANES), f32),
            struct((heads, length, LANES), bf16),
            struct((LANES, length), bf16),
            struct((length, LANES), bf16),
        ],
        in_specs=[vmem] * (ranks + 4) + [anywhere],
        out_specs=[vmem] * 6,
        scratch_shapes=[
            VMEM((LANES, length), f32),
            VMEM((length, LANES), bf16),
            VMEM((length, LANES), bf16),
            VMEM((KERNEL, LANES), f32),
            pltpu.SemaphoreType.DMA,
        ],
        compiler_params=params,
        cost_estimate=cost(400 * MIB, 3 * MIB),
        name="forward",
    )(*[received[step] for step in order], own, col, row, after, before, conv_weight)

    mixed, grad_pad, own_taps = pl.pallas_call(
        functools.partial(taps_kernel, ranks, frames),
        out_shape=[
            struct((length, LANES), bf16),
            struct((length + 2 * PAD, LANES), f32),
            struct((taps, LANES), f32),
        ],
        in_specs=[vmem] * (ranks + 4),
        out_specs=[vmem] * 3,
        scratch_shapes=[VMEM((length, LANES), bf16), VMEM((taps, 8, LANES), f32)],
        compiler_params=params,
        cost_estimate=cost(400 * MIB, 3 * MIB),
        name="taps",
    )(*[cots[step] for step in order], own, att, pre, after, before)

    copies = lax.axis_size("dp")
    part_taps = [own_taps] + [
        lax.ppermute(own_taps, "dp", [(one, (one + shift) % copies) for one in range(copies)])
        for shift in range(1, copies)
    ]

    results = pl.pallas_call(
        backward_kernel,
        out_shape=[struct((length, LANES), bf16)] * 3,
        in_specs=[vmem] * 8 + [anywhere],
        out_specs=[vmem] * 3,
        scratch_shapes=[
            VMEM((length, LANES), bf16),
            VMEM((LANES, length), f32),
            VMEM((KERNEL, LANES), f32),
            pltpu.SemaphoreType.DMA,
        ],
        compiler_params=params,
        cost_estimate=cost(800 * MIB, 3 * MIB),
        name="backward",
    )(soft, att, grad_pad, after, before, q_heads, k_t, v_full, conv_weight)

    def blocks_of(steps):
        return pl.pallas_call(
            functools.partial(block_kernel, steps, frames),
            out_shape=[struct((4 * frames + taps, LANES), bf16)] * len(steps),
            in_specs=[vmem] * (4 + copies),
            out_specs=[vmem] * len(steps),
            compiler_params=params,
            cost_estimate=cost(MIB, MIB),
            name="blocks",
        )(mixed, *results, *part_taps)

    cores = lax.axis_size("mp")

    def exchange(array, turn):
        pairs = [
            (rank * cores + core, (rank ^ turn[core % 2]) * cores + core)
            for rank in range(ranks)
            for core in range(cores)
        ]
        return lax.ppermute(array, ("seq", "mp"), pairs)

    order = turns(ranks)
    first, last = order[: ranks // 2], order[ranks // 2 :]
    far = blocks_of(first)
    *near, kept = blocks_of(last + [(0, 0)])
    back = [exchange(block, turn) for block, turn in zip([*far, *near], order)]

    return pl.pallas_call(
        functools.partial(spread_kernel, order + [(0, 0)], frames),
        out_shape=[struct(queries.shape, bf16)] * 4 + [struct(conv_weight.shape, f32)],
        in_specs=[vmem] * ranks,
        out_specs=[vmem] * 5,
        compiler_params=params,
        name="spread",
    )(*back, kept)


def on_device_any(queries, keys, values, cotangent, conv_weight, rec_lengths):
    ranks = lax.axis_size("seq")
    frames, channels = queries.shape[1], queries.shape[2]
    fits = channels == ranks * LANES and ranks & (ranks - 1) == 0 and frames % LANES == 0
    if fits and ranks > 1 and ranks * frames <= 1024 and lax.axis_size("dp") == 2:
        return on_device_heads(queries, keys, values, cotangent, conv_weight, rec_lengths)
    return on_device(queries, keys, values, cotangent, conv_weight, rec_lengths)


def solution(mesh):
    placed = (
        P(("groups", "dp"), "seq", "mp"),
        P(("groups", "dp"), "seq", "mp"),
        P(("groups", "dp"), "seq", "mp"),
        P(("groups", "dp"), "seq", "mp"),
        P(None, "mp"),
        P(("groups", "dp"), None),
    )
    return jax.shard_map(
        on_device_any,
        mesh=mesh,
        in_specs=placed,
        out_specs=(
            P(("groups", "dp"), "seq", "mp"),
            P(("groups", "dp"), "seq", "mp"),
            P(("groups", "dp"), "seq", "mp"),
            P(("groups", "dp"), "seq", "mp"),
            P("groups", "mp"),
        ),
        check_vma=False,
    )
```

```python
import functools
import math

import jax
import jax.numpy as jnp
from jax import lax
from jax.experimental import pallas as pl
from jax.experimental.pallas import tpu as pltpu
from jax.sharding import PartitionSpec as P

HDIM = 64
KERNEL = 31
HALF = 15


NEGATIVE_FILL = -1e30


def extended(block, sides, width):
    for axis, dim in sides:
        count = lax.axis_size(axis)
        forward = [(i, i + 1) for i in range(count - 1)]
        backward = [(target, source) for source, target in forward]
        low = lax.ppermute(
            lax.slice_in_dim(block, block.shape[dim] - width, None, axis=dim), axis, forward
        )
        high = lax.ppermute(lax.slice_in_dim(block, 0, width, axis=dim), axis, backward)
        block = jnp.concatenate([low, block, high], axis=dim)
    return block


def pick_block(total_rows):
    for candidate in (512, 256, 128):
        return candidate
    return total_rows


def over_blocks(total_rows, advance, initial):
    block_rows = pick_block(total_rows)
    block_count = total_rows // block_rows
    if block_count == 1:
        return advance(initial, 0, block_rows)
    return lax.fori_loop(
        0,
        block_count,
        lambda number, running: advance(running, number * block_rows, block_rows),
        initial,
    )


def when_shared(compute, running):
    result = compute(running)
    return result


def on_device(queries, keys, values, cotangent, conv_weight, rec_lengths):
    frames = queries.shape[1]
    channels = queries.shape[2]
    local_heads = channels // HDIM
    score_scale = 1.0 / math.sqrt(HDIM)
    length_all = frames * lax.axis_size("seq")
    offset = lax.axis_index("seq") * frames
    record_ends = jnp.cumsum(rec_lengths[0], dtype=jnp.int32)

    def segment_of(positions):
        return jnp.sum((record_ends[None, :] <= positions[:, None]).astype(jnp.int32), axis=1)

    own_seg = segment_of(offset + jnp.arange(frames, dtype=jnp.int32))

    def to_heads(array):
        return array.reshape(array.shape[0], local_heads, HDIM).transpose(1, 0, 2)

    def from_heads(array):
        return array.transpose(1, 0, 2).reshape(array.shape[1], channels)

    q_heads = to_heads(queries[0])
    k_heads = to_heads(keys[0])
    v_heads = to_heads(values[0])

    def over_rows(advance, initial, members, first_row):
        total_rows = members[0].shape[1]

        def one_block(running, block_start, block_rows):
            sliced = tuple(
                (lax.dynamic_slice_in_dim(member, block_start, block_rows, 1) for member in members)
            )
            other_seg = segment_of(
                first_row + block_start + jnp.arange(block_rows, dtype=jnp.int32)
            )
            return when_shared(lambda current: advance(current, sliced, other_seg), running)

        return over_blocks(total_rows, one_block, initial)

    def query_scores(key_block, key_seg):
        raw_scores = (
            jnp.einsum("hqd,hkd->hqk", q_heads, key_block, preferred_element_type=jnp.float32)
            * score_scale
        )
        return jnp.where((own_seg[:, None] == key_seg[None, :])[None], raw_scores, NEGATIVE_FILL)

    def stats_step(running, sliced, key_seg):
        top_now, total_now = running
        scores = query_scores(sliced[0], key_seg)
        top_new = jnp.maximum(top_now, jnp.max(scores, axis=2))
        total_new = total_now * jnp.exp(top_now - top_new) + jnp.sum(
            jnp.exp(scores - top_new[:, :, None]), axis=2
        )
        return (top_new, total_new)

    stats_init = (
        jnp.full((local_heads, frames), NEGATIVE_FILL, jnp.float32),
        jnp.zeros((local_heads, frames), jnp.float32),
    )
    gathered = (
        lax.all_gather(keys, "seq", axis=1, tiled=True),
        lax.all_gather(values, "seq", axis=1, tiled=True),
    )
    key_whole = to_heads(gathered[0][0])
    value_whole = to_heads(gathered[1][0])
    row_stats = over_rows(stats_step, stats_init, (key_whole,), 0)
    log_total = row_stats[0] + jnp.log(row_stats[1])

    def output_step(running, sliced, key_seg):
        scores = query_scores(sliced[0], key_seg)
        soft_rounded = jnp.exp(scores - log_total[:, :, None]).astype(jnp.bfloat16)
        return running + jnp.einsum(
            "hqk,hkd->hqd", soft_rounded, sliced[1], preferred_element_type=jnp.float32
        )

    frame_zeros = jnp.zeros((local_heads, frames, HDIM), jnp.float32)
    attended_sum = over_rows(output_step, frame_zeros, (key_whole, value_whole), 0)
    attended_heads = attended_sum.astype(jnp.bfloat16)
    attended = from_heads(attended_heads)
    padded = extended(attended[None], (("seq", 1),), HALF)
    padded_wide = padded[0].astype(jnp.float32)
    pad_positions = offset - HALF + jnp.arange(frames + 2 * HALF, dtype=jnp.int32)
    inside = jnp.logical_and(pad_positions >= 0, pad_positions < length_all)
    pad_seg = jnp.where(inside, segment_of(pad_positions), -1)
    conv_pre = jnp.zeros((frames, channels), jnp.float32)
    for tap_index in range(KERNEL):
        tap_mask = (pad_seg[tap_index : tap_index + frames] == own_seg)[:, None]
        conv_pre = conv_pre + jnp.where(
            tap_mask, conv_weight[tap_index] * padded_wide[tap_index : tap_index + frames], 0.0
        )
    gate_value = jax.nn.sigmoid(conv_pre)
    mixed = (conv_pre * gate_value).astype(jnp.bfloat16)
    conv_grad = (
        cotangent[0].astype(jnp.float32) * gate_value * (1.0 + conv_pre * (1.0 - gate_value))
    ).astype(jnp.bfloat16)
    padded_grad = extended(conv_grad[None], (("seq", 1),), HALF)
    grad_wide = padded_grad[0].astype(jnp.float32)
    conv_grad_wide = conv_grad.astype(jnp.float32)
    grad_attended = jnp.zeros((frames, channels), jnp.float32)
    kernel_rows = []
    for tap_index in range(KERNEL):
        back_start = 2 * HALF - tap_index
        back_mask = (pad_seg[back_start : back_start + frames] == own_seg)[:, None]
        grad_attended = grad_attended + jnp.where(
            back_mask, conv_weight[tap_index] * grad_wide[back_start : back_start + frames], 0.0
        )
        tap_mask = (pad_seg[tap_index : tap_index + frames] == own_seg)[:, None]
        product = conv_grad_wide * padded_wide[tap_index : tap_index + frames]
        kernel_rows.append(jnp.sum(jnp.where(tap_mask, product, 0.0), axis=0))
    grad_kernel = lax.psum(jnp.stack(kernel_rows), ("dp", "seq"))
    grad_attended = grad_attended.astype(jnp.bfloat16)
    g_heads = to_heads(grad_attended)
    row_delta = jnp.sum(g_heads.astype(jnp.float32) * attended_heads.astype(jnp.float32), axis=2)

    def query_grad_step(running, sliced, key_seg):
        key_block = sliced[0]
        value_block = sliced[1]
        soft_weights = jnp.exp(query_scores(key_block, key_seg) - log_total[:, :, None])
        slopes = jnp.einsum(
            "hqd,hkd->hqk", g_heads, value_block, preferred_element_type=jnp.float32
        )
        mixed_grad = (soft_weights * (slopes - row_delta[:, :, None])).astype(jnp.bfloat16)
        return running + jnp.einsum(
            "hqk,hkd->hqd", mixed_grad, key_block, preferred_element_type=jnp.float32
        )

    grad_query = over_rows(query_grad_step, frame_zeros, (key_whole, value_whole), 0)

    def key_grad_step(running, sliced, query_seg):
        grad_key_now, grad_value_now = running
        query_block = sliced[0]
        grad_block = sliced[1]
        total_block = sliced[2]
        delta_block = sliced[3]
        raw_scores = (
            jnp.einsum("hqd,hkd->hqk", query_block, k_heads, preferred_element_type=jnp.float32)
            * score_scale
        )
        scores = jnp.where(
            (query_seg[:, None] == own_seg[None, :])[None], raw_scores, NEGATIVE_FILL
        )
        soft_weights = jnp.exp(scores - total_block[:, :, None])
        grad_value_new = grad_value_now + jnp.einsum(
            "hqk,hqd->hkd",
            soft_weights.astype(jnp.bfloat16),
            grad_block,
            preferred_element_type=jnp.float32,
        )
        slopes = jnp.einsum("hqd,hkd->hqk", grad_block, v_heads, preferred_element_type=jnp.float32)
        mixed_grad = (soft_weights * (slopes - delta_block[:, :, None])).astype(jnp.bfloat16)
        grad_key_new = grad_key_now + jnp.einsum(
            "hqk,hqd->hkd", mixed_grad, query_block, preferred_element_type=jnp.float32
        )
        return (grad_key_new, grad_value_new)

    all_totals, all_deltas = (
        lax.all_gather(log_total[None], "seq", axis=2, tiled=True),
        lax.all_gather(row_delta[None], "seq", axis=2, tiled=True),
    )
    member = (
        lax.all_gather(queries, "seq", axis=1, tiled=True),
        lax.all_gather(grad_attended[None], "seq", axis=1, tiled=True),
    )
    totals_piece = all_totals[0]
    deltas_piece = all_deltas[0]
    grad_key, grad_value = over_rows(
        key_grad_step,
        (frame_zeros, frame_zeros),
        (to_heads(member[0][0]), to_heads(member[1][0]), totals_piece, deltas_piece),
        jnp.int32(0),
    )
    grad_queries = from_heads(grad_query * score_scale).astype(jnp.bfloat16)[None]
    grad_keys = from_heads(grad_key * score_scale).astype(jnp.bfloat16)[None]
    grad_values = from_heads(grad_value).astype(jnp.bfloat16)[None]
    return (mixed[None], grad_queries, grad_keys, grad_values, grad_kernel)


LANES = 128
PAD = 16
VMEM = pltpu.VMEM
MIB = 1024 * 1024


def mm(left, right):
    return lax.dot_general(
        left, right, (((1,), (0,)), ((), ())), preferred_element_type=jnp.float32
    )


def mm_nt(left, right):
    return lax.dot_general(
        left, right, (((1,), (1,)), ((), ())), preferred_element_type=jnp.float32
    )


def rows_at(block, frames):
    return pl.ds(pl.multiple_of(block * frames, frames), frames)


def lanes_at(block):
    return pl.ds(pl.multiple_of(block * LANES, LANES), LANES)


def turns(ranks):
    middle = ranks // 2
    even = [middle] + [step for step in range(ranks - 1, 0, -1) if step != middle]
    return list(zip(even, even[1:] + even[:1]))


def step_of(turn):
    even, odd = turn
    return jnp.where(lax.axis_index("mp") % 2 == 0, even, odd)


def pack_kernel(ranks, q_ref, k_ref, v_ref, *rest):
    outs, sems = rest[:-1], rest[-1]
    me = lax.axis_index("seq")
    pairs = []
    for step in range(ranks - 1, 0, -1):
        for place, source in enumerate((q_ref, k_ref, v_ref)):
            pairs.append((source.at[0, :, lanes_at(me ^ step)], outs[step - 1].at[place]))
    run_copies(pairs, sems)


def run_copies(pairs, sems, meanwhile=None):
    copies = [
        pltpu.make_async_copy(source, target, sems.at[number])
        for number, (source, target) in enumerate(pairs)
    ]
    for copy in copies:
        copy.start()
    if meanwhile is not None:
        meanwhile()
    for copy in copies:
        copy.wait()


def mask_kernel(ranks, length, lens_ref, q_ref, k_ref, v_ref, c_ref, *refs):
    cot_refs = refs[: ranks - 1]
    own_ref, col_ref, row_ref, after_ref, before_ref, sems = refs[ranks - 1 :]
    me = lax.axis_index("seq")
    pairs = [(c_ref.at[0, :, lanes_at(me ^ step)], cot_refs[step - 1]) for step in range(1, ranks)]
    for place, source in enumerate((q_ref, k_ref, v_ref, c_ref)):
        pairs.append((source.at[0, :, lanes_at(me)], own_ref.at[place]))

    def extents():
        ends = []
        running = jnp.int32(0)
        for number in range(lens_ref.shape[1]):
            running = running + lens_ref[0, number]
            ends.append(running)
        row_time = lax.broadcasted_iota(jnp.int32, row_ref.shape, 1)
        row_first = jnp.zeros(row_ref.shape, jnp.int32)
        for end in ends:
            row_first = jnp.where(row_time >= end, end, row_first)
        row_ref[...] = row_first
        chunk = 64

        def some_rows(number, carry):
            base = pl.multiple_of(number * chunk, chunk)
            time = base + lax.broadcasted_iota(jnp.int32, (chunk, LANES), 0)
            first = jnp.zeros((chunk, LANES), jnp.int32)
            last = jnp.full((chunk, LANES), length, jnp.int32)
            for end in ends:
                first = jnp.where(time >= end, end, first)
            for end in reversed(ends):
                last = jnp.where(time < end, end, last)
            rows = pl.ds(base, chunk)
            col_ref[rows, :] = first
            after_ref[rows, :] = last - 1 - time
            before_ref[rows, :] = time - first
            return carry

        lax.fori_loop(0, length // chunk, some_rows, 0)

    run_copies(pairs, sems, extents)


def forward_kernel(ranks, frames, *refs):
    recvs = refs[: ranks - 1]
    own_ref, col_ref, row_ref, after_ref, before_ref, w_ref = refs[ranks - 1 : ranks + 5]
    soft_ref, att_ref, pre_ref, q_ref, k_t_ref, v_ref = refs[ranks + 5 : ranks + 11]
    att_t_ref, k_full, q_full, w_own, w_sem = refs[ranks + 11 :]
    me = lax.axis_index("seq")
    length = ranks * frames
    copy = pltpu.make_async_copy(w_ref.at[:, lanes_at(me)], w_own, w_sem)
    copy.start()
    for place, target in enumerate((q_full, k_full, v_ref)):
        target[rows_at(me, frames), :] = own_ref[place]
        for step in range(1, ranks):
            target[rows_at(me ^ step, frames), :] = recvs[ranks - 1 - step][place]
    heads = LANES // HDIM
    lane_head = lax.broadcasted_iota(jnp.int32, (1, LANES), 1) // HDIM
    scaled = q_full[...].astype(jnp.float32) * (1.0 / math.sqrt(HDIM))
    for head in range(heads):
        q_ref[head] = jnp.where(lane_head == head, scaled, 0.0).astype(jnp.bfloat16)
    k_t_ref[...] = k_full[...].astype(jnp.float32).T.astype(jnp.bfloat16)
    v_t = v_ref[...].astype(jnp.float32).T.astype(jnp.bfloat16)
    wide = 512
    for head in range(heads):
        for start in range(0, length, wide):
            cols = slice(start, start + wide)
            raw = mm_nt(k_full[...], q_ref[head, cols, :])
            same = jnp.concatenate([col_ref[...]] * (wide // LANES), axis=1) == row_ref[0:1, cols]
            scores = jnp.where(same, raw, NEGATIVE_FILL)
            top = jnp.max(scores, axis=0, keepdims=True)
            powers = jnp.exp(scores - top)
            share = 1.0 / jnp.sum(powers, axis=0, keepdims=True)
            soft = (powers * share).astype(jnp.bfloat16)
            soft_ref[head, :, cols] = soft
            rows = slice(head * HDIM, (head + 1) * HDIM)
            att_t_ref[rows, cols] = mm(v_t[rows], soft).astype(jnp.bfloat16).astype(jnp.float32)
    zeros = jnp.zeros((PAD, LANES), jnp.float32)
    att_ref[0:PAD, :] = zeros
    att_ref[PAD : PAD + length, :] = att_t_ref[...].T
    att_ref[PAD + length :, :] = zeros
    copy.wait()

    chunk = 64

    def some_rows(number, carry):
        base = pl.multiple_of(number * chunk, chunk)
        rows = pl.ds(base, chunk)
        after, before = after_ref[rows, :], before_ref[rows, :]
        total = jnp.zeros((chunk, LANES), jnp.float32)
        for tap in range(KERNEL):
            off = tap - HALF
            piece = att_ref[pl.ds(base + (PAD + off), chunk), :]
            if off > 0:
                piece = jnp.where(after >= off, piece, 0.0)
            if off < 0:
                piece = jnp.where(before >= -off, piece, 0.0)
            total = total + w_own[tap : tap + 1, :] * piece
        pre_ref[rows, :] = total
        return carry

    lax.fori_loop(0, length // chunk, some_rows, 0)


def masked(source, base, chunk, off, before, after):
    piece = source[pl.ds(base + (PAD + off), chunk), :]
    if off > 0:
        piece = jnp.where(after >= off, piece, 0.0)
    if off < 0:
        piece = jnp.where(before >= -off, piece, 0.0)
    return piece


def taps_kernel(ranks, frames, *refs):
    cots = refs[: ranks - 1]
    own_ref, att_ref, pre_ref, after_ref, before_ref = refs[ranks - 1 : ranks + 4]
    mixed_ref, grad_pad, taps_ref, cot, tap_sum = refs[ranks + 4 :]
    me = lax.axis_index("seq")
    length = ranks * frames
    cot[rows_at(me, frames), :] = own_ref[3]
    for step in range(1, ranks):
        cot[rows_at(me ^ step, frames), :] = cots[ranks - 1 - step][...]
    zeros = jnp.zeros((PAD, LANES), jnp.float32)
    grad_pad[0:PAD, :] = zeros
    grad_pad[PAD + length :, :] = zeros
    tap_sum[...] = jnp.zeros(tap_sum.shape, jnp.float32)
    chunk = 64

    def some_rows(number, carry):
        base = pl.multiple_of(number * chunk, chunk)
        rows = pl.ds(base, chunk)
        pre = pre_ref[rows, :]
        gate = jax.nn.sigmoid(pre)
        mixed_ref[rows, :] = (pre * gate).astype(jnp.bfloat16)
        conv_grad = cot[rows, :].astype(jnp.float32) * gate * (1.0 + pre * (1.0 - gate))
        conv_grad = conv_grad.astype(jnp.bfloat16).astype(jnp.float32)
        grad_pad[pl.ds(base + PAD, chunk), :] = conv_grad
        after, before = after_ref[rows, :], before_ref[rows, :]
        for tap in range(KERNEL):
            part = conv_grad * masked(att_ref, base, chunk, tap - HALF, before, after)
            tap_sum[tap] = tap_sum[tap] + jnp.sum(part.reshape(chunk // 8, 8, LANES), axis=0)
        return carry

    lax.fori_loop(0, length // chunk, some_rows, 0)
    taps_ref[...] = jnp.sum(tap_sum[...], axis=1)


def backward_kernel(soft_ref, att_ref, grad_pad, after_ref, before_ref, q_ref, k_t_ref, v_ref, w_ref, *refs):
    res_q, res_k, res_v, g_att, grad_t, w_own, w_sem = refs
    length = v_ref.shape[0]
    copy = pltpu.make_async_copy(w_ref.at[:, lanes_at(lax.axis_index("seq"))], w_own, w_sem)
    copy.start()
    copy.wait()
    chunk = 64

    def some_rows(number, carry):
        base = pl.multiple_of(number * chunk, chunk)
        rows = pl.ds(base, chunk)
        after, before = after_ref[rows, :], before_ref[rows, :]
        total = jnp.zeros((chunk, LANES), jnp.float32)
        for tap in range(KERNEL):
            total = total + w_own[tap : tap + 1, :] * masked(grad_pad, base, chunk, HALF - tap, before, after)
        g_att[rows, :] = total.astype(jnp.bfloat16)
        return carry

    lax.fori_loop(0, length // chunk, some_rows, 0)
    heads = LANES // HDIM
    lane_head = lax.broadcasted_iota(jnp.int32, (1, LANES), 1) // HDIM
    g_wide = g_att[...].astype(jnp.float32)
    products_t = (g_wide * att_ref[PAD : PAD + length, :]).T
    grad_v = jnp.zeros((length, LANES), jnp.float32)
    grad_k = jnp.zeros((length, LANES), jnp.float32)
    for head in range(heads):
        rows = slice(head * HDIM, (head + 1) * HDIM)
        g_head = jnp.where(lane_head == head, g_wide, 0.0).astype(jnp.bfloat16)
        delta = jnp.sum(products_t[rows], axis=0, keepdims=True)
        soft = soft_ref[head]
        slopes = mm_nt(v_ref[...], g_head)
        mixed_grad = (soft.astype(jnp.float32) * (slopes - delta)).astype(jnp.bfloat16)
        grad_v = grad_v + mm(soft, g_head)
        grad_k = grad_k + mm(mixed_grad, q_ref[head])
        grad_t[rows, :] = mm(k_t_ref[rows, :], mixed_grad) * (1.0 / math.sqrt(HDIM))
    res_k[...] = grad_k.astype(jnp.bfloat16)
    res_v[...] = grad_v.astype(jnp.bfloat16)
    res_q[...] = grad_t[...].T.astype(jnp.bfloat16)


def block_kernel(steps, frames, *refs):
    sources, tap_refs, outs = refs[:4], refs[4 : -len(steps)], refs[-len(steps) :]
    me = lax.axis_index("seq")
    taps = tap_refs[0][...]
    for other in tap_refs[1:]:
        taps = taps + other[...]
    for turn, out in zip(steps, outs):
        rows = rows_at(me ^ step_of(turn), frames)
        for place, source in enumerate(sources):
            out[place * frames : (place + 1) * frames, :] = source[rows, :]
        out[4 * frames :, :] = taps.astype(jnp.bfloat16)


def spread_kernel(steps, frames, *refs):
    ranks = len(steps)
    blocks = refs[:ranks]
    targets, taps_ref = refs[ranks : ranks + 4], refs[ranks + 4]
    me = lax.axis_index("seq")
    for turn, block in zip(steps, blocks):
        lanes = lanes_at(me ^ step_of(turn))
        for place, target in enumerate(targets):
            target[0, :, lanes] = block[place * frames : (place + 1) * frames, :]
        taps = block[4 * frames :, :].astype(jnp.float32)
        taps_ref[:, lanes] = taps[:KERNEL]


def cost(flops, moved):
    return pl.CostEstimate(flops=flops, bytes_accessed=moved, transcendentals=0)


def on_device_heads(queries, keys, values, cotangent, conv_weight, rec_lengths):
    ranks = lax.axis_size("seq")
    frames = queries.shape[1]
    length = ranks * frames
    heads = LANES // HDIM
    bf16, f32, i32 = jnp.bfloat16, jnp.float32, jnp.int32
    struct = jax.ShapeDtypeStruct
    hbm = pl.BlockSpec(memory_space=pltpu.HBM)
    anywhere = pl.BlockSpec(memory_space=pl.ANY)
    vmem = pl.BlockSpec(memory_space=VMEM)
    smem = pl.BlockSpec(memory_space=pltpu.SMEM)
    params = pltpu.CompilerParams(vmem_limit_bytes=24 * MIB)
    taps = KERNEL + 1

    sends = pl.pallas_call(
        functools.partial(pack_kernel, ranks),
        out_shape=[struct((3, frames, LANES), bf16)] * (ranks - 1),
        in_specs=[hbm] * 3,
        out_specs=[vmem] * (ranks - 1),
        scratch_shapes=[pltpu.SemaphoreType.DMA((3 * (ranks - 1),))],
        compiler_params=pltpu.CompilerParams(vmem_limit_bytes=54912 * 1024),
        name="pack",
    )(queries, keys, values)

    def swap(array, step):
        return lax.ppermute(array, "seq", [(rank, rank ^ step) for rank in range(ranks)])

    order = list(range(ranks - 1, 0, -1))
    received = {step: swap(sends[step - 1], step) for step in order}

    *cot_sends, own, col, row, after, before = pl.pallas_call(
        functools.partial(mask_kernel, ranks, length),
        out_shape=[struct((frames, LANES), bf16)] * (ranks - 1)
        + [
            struct((4, frames, LANES), bf16),
            struct((length, LANES), i32),
            struct((8, length), i32),
            struct((length, LANES), i32),
            struct((length, LANES), i32),
        ],
        in_specs=[smem] + [hbm] * 4,
        out_specs=[vmem] * (ranks + 4),
        scratch_shapes=[pltpu.SemaphoreType.DMA((ranks + 3,))],
        compiler_params=params,
        cost_estimate=cost(4 * MIB, MIB),
        name="masks",
    )(rec_lengths, queries, keys, values, cotangent)
    cots = {step: swap(cot_sends[step - 1], step) for step in order}

    soft, att, pre, q_heads, k_t, v_full = pl.pallas_call(
        functools.partial(forward_kernel, ranks, frames),
        out_shape=[
            struct((heads, length, length), bf16),
            struct((length + 2 * PAD, LANES), f32),
            struct((length, LANES), f32),
            struct((heads, length, LANES), bf16),
            struct((LANES, length), bf16),
            struct((length, LANES), bf16),
        ],
        in_specs=[vmem] * (ranks + 4) + [anywhere],
        out_specs=[vmem] * 6,
        scratch_shapes=[
            VMEM((LANES, length), f32),
            VMEM((length, LANES), bf16),
            VMEM((length, LANES), bf16),
            VMEM((KERNEL, LANES), f32),
            pltpu.SemaphoreType.DMA,
        ],
        compiler_params=params,
        cost_estimate=cost(400 * MIB, 3 * MIB),
        name="forward",
    )(*[received[step] for step in order], own, col, row, after, before, conv_weight)

    mixed, grad_pad, own_taps = pl.pallas_call(
        functools.partial(taps_kernel, ranks, frames),
        out_shape=[
            struct((length, LANES), bf16),
            struct((length + 2 * PAD, LANES), f32),
            struct((taps, LANES), f32),
        ],
        in_specs=[vmem] * (ranks + 4),
        out_specs=[vmem] * 3,
        scratch_shapes=[VMEM((length, LANES), bf16), VMEM((taps, 8, LANES), f32)],
        compiler_params=params,
        cost_estimate=cost(400 * MIB, 3 * MIB),
        name="taps",
    )(*[cots[step] for step in order], own, att, pre, after, before)

    copies = lax.axis_size("dp")
    part_taps = [own_taps] + [
        lax.ppermute(own_taps, "dp", [(one, (one + shift) % copies) for one in range(copies)])
        for shift in range(1, copies)
    ]

    results = pl.pallas_call(
        backward_kernel,
        out_shape=[struct((length, LANES), bf16)] * 3,
        in_specs=[vmem] * 8 + [anywhere],
        out_specs=[vmem] * 3,
        scratch_shapes=[
            VMEM((length, LANES), bf16),
            VMEM((LANES, length), f32),
            VMEM((KERNEL, LANES), f32),
            pltpu.SemaphoreType.DMA,
        ],
        compiler_params=params,
        cost_estimate=cost(800 * MIB, 3 * MIB),
        name="backward",
    )(soft, att, grad_pad, after, before, q_heads, k_t, v_full, conv_weight)

    def blocks_of(steps):
        return pl.pallas_call(
            functools.partial(block_kernel, steps, frames),
            out_shape=[struct((4 * frames + taps, LANES), bf16)] * len(steps),
            in_specs=[vmem] * (4 + copies),
            out_specs=[vmem] * len(steps),
            compiler_params=params,
            cost_estimate=cost(MIB, MIB),
            name="blocks",
        )(mixed, *results, *part_taps)

    cores = lax.axis_size("mp")

    def exchange(array, turn):
        pairs = [
            (rank * cores + core, (rank ^ turn[core % 2]) * cores + core)
            for rank in range(ranks)
            for core in range(cores)
        ]
        return lax.ppermute(array, ("seq", "mp"), pairs)

    order = turns(ranks)
    *sent, kept = blocks_of(order + [(0, 0)])
    back = [exchange(block, turn) for block, turn in zip(sent, order)]

    return pl.pallas_call(
        functools.partial(spread_kernel, order + [(0, 0)], frames),
        out_shape=[struct(queries.shape, bf16)] * 4 + [struct(conv_weight.shape, f32)],
        in_specs=[vmem] * ranks,
        out_specs=[vmem] * 5,
        compiler_params=params,
        name="spread",
    )(*back, kept)


def on_device_any(queries, keys, values, cotangent, conv_weight, rec_lengths):
    ranks = lax.axis_size("seq")
    frames, channels = queries.shape[1], queries.shape[2]
    fits = channels == ranks * LANES and ranks & (ranks - 1) == 0 and frames % LANES == 0
    if fits and ranks > 1 and ranks * frames <= 1024 and lax.axis_size("dp") == 2:
        return on_device_heads(queries, keys, values, cotangent, conv_weight, rec_lengths)
    return on_device(queries, keys, values, cotangent, conv_weight, rec_lengths)


def solution(mesh):
    placed = (
        P(("groups", "dp"), "seq", "mp"),
        P(("groups", "dp"), "seq", "mp"),
        P(("groups", "dp"), "seq", "mp"),
        P(("groups", "dp"), "seq", "mp"),
        P(None, "mp"),
        P(("groups", "dp"), None),
    )
    return jax.shard_map(
        on_device_any,
        mesh=mesh,
        in_specs=placed,
        out_specs=(
            P(("groups", "dp"), "seq", "mp"),
            P(("groups", "dp"), "seq", "mp"),
            P(("groups", "dp"), "seq", "mp"),
            P(("groups", "dp"), "seq", "mp"),
            P("groups", "mp"),
        ),
        check_vma=False,
    )
```

```python
import functools
import math

import jax
import jax.numpy as jnp
from jax import lax
from jax.experimental import pallas as pl
from jax.experimental.pallas import tpu as pltpu
from jax.sharding import PartitionSpec as P

HDIM = 64
KERNEL = 31
HALF = 15


NEGATIVE_FILL = -1e30


def extended(block, sides, width):
    for axis, dim in sides:
        count = lax.axis_size(axis)
        forward = [(i, i + 1) for i in range(count - 1)]
        backward = [(target, source) for source, target in forward]
        low = lax.ppermute(
            lax.slice_in_dim(block, block.shape[dim] - width, None, axis=dim), axis, forward
        )
        high = lax.ppermute(lax.slice_in_dim(block, 0, width, axis=dim), axis, backward)
        block = jnp.concatenate([low, block, high], axis=dim)
    return block


def pick_block(total_rows):
    for candidate in (512, 256, 128):
        return candidate
    return total_rows


def over_blocks(total_rows, advance, initial):
    block_rows = pick_block(total_rows)
    block_count = total_rows // block_rows
    if block_count == 1:
        return advance(initial, 0, block_rows)
    return lax.fori_loop(
        0,
        block_count,
        lambda number, running: advance(running, number * block_rows, block_rows),
        initial,
    )


def when_shared(compute, running):
    result = compute(running)
    return result


def on_device(queries, keys, values, cotangent, conv_weight, rec_lengths):
    frames = queries.shape[1]
    channels = queries.shape[2]
    local_heads = channels // HDIM
    score_scale = 1.0 / math.sqrt(HDIM)
    length_all = frames * lax.axis_size("seq")
    offset = lax.axis_index("seq") * frames
    record_ends = jnp.cumsum(rec_lengths[0], dtype=jnp.int32)

    def segment_of(positions):
        return jnp.sum((record_ends[None, :] <= positions[:, None]).astype(jnp.int32), axis=1)

    own_seg = segment_of(offset + jnp.arange(frames, dtype=jnp.int32))

    def to_heads(array):
        return array.reshape(array.shape[0], local_heads, HDIM).transpose(1, 0, 2)

    def from_heads(array):
        return array.transpose(1, 0, 2).reshape(array.shape[1], channels)

    q_heads = to_heads(queries[0])
    k_heads = to_heads(keys[0])
    v_heads = to_heads(values[0])

    def over_rows(advance, initial, members, first_row):
        total_rows = members[0].shape[1]

        def one_block(running, block_start, block_rows):
            sliced = tuple(
                (lax.dynamic_slice_in_dim(member, block_start, block_rows, 1) for member in members)
            )
            other_seg = segment_of(
                first_row + block_start + jnp.arange(block_rows, dtype=jnp.int32)
            )
            return when_shared(lambda current: advance(current, sliced, other_seg), running)

        return over_blocks(total_rows, one_block, initial)

    def query_scores(key_block, key_seg):
        raw_scores = (
            jnp.einsum("hqd,hkd->hqk", q_heads, key_block, preferred_element_type=jnp.float32)
            * score_scale
        )
        return jnp.where((own_seg[:, None] == key_seg[None, :])[None], raw_scores, NEGATIVE_FILL)

    def stats_step(running, sliced, key_seg):
        top_now, total_now = running
        scores = query_scores(sliced[0], key_seg)
        top_new = jnp.maximum(top_now, jnp.max(scores, axis=2))
        total_new = total_now * jnp.exp(top_now - top_new) + jnp.sum(
            jnp.exp(scores - top_new[:, :, None]), axis=2
        )
        return (top_new, total_new)

    stats_init = (
        jnp.full((local_heads, frames), NEGATIVE_FILL, jnp.float32),
        jnp.zeros((local_heads, frames), jnp.float32),
    )
    gathered = (
        lax.all_gather(keys, "seq", axis=1, tiled=True),
        lax.all_gather(values, "seq", axis=1, tiled=True),
    )
    key_whole = to_heads(gathered[0][0])
    value_whole = to_heads(gathered[1][0])
    row_stats = over_rows(stats_step, stats_init, (key_whole,), 0)
    log_total = row_stats[0] + jnp.log(row_stats[1])

    def output_step(running, sliced, key_seg):
        scores = query_scores(sliced[0], key_seg)
        soft_rounded = jnp.exp(scores - log_total[:, :, None]).astype(jnp.bfloat16)
        return running + jnp.einsum(
            "hqk,hkd->hqd", soft_rounded, sliced[1], preferred_element_type=jnp.float32
        )

    frame_zeros = jnp.zeros((local_heads, frames, HDIM), jnp.float32)
    attended_sum = over_rows(output_step, frame_zeros, (key_whole, value_whole), 0)
    attended_heads = attended_sum.astype(jnp.bfloat16)
    attended = from_heads(attended_heads)
    padded = extended(attended[None], (("seq", 1),), HALF)
    padded_wide = padded[0].astype(jnp.float32)
    pad_positions = offset - HALF + jnp.arange(frames + 2 * HALF, dtype=jnp.int32)
    inside = jnp.logical_and(pad_positions >= 0, pad_positions < length_all)
    pad_seg = jnp.where(inside, segment_of(pad_positions), -1)
    conv_pre = jnp.zeros((frames, channels), jnp.float32)
    for tap_index in range(KERNEL):
        tap_mask = (pad_seg[tap_index : tap_index + frames] == own_seg)[:, None]
        conv_pre = conv_pre + jnp.where(
            tap_mask, conv_weight[tap_index] * padded_wide[tap_index : tap_index + frames], 0.0
        )
    gate_value = jax.nn.sigmoid(conv_pre)
    mixed = (conv_pre * gate_value).astype(jnp.bfloat16)
    conv_grad = (
        cotangent[0].astype(jnp.float32) * gate_value * (1.0 + conv_pre * (1.0 - gate_value))
    ).astype(jnp.bfloat16)
    padded_grad = extended(conv_grad[None], (("seq", 1),), HALF)
    grad_wide = padded_grad[0].astype(jnp.float32)
    conv_grad_wide = conv_grad.astype(jnp.float32)
    grad_attended = jnp.zeros((frames, channels), jnp.float32)
    kernel_rows = []
    for tap_index in range(KERNEL):
        back_start = 2 * HALF - tap_index
        back_mask = (pad_seg[back_start : back_start + frames] == own_seg)[:, None]
        grad_attended = grad_attended + jnp.where(
            back_mask, conv_weight[tap_index] * grad_wide[back_start : back_start + frames], 0.0
        )
        tap_mask = (pad_seg[tap_index : tap_index + frames] == own_seg)[:, None]
        product = conv_grad_wide * padded_wide[tap_index : tap_index + frames]
        kernel_rows.append(jnp.sum(jnp.where(tap_mask, product, 0.0), axis=0))
    grad_kernel = lax.psum(jnp.stack(kernel_rows), ("dp", "seq"))
    grad_attended = grad_attended.astype(jnp.bfloat16)
    g_heads = to_heads(grad_attended)
    row_delta = jnp.sum(g_heads.astype(jnp.float32) * attended_heads.astype(jnp.float32), axis=2)

    def query_grad_step(running, sliced, key_seg):
        key_block = sliced[0]
        value_block = sliced[1]
        soft_weights = jnp.exp(query_scores(key_block, key_seg) - log_total[:, :, None])
        slopes = jnp.einsum(
            "hqd,hkd->hqk", g_heads, value_block, preferred_element_type=jnp.float32
        )
        mixed_grad = (soft_weights * (slopes - row_delta[:, :, None])).astype(jnp.bfloat16)
        return running + jnp.einsum(
            "hqk,hkd->hqd", mixed_grad, key_block, preferred_element_type=jnp.float32
        )

    grad_query = over_rows(query_grad_step, frame_zeros, (key_whole, value_whole), 0)

    def key_grad_step(running, sliced, query_seg):
        grad_key_now, grad_value_now = running
        query_block = sliced[0]
        grad_block = sliced[1]
        total_block = sliced[2]
        delta_block = sliced[3]
        raw_scores = (
            jnp.einsum("hqd,hkd->hqk", query_block, k_heads, preferred_element_type=jnp.float32)
            * score_scale
        )
        scores = jnp.where(
            (query_seg[:, None] == own_seg[None, :])[None], raw_scores, NEGATIVE_FILL
        )
        soft_weights = jnp.exp(scores - total_block[:, :, None])
        grad_value_new = grad_value_now + jnp.einsum(
            "hqk,hqd->hkd",
            soft_weights.astype(jnp.bfloat16),
            grad_block,
            preferred_element_type=jnp.float32,
        )
        slopes = jnp.einsum("hqd,hkd->hqk", grad_block, v_heads, preferred_element_type=jnp.float32)
        mixed_grad = (soft_weights * (slopes - delta_block[:, :, None])).astype(jnp.bfloat16)
        grad_key_new = grad_key_now + jnp.einsum(
            "hqk,hqd->hkd", mixed_grad, query_block, preferred_element_type=jnp.float32
        )
        return (grad_key_new, grad_value_new)

    all_totals, all_deltas = (
        lax.all_gather(log_total[None], "seq", axis=2, tiled=True),
        lax.all_gather(row_delta[None], "seq", axis=2, tiled=True),
    )
    member = (
        lax.all_gather(queries, "seq", axis=1, tiled=True),
        lax.all_gather(grad_attended[None], "seq", axis=1, tiled=True),
    )
    totals_piece = all_totals[0]
    deltas_piece = all_deltas[0]
    grad_key, grad_value = over_rows(
        key_grad_step,
        (frame_zeros, frame_zeros),
        (to_heads(member[0][0]), to_heads(member[1][0]), totals_piece, deltas_piece),
        jnp.int32(0),
    )
    grad_queries = from_heads(grad_query * score_scale).astype(jnp.bfloat16)[None]
    grad_keys = from_heads(grad_key * score_scale).astype(jnp.bfloat16)[None]
    grad_values = from_heads(grad_value).astype(jnp.bfloat16)[None]
    return (mixed[None], grad_queries, grad_keys, grad_values, grad_kernel)


LANES = 128
PAD = 16
VMEM = pltpu.VMEM
MIB = 1024 * 1024


def mm(left, right):
    return lax.dot_general(
        left, right, (((1,), (0,)), ((), ())), preferred_element_type=jnp.float32
    )


def mm_nt(left, right):
    return lax.dot_general(
        left, right, (((1,), (1,)), ((), ())), preferred_element_type=jnp.float32
    )


def rows_at(block, frames):
    return pl.ds(pl.multiple_of(block * frames, frames), frames)


def lanes_at(block):
    return pl.ds(pl.multiple_of(block * LANES, LANES), LANES)


def pack_kernel(ranks, q_ref, k_ref, v_ref, *rest):
    outs, sems = rest[:-1], rest[-1]
    me = lax.axis_index("seq")
    pairs = []
    for step in range(ranks - 1, 0, -1):
        for place, source in enumerate((q_ref, k_ref, v_ref)):
            pairs.append((source.at[0, :, lanes_at(me ^ step)], outs[step - 1].at[place]))
    run_copies(pairs, sems)


def run_copies(pairs, sems, meanwhile=None):
    copies = [
        pltpu.make_async_copy(source, target, sems.at[number])
        for number, (source, target) in enumerate(pairs)
    ]
    for copy in copies:
        copy.start()
    if meanwhile is not None:
        meanwhile()
    for copy in copies:
        copy.wait()


def mask_kernel(ranks, length, lens_ref, q_ref, k_ref, v_ref, c_ref, *refs):
    cot_refs = refs[: ranks - 1]
    own_ref, col_ref, row_ref, after_ref, before_ref, sems = refs[ranks - 1 :]
    me = lax.axis_index("seq")
    pairs = [(c_ref.at[0, :, lanes_at(me ^ step)], cot_refs[step - 1]) for step in range(1, ranks)]
    for place, source in enumerate((q_ref, k_ref, v_ref, c_ref)):
        pairs.append((source.at[0, :, lanes_at(me)], own_ref.at[place]))

    def extents():
        ends = []
        running = jnp.int32(0)
        for number in range(lens_ref.shape[1]):
            running = running + lens_ref[0, number]
            ends.append(running)
        row_time = lax.broadcasted_iota(jnp.int32, row_ref.shape, 1)
        row_first = jnp.zeros(row_ref.shape, jnp.int32)
        for end in ends:
            row_first = jnp.where(row_time >= end, end, row_first)
        row_ref[...] = row_first
        chunk = 64

        def some_rows(number, carry):
            base = pl.multiple_of(number * chunk, chunk)
            time = base + lax.broadcasted_iota(jnp.int32, (chunk, LANES), 0)
            first = jnp.zeros((chunk, LANES), jnp.int32)
            last = jnp.full((chunk, LANES), length, jnp.int32)
            for end in ends:
                first = jnp.where(time >= end, end, first)
            for end in reversed(ends):
                last = jnp.where(time < end, end, last)
            rows = pl.ds(base, chunk)
            col_ref[rows, :] = first
            after_ref[rows, :] = last - 1 - time
            before_ref[rows, :] = time - first
            return carry

        lax.fori_loop(0, length // chunk, some_rows, 0)

    run_copies(pairs, sems, extents)


def forward_kernel(ranks, frames, *refs):
    recvs = refs[: ranks - 1]
    own_ref, col_ref, row_ref, span_ref, w_ref = refs[ranks - 1 : ranks + 4]
    soft_ref, att_ref, pre_ref, q_ref, k_t_ref, v_ref = refs[ranks + 4 : ranks + 10]
    att_t_ref, k_full, q_full, w_own, w_sem = refs[ranks + 10 :]
    me = lax.axis_index("seq")
    length = ranks * frames
    copy = pltpu.make_async_copy(w_ref.at[:, lanes_at(me)], w_own, w_sem)
    copy.start()
    for place, target in enumerate((q_full, k_full, v_ref)):
        target[rows_at(me, frames), :] = own_ref[place]
        for step in range(1, ranks):
            target[rows_at(me ^ step, frames), :] = recvs[ranks - 1 - step][place]
    heads = LANES // HDIM
    lane_head = lax.broadcasted_iota(jnp.int32, (1, LANES), 1) // HDIM
    scaled = q_full[...].astype(jnp.float32) * (1.0 / math.sqrt(HDIM))
    for head in range(heads):
        q_ref[head] = jnp.where(lane_head == head, scaled, 0.0).astype(jnp.bfloat16)
    k_t_ref[...] = k_full[...].astype(jnp.float32).T.astype(jnp.bfloat16)
    v_t = v_ref[...].astype(jnp.float32).T.astype(jnp.bfloat16)
    wide = 512
    for head in range(heads):
        for start in range(0, length, wide):
            cols = slice(start, start + wide)
            raw = mm_nt(k_full[...], q_ref[head, cols, :])
            same = jnp.concatenate([col_ref[...]] * (wide // LANES), axis=1) == row_ref[0:1, cols]
            scores = jnp.where(same, raw, NEGATIVE_FILL)
            top = jnp.max(scores, axis=0, keepdims=True)
            powers = jnp.exp(scores - top)
            share = 1.0 / jnp.sum(powers, axis=0, keepdims=True)
            soft = (powers * share).astype(jnp.bfloat16)
            soft_ref[head, :, cols] = soft
            rows = slice(head * HDIM, (head + 1) * HDIM)
            att_t_ref[rows, cols] = mm(v_t[rows], soft).astype(jnp.bfloat16).astype(jnp.float32)
    zeros = jnp.zeros((PAD, LANES), jnp.float32)
    att_ref[0:PAD, :] = zeros
    att_ref[PAD : PAD + length, :] = att_t_ref[...].T
    att_ref[PAD + length :, :] = zeros
    copy.wait()

    chunk = 64

    def some_rows(number, carry):
        base = pl.multiple_of(number * chunk, chunk)
        rows = pl.ds(base, chunk)
        total = jnp.zeros((chunk, LANES), jnp.float32)
        for tap in range(KERNEL):
            total = total + w_own[tap : tap + 1, :] * masked(att_ref, base, chunk, tap - HALF, span_ref)
        pre_ref[rows, :] = total
        return carry

    lax.fori_loop(0, length // chunk, some_rows, 0)


def span_kernel(after_ref, before_ref, span_ref):
    chunk = 64

    def some_rows(number, carry):
        rows = pl.ds(pl.multiple_of(number * chunk, chunk), chunk)
        after, before = after_ref[rows, :], before_ref[rows, :]
        for tap in range(KERNEL):
            off = tap - HALF
            inside = after >= off if off > 0 else before >= -off
            span_ref[tap, rows, :] = jnp.where(inside, 1.0, 0.0)
        return carry

    lax.fori_loop(0, after_ref.shape[0] // chunk, some_rows, 0)


def masked(source, base, chunk, off, span_ref):
    piece = source[pl.ds(base + (PAD + off), chunk), :]
    return piece * span_ref[HALF + off, pl.ds(base, chunk), :] if off else piece


def taps_kernel(ranks, frames, *refs):
    cots = refs[: ranks - 1]
    own_ref, att_ref, pre_ref, span_ref = refs[ranks - 1 : ranks + 3]
    mixed_ref, grad_pad, taps_ref, cot, tap_sum = refs[ranks + 3 :]
    me = lax.axis_index("seq")
    length = ranks * frames
    cot[rows_at(me, frames), :] = own_ref[3]
    for step in range(1, ranks):
        cot[rows_at(me ^ step, frames), :] = cots[ranks - 1 - step][...]
    zeros = jnp.zeros((PAD, LANES), jnp.float32)
    grad_pad[0:PAD, :] = zeros
    grad_pad[PAD + length :, :] = zeros
    tap_sum[...] = jnp.zeros(tap_sum.shape, jnp.float32)
    chunk = 64

    def some_rows(number, carry):
        base = pl.multiple_of(number * chunk, chunk)
        rows = pl.ds(base, chunk)
        pre = pre_ref[rows, :]
        gate = jax.nn.sigmoid(pre)
        mixed_ref[rows, :] = (pre * gate).astype(jnp.bfloat16)
        conv_grad = cot[rows, :].astype(jnp.float32) * gate * (1.0 + pre * (1.0 - gate))
        conv_grad = conv_grad.astype(jnp.bfloat16).astype(jnp.float32)
        grad_pad[pl.ds(base + PAD, chunk), :] = conv_grad
        for tap in range(KERNEL):
            part = conv_grad * masked(att_ref, base, chunk, tap - HALF, span_ref)
            tap_sum[tap] = tap_sum[tap] + jnp.sum(part.reshape(chunk // 8, 8, LANES), axis=0)
        return carry

    lax.fori_loop(0, length // chunk, some_rows, 0)
    taps_ref[...] = jnp.sum(tap_sum[...], axis=1)


def backward_kernel(soft_ref, att_ref, grad_pad, span_ref, q_ref, k_t_ref, v_ref, w_ref, *refs):
    res_q, res_k, res_v, g_att, grad_t, w_own, w_sem = refs
    length = v_ref.shape[0]
    copy = pltpu.make_async_copy(w_ref.at[:, lanes_at(lax.axis_index("seq"))], w_own, w_sem)
    copy.start()
    copy.wait()
    chunk = 64

    def some_rows(number, carry):
        base = pl.multiple_of(number * chunk, chunk)
        rows = pl.ds(base, chunk)
        total = jnp.zeros((chunk, LANES), jnp.float32)
        for tap in range(KERNEL):
            total = total + w_own[tap : tap + 1, :] * masked(grad_pad, base, chunk, HALF - tap, span_ref)
        g_att[rows, :] = total.astype(jnp.bfloat16)
        return carry

    lax.fori_loop(0, length // chunk, some_rows, 0)
    heads = LANES // HDIM
    lane_head = lax.broadcasted_iota(jnp.int32, (1, LANES), 1) // HDIM
    g_wide = g_att[...].astype(jnp.float32)
    products_t = (g_wide * att_ref[PAD : PAD + length, :]).T
    grad_v = jnp.zeros((length, LANES), jnp.float32)
    grad_k = jnp.zeros((length, LANES), jnp.float32)
    for head in range(heads):
        rows = slice(head * HDIM, (head + 1) * HDIM)
        g_head = jnp.where(lane_head == head, g_wide, 0.0).astype(jnp.bfloat16)
        delta = jnp.sum(products_t[rows], axis=0, keepdims=True)
        soft = soft_ref[head]
        slopes = mm_nt(v_ref[...], g_head)
        mixed_grad = (soft.astype(jnp.float32) * (slopes - delta)).astype(jnp.bfloat16)
        grad_v = grad_v + mm(soft, g_head)
        grad_k = grad_k + mm(mixed_grad, q_ref[head])
        grad_t[rows, :] = mm(k_t_ref[rows, :], mixed_grad) * (1.0 / math.sqrt(HDIM))
    res_k[...] = grad_k.astype(jnp.bfloat16)
    res_v[...] = grad_v.astype(jnp.bfloat16)
    res_q[...] = grad_t[...].T.astype(jnp.bfloat16)


def block_kernel(steps, frames, *refs):
    sources, tap_refs, outs = refs[:4], refs[4 : -len(steps)], refs[-len(steps) :]
    me = lax.axis_index("seq")
    taps = tap_refs[0][...]
    for other in tap_refs[1:]:
        taps = taps + other[...]
    for step, out in zip(steps, outs):
        rows = rows_at(me ^ step, frames)
        for place, source in enumerate(sources):
            out[place * frames : (place + 1) * frames, :] = source[rows, :]
        out[4 * frames :, :] = taps.astype(jnp.bfloat16)


def spread_kernel(ranks, frames, *refs):
    blocks = refs[:ranks]
    targets, taps_ref = refs[ranks : ranks + 4], refs[ranks + 4]
    me = lax.axis_index("seq")
    for step in range(ranks):
        lanes = lanes_at(me ^ step)
        for place, target in enumerate(targets):
            target[0, :, lanes] = blocks[step][place * frames : (place + 1) * frames, :]
        taps = blocks[step][4 * frames :, :].astype(jnp.float32)
        taps_ref[:, lanes] = taps[:KERNEL]


def cost(flops, moved):
    return pl.CostEstimate(flops=flops, bytes_accessed=moved, transcendentals=0)


def on_device_heads(queries, keys, values, cotangent, conv_weight, rec_lengths):
    ranks = lax.axis_size("seq")
    frames = queries.shape[1]
    length = ranks * frames
    heads = LANES // HDIM
    bf16, f32, i32 = jnp.bfloat16, jnp.float32, jnp.int32
    struct = jax.ShapeDtypeStruct
    hbm = pl.BlockSpec(memory_space=pltpu.HBM)
    anywhere = pl.BlockSpec(memory_space=pl.ANY)
    vmem = pl.BlockSpec(memory_space=VMEM)
    smem = pl.BlockSpec(memory_space=pltpu.SMEM)
    params = pltpu.CompilerParams(vmem_limit_bytes=24 * MIB)
    taps = KERNEL + 1

    sends = pl.pallas_call(
        functools.partial(pack_kernel, ranks),
        out_shape=[struct((3, frames, LANES), bf16)] * (ranks - 1),
        in_specs=[hbm] * 3,
        out_specs=[vmem] * (ranks - 1),
        scratch_shapes=[pltpu.SemaphoreType.DMA((3 * (ranks - 1),))],
        compiler_params=pltpu.CompilerParams(vmem_limit_bytes=54912 * 1024),
        name="pack",
    )(queries, keys, values)

    def swap(array, step):
        return lax.ppermute(array, "seq", [(rank, rank ^ step) for rank in range(ranks)])

    order = list(range(ranks - 1, 0, -1))
    received = {step: swap(sends[step - 1], step) for step in order}

    *cot_sends, own, col, row, after, before = pl.pallas_call(
        functools.partial(mask_kernel, ranks, length),
        out_shape=[struct((frames, LANES), bf16)] * (ranks - 1)
        + [
            struct((4, frames, LANES), bf16),
            struct((length, LANES), i32),
            struct((8, length), i32),
            struct((length, LANES), i32),
            struct((length, LANES), i32),
        ],
        in_specs=[smem] + [hbm] * 4,
        out_specs=[vmem] * (ranks + 4),
        scratch_shapes=[pltpu.SemaphoreType.DMA((ranks + 3,))],
        compiler_params=params,
        cost_estimate=cost(4 * MIB, MIB),
        name="masks",
    )(rec_lengths, queries, keys, values, cotangent)
    cots = {step: swap(cot_sends[step - 1], step) for step in order}

    span = pl.pallas_call(
        span_kernel,
        out_shape=struct((KERNEL, length, LANES), f32),
        in_specs=[vmem] * 2,
        out_specs=vmem,
        compiler_params=params,
        cost_estimate=cost(400 * MIB, 3 * MIB),
        name="spans",
    )(after, before)

    soft, att, pre, q_heads, k_t, v_full = pl.pallas_call(
        functools.partial(forward_kernel, ranks, frames),
        out_shape=[
            struct((heads, length, length), bf16),
            struct((length + 2 * PAD, LANES), f32),
            struct((length, LANES), f32),
            struct((heads, length, LANES), bf16),
            struct((LANES, length), bf16),
            struct((length, LANES), bf16),
        ],
        in_specs=[vmem] * (ranks + 3) + [anywhere],
        out_specs=[vmem] * 6,
        scratch_shapes=[
            VMEM((LANES, length), f32),
            VMEM((length, LANES), bf16),
            VMEM((length, LANES), bf16),
            VMEM((KERNEL, LANES), f32),
            pltpu.SemaphoreType.DMA,
        ],
        compiler_params=params,
        cost_estimate=cost(400 * MIB, 3 * MIB),
        name="forward",
    )(*[received[step] for step in order], own, col, row, span, conv_weight)

    mixed, grad_pad, own_taps = pl.pallas_call(
        functools.partial(taps_kernel, ranks, frames),
        out_shape=[
            struct((length, LANES), bf16),
            struct((length + 2 * PAD, LANES), f32),
            struct((taps, LANES), f32),
        ],
        in_specs=[vmem] * (ranks + 3),
        out_specs=[vmem] * 3,
        scratch_shapes=[VMEM((length, LANES), bf16), VMEM((taps, 8, LANES), f32)],
        compiler_params=params,
        cost_estimate=cost(400 * MIB, 3 * MIB),
        name="taps",
    )(*[cots[step] for step in order], own, att, pre, span)

    copies = lax.axis_size("dp")
    part_taps = [own_taps] + [
        lax.ppermute(own_taps, "dp", [(one, (one + shift) % copies) for one in range(copies)])
        for shift in range(1, copies)
    ]

    results = pl.pallas_call(
        backward_kernel,
        out_shape=[struct((length, LANES), bf16)] * 3,
        in_specs=[vmem] * 7 + [anywhere],
        out_specs=[vmem] * 3,
        scratch_shapes=[
            VMEM((length, LANES), bf16),
            VMEM((LANES, length), f32),
            VMEM((KERNEL, LANES), f32),
            pltpu.SemaphoreType.DMA,
        ],
        compiler_params=params,
        cost_estimate=cost(800 * MIB, 3 * MIB),
        name="backward",
    )(soft, att, grad_pad, span, q_heads, k_t, v_full, conv_weight)

    def blocks_of(steps):
        return pl.pallas_call(
            functools.partial(block_kernel, steps, frames),
            out_shape=[struct((4 * frames + taps, LANES), bf16)] * len(steps),
            in_specs=[vmem] * (4 + copies),
            out_specs=[vmem] * len(steps),
            compiler_params=params,
            cost_estimate=cost(MIB, MIB),
            name="blocks",
        )(mixed, *results, *part_taps)

    half = ranks // 2
    far = blocks_of(list(range(half, ranks)))
    near = blocks_of(list(range(half)))
    back = {step: swap(far[step - half], step) for step in range(half, ranks)}
    back |= {step: swap(near[step], step) for step in range(1, half)}
    back[0] = near[0]

    return pl.pallas_call(
        functools.partial(spread_kernel, ranks, frames),
        out_shape=[struct(queries.shape, bf16)] * 4 + [struct(conv_weight.shape, f32)],
        in_specs=[vmem] * ranks,
        out_specs=[vmem] * 5,
        compiler_params=params,
        name="spread",
    )(*[back[step] for step in range(ranks)])


def on_device_any(queries, keys, values, cotangent, conv_weight, rec_lengths):
    ranks = lax.axis_size("seq")
    frames, channels = queries.shape[1], queries.shape[2]
    fits = channels == ranks * LANES and ranks & (ranks - 1) == 0 and frames % LANES == 0
    if fits and ranks > 1 and ranks * frames <= 1024 and lax.axis_size("dp") == 2:
        return on_device_heads(queries, keys, values, cotangent, conv_weight, rec_lengths)
    return on_device(queries, keys, values, cotangent, conv_weight, rec_lengths)


def solution(mesh):
    placed = (
        P(("groups", "dp"), "seq", "mp"),
        P(("groups", "dp"), "seq", "mp"),
        P(("groups", "dp"), "seq", "mp"),
        P(("groups", "dp"), "seq", "mp"),
        P(None, "mp"),
        P(("groups", "dp"), None),
    )
    return jax.shard_map(
        on_device_any,
        mesh=mesh,
        in_specs=placed,
        out_specs=(
            P(("groups", "dp"), "seq", "mp"),
            P(("groups", "dp"), "seq", "mp"),
            P(("groups", "dp"), "seq", "mp"),
            P(("groups", "dp"), "seq", "mp"),
            P("groups", "mp"),
        ),
        check_vma=False,
    )
```

```python
import functools
import math

import jax
import jax.numpy as jnp
from jax import lax
from jax.experimental import pallas as pl
from jax.experimental.pallas import tpu as pltpu
from jax.sharding import PartitionSpec as P

HDIM = 64
KERNEL = 31
HALF = 15


NEGATIVE_FILL = -1e30


def extended(block, sides, width):
    for axis, dim in sides:
        count = lax.axis_size(axis)
        forward = [(i, i + 1) for i in range(count - 1)]
        backward = [(target, source) for source, target in forward]
        low = lax.ppermute(
            lax.slice_in_dim(block, block.shape[dim] - width, None, axis=dim), axis, forward
        )
        high = lax.ppermute(lax.slice_in_dim(block, 0, width, axis=dim), axis, backward)
        block = jnp.concatenate([low, block, high], axis=dim)
    return block


def pick_block(total_rows):
    for candidate in (512, 256, 128):
        return candidate
    return total_rows


def over_blocks(total_rows, advance, initial):
    block_rows = pick_block(total_rows)
    block_count = total_rows // block_rows
    if block_count == 1:
        return advance(initial, 0, block_rows)
    return lax.fori_loop(
        0,
        block_count,
        lambda number, running: advance(running, number * block_rows, block_rows),
        initial,
    )


def when_shared(compute, running):
    result = compute(running)
    return result


def on_device(queries, keys, values, cotangent, conv_weight, rec_lengths):
    frames = queries.shape[1]
    channels = queries.shape[2]
    local_heads = channels // HDIM
    score_scale = 1.0 / math.sqrt(HDIM)
    length_all = frames * lax.axis_size("seq")
    offset = lax.axis_index("seq") * frames
    record_ends = jnp.cumsum(rec_lengths[0], dtype=jnp.int32)

    def segment_of(positions):
        return jnp.sum((record_ends[None, :] <= positions[:, None]).astype(jnp.int32), axis=1)

    own_seg = segment_of(offset + jnp.arange(frames, dtype=jnp.int32))

    def to_heads(array):
        return array.reshape(array.shape[0], local_heads, HDIM).transpose(1, 0, 2)

    def from_heads(array):
        return array.transpose(1, 0, 2).reshape(array.shape[1], channels)

    q_heads = to_heads(queries[0])
    k_heads = to_heads(keys[0])
    v_heads = to_heads(values[0])

    def over_rows(advance, initial, members, first_row):
        total_rows = members[0].shape[1]

        def one_block(running, block_start, block_rows):
            sliced = tuple(
                (lax.dynamic_slice_in_dim(member, block_start, block_rows, 1) for member in members)
            )
            other_seg = segment_of(
                first_row + block_start + jnp.arange(block_rows, dtype=jnp.int32)
            )
            return when_shared(lambda current: advance(current, sliced, other_seg), running)

        return over_blocks(total_rows, one_block, initial)

    def query_scores(key_block, key_seg):
        raw_scores = (
            jnp.einsum("hqd,hkd->hqk", q_heads, key_block, preferred_element_type=jnp.float32)
            * score_scale
        )
        return jnp.where((own_seg[:, None] == key_seg[None, :])[None], raw_scores, NEGATIVE_FILL)

    def stats_step(running, sliced, key_seg):
        top_now, total_now = running
        scores = query_scores(sliced[0], key_seg)
        top_new = jnp.maximum(top_now, jnp.max(scores, axis=2))
        total_new = total_now * jnp.exp(top_now - top_new) + jnp.sum(
            jnp.exp(scores - top_new[:, :, None]), axis=2
        )
        return (top_new, total_new)

    stats_init = (
        jnp.full((local_heads, frames), NEGATIVE_FILL, jnp.float32),
        jnp.zeros((local_heads, frames), jnp.float32),
    )
    gathered = (
        lax.all_gather(keys, "seq", axis=1, tiled=True),
        lax.all_gather(values, "seq", axis=1, tiled=True),
    )
    key_whole = to_heads(gathered[0][0])
    value_whole = to_heads(gathered[1][0])
    row_stats = over_rows(stats_step, stats_init, (key_whole,), 0)
    log_total = row_stats[0] + jnp.log(row_stats[1])

    def output_step(running, sliced, key_seg):
        scores = query_scores(sliced[0], key_seg)
        soft_rounded = jnp.exp(scores - log_total[:, :, None]).astype(jnp.bfloat16)
        return running + jnp.einsum(
            "hqk,hkd->hqd", soft_rounded, sliced[1], preferred_element_type=jnp.float32
        )

    frame_zeros = jnp.zeros((local_heads, frames, HDIM), jnp.float32)
    attended_sum = over_rows(output_step, frame_zeros, (key_whole, value_whole), 0)
    attended_heads = attended_sum.astype(jnp.bfloat16)
    attended = from_heads(attended_heads)
    padded = extended(attended[None], (("seq", 1),), HALF)
    padded_wide = padded[0].astype(jnp.float32)
    pad_positions = offset - HALF + jnp.arange(frames + 2 * HALF, dtype=jnp.int32)
    inside = jnp.logical_and(pad_positions >= 0, pad_positions < length_all)
    pad_seg = jnp.where(inside, segment_of(pad_positions), -1)
    conv_pre = jnp.zeros((frames, channels), jnp.float32)
    for tap_index in range(KERNEL):
        tap_mask = (pad_seg[tap_index : tap_index + frames] == own_seg)[:, None]
        conv_pre = conv_pre + jnp.where(
            tap_mask, conv_weight[tap_index] * padded_wide[tap_index : tap_index + frames], 0.0
        )
    gate_value = jax.nn.sigmoid(conv_pre)
    mixed = (conv_pre * gate_value).astype(jnp.bfloat16)
    conv_grad = (
        cotangent[0].astype(jnp.float32) * gate_value * (1.0 + conv_pre * (1.0 - gate_value))
    ).astype(jnp.bfloat16)
    padded_grad = extended(conv_grad[None], (("seq", 1),), HALF)
    grad_wide = padded_grad[0].astype(jnp.float32)
    conv_grad_wide = conv_grad.astype(jnp.float32)
    grad_attended = jnp.zeros((frames, channels), jnp.float32)
    kernel_rows = []
    for tap_index in range(KERNEL):
        back_start = 2 * HALF - tap_index
        back_mask = (pad_seg[back_start : back_start + frames] == own_seg)[:, None]
        grad_attended = grad_attended + jnp.where(
            back_mask, conv_weight[tap_index] * grad_wide[back_start : back_start + frames], 0.0
        )
        tap_mask = (pad_seg[tap_index : tap_index + frames] == own_seg)[:, None]
        product = conv_grad_wide * padded_wide[tap_index : tap_index + frames]
        kernel_rows.append(jnp.sum(jnp.where(tap_mask, product, 0.0), axis=0))
    grad_kernel = lax.psum(jnp.stack(kernel_rows), ("dp", "seq"))
    grad_attended = grad_attended.astype(jnp.bfloat16)
    g_heads = to_heads(grad_attended)
    row_delta = jnp.sum(g_heads.astype(jnp.float32) * attended_heads.astype(jnp.float32), axis=2)

    def query_grad_step(running, sliced, key_seg):
        key_block = sliced[0]
        value_block = sliced[1]
        soft_weights = jnp.exp(query_scores(key_block, key_seg) - log_total[:, :, None])
        slopes = jnp.einsum(
            "hqd,hkd->hqk", g_heads, value_block, preferred_element_type=jnp.float32
        )
        mixed_grad = (soft_weights * (slopes - row_delta[:, :, None])).astype(jnp.bfloat16)
        return running + jnp.einsum(
            "hqk,hkd->hqd", mixed_grad, key_block, preferred_element_type=jnp.float32
        )

    grad_query = over_rows(query_grad_step, frame_zeros, (key_whole, value_whole), 0)

    def key_grad_step(running, sliced, query_seg):
        grad_key_now, grad_value_now = running
        query_block = sliced[0]
        grad_block = sliced[1]
        total_block = sliced[2]
        delta_block = sliced[3]
        raw_scores = (
            jnp.einsum("hqd,hkd->hqk", query_block, k_heads, preferred_element_type=jnp.float32)
            * score_scale
        )
        scores = jnp.where(
            (query_seg[:, None] == own_seg[None, :])[None], raw_scores, NEGATIVE_FILL
        )
        soft_weights = jnp.exp(scores - total_block[:, :, None])
        grad_value_new = grad_value_now + jnp.einsum(
            "hqk,hqd->hkd",
            soft_weights.astype(jnp.bfloat16),
            grad_block,
            preferred_element_type=jnp.float32,
        )
        slopes = jnp.einsum("hqd,hkd->hqk", grad_block, v_heads, preferred_element_type=jnp.float32)
        mixed_grad = (soft_weights * (slopes - delta_block[:, :, None])).astype(jnp.bfloat16)
        grad_key_new = grad_key_now + jnp.einsum(
            "hqk,hqd->hkd", mixed_grad, query_block, preferred_element_type=jnp.float32
        )
        return (grad_key_new, grad_value_new)

    all_totals, all_deltas = (
        lax.all_gather(log_total[None], "seq", axis=2, tiled=True),
        lax.all_gather(row_delta[None], "seq", axis=2, tiled=True),
    )
    member = (
        lax.all_gather(queries, "seq", axis=1, tiled=True),
        lax.all_gather(grad_attended[None], "seq", axis=1, tiled=True),
    )
    totals_piece = all_totals[0]
    deltas_piece = all_deltas[0]
    grad_key, grad_value = over_rows(
        key_grad_step,
        (frame_zeros, frame_zeros),
        (to_heads(member[0][0]), to_heads(member[1][0]), totals_piece, deltas_piece),
        jnp.int32(0),
    )
    grad_queries = from_heads(grad_query * score_scale).astype(jnp.bfloat16)[None]
    grad_keys = from_heads(grad_key * score_scale).astype(jnp.bfloat16)[None]
    grad_values = from_heads(grad_value).astype(jnp.bfloat16)[None]
    return (mixed[None], grad_queries, grad_keys, grad_values, grad_kernel)


LANES = 128
PAD = 16
VMEM = pltpu.VMEM
MIB = 1024 * 1024


def mm(left, right):
    return lax.dot_general(
        left, right, (((1,), (0,)), ((), ())), preferred_element_type=jnp.float32
    )


def mm_nt(left, right):
    return lax.dot_general(
        left, right, (((1,), (1,)), ((), ())), preferred_element_type=jnp.float32
    )


def rows_at(block, frames):
    return pl.ds(pl.multiple_of(block * frames, frames), frames)


def lanes_at(block):
    return pl.ds(pl.multiple_of(block * LANES, LANES), LANES)


def pack_kernel(ranks, q_ref, k_ref, v_ref, c_ref, *rest):
    outs, sems = rest[:-1], rest[-1]
    me = lax.axis_index("seq")
    pairs = []
    for step in range(ranks - 1, 0, -1):
        for place, source in enumerate((q_ref, k_ref, v_ref)):
            pairs.append((source.at[0, :, lanes_at(me ^ step)], outs[step - 1].at[place]))
        pairs.append((c_ref.at[0, :, lanes_at(me ^ step)], outs[ranks + step - 2]))
    for place, source in enumerate((q_ref, k_ref, v_ref, c_ref)):
        pairs.append((source.at[0, :, lanes_at(me)], outs[-1].at[place]))
    run_copies(pairs, sems)


def run_copies(pairs, sems, meanwhile=None):
    copies = [
        pltpu.make_async_copy(source, target, sems.at[number])
        for number, (source, target) in enumerate(pairs)
    ]
    for copy in copies:
        copy.start()
    if meanwhile is not None:
        meanwhile()
    for copy in copies:
        copy.wait()


def mask_kernel(length, lens_ref, *refs):
    col_ref, row_ref, after_ref, before_ref = refs[-4:]
    count = (len(refs) - 4) // 2
    for source, target in zip(refs[:count], refs[count:]):
        target[...] = source[...]
    ends = []
    running = jnp.int32(0)
    for number in range(lens_ref.shape[1]):
        running = running + lens_ref[0, number]
        ends.append(running)
    row_time = lax.broadcasted_iota(jnp.int32, row_ref.shape, 1)
    row_first = jnp.zeros(row_ref.shape, jnp.int32)
    for end in ends:
        row_first = jnp.where(row_time >= end, end, row_first)
    row_ref[...] = row_first
    chunk = 64

    def some_rows(number, carry):
        base = pl.multiple_of(number * chunk, chunk)
        time = base + lax.broadcasted_iota(jnp.int32, (chunk, LANES), 0)
        first = jnp.zeros((chunk, LANES), jnp.int32)
        last = jnp.full((chunk, LANES), length, jnp.int32)
        for end in ends:
            first = jnp.where(time >= end, end, first)
        for end in reversed(ends):
            last = jnp.where(time < end, end, last)
        rows = pl.ds(base, chunk)
        col_ref[rows, :] = first
        after_ref[rows, :] = last - 1 - time
        before_ref[rows, :] = time - first
        return carry

    lax.fori_loop(0, length // chunk, some_rows, 0)


def forward_kernel(ranks, frames, *refs):
    recvs = refs[: ranks - 1]
    own_ref, col_ref, row_ref, span_ref, w_ref = refs[ranks - 1 : ranks + 4]
    soft_ref, att_ref, pre_ref, q_ref, k_t_ref, v_ref = refs[ranks + 4 : ranks + 10]
    att_t_ref, k_full, q_full, w_own, w_sem = refs[ranks + 10 :]
    me = lax.axis_index("seq")
    length = ranks * frames
    copy = pltpu.make_async_copy(w_ref.at[:, lanes_at(me)], w_own, w_sem)
    copy.start()
    for place, target in enumerate((q_full, k_full, v_ref)):
        target[rows_at(me, frames), :] = own_ref[place]
        for step in range(1, ranks):
            target[rows_at(me ^ step, frames), :] = recvs[ranks - 1 - step][place]
    heads = LANES // HDIM
    lane_head = lax.broadcasted_iota(jnp.int32, (1, LANES), 1) // HDIM
    scaled = q_full[...].astype(jnp.float32) * (1.0 / math.sqrt(HDIM))
    for head in range(heads):
        q_ref[head] = jnp.where(lane_head == head, scaled, 0.0).astype(jnp.bfloat16)
    k_t_ref[...] = k_full[...].astype(jnp.float32).T.astype(jnp.bfloat16)
    v_t = v_ref[...].astype(jnp.float32).T.astype(jnp.bfloat16)
    wide = 512
    for head in range(heads):
        for start in range(0, length, wide):
            cols = slice(start, start + wide)
            raw = mm_nt(k_full[...], q_ref[head, cols, :])
            same = jnp.concatenate([col_ref[...]] * (wide // LANES), axis=1) == row_ref[0:1, cols]
            scores = jnp.where(same, raw, NEGATIVE_FILL)
            top = jnp.max(scores, axis=0, keepdims=True)
            powers = jnp.exp(scores - top)
            share = 1.0 / jnp.sum(powers, axis=0, keepdims=True)
            soft = (powers * share).astype(jnp.bfloat16)
            soft_ref[head, :, cols] = soft
            rows = slice(head * HDIM, (head + 1) * HDIM)
            att_t_ref[rows, cols] = mm(v_t[rows], soft).astype(jnp.bfloat16).astype(jnp.float32)
    zeros = jnp.zeros((PAD, LANES), jnp.float32)
    att_ref[0:PAD, :] = zeros
    att_ref[PAD : PAD + length, :] = att_t_ref[...].T
    att_ref[PAD + length :, :] = zeros
    copy.wait()

    chunk = 64

    def some_rows(number, carry):
        base = pl.multiple_of(number * chunk, chunk)
        rows = pl.ds(base, chunk)
        total = jnp.zeros((chunk, LANES), jnp.float32)
        for tap in range(KERNEL):
            total = total + w_own[tap : tap + 1, :] * masked(att_ref, base, chunk, tap - HALF, span_ref)
        pre_ref[rows, :] = total
        return carry

    lax.fori_loop(0, length // chunk, some_rows, 0)


def span_kernel(after_ref, before_ref, span_ref):
    chunk = 64

    def some_rows(number, carry):
        rows = pl.ds(pl.multiple_of(number * chunk, chunk), chunk)
        after, before = after_ref[rows, :], before_ref[rows, :]
        for tap in range(KERNEL):
            off = tap - HALF
            inside = after >= off if off > 0 else before >= -off
            span_ref[tap, rows, :] = jnp.where(inside, 1.0, 0.0)
        return carry

    lax.fori_loop(0, after_ref.shape[0] // chunk, some_rows, 0)


def masked(source, base, chunk, off, span_ref):
    piece = source[pl.ds(base + (PAD + off), chunk), :]
    return piece * span_ref[HALF + off, pl.ds(base, chunk), :] if off else piece


def taps_kernel(ranks, frames, *refs):
    cots = refs[: ranks - 1]
    own_ref, att_ref, pre_ref, span_ref = refs[ranks - 1 : ranks + 3]
    mixed_ref, grad_pad, taps_ref, cot, tap_sum = refs[ranks + 3 :]
    me = lax.axis_index("seq")
    length = ranks * frames
    cot[rows_at(me, frames), :] = own_ref[3]
    for step in range(1, ranks):
        cot[rows_at(me ^ step, frames), :] = cots[ranks - 1 - step][...]
    zeros = jnp.zeros((PAD, LANES), jnp.float32)
    grad_pad[0:PAD, :] = zeros
    grad_pad[PAD + length :, :] = zeros
    tap_sum[...] = jnp.zeros(tap_sum.shape, jnp.float32)
    chunk = 64

    def some_rows(number, carry):
        base = pl.multiple_of(number * chunk, chunk)
        rows = pl.ds(base, chunk)
        pre = pre_ref[rows, :]
        gate = jax.nn.sigmoid(pre)
        mixed_ref[rows, :] = (pre * gate).astype(jnp.bfloat16)
        conv_grad = cot[rows, :].astype(jnp.float32) * gate * (1.0 + pre * (1.0 - gate))
        conv_grad = conv_grad.astype(jnp.bfloat16).astype(jnp.float32)
        grad_pad[pl.ds(base + PAD, chunk), :] = conv_grad
        for tap in range(KERNEL):
            part = conv_grad * masked(att_ref, base, chunk, tap - HALF, span_ref)
            tap_sum[tap] = tap_sum[tap] + jnp.sum(part.reshape(chunk // 8, 8, LANES), axis=0)
        return carry

    lax.fori_loop(0, length // chunk, some_rows, 0)
    taps_ref[...] = jnp.sum(tap_sum[...], axis=1)


def backward_kernel(soft_ref, att_ref, grad_pad, span_ref, q_ref, k_t_ref, v_ref, w_ref, *refs):
    res_q, res_k, res_v, g_att, grad_t, w_own, w_sem = refs
    length = v_ref.shape[0]
    copy = pltpu.make_async_copy(w_ref.at[:, lanes_at(lax.axis_index("seq"))], w_own, w_sem)
    copy.start()
    copy.wait()
    chunk = 64

    def some_rows(number, carry):
        base = pl.multiple_of(number * chunk, chunk)
        rows = pl.ds(base, chunk)
        total = jnp.zeros((chunk, LANES), jnp.float32)
        for tap in range(KERNEL):
            total = total + w_own[tap : tap + 1, :] * masked(grad_pad, base, chunk, HALF - tap, span_ref)
        g_att[rows, :] = total.astype(jnp.bfloat16)
        return carry

    lax.fori_loop(0, length // chunk, some_rows, 0)
    heads = LANES // HDIM
    lane_head = lax.broadcasted_iota(jnp.int32, (1, LANES), 1) // HDIM
    g_wide = g_att[...].astype(jnp.float32)
    products_t = (g_wide * att_ref[PAD : PAD + length, :]).T
    grad_v = jnp.zeros((length, LANES), jnp.float32)
    grad_k = jnp.zeros((length, LANES), jnp.float32)
    for head in range(heads):
        rows = slice(head * HDIM, (head + 1) * HDIM)
        g_head = jnp.where(lane_head == head, g_wide, 0.0).astype(jnp.bfloat16)
        delta = jnp.sum(products_t[rows], axis=0, keepdims=True)
        soft = soft_ref[head]
        slopes = mm_nt(v_ref[...], g_head)
        mixed_grad = (soft.astype(jnp.float32) * (slopes - delta)).astype(jnp.bfloat16)
        grad_v = grad_v + mm(soft, g_head)
        grad_k = grad_k + mm(mixed_grad, q_ref[head])
        grad_t[rows, :] = mm(k_t_ref[rows, :], mixed_grad) * (1.0 / math.sqrt(HDIM))
    res_k[...] = grad_k.astype(jnp.bfloat16)
    res_v[...] = grad_v.astype(jnp.bfloat16)
    res_q[...] = grad_t[...].T.astype(jnp.bfloat16)


def block_kernel(steps, frames, *refs):
    sources, tap_refs, outs = refs[:4], refs[4 : -len(steps)], refs[-len(steps) :]
    me = lax.axis_index("seq")
    taps = tap_refs[0][...]
    for other in tap_refs[1:]:
        taps = taps + other[...]
    for step, out in zip(steps, outs):
        rows = rows_at(me ^ step, frames)
        for place, source in enumerate(sources):
            out[place * frames : (place + 1) * frames, :] = source[rows, :]
        out[4 * frames :, :] = taps.astype(jnp.bfloat16)


def spread_kernel(ranks, frames, *refs):
    blocks = refs[:ranks]
    targets, taps_ref = refs[ranks : ranks + 4], refs[ranks + 4]
    me = lax.axis_index("seq")
    for step in range(ranks):
        lanes = lanes_at(me ^ step)
        for place, target in enumerate(targets):
            target[0, :, lanes] = blocks[step][place * frames : (place + 1) * frames, :]
        taps = blocks[step][4 * frames :, :].astype(jnp.float32)
        taps_ref[:, lanes] = taps[:KERNEL]


def cost(flops, moved):
    return pl.CostEstimate(flops=flops, bytes_accessed=moved, transcendentals=0)


def on_device_heads(queries, keys, values, cotangent, conv_weight, rec_lengths):
    ranks = lax.axis_size("seq")
    frames = queries.shape[1]
    length = ranks * frames
    heads = LANES // HDIM
    bf16, f32, i32 = jnp.bfloat16, jnp.float32, jnp.int32
    struct = jax.ShapeDtypeStruct
    hbm = pl.BlockSpec(memory_space=pltpu.HBM)
    anywhere = pl.BlockSpec(memory_space=pl.ANY)
    vmem = pl.BlockSpec(memory_space=VMEM)
    smem = pl.BlockSpec(memory_space=pltpu.SMEM)
    params = pltpu.CompilerParams(vmem_limit_bytes=24 * MIB)
    taps = KERNEL + 1

    *sends, own = pl.pallas_call(
        functools.partial(pack_kernel, ranks),
        out_shape=[struct((3, frames, LANES), bf16)] * (ranks - 1)
        + [struct((frames, LANES), bf16)] * (ranks - 1)
        + [struct((4, frames, LANES), bf16)],
        in_specs=[hbm] * 4,
        out_specs=[vmem] * (2 * ranks - 1),
        scratch_shapes=[pltpu.SemaphoreType.DMA((4 * ranks,))],
        compiler_params=pltpu.CompilerParams(vmem_limit_bytes=54672 * 1024),
        name="pack",
    )(queries, keys, values, cotangent)

    def swap(array, step):
        return lax.ppermute(array, "seq", [(rank, rank ^ step) for rank in range(ranks)])

    order = list(range(ranks - 1, 0, -1))
    received = {step: swap(sends[step - 1], step) for step in order}

    *cot_sends, col, row, after, before = pl.pallas_call(
        functools.partial(mask_kernel, length),
        out_shape=[struct((frames, LANES), bf16)] * (ranks - 1)
        + [
            struct((length, LANES), i32),
            struct((8, length), i32),
            struct((length, LANES), i32),
            struct((length, LANES), i32),
        ],
        in_specs=[smem] + [vmem] * (ranks - 1),
        out_specs=[vmem] * (ranks + 3),
        compiler_params=params,
        cost_estimate=cost(4 * MIB, MIB),
        name="masks",
    )(rec_lengths, *sends[ranks - 1 :])
    cots = {step: swap(cot_sends[step - 1], step) for step in order}

    span = pl.pallas_call(
        span_kernel,
        out_shape=struct((KERNEL, length, LANES), f32),
        in_specs=[vmem] * 2,
        out_specs=vmem,
        compiler_params=params,
        cost_estimate=cost(400 * MIB, 3 * MIB),
        name="spans",
    )(after, before)

    soft, att, pre, q_heads, k_t, v_full = pl.pallas_call(
        functools.partial(forward_kernel, ranks, frames),
        out_shape=[
            struct((heads, length, length), bf16),
            struct((length + 2 * PAD, LANES), f32),
            struct((length, LANES), f32),
            struct((heads, length, LANES), bf16),
            struct((LANES, length), bf16),
            struct((length, LANES), bf16),
        ],
        in_specs=[vmem] * (ranks + 3) + [anywhere],
        out_specs=[vmem] * 6,
        scratch_shapes=[
            VMEM((LANES, length), f32),
            VMEM((length, LANES), bf16),
            VMEM((length, LANES), bf16),
            VMEM((KERNEL, LANES), f32),
            pltpu.SemaphoreType.DMA,
        ],
        compiler_params=params,
        cost_estimate=cost(400 * MIB, 3 * MIB),
        name="forward",
    )(*[received[step] for step in order], own, col, row, span, conv_weight)

    mixed, grad_pad, own_taps = pl.pallas_call(
        functools.partial(taps_kernel, ranks, frames),
        out_shape=[
            struct((length, LANES), bf16),
            struct((length + 2 * PAD, LANES), f32),
            struct((taps, LANES), f32),
        ],
        in_specs=[vmem] * (ranks + 3),
        out_specs=[vmem] * 3,
        scratch_shapes=[VMEM((length, LANES), bf16), VMEM((taps, 8, LANES), f32)],
        compiler_params=params,
        cost_estimate=cost(400 * MIB, 3 * MIB),
        name="taps",
    )(*[cots[step] for step in order], own, att, pre, span)

    copies = lax.axis_size("dp")
    part_taps = [own_taps] + [
        lax.ppermute(own_taps, "dp", [(one, (one + shift) % copies) for one in range(copies)])
        for shift in range(1, copies)
    ]

    results = pl.pallas_call(
        backward_kernel,
        out_shape=[struct((length, LANES), bf16)] * 3,
        in_specs=[vmem] * 7 + [anywhere],
        out_specs=[vmem] * 3,
        scratch_shapes=[
            VMEM((length, LANES), bf16),
            VMEM((LANES, length), f32),
            VMEM((KERNEL, LANES), f32),
            pltpu.SemaphoreType.DMA,
        ],
        compiler_params=params,
        cost_estimate=cost(800 * MIB, 3 * MIB),
        name="backward",
    )(soft, att, grad_pad, span, q_heads, k_t, v_full, conv_weight)

    def blocks_of(steps):
        return pl.pallas_call(
            functools.partial(block_kernel, steps, frames),
            out_shape=[struct((4 * frames + taps, LANES), bf16)] * len(steps),
            in_specs=[vmem] * (4 + copies),
            out_specs=[vmem] * len(steps),
            compiler_params=params,
            cost_estimate=cost(MIB, MIB),
            name="blocks",
        )(mixed, *results, *part_taps)

    half = ranks // 2
    far = blocks_of(list(range(half, ranks)))
    near = blocks_of(list(range(half)))
    back = {step: swap(far[step - half], step) for step in range(half, ranks)}
    back |= {step: swap(near[step], step) for step in range(1, half)}
    back[0] = near[0]

    return pl.pallas_call(
        functools.partial(spread_kernel, ranks, frames),
        out_shape=[struct(queries.shape, bf16)] * 4 + [struct(conv_weight.shape, f32)],
        in_specs=[vmem] * ranks,
        out_specs=[vmem] * 5,
        compiler_params=params,
        name="spread",
    )(*[back[step] for step in range(ranks)])


def on_device_any(queries, keys, values, cotangent, conv_weight, rec_lengths):
    ranks = lax.axis_size("seq")
    frames, channels = queries.shape[1], queries.shape[2]
    fits = channels == ranks * LANES and ranks & (ranks - 1) == 0 and frames % LANES == 0
    if fits and ranks > 1 and ranks * frames <= 1024 and lax.axis_size("dp") == 2:
        return on_device_heads(queries, keys, values, cotangent, conv_weight, rec_lengths)
    return on_device(queries, keys, values, cotangent, conv_weight, rec_lengths)


def solution(mesh):
    placed = (
        P(("groups", "dp"), "seq", "mp"),
        P(("groups", "dp"), "seq", "mp"),
        P(("groups", "dp"), "seq", "mp"),
        P(("groups", "dp"), "seq", "mp"),
        P(None, "mp"),
        P(("groups", "dp"), None),
    )
    return jax.shard_map(
        on_device_any,
        mesh=mesh,
        in_specs=placed,
        out_specs=(
            P(("groups", "dp"), "seq", "mp"),
            P(("groups", "dp"), "seq", "mp"),
            P(("groups", "dp"), "seq", "mp"),
            P(("groups", "dp"), "seq", "mp"),
            P("groups", "mp"),
        ),
        check_vma=False,
    )
```

```python
import functools
import math

import jax
import jax.numpy as jnp
from jax import lax
from jax.experimental import pallas as pl
from jax.experimental.pallas import tpu as pltpu
from jax.sharding import PartitionSpec as P

HDIM = 64
KERNEL = 31
HALF = 15


NEGATIVE_FILL = -1e30


def extended(block, sides, width):
    for axis, dim in sides:
        count = lax.axis_size(axis)
        forward = [(i, i + 1) for i in range(count - 1)]
        backward = [(target, source) for source, target in forward]
        low = lax.ppermute(
            lax.slice_in_dim(block, block.shape[dim] - width, None, axis=dim), axis, forward
        )
        high = lax.ppermute(lax.slice_in_dim(block, 0, width, axis=dim), axis, backward)
        block = jnp.concatenate([low, block, high], axis=dim)
    return block


def pick_block(total_rows):
    for candidate in (512, 256, 128):
        return candidate
    return total_rows


def over_blocks(total_rows, advance, initial):
    block_rows = pick_block(total_rows)
    block_count = total_rows // block_rows
    if block_count == 1:
        return advance(initial, 0, block_rows)
    return lax.fori_loop(
        0,
        block_count,
        lambda number, running: advance(running, number * block_rows, block_rows),
        initial,
    )


def when_shared(compute, running):
    result = compute(running)
    return result


def on_device(queries, keys, values, cotangent, conv_weight, rec_lengths):
    frames = queries.shape[1]
    channels = queries.shape[2]
    local_heads = channels // HDIM
    score_scale = 1.0 / math.sqrt(HDIM)
    length_all = frames * lax.axis_size("seq")
    offset = lax.axis_index("seq") * frames
    record_ends = jnp.cumsum(rec_lengths[0], dtype=jnp.int32)

    def segment_of(positions):
        return jnp.sum((record_ends[None, :] <= positions[:, None]).astype(jnp.int32), axis=1)

    own_seg = segment_of(offset + jnp.arange(frames, dtype=jnp.int32))

    def to_heads(array):
        return array.reshape(array.shape[0], local_heads, HDIM).transpose(1, 0, 2)

    def from_heads(array):
        return array.transpose(1, 0, 2).reshape(array.shape[1], channels)

    q_heads = to_heads(queries[0])
    k_heads = to_heads(keys[0])
    v_heads = to_heads(values[0])

    def over_rows(advance, initial, members, first_row):
        total_rows = members[0].shape[1]

        def one_block(running, block_start, block_rows):
            sliced = tuple(
                (lax.dynamic_slice_in_dim(member, block_start, block_rows, 1) for member in members)
            )
            other_seg = segment_of(
                first_row + block_start + jnp.arange(block_rows, dtype=jnp.int32)
            )
            return when_shared(lambda current: advance(current, sliced, other_seg), running)

        return over_blocks(total_rows, one_block, initial)

    def query_scores(key_block, key_seg):
        raw_scores = (
            jnp.einsum("hqd,hkd->hqk", q_heads, key_block, preferred_element_type=jnp.float32)
            * score_scale
        )
        return jnp.where((own_seg[:, None] == key_seg[None, :])[None], raw_scores, NEGATIVE_FILL)

    def stats_step(running, sliced, key_seg):
        top_now, total_now = running
        scores = query_scores(sliced[0], key_seg)
        top_new = jnp.maximum(top_now, jnp.max(scores, axis=2))
        total_new = total_now * jnp.exp(top_now - top_new) + jnp.sum(
            jnp.exp(scores - top_new[:, :, None]), axis=2
        )
        return (top_new, total_new)

    stats_init = (
        jnp.full((local_heads, frames), NEGATIVE_FILL, jnp.float32),
        jnp.zeros((local_heads, frames), jnp.float32),
    )
    gathered = (
        lax.all_gather(keys, "seq", axis=1, tiled=True),
        lax.all_gather(values, "seq", axis=1, tiled=True),
    )
    key_whole = to_heads(gathered[0][0])
    value_whole = to_heads(gathered[1][0])
    row_stats = over_rows(stats_step, stats_init, (key_whole,), 0)
    log_total = row_stats[0] + jnp.log(row_stats[1])

    def output_step(running, sliced, key_seg):
        scores = query_scores(sliced[0], key_seg)
        soft_rounded = jnp.exp(scores - log_total[:, :, None]).astype(jnp.bfloat16)
        return running + jnp.einsum(
            "hqk,hkd->hqd", soft_rounded, sliced[1], preferred_element_type=jnp.float32
        )

    frame_zeros = jnp.zeros((local_heads, frames, HDIM), jnp.float32)
    attended_sum = over_rows(output_step, frame_zeros, (key_whole, value_whole), 0)
    attended_heads = attended_sum.astype(jnp.bfloat16)
    attended = from_heads(attended_heads)
    padded = extended(attended[None], (("seq", 1),), HALF)
    padded_wide = padded[0].astype(jnp.float32)
    pad_positions = offset - HALF + jnp.arange(frames + 2 * HALF, dtype=jnp.int32)
    inside = jnp.logical_and(pad_positions >= 0, pad_positions < length_all)
    pad_seg = jnp.where(inside, segment_of(pad_positions), -1)
    conv_pre = jnp.zeros((frames, channels), jnp.float32)
    for tap_index in range(KERNEL):
        tap_mask = (pad_seg[tap_index : tap_index + frames] == own_seg)[:, None]
        conv_pre = conv_pre + jnp.where(
            tap_mask, conv_weight[tap_index] * padded_wide[tap_index : tap_index + frames], 0.0
        )
    gate_value = jax.nn.sigmoid(conv_pre)
    mixed = (conv_pre * gate_value).astype(jnp.bfloat16)
    conv_grad = (
        cotangent[0].astype(jnp.float32) * gate_value * (1.0 + conv_pre * (1.0 - gate_value))
    ).astype(jnp.bfloat16)
    padded_grad = extended(conv_grad[None], (("seq", 1),), HALF)
    grad_wide = padded_grad[0].astype(jnp.float32)
    conv_grad_wide = conv_grad.astype(jnp.float32)
    grad_attended = jnp.zeros((frames, channels), jnp.float32)
    kernel_rows = []
    for tap_index in range(KERNEL):
        back_start = 2 * HALF - tap_index
        back_mask = (pad_seg[back_start : back_start + frames] == own_seg)[:, None]
        grad_attended = grad_attended + jnp.where(
            back_mask, conv_weight[tap_index] * grad_wide[back_start : back_start + frames], 0.0
        )
        tap_mask = (pad_seg[tap_index : tap_index + frames] == own_seg)[:, None]
        product = conv_grad_wide * padded_wide[tap_index : tap_index + frames]
        kernel_rows.append(jnp.sum(jnp.where(tap_mask, product, 0.0), axis=0))
    grad_kernel = lax.psum(jnp.stack(kernel_rows), ("dp", "seq"))
    grad_attended = grad_attended.astype(jnp.bfloat16)
    g_heads = to_heads(grad_attended)
    row_delta = jnp.sum(g_heads.astype(jnp.float32) * attended_heads.astype(jnp.float32), axis=2)

    def query_grad_step(running, sliced, key_seg):
        key_block = sliced[0]
        value_block = sliced[1]
        soft_weights = jnp.exp(query_scores(key_block, key_seg) - log_total[:, :, None])
        slopes = jnp.einsum(
            "hqd,hkd->hqk", g_heads, value_block, preferred_element_type=jnp.float32
        )
        mixed_grad = (soft_weights * (slopes - row_delta[:, :, None])).astype(jnp.bfloat16)
        return running + jnp.einsum(
            "hqk,hkd->hqd", mixed_grad, key_block, preferred_element_type=jnp.float32
        )

    grad_query = over_rows(query_grad_step, frame_zeros, (key_whole, value_whole), 0)

    def key_grad_step(running, sliced, query_seg):
        grad_key_now, grad_value_now = running
        query_block = sliced[0]
        grad_block = sliced[1]
        total_block = sliced[2]
        delta_block = sliced[3]
        raw_scores = (
            jnp.einsum("hqd,hkd->hqk", query_block, k_heads, preferred_element_type=jnp.float32)
            * score_scale
        )
        scores = jnp.where(
            (query_seg[:, None] == own_seg[None, :])[None], raw_scores, NEGATIVE_FILL
        )
        soft_weights = jnp.exp(scores - total_block[:, :, None])
        grad_value_new = grad_value_now + jnp.einsum(
            "hqk,hqd->hkd",
            soft_weights.astype(jnp.bfloat16),
            grad_block,
            preferred_element_type=jnp.float32,
        )
        slopes = jnp.einsum("hqd,hkd->hqk", grad_block, v_heads, preferred_element_type=jnp.float32)
        mixed_grad = (soft_weights * (slopes - delta_block[:, :, None])).astype(jnp.bfloat16)
        grad_key_new = grad_key_now + jnp.einsum(
            "hqk,hqd->hkd", mixed_grad, query_block, preferred_element_type=jnp.float32
        )
        return (grad_key_new, grad_value_new)

    all_totals, all_deltas = (
        lax.all_gather(log_total[None], "seq", axis=2, tiled=True),
        lax.all_gather(row_delta[None], "seq", axis=2, tiled=True),
    )
    member = (
        lax.all_gather(queries, "seq", axis=1, tiled=True),
        lax.all_gather(grad_attended[None], "seq", axis=1, tiled=True),
    )
    totals_piece = all_totals[0]
    deltas_piece = all_deltas[0]
    grad_key, grad_value = over_rows(
        key_grad_step,
        (frame_zeros, frame_zeros),
        (to_heads(member[0][0]), to_heads(member[1][0]), totals_piece, deltas_piece),
        jnp.int32(0),
    )
    grad_queries = from_heads(grad_query * score_scale).astype(jnp.bfloat16)[None]
    grad_keys = from_heads(grad_key * score_scale).astype(jnp.bfloat16)[None]
    grad_values = from_heads(grad_value).astype(jnp.bfloat16)[None]
    return (mixed[None], grad_queries, grad_keys, grad_values, grad_kernel)


LANES = 128
PAD = 16
VMEM = pltpu.VMEM
MIB = 1024 * 1024


def mm(left, right):
    return lax.dot_general(
        left, right, (((1,), (0,)), ((), ())), preferred_element_type=jnp.float32
    )


def mm_nt(left, right):
    return lax.dot_general(
        left, right, (((1,), (1,)), ((), ())), preferred_element_type=jnp.float32
    )


def rows_at(block, frames):
    return pl.ds(pl.multiple_of(block * frames, frames), frames)


def lanes_at(block):
    return pl.ds(pl.multiple_of(block * LANES, LANES), LANES)


def pack_kernel(ranks, q_ref, k_ref, v_ref, c_ref, *rest):
    outs, sems = rest[:-1], rest[-1]
    me = lax.axis_index("seq")
    pairs = []
    for step in range(ranks - 1, 0, -1):
        for place, source in enumerate((q_ref, k_ref, v_ref)):
            pairs.append((source.at[0, :, lanes_at(me ^ step)], outs[step - 1].at[place]))
        pairs.append((c_ref.at[0, :, lanes_at(me ^ step)], outs[ranks + step - 2]))
    for place, source in enumerate((q_ref, k_ref, v_ref, c_ref)):
        pairs.append((source.at[0, :, lanes_at(me)], outs[-1].at[place]))
    run_copies(pairs, sems)


def run_copies(pairs, sems, meanwhile=None):
    copies = [
        pltpu.make_async_copy(source, target, sems.at[number])
        for number, (source, target) in enumerate(pairs)
    ]
    for copy in copies:
        copy.start()
    if meanwhile is not None:
        meanwhile()
    for copy in copies:
        copy.wait()


def mask_kernel(length, lens_ref, *refs):
    col_ref, row_ref, after_ref, before_ref = refs[-4:]
    count = (len(refs) - 4) // 2
    for source, target in zip(refs[:count], refs[count:]):
        target[...] = source[...]
    ends = []
    running = jnp.int32(0)
    for number in range(lens_ref.shape[1]):
        running = running + lens_ref[0, number]
        ends.append(running)
    row_time = lax.broadcasted_iota(jnp.int32, row_ref.shape, 1)
    row_first = jnp.zeros(row_ref.shape, jnp.int32)
    for end in ends:
        row_first = jnp.where(row_time >= end, end, row_first)
    row_ref[...] = row_first
    chunk = 64

    def some_rows(number, carry):
        base = pl.multiple_of(number * chunk, chunk)
        time = base + lax.broadcasted_iota(jnp.int32, (chunk, LANES), 0)
        first = jnp.zeros((chunk, LANES), jnp.int32)
        last = jnp.full((chunk, LANES), length, jnp.int32)
        for end in ends:
            first = jnp.where(time >= end, end, first)
        for end in reversed(ends):
            last = jnp.where(time < end, end, last)
        rows = pl.ds(base, chunk)
        col_ref[rows, :] = first
        after_ref[rows, :] = last - 1 - time
        before_ref[rows, :] = time - first
        return carry

    lax.fori_loop(0, length // chunk, some_rows, 0, unroll=True)


def forward_kernel(ranks, frames, *refs):
    recvs = refs[: ranks - 1]
    own_ref, col_ref, row_ref, span_ref, w_ref = refs[ranks - 1 : ranks + 4]
    soft_ref, att_ref, pre_ref, q_ref, k_t_ref, v_ref = refs[ranks + 4 : ranks + 10]
    att_t_ref, k_full, q_full, w_own, w_sem = refs[ranks + 10 :]
    me = lax.axis_index("seq")
    length = ranks * frames
    copy = pltpu.make_async_copy(w_ref.at[:, lanes_at(me)], w_own, w_sem)
    copy.start()
    for place, target in enumerate((q_full, k_full, v_ref)):
        target[rows_at(me, frames), :] = own_ref[place]
        for step in range(1, ranks):
            target[rows_at(me ^ step, frames), :] = recvs[ranks - 1 - step][place]
    heads = LANES // HDIM
    lane_head = lax.broadcasted_iota(jnp.int32, (1, LANES), 1) // HDIM
    scaled = q_full[...].astype(jnp.float32) * (1.0 / math.sqrt(HDIM))
    for head in range(heads):
        q_ref[head] = jnp.where(lane_head == head, scaled, 0.0).astype(jnp.bfloat16)
    k_t_ref[...] = k_full[...].astype(jnp.float32).T.astype(jnp.bfloat16)
    v_t = v_ref[...].astype(jnp.float32).T.astype(jnp.bfloat16)
    wide = 512
    for head in range(heads):
        for start in range(0, length, wide):
            cols = slice(start, start + wide)
            raw = mm_nt(k_full[...], q_ref[head, cols, :])
            same = jnp.concatenate([col_ref[...]] * (wide // LANES), axis=1) == row_ref[0:1, cols]
            scores = jnp.where(same, raw, NEGATIVE_FILL)
            top = jnp.max(scores, axis=0, keepdims=True)
            powers = jnp.exp(scores - top)
            share = 1.0 / jnp.sum(powers, axis=0, keepdims=True)
            soft = (powers * share).astype(jnp.bfloat16)
            soft_ref[head, :, cols] = soft
            rows = slice(head * HDIM, (head + 1) * HDIM)
            att_t_ref[rows, cols] = mm(v_t[rows], soft).astype(jnp.bfloat16).astype(jnp.float32)
    zeros = jnp.zeros((PAD, LANES), jnp.float32)
    att_ref[0:PAD, :] = zeros
    att_ref[PAD : PAD + length, :] = att_t_ref[...].T
    att_ref[PAD + length :, :] = zeros
    copy.wait()

    chunk = 64

    def some_rows(number, carry):
        base = pl.multiple_of(number * chunk, chunk)
        rows = pl.ds(base, chunk)
        total = jnp.zeros((chunk, LANES), jnp.float32)
        for tap in range(KERNEL):
            total = total + w_own[tap : tap + 1, :] * masked(att_ref, base, chunk, tap - HALF, span_ref)
        pre_ref[rows, :] = total
        return carry

    lax.fori_loop(0, length // chunk, some_rows, 0, unroll=True)


def span_kernel(after_ref, before_ref, span_ref):
    chunk = 64

    def some_rows(number, carry):
        rows = pl.ds(pl.multiple_of(number * chunk, chunk), chunk)
        after, before = after_ref[rows, :], before_ref[rows, :]
        for tap in range(KERNEL):
            off = tap - HALF
            inside = after >= off if off > 0 else before >= -off
            span_ref[tap, rows, :] = jnp.where(inside, 1.0, 0.0)
        return carry

    lax.fori_loop(0, after_ref.shape[0] // chunk, some_rows, 0)


def masked(source, base, chunk, off, span_ref):
    piece = source[pl.ds(base + (PAD + off), chunk), :]
    return piece * span_ref[HALF + off, pl.ds(base, chunk), :] if off else piece


def taps_kernel(ranks, frames, *refs):
    cots = refs[: ranks - 1]
    own_ref, att_ref, pre_ref, span_ref = refs[ranks - 1 : ranks + 3]
    mixed_ref, grad_pad, taps_ref, cot, tap_sum = refs[ranks + 3 :]
    me = lax.axis_index("seq")
    length = ranks * frames
    cot[rows_at(me, frames), :] = own_ref[3]
    for step in range(1, ranks):
        cot[rows_at(me ^ step, frames), :] = cots[ranks - 1 - step][...]
    zeros = jnp.zeros((PAD, LANES), jnp.float32)
    grad_pad[0:PAD, :] = zeros
    grad_pad[PAD + length :, :] = zeros
    tap_sum[...] = jnp.zeros(tap_sum.shape, jnp.float32)
    chunk = 64

    def some_rows(number, carry):
        base = pl.multiple_of(number * chunk, chunk)
        rows = pl.ds(base, chunk)
        pre = pre_ref[rows, :]
        gate = jax.nn.sigmoid(pre)
        mixed_ref[rows, :] = (pre * gate).astype(jnp.bfloat16)
        conv_grad = cot[rows, :].astype(jnp.float32) * gate * (1.0 + pre * (1.0 - gate))
        conv_grad = conv_grad.astype(jnp.bfloat16).astype(jnp.float32)
        grad_pad[pl.ds(base + PAD, chunk), :] = conv_grad
        for tap in range(KERNEL):
            part = conv_grad * masked(att_ref, base, chunk, tap - HALF, span_ref)
            tap_sum[tap] = tap_sum[tap] + jnp.sum(part.reshape(chunk // 8, 8, LANES), axis=0)
        return carry

    lax.fori_loop(0, length // chunk, some_rows, 0, unroll=True)
    taps_ref[...] = jnp.sum(tap_sum[...], axis=1)


def backward_kernel(soft_ref, att_ref, grad_pad, span_ref, q_ref, k_t_ref, v_ref, w_ref, *refs):
    res_q, res_k, res_v, g_att, grad_t, w_own, w_sem = refs
    length = v_ref.shape[0]
    copy = pltpu.make_async_copy(w_ref.at[:, lanes_at(lax.axis_index("seq"))], w_own, w_sem)
    copy.start()
    copy.wait()
    chunk = 64

    def some_rows(number, carry):
        base = pl.multiple_of(number * chunk, chunk)
        rows = pl.ds(base, chunk)
        total = jnp.zeros((chunk, LANES), jnp.float32)
        for tap in range(KERNEL):
            total = total + w_own[tap : tap + 1, :] * masked(grad_pad, base, chunk, HALF - tap, span_ref)
        g_att[rows, :] = total.astype(jnp.bfloat16)
        return carry

    lax.fori_loop(0, length // chunk, some_rows, 0, unroll=True)
    heads = LANES // HDIM
    lane_head = lax.broadcasted_iota(jnp.int32, (1, LANES), 1) // HDIM
    g_wide = g_att[...].astype(jnp.float32)
    products_t = (g_wide * att_ref[PAD : PAD + length, :]).T
    grad_v = jnp.zeros((length, LANES), jnp.float32)
    grad_k = jnp.zeros((length, LANES), jnp.float32)
    for head in range(heads):
        rows = slice(head * HDIM, (head + 1) * HDIM)
        g_head = jnp.where(lane_head == head, g_wide, 0.0).astype(jnp.bfloat16)
        delta = jnp.sum(products_t[rows], axis=0, keepdims=True)
        soft = soft_ref[head]
        slopes = mm_nt(v_ref[...], g_head)
        mixed_grad = (soft.astype(jnp.float32) * (slopes - delta)).astype(jnp.bfloat16)
        grad_v = grad_v + mm(soft, g_head)
        grad_k = grad_k + mm(mixed_grad, q_ref[head])
        grad_t[rows, :] = mm(k_t_ref[rows, :], mixed_grad) * (1.0 / math.sqrt(HDIM))
    res_k[...] = grad_k.astype(jnp.bfloat16)
    res_v[...] = grad_v.astype(jnp.bfloat16)
    res_q[...] = grad_t[...].T.astype(jnp.bfloat16)


def block_kernel(steps, frames, *refs):
    sources, tap_refs, outs = refs[:4], refs[4 : -len(steps)], refs[-len(steps) :]
    me = lax.axis_index("seq")
    taps = tap_refs[0][...]
    for other in tap_refs[1:]:
        taps = taps + other[...]
    for step, out in zip(steps, outs):
        rows = rows_at(me ^ step, frames)
        for place, source in enumerate(sources):
            out[place * frames : (place + 1) * frames, :] = source[rows, :]
        out[4 * frames :, :] = taps.astype(jnp.bfloat16)


def spread_kernel(ranks, frames, *refs):
    blocks = refs[:ranks]
    targets, taps_ref = refs[ranks : ranks + 4], refs[ranks + 4]
    me = lax.axis_index("seq")
    for step in range(ranks):
        lanes = lanes_at(me ^ step)
        for place, target in enumerate(targets):
            target[0, :, lanes] = blocks[step][place * frames : (place + 1) * frames, :]
        taps = blocks[step][4 * frames :, :].astype(jnp.float32)
        taps_ref[:, lanes] = taps[:KERNEL]


def cost(flops, moved):
    return pl.CostEstimate(flops=flops, bytes_accessed=moved, transcendentals=0)


def on_device_heads(queries, keys, values, cotangent, conv_weight, rec_lengths):
    ranks = lax.axis_size("seq")
    frames = queries.shape[1]
    length = ranks * frames
    heads = LANES // HDIM
    bf16, f32, i32 = jnp.bfloat16, jnp.float32, jnp.int32
    struct = jax.ShapeDtypeStruct
    hbm = pl.BlockSpec(memory_space=pltpu.HBM)
    anywhere = pl.BlockSpec(memory_space=pl.ANY)
    vmem = pl.BlockSpec(memory_space=VMEM)
    smem = pl.BlockSpec(memory_space=pltpu.SMEM)
    params = pltpu.CompilerParams(vmem_limit_bytes=24 * MIB)
    taps = KERNEL + 1

    *sends, own = pl.pallas_call(
        functools.partial(pack_kernel, ranks),
        out_shape=[struct((3, frames, LANES), bf16)] * (ranks - 1)
        + [struct((frames, LANES), bf16)] * (ranks - 1)
        + [struct((4, frames, LANES), bf16)],
        in_specs=[hbm] * 4,
        out_specs=[vmem] * (2 * ranks - 1),
        scratch_shapes=[pltpu.SemaphoreType.DMA((4 * ranks,))],
        compiler_params=pltpu.CompilerParams(vmem_limit_bytes=54672 * 1024),
        name="pack",
    )(queries, keys, values, cotangent)

    def swap(array, step):
        return lax.ppermute(array, "seq", [(rank, rank ^ step) for rank in range(ranks)])

    order = list(range(ranks - 1, 0, -1))
    received = {step: swap(sends[step - 1], step) for step in order}

    *cot_sends, col, row, after, before = pl.pallas_call(
        functools.partial(mask_kernel, length),
        out_shape=[struct((frames, LANES), bf16)] * (ranks - 1)
        + [
            struct((length, LANES), i32),
            struct((8, length), i32),
            struct((length, LANES), i32),
            struct((length, LANES), i32),
        ],
        in_specs=[smem] + [vmem] * (ranks - 1),
        out_specs=[vmem] * (ranks + 3),
        compiler_params=params,
        cost_estimate=cost(4 * MIB, MIB),
        name="masks",
    )(rec_lengths, *sends[ranks - 1 :])
    cots = {step: swap(cot_sends[step - 1], step) for step in order}

    span = pl.pallas_call(
        span_kernel,
        out_shape=struct((KERNEL, length, LANES), f32),
        in_specs=[vmem] * 2,
        out_specs=vmem,
        compiler_params=params,
        cost_estimate=cost(400 * MIB, 3 * MIB),
        name="spans",
    )(after, before)

    soft, att, pre, q_heads, k_t, v_full = pl.pallas_call(
        functools.partial(forward_kernel, ranks, frames),
        out_shape=[
            struct((heads, length, length), bf16),
            struct((length + 2 * PAD, LANES), f32),
            struct((length, LANES), f32),
            struct((heads, length, LANES), bf16),
            struct((LANES, length), bf16),
            struct((length, LANES), bf16),
        ],
        in_specs=[vmem] * (ranks + 3) + [anywhere],
        out_specs=[vmem] * 6,
        scratch_shapes=[
            VMEM((LANES, length), f32),
            VMEM((length, LANES), bf16),
            VMEM((length, LANES), bf16),
            VMEM((KERNEL, LANES), f32),
            pltpu.SemaphoreType.DMA,
        ],
        compiler_params=params,
        cost_estimate=cost(400 * MIB, 3 * MIB),
        name="forward",
    )(*[received[step] for step in order], own, col, row, span, conv_weight)

    mixed, grad_pad, own_taps = pl.pallas_call(
        functools.partial(taps_kernel, ranks, frames),
        out_shape=[
            struct((length, LANES), bf16),
            struct((length + 2 * PAD, LANES), f32),
            struct((taps, LANES), f32),
        ],
        in_specs=[vmem] * (ranks + 3),
        out_specs=[vmem] * 3,
        scratch_shapes=[VMEM((length, LANES), bf16), VMEM((taps, 8, LANES), f32)],
        compiler_params=params,
        cost_estimate=cost(400 * MIB, 3 * MIB),
        name="taps",
    )(*[cots[step] for step in order], own, att, pre, span)

    copies = lax.axis_size("dp")
    part_taps = [own_taps] + [
        lax.ppermute(own_taps, "dp", [(one, (one + shift) % copies) for one in range(copies)])
        for shift in range(1, copies)
    ]

    results = pl.pallas_call(
        backward_kernel,
        out_shape=[struct((length, LANES), bf16)] * 3,
        in_specs=[vmem] * 7 + [anywhere],
        out_specs=[vmem] * 3,
        scratch_shapes=[
            VMEM((length, LANES), bf16),
            VMEM((LANES, length), f32),
            VMEM((KERNEL, LANES), f32),
            pltpu.SemaphoreType.DMA,
        ],
        compiler_params=params,
        cost_estimate=cost(800 * MIB, 3 * MIB),
        name="backward",
    )(soft, att, grad_pad, span, q_heads, k_t, v_full, conv_weight)

    def blocks_of(steps):
        return pl.pallas_call(
            functools.partial(block_kernel, steps, frames),
            out_shape=[struct((4 * frames + taps, LANES), bf16)] * len(steps),
            in_specs=[vmem] * (4 + copies),
            out_specs=[vmem] * len(steps),
            compiler_params=params,
            cost_estimate=cost(MIB, MIB),
            name="blocks",
        )(mixed, *results, *part_taps)

    half = ranks // 2
    far = blocks_of(list(range(half, ranks)))
    near = blocks_of(list(range(half)))
    back = {step: swap(far[step - half], step) for step in range(half, ranks)}
    back |= {step: swap(near[step], step) for step in range(1, half)}
    back[0] = near[0]

    return pl.pallas_call(
        functools.partial(spread_kernel, ranks, frames),
        out_shape=[struct(queries.shape, bf16)] * 4 + [struct(conv_weight.shape, f32)],
        in_specs=[vmem] * ranks,
        out_specs=[vmem] * 5,
        compiler_params=params,
        name="spread",
    )(*[back[step] for step in range(ranks)])


def on_device_any(queries, keys, values, cotangent, conv_weight, rec_lengths):
    ranks = lax.axis_size("seq")
    frames, channels = queries.shape[1], queries.shape[2]
    fits = channels == ranks * LANES and ranks & (ranks - 1) == 0 and frames % LANES == 0
    if fits and ranks > 1 and ranks * frames <= 1024 and lax.axis_size("dp") == 2:
        return on_device_heads(queries, keys, values, cotangent, conv_weight, rec_lengths)
    return on_device(queries, keys, values, cotangent, conv_weight, rec_lengths)


def solution(mesh):
    placed = (
        P(("groups", "dp"), "seq", "mp"),
        P(("groups", "dp"), "seq", "mp"),
        P(("groups", "dp"), "seq", "mp"),
        P(("groups", "dp"), "seq", "mp"),
        P(None, "mp"),
        P(("groups", "dp"), None),
    )
    return jax.shard_map(
        on_device_any,
        mesh=mesh,
        in_specs=placed,
        out_specs=(
            P(("groups", "dp"), "seq", "mp"),
            P(("groups", "dp"), "seq", "mp"),
            P(("groups", "dp"), "seq", "mp"),
            P(("groups", "dp"), "seq", "mp"),
            P("groups", "mp"),
        ),
        check_vma=False,
    )
```

```python
import functools
import math

import jax
import jax.numpy as jnp
from jax import lax
from jax.experimental import pallas as pl
from jax.experimental.pallas import tpu as pltpu
from jax.sharding import PartitionSpec as P

HDIM = 64
KERNEL = 31
HALF = 15


NEGATIVE_FILL = -1e30


def extended(block, sides, width):
    for axis, dim in sides:
        count = lax.axis_size(axis)
        forward = [(i, i + 1) for i in range(count - 1)]
        backward = [(target, source) for source, target in forward]
        low = lax.ppermute(
            lax.slice_in_dim(block, block.shape[dim] - width, None, axis=dim), axis, forward
        )
        high = lax.ppermute(lax.slice_in_dim(block, 0, width, axis=dim), axis, backward)
        block = jnp.concatenate([low, block, high], axis=dim)
    return block


def pick_block(total_rows):
    for candidate in (512, 256, 128):
        return candidate
    return total_rows


def over_blocks(total_rows, advance, initial):
    block_rows = pick_block(total_rows)
    block_count = total_rows // block_rows
    if block_count == 1:
        return advance(initial, 0, block_rows)
    return lax.fori_loop(
        0,
        block_count,
        lambda number, running: advance(running, number * block_rows, block_rows),
        initial,
    )


def when_shared(compute, running):
    result = compute(running)
    return result


def on_device(queries, keys, values, cotangent, conv_weight, rec_lengths):
    frames = queries.shape[1]
    channels = queries.shape[2]
    local_heads = channels // HDIM
    score_scale = 1.0 / math.sqrt(HDIM)
    length_all = frames * lax.axis_size("seq")
    offset = lax.axis_index("seq") * frames
    record_ends = jnp.cumsum(rec_lengths[0], dtype=jnp.int32)

    def segment_of(positions):
        return jnp.sum((record_ends[None, :] <= positions[:, None]).astype(jnp.int32), axis=1)

    own_seg = segment_of(offset + jnp.arange(frames, dtype=jnp.int32))

    def to_heads(array):
        return array.reshape(array.shape[0], local_heads, HDIM).transpose(1, 0, 2)

    def from_heads(array):
        return array.transpose(1, 0, 2).reshape(array.shape[1], channels)

    q_heads = to_heads(queries[0])
    k_heads = to_heads(keys[0])
    v_heads = to_heads(values[0])

    def over_rows(advance, initial, members, first_row):
        total_rows = members[0].shape[1]

        def one_block(running, block_start, block_rows):
            sliced = tuple(
                (lax.dynamic_slice_in_dim(member, block_start, block_rows, 1) for member in members)
            )
            other_seg = segment_of(
                first_row + block_start + jnp.arange(block_rows, dtype=jnp.int32)
            )
            return when_shared(lambda current: advance(current, sliced, other_seg), running)

        return over_blocks(total_rows, one_block, initial)

    def query_scores(key_block, key_seg):
        raw_scores = (
            jnp.einsum("hqd,hkd->hqk", q_heads, key_block, preferred_element_type=jnp.float32)
            * score_scale
        )
        return jnp.where((own_seg[:, None] == key_seg[None, :])[None], raw_scores, NEGATIVE_FILL)

    def stats_step(running, sliced, key_seg):
        top_now, total_now = running
        scores = query_scores(sliced[0], key_seg)
        top_new = jnp.maximum(top_now, jnp.max(scores, axis=2))
        total_new = total_now * jnp.exp(top_now - top_new) + jnp.sum(
            jnp.exp(scores - top_new[:, :, None]), axis=2
        )
        return (top_new, total_new)

    stats_init = (
        jnp.full((local_heads, frames), NEGATIVE_FILL, jnp.float32),
        jnp.zeros((local_heads, frames), jnp.float32),
    )
    gathered = (
        lax.all_gather(keys, "seq", axis=1, tiled=True),
        lax.all_gather(values, "seq", axis=1, tiled=True),
    )
    key_whole = to_heads(gathered[0][0])
    value_whole = to_heads(gathered[1][0])
    row_stats = over_rows(stats_step, stats_init, (key_whole,), 0)
    log_total = row_stats[0] + jnp.log(row_stats[1])

    def output_step(running, sliced, key_seg):
        scores = query_scores(sliced[0], key_seg)
        soft_rounded = jnp.exp(scores - log_total[:, :, None]).astype(jnp.bfloat16)
        return running + jnp.einsum(
            "hqk,hkd->hqd", soft_rounded, sliced[1], preferred_element_type=jnp.float32
        )

    frame_zeros = jnp.zeros((local_heads, frames, HDIM), jnp.float32)
    attended_sum = over_rows(output_step, frame_zeros, (key_whole, value_whole), 0)
    attended_heads = attended_sum.astype(jnp.bfloat16)
    attended = from_heads(attended_heads)
    padded = extended(attended[None], (("seq", 1),), HALF)
    padded_wide = padded[0].astype(jnp.float32)
    pad_positions = offset - HALF + jnp.arange(frames + 2 * HALF, dtype=jnp.int32)
    inside = jnp.logical_and(pad_positions >= 0, pad_positions < length_all)
    pad_seg = jnp.where(inside, segment_of(pad_positions), -1)
    conv_pre = jnp.zeros((frames, channels), jnp.float32)
    for tap_index in range(KERNEL):
        tap_mask = (pad_seg[tap_index : tap_index + frames] == own_seg)[:, None]
        conv_pre = conv_pre + jnp.where(
            tap_mask, conv_weight[tap_index] * padded_wide[tap_index : tap_index + frames], 0.0
        )
    gate_value = jax.nn.sigmoid(conv_pre)
    mixed = (conv_pre * gate_value).astype(jnp.bfloat16)
    conv_grad = (
        cotangent[0].astype(jnp.float32) * gate_value * (1.0 + conv_pre * (1.0 - gate_value))
    ).astype(jnp.bfloat16)
    padded_grad = extended(conv_grad[None], (("seq", 1),), HALF)
    grad_wide = padded_grad[0].astype(jnp.float32)
    conv_grad_wide = conv_grad.astype(jnp.float32)
    grad_attended = jnp.zeros((frames, channels), jnp.float32)
    kernel_rows = []
    for tap_index in range(KERNEL):
        back_start = 2 * HALF - tap_index
        back_mask = (pad_seg[back_start : back_start + frames] == own_seg)[:, None]
        grad_attended = grad_attended + jnp.where(
            back_mask, conv_weight[tap_index] * grad_wide[back_start : back_start + frames], 0.0
        )
        tap_mask = (pad_seg[tap_index : tap_index + frames] == own_seg)[:, None]
        product = conv_grad_wide * padded_wide[tap_index : tap_index + frames]
        kernel_rows.append(jnp.sum(jnp.where(tap_mask, product, 0.0), axis=0))
    grad_kernel = lax.psum(jnp.stack(kernel_rows), ("dp", "seq"))
    grad_attended = grad_attended.astype(jnp.bfloat16)
    g_heads = to_heads(grad_attended)
    row_delta = jnp.sum(g_heads.astype(jnp.float32) * attended_heads.astype(jnp.float32), axis=2)

    def query_grad_step(running, sliced, key_seg):
        key_block = sliced[0]
        value_block = sliced[1]
        soft_weights = jnp.exp(query_scores(key_block, key_seg) - log_total[:, :, None])
        slopes = jnp.einsum(
            "hqd,hkd->hqk", g_heads, value_block, preferred_element_type=jnp.float32
        )
        mixed_grad = (soft_weights * (slopes - row_delta[:, :, None])).astype(jnp.bfloat16)
        return running + jnp.einsum(
            "hqk,hkd->hqd", mixed_grad, key_block, preferred_element_type=jnp.float32
        )

    grad_query = over_rows(query_grad_step, frame_zeros, (key_whole, value_whole), 0)

    def key_grad_step(running, sliced, query_seg):
        grad_key_now, grad_value_now = running
        query_block = sliced[0]
        grad_block = sliced[1]
        total_block = sliced[2]
        delta_block = sliced[3]
        raw_scores = (
            jnp.einsum("hqd,hkd->hqk", query_block, k_heads, preferred_element_type=jnp.float32)
            * score_scale
        )
        scores = jnp.where(
            (query_seg[:, None] == own_seg[None, :])[None], raw_scores, NEGATIVE_FILL
        )
        soft_weights = jnp.exp(scores - total_block[:, :, None])
        grad_value_new = grad_value_now + jnp.einsum(
            "hqk,hqd->hkd",
            soft_weights.astype(jnp.bfloat16),
            grad_block,
            preferred_element_type=jnp.float32,
        )
        slopes = jnp.einsum("hqd,hkd->hqk", grad_block, v_heads, preferred_element_type=jnp.float32)
        mixed_grad = (soft_weights * (slopes - delta_block[:, :, None])).astype(jnp.bfloat16)
        grad_key_new = grad_key_now + jnp.einsum(
            "hqk,hqd->hkd", mixed_grad, query_block, preferred_element_type=jnp.float32
        )
        return (grad_key_new, grad_value_new)

    all_totals, all_deltas = (
        lax.all_gather(log_total[None], "seq", axis=2, tiled=True),
        lax.all_gather(row_delta[None], "seq", axis=2, tiled=True),
    )
    member = (
        lax.all_gather(queries, "seq", axis=1, tiled=True),
        lax.all_gather(grad_attended[None], "seq", axis=1, tiled=True),
    )
    totals_piece = all_totals[0]
    deltas_piece = all_deltas[0]
    grad_key, grad_value = over_rows(
        key_grad_step,
        (frame_zeros, frame_zeros),
        (to_heads(member[0][0]), to_heads(member[1][0]), totals_piece, deltas_piece),
        jnp.int32(0),
    )
    grad_queries = from_heads(grad_query * score_scale).astype(jnp.bfloat16)[None]
    grad_keys = from_heads(grad_key * score_scale).astype(jnp.bfloat16)[None]
    grad_values = from_heads(grad_value).astype(jnp.bfloat16)[None]
    return (mixed[None], grad_queries, grad_keys, grad_values, grad_kernel)


LANES = 128
PAD = 16
VMEM = pltpu.VMEM
MIB = 1024 * 1024


def mm(left, right):
    return lax.dot_general(
        left, right, (((1,), (0,)), ((), ())), preferred_element_type=jnp.float32
    )


def mm_nt(left, right):
    return lax.dot_general(
        left, right, (((1,), (1,)), ((), ())), preferred_element_type=jnp.float32
    )


def rows_at(block, frames):
    return pl.ds(pl.multiple_of(block * frames, frames), frames)


def lanes_at(block):
    return pl.ds(pl.multiple_of(block * LANES, LANES), LANES)


def late_order(ranks):
    middle = ranks // 2
    return [step for step in range(ranks - 1, 0, -1) if step != middle] + [middle]


def pack_kernel(ranks, q_ref, k_ref, v_ref, c_ref, *rest):
    outs, sems = rest[:-1], rest[-1]
    me = lax.axis_index("seq")
    pairs = []
    for step in range(ranks - 1, 0, -1):
        for place, source in enumerate((q_ref, k_ref, v_ref)):
            pairs.append((source.at[0, :, lanes_at(me ^ step)], outs[step - 1].at[place]))
        pairs.append((c_ref.at[0, :, lanes_at(me ^ step)], outs[ranks + step - 2]))
    for place, source in enumerate((q_ref, k_ref, v_ref, c_ref)):
        pairs.append((source.at[0, :, lanes_at(me)], outs[-1].at[place]))
    run_copies(pairs, sems)


def run_copies(pairs, sems, meanwhile=None):
    copies = [
        pltpu.make_async_copy(source, target, sems.at[number])
        for number, (source, target) in enumerate(pairs)
    ]
    for copy in copies:
        copy.start()
    if meanwhile is not None:
        meanwhile()
    for copy in copies:
        copy.wait()


def mask_kernel(length, lens_ref, *refs):
    col_ref, row_ref, after_ref, before_ref = refs[-4:]
    count = (len(refs) - 4) // 2
    for source, target in zip(refs[:count], refs[count:]):
        target[...] = source[...]
    ends = []
    running = jnp.int32(0)
    for number in range(lens_ref.shape[1]):
        running = running + lens_ref[0, number]
        ends.append(running)
    row_time = lax.broadcasted_iota(jnp.int32, row_ref.shape, 1)
    row_first = jnp.zeros(row_ref.shape, jnp.int32)
    for end in ends:
        row_first = jnp.where(row_time >= end, end, row_first)
    row_ref[...] = row_first
    chunk = 64

    def some_rows(number, carry):
        base = pl.multiple_of(number * chunk, chunk)
        time = base + lax.broadcasted_iota(jnp.int32, (chunk, LANES), 0)
        first = jnp.zeros((chunk, LANES), jnp.int32)
        last = jnp.full((chunk, LANES), length, jnp.int32)
        for end in ends:
            first = jnp.where(time >= end, end, first)
        for end in reversed(ends):
            last = jnp.where(time < end, end, last)
        rows = pl.ds(base, chunk)
        col_ref[rows, :] = first
        after_ref[rows, :] = last - 1 - time
        before_ref[rows, :] = time - first
        return carry

    lax.fori_loop(0, length // chunk, some_rows, 0, unroll=True)


def forward_kernel(ranks, frames, *refs):
    recvs = refs[: ranks - 1]
    own_ref, col_ref, row_ref, span_ref, w_ref = refs[ranks - 1 : ranks + 4]
    soft_ref, att_ref, pre_ref, q_ref, k_t_ref, v_ref = refs[ranks + 4 : ranks + 10]
    att_t_ref, k_full, q_full, w_own, w_sem = refs[ranks + 10 :]
    me = lax.axis_index("seq")
    length = ranks * frames
    copy = pltpu.make_async_copy(w_ref.at[:, lanes_at(me)], w_own, w_sem)
    copy.start()
    for place, target in enumerate((q_full, k_full, v_ref)):
        target[rows_at(me, frames), :] = own_ref[place]
        for step in range(1, ranks):
            target[rows_at(me ^ step, frames), :] = recvs[ranks - 1 - step][place]
    heads = LANES // HDIM
    lane_head = lax.broadcasted_iota(jnp.int32, (1, LANES), 1) // HDIM
    scaled = q_full[...].astype(jnp.float32) * (1.0 / math.sqrt(HDIM))
    for head in range(heads):
        q_ref[head] = jnp.where(lane_head == head, scaled, 0.0).astype(jnp.bfloat16)
    k_t_ref[...] = k_full[...].astype(jnp.float32).T.astype(jnp.bfloat16)
    v_t = v_ref[...].astype(jnp.float32).T.astype(jnp.bfloat16)
    wide = 512
    for head in range(heads):
        for start in range(0, length, wide):
            cols = slice(start, start + wide)
            raw = mm_nt(k_full[...], q_ref[head, cols, :])
            same = jnp.concatenate([col_ref[...]] * (wide // LANES), axis=1) == row_ref[0:1, cols]
            scores = jnp.where(same, raw, NEGATIVE_FILL)
            top = jnp.max(scores, axis=0, keepdims=True)
            powers = jnp.exp(scores - top)
            share = 1.0 / jnp.sum(powers, axis=0, keepdims=True)
            soft = (powers * share).astype(jnp.bfloat16)
            soft_ref[head, :, cols] = soft
            rows = slice(head * HDIM, (head + 1) * HDIM)
            att_t_ref[rows, cols] = mm(v_t[rows], soft).astype(jnp.bfloat16).astype(jnp.float32)
    zeros = jnp.zeros((PAD, LANES), jnp.float32)
    att_ref[0:PAD, :] = zeros
    att_ref[PAD : PAD + length, :] = att_t_ref[...].T
    att_ref[PAD + length :, :] = zeros
    copy.wait()

    chunk = 64

    def some_rows(number, carry):
        base = pl.multiple_of(number * chunk, chunk)
        rows = pl.ds(base, chunk)
        total = jnp.zeros((chunk, LANES), jnp.float32)
        for tap in range(KERNEL):
            total = total + w_own[tap : tap + 1, :] * masked(att_ref, base, chunk, tap - HALF, span_ref)
        pre_ref[rows, :] = total
        return carry

    lax.fori_loop(0, length // chunk, some_rows, 0, unroll=True)


def span_kernel(after_ref, before_ref, span_ref):
    chunk = 64

    def some_rows(number, carry):
        rows = pl.ds(pl.multiple_of(number * chunk, chunk), chunk)
        after, before = after_ref[rows, :], before_ref[rows, :]
        for tap in range(KERNEL):
            off = tap - HALF
            inside = after >= off if off > 0 else before >= -off
            span_ref[tap, rows, :] = jnp.where(inside, 1.0, 0.0)
        return carry

    lax.fori_loop(0, after_ref.shape[0] // chunk, some_rows, 0)


def masked(source, base, chunk, off, span_ref):
    piece = source[pl.ds(base + (PAD + off), chunk), :]
    return piece * span_ref[HALF + off, pl.ds(base, chunk), :] if off else piece


def taps_kernel(ranks, frames, *refs):
    cots = dict(zip(late_order(ranks), refs))
    own_ref, att_ref, pre_ref, span_ref = refs[ranks - 1 : ranks + 3]
    mixed_ref, grad_pad, taps_ref, cot, tap_sum = refs[ranks + 3 :]
    me = lax.axis_index("seq")
    length = ranks * frames
    cot[rows_at(me, frames), :] = own_ref[3]
    for step in range(1, ranks):
        cot[rows_at(me ^ step, frames), :] = cots[step][...]
    zeros = jnp.zeros((PAD, LANES), jnp.float32)
    grad_pad[0:PAD, :] = zeros
    grad_pad[PAD + length :, :] = zeros
    tap_sum[...] = jnp.zeros(tap_sum.shape, jnp.float32)
    chunk = 64

    def some_rows(number, carry):
        base = pl.multiple_of(number * chunk, chunk)
        rows = pl.ds(base, chunk)
        pre = pre_ref[rows, :]
        gate = jax.nn.sigmoid(pre)
        mixed_ref[rows, :] = (pre * gate).astype(jnp.bfloat16)
        conv_grad = cot[rows, :].astype(jnp.float32) * gate * (1.0 + pre * (1.0 - gate))
        conv_grad = conv_grad.astype(jnp.bfloat16).astype(jnp.float32)
        grad_pad[pl.ds(base + PAD, chunk), :] = conv_grad
        for tap in range(KERNEL):
            part = conv_grad * masked(att_ref, base, chunk, tap - HALF, span_ref)
            tap_sum[tap] = tap_sum[tap] + jnp.sum(part.reshape(chunk // 8, 8, LANES), axis=0)
        return carry

    lax.fori_loop(0, length // chunk, some_rows, 0, unroll=True)
    taps_ref[...] = jnp.sum(tap_sum[...], axis=1)


def backward_kernel(soft_ref, att_ref, grad_pad, span_ref, q_ref, k_t_ref, v_ref, w_ref, *refs):
    res_q, res_k, res_v, g_att, grad_t, w_own, w_sem = refs
    length = v_ref.shape[0]
    copy = pltpu.make_async_copy(w_ref.at[:, lanes_at(lax.axis_index("seq"))], w_own, w_sem)
    copy.start()
    copy.wait()
    chunk = 64

    def some_rows(number, carry):
        base = pl.multiple_of(number * chunk, chunk)
        rows = pl.ds(base, chunk)
        total = jnp.zeros((chunk, LANES), jnp.float32)
        for tap in range(KERNEL):
            total = total + w_own[tap : tap + 1, :] * masked(grad_pad, base, chunk, HALF - tap, span_ref)
        g_att[rows, :] = total.astype(jnp.bfloat16)
        return carry

    lax.fori_loop(0, length // chunk, some_rows, 0, unroll=True)
    heads = LANES // HDIM
    lane_head = lax.broadcasted_iota(jnp.int32, (1, LANES), 1) // HDIM
    g_wide = g_att[...].astype(jnp.float32)
    products_t = (g_wide * att_ref[PAD : PAD + length, :]).T
    grad_v = jnp.zeros((length, LANES), jnp.float32)
    grad_k = jnp.zeros((length, LANES), jnp.float32)
    for head in range(heads):
        rows = slice(head * HDIM, (head + 1) * HDIM)
        g_head = jnp.where(lane_head == head, g_wide, 0.0).astype(jnp.bfloat16)
        delta = jnp.sum(products_t[rows], axis=0, keepdims=True)
        soft = soft_ref[head]
        slopes = mm_nt(v_ref[...], g_head)
        mixed_grad = (soft.astype(jnp.float32) * (slopes - delta)).astype(jnp.bfloat16)
        grad_v = grad_v + mm(soft, g_head)
        grad_k = grad_k + mm(mixed_grad, q_ref[head])
        grad_t[rows, :] = mm(k_t_ref[rows, :], mixed_grad) * (1.0 / math.sqrt(HDIM))
    res_k[...] = grad_k.astype(jnp.bfloat16)
    res_v[...] = grad_v.astype(jnp.bfloat16)
    res_q[...] = grad_t[...].T.astype(jnp.bfloat16)


def block_kernel(steps, frames, *refs):
    sources, tap_refs, outs = refs[:4], refs[4 : -len(steps)], refs[-len(steps) :]
    me = lax.axis_index("seq")
    taps = tap_refs[0][...]
    for other in tap_refs[1:]:
        taps = taps + other[...]
    for step, out in zip(steps, outs):
        rows = rows_at(me ^ step, frames)
        for place, source in enumerate(sources):
            out[place * frames : (place + 1) * frames, :] = source[rows, :]
        out[4 * frames :, :] = taps.astype(jnp.bfloat16)


def spread_kernel(ranks, frames, *refs):
    blocks = refs[:ranks]
    targets, taps_ref = refs[ranks : ranks + 4], refs[ranks + 4]
    me = lax.axis_index("seq")
    for step in range(ranks):
        lanes = lanes_at(me ^ step)
        for place, target in enumerate(targets):
            target[0, :, lanes] = blocks[step][place * frames : (place + 1) * frames, :]
        taps = blocks[step][4 * frames :, :].astype(jnp.float32)
        taps_ref[:, lanes] = taps[:KERNEL]


def cost(flops, moved):
    return pl.CostEstimate(flops=flops, bytes_accessed=moved, transcendentals=0)


def on_device_heads(queries, keys, values, cotangent, conv_weight, rec_lengths):
    ranks = lax.axis_size("seq")
    frames = queries.shape[1]
    length = ranks * frames
    heads = LANES // HDIM
    bf16, f32, i32 = jnp.bfloat16, jnp.float32, jnp.int32
    struct = jax.ShapeDtypeStruct
    hbm = pl.BlockSpec(memory_space=pltpu.HBM)
    anywhere = pl.BlockSpec(memory_space=pl.ANY)
    vmem = pl.BlockSpec(memory_space=VMEM)
    smem = pl.BlockSpec(memory_space=pltpu.SMEM)
    params = pltpu.CompilerParams(vmem_limit_bytes=24 * MIB)
    taps = KERNEL + 1

    *sends, own = pl.pallas_call(
        functools.partial(pack_kernel, ranks),
        out_shape=[struct((3, frames, LANES), bf16)] * (ranks - 1)
        + [struct((frames, LANES), bf16)] * (ranks - 1)
        + [struct((4, frames, LANES), bf16)],
        in_specs=[hbm] * 4,
        out_specs=[vmem] * (2 * ranks - 1),
        scratch_shapes=[pltpu.SemaphoreType.DMA((4 * ranks,))],
        compiler_params=pltpu.CompilerParams(vmem_limit_bytes=54672 * 1024),
        name="pack",
    )(queries, keys, values, cotangent)

    def swap(array, step):
        return lax.ppermute(array, "seq", [(rank, rank ^ step) for rank in range(ranks)])

    order = list(range(ranks - 1, 0, -1))
    received = {step: swap(sends[step - 1], step) for step in order}

    *cot_sends, col, row, after, before = pl.pallas_call(
        functools.partial(mask_kernel, length),
        out_shape=[struct((frames, LANES), bf16)] * (ranks - 1)
        + [
            struct((length, LANES), i32),
            struct((8, length), i32),
            struct((length, LANES), i32),
            struct((length, LANES), i32),
        ],
        in_specs=[smem] + [vmem] * (ranks - 1),
        out_specs=[vmem] * (ranks + 3),
        compiler_params=params,
        cost_estimate=cost(4 * MIB, MIB),
        name="masks",
    )(rec_lengths, *sends[ranks - 1 :])
    cots = {step: swap(cot_sends[step - 1], step) for step in order}

    span = pl.pallas_call(
        span_kernel,
        out_shape=struct((KERNEL, length, LANES), f32),
        in_specs=[vmem] * 2,
        out_specs=vmem,
        compiler_params=params,
        cost_estimate=cost(400 * MIB, 3 * MIB),
        name="spans",
    )(after, before)

    soft, att, pre, q_heads, k_t, v_full = pl.pallas_call(
        functools.partial(forward_kernel, ranks, frames),
        out_shape=[
            struct((heads, length, length), bf16),
            struct((length + 2 * PAD, LANES), f32),
            struct((length, LANES), f32),
            struct((heads, length, LANES), bf16),
            struct((LANES, length), bf16),
            struct((length, LANES), bf16),
        ],
        in_specs=[vmem] * (ranks + 3) + [anywhere],
        out_specs=[vmem] * 6,
        scratch_shapes=[
            VMEM((LANES, length), f32),
            VMEM((length, LANES), bf16),
            VMEM((length, LANES), bf16),
            VMEM((KERNEL, LANES), f32),
            pltpu.SemaphoreType.DMA,
        ],
        compiler_params=params,
        cost_estimate=cost(400 * MIB, 3 * MIB),
        name="forward",
    )(*[received[step] for step in order], own, col, row, span, conv_weight)

    mixed, grad_pad, own_taps = pl.pallas_call(
        functools.partial(taps_kernel, ranks, frames),
        out_shape=[
            struct((length, LANES), bf16),
            struct((length + 2 * PAD, LANES), f32),
            struct((taps, LANES), f32),
        ],
        in_specs=[vmem] * (ranks + 3),
        out_specs=[vmem] * 3,
        scratch_shapes=[VMEM((length, LANES), bf16), VMEM((taps, 8, LANES), f32)],
        compiler_params=params,
        cost_estimate=cost(400 * MIB, 3 * MIB),
        name="taps",
    )(*[cots[step] for step in late_order(ranks)], own, att, pre, span)

    copies = lax.axis_size("dp")
    part_taps = [own_taps] + [
        lax.ppermute(own_taps, "dp", [(one, (one + shift) % copies) for one in range(copies)])
        for shift in range(1, copies)
    ]

    results = pl.pallas_call(
        backward_kernel,
        out_shape=[struct((length, LANES), bf16)] * 3,
        in_specs=[vmem] * 7 + [anywhere],
        out_specs=[vmem] * 3,
        scratch_shapes=[
            VMEM((length, LANES), bf16),
            VMEM((LANES, length), f32),
            VMEM((KERNEL, LANES), f32),
            pltpu.SemaphoreType.DMA,
        ],
        compiler_params=params,
        cost_estimate=cost(800 * MIB, 3 * MIB),
        name="backward",
    )(soft, att, grad_pad, span, q_heads, k_t, v_full, conv_weight)

    def blocks_of(steps):
        return pl.pallas_call(
            functools.partial(block_kernel, steps, frames),
            out_shape=[struct((4 * frames + taps, LANES), bf16)] * len(steps),
            in_specs=[vmem] * (4 + copies),
            out_specs=[vmem] * len(steps),
            compiler_params=params,
            cost_estimate=cost(MIB, MIB),
            name="blocks",
        )(mixed, *results, *part_taps)

    half = ranks // 2
    far = blocks_of(list(range(half, ranks)))
    near = blocks_of(list(range(half)))
    back = {step: swap(far[step - half], step) for step in range(half, ranks)}
    back |= {step: swap(near[step], step) for step in range(1, half)}
    back[0] = near[0]

    return pl.pallas_call(
        functools.partial(spread_kernel, ranks, frames),
        out_shape=[struct(queries.shape, bf16)] * 4 + [struct(conv_weight.shape, f32)],
        in_specs=[vmem] * ranks,
        out_specs=[vmem] * 5,
        compiler_params=params,
        name="spread",
    )(*[back[step] for step in range(ranks)])


def on_device_any(queries, keys, values, cotangent, conv_weight, rec_lengths):
    ranks = lax.axis_size("seq")
    frames, channels = queries.shape[1], queries.shape[2]
    fits = channels == ranks * LANES and ranks & (ranks - 1) == 0 and frames % LANES == 0
    if fits and ranks > 1 and ranks * frames <= 1024 and lax.axis_size("dp") == 2:
        return on_device_heads(queries, keys, values, cotangent, conv_weight, rec_lengths)
    return on_device(queries, keys, values, cotangent, conv_weight, rec_lengths)


def solution(mesh):
    placed = (
        P(("groups", "dp"), "seq", "mp"),
        P(("groups", "dp"), "seq", "mp"),
        P(("groups", "dp"), "seq", "mp"),
        P(("groups", "dp"), "seq", "mp"),
        P(None, "mp"),
        P(("groups", "dp"), None),
    )
    return jax.shard_map(
        on_device_any,
        mesh=mesh,
        in_specs=placed,
        out_specs=(
            P(("groups", "dp"), "seq", "mp"),
            P(("groups", "dp"), "seq", "mp"),
            P(("groups", "dp"), "seq", "mp"),
            P(("groups", "dp"), "seq", "mp"),
            P("groups", "mp"),
        ),
        check_vma=False,
    )
```
